32 devices in a mesh: batch: 8 (over z, x), mp: 4 (over y, core).
Axes of the slice: x: 2, y: 2, z: 4, core: 2. Of those that a mesh axis runs over, the one named last changes fastest.
Arguments:
- tokens: bfloat16 [4096, 768], P(('batch', 'mp')), may hold values from -6 to 6
- cotangent: bfloat16 [4096, 768], P(('batch', 'mp')), may hold values from -6 to 6
- seq_lengths: int32 [8, 3], P('batch'), may hold values from 0 to 512, as said below
- joined_qkv: bfloat16 [2, 768, 3, 768], P(None, 'batch', None, 'mp'), may hold values from -0.21875 to 0.21875
- attn_proj: bfloat16 [2, 768, 768], P(None, 'mp', 'batch'), may hold values from -0.875 to 0.875
- mlp_up: bfloat16 [2, 768, 3072], P(None, 'batch', 'mp'), may hold values from -0.21875 to 0.21875
- mlp_down: bfloat16 [2, 3072, 768], P(None, 'mp', 'batch'), may hold values from -0.109375 to 0.109375
- query_map: bfloat16 [2, 12, 64, 64], P(None, 'mp'), may hold values from -1.5 to 1.5
- query_bias: bfloat16 [2, 12, 64], P(None, 'mp'), may hold values from -4 to 4
- key_map: bfloat16 [2, 12, 64, 64], P(None, 'mp'), may hold values from -1.5 to 1.5
- key_bias: bfloat16 [2, 12, 64], P(None, 'mp'), may hold values from -4 to 4
Outputs:
- layer_out: bfloat16 [4096, 768], P(('batch', 'mp'))
- input_grad: bfloat16 [4096, 768], P(('batch', 'mp'))
- query_map_grad: float32 [2, 12, 64, 64], P(None, 'mp')
- query_bias_grad: float32 [2, 12, 64], P(None, 'mp')
- key_map_grad: float32 [2, 12, 64, 64], P(None, 'mp')
- key_bias_grad: float32 [2, 12, 64], P(None, 'mp')
The draws below stay inside these ranges and needn't reach their ends.
Inputs may be any that keep to these rules, and one draw needn't show every extreme that they name: `seq_lengths`: row g lists the true lengths of the sequences packed into batch group g, in the order in which they lie from slot 0, each padded to a multiple of 64; the padded lengths of a row sum to at most 512; zeros mark unused entries and come last.
All inputs are finite; a program needn't handle non-finite values.
Results may differ from the reference program's by a relative error of at most 0.03.
Values may be sent and summed in bfloat16 or wider, within the bound.
A program may use at most 128 MiB of HBM per device.

```python
import jax
import jax.numpy as jnp
from jax import lax

D = 768
HEADS = 12
HD = 64
MLP = 3072
SPAN = 64
LAYERS = 2
TOK_GRP = 512
TOKENS = 4096
MAXSEQ = 3
N_BATCH = 8


def draw_seq_lengths(key, part):
    key = jax.random.fold_in(key, 11)
    keys_all = jax.random.split(key, 5)
    blocks = TOK_GRP // SPAN
    groups = jnp.arange(N_BATCH, dtype=jnp.int32)
    long_blocks = jax.random.randint(keys_all[0], (N_BATCH,), 3 * blocks // 4 + 1, blocks + 1)
    full_group = jax.random.randint(keys_all[1], (), 0, N_BATCH)
    long_blocks = jnp.where(groups == full_group, blocks, long_blocks)
    trims = jax.random.randint(keys_all[2], (N_BATCH,), 0, SPAN)
    trims = jnp.where(groups == full_group, 0, trims)
    long_len = long_blocks * SPAN - trims
    spare = blocks - long_blocks
    short_blocks = jax.random.randint(keys_all[3], (N_BATCH, MAXSEQ - 1), 2, 4)
    reach = jnp.cumsum(short_blocks, axis=1)
    short_trims = jax.random.randint(keys_all[4], (N_BATCH, MAXSEQ - 1), 0, SPAN)
    short_len = jnp.where(reach <= spare[:, None], short_blocks * SPAN - short_trims, 0)
    return jnp.concatenate([long_len[:, None], short_len], axis=1).astype(jnp.int32)


def block_levels(stream_key, shape, pieces, least, high):
    gain = 1.0
    for position, blocks in pieces:
        heights = jax.random.uniform(jax.random.fold_in(jax.random.fold_in(stream_key, 6), position), (blocks,), jnp.float32, least / len(pieces), high / len(pieces))
        gain = gain * jnp.repeat(jnp.exp(heights), shape[position] // blocks).reshape((-1,) + (1,) * (len(shape) - 1 - position))
    return gain


def normal_values(key, shape, deviation, most, shards=(), held_as=jnp.bfloat16):
    level = block_levels(key, shape, shards, -0.22, 0.18) if shards else 1.0
    entries = jax.random.normal(key, shape, jnp.float32) * deviation * level
    return jnp.minimum(jnp.maximum(entries, -most), most).astype(held_as)


def setup_inputs(seed: int = 0) -> dict:
    seeds = jax.random.split(jax.random.key(seed), 12)
    tokens = normal_values(seeds[0], (TOKENS, D), 1.0, 6.0, ((0, 32),))
    cotangent = normal_values(seeds[1], (TOKENS, D), 1.0, 6.0, ((0, 32),))
    seq_lengths = draw_seq_lengths(jax.random.fold_in(seeds[11], 71), 0)
    joined_qkv = normal_values(seeds[3], (LAYERS, D, 3, D), D ** -0.5, 0.21875, ((1, 8), (3, 4)))
    attn_proj = normal_values(seeds[4], (LAYERS, D, D), (D // 16) ** -0.5, 0.875, ((1, 4), (2, 8)))
    mlp_up = normal_values(seeds[5], (LAYERS, D, MLP), D ** -0.5, 0.21875, ((1, 8), (2, 4)))
    mlp_down = normal_values(seeds[6], (LAYERS, MLP, D), MLP ** -0.5, 0.109375, ((1, 4), (2, 8)))
    query_map = normal_values(seeds[7], (LAYERS, HEADS, HD, HD), (HD // 4) ** -0.5, 1.5, ((1, 4),))
    query_bias = normal_values(seeds[8], (LAYERS, HEADS, HD), 1.0, 4.0, ((1, 4),))
    key_map = normal_values(seeds[9], (LAYERS, HEADS, HD, HD), (HD // 4) ** -0.5, 1.5, ((1, 4),))
    key_bias = normal_values(seeds[10], (LAYERS, HEADS, HD), 1.0, 4.0, ((1, 4),))
    return {"tokens": tokens, "cotangent": cotangent, "seq_lengths": seq_lengths, "joined_qkv": joined_qkv, "attn_proj": attn_proj, "mlp_up": mlp_up, "mlp_down": mlp_down, "query_map": query_map, "query_bias": query_bias, "key_map": key_map, "key_bias": key_bias}


precise = lax.Precision.HIGHEST
epsilon = 1e-05

@jax.custom_vjp
def low(v):
    return lax.optimization_barrier(v.astype(jnp.bfloat16)).astype(jnp.float32)

@jax.custom_vjp
def low_back(v):
    return v

def low_keep(v):
    return (low(v), None)

def low_pass(kept, grad):
    return (grad,)

def back_keep(v):
    return (v, None)

def back_low(kept, grad):
    return (low(grad),)
low.defvjp(low_keep, low_pass)
low_back.defvjp(back_keep, back_low)

def layout(lengths, extent):
    padded = (lengths + SPAN - 1) // SPAN * SPAN
    endings = jnp.cumsum(padded).astype(jnp.int32)
    starts = endings - padded
    places = jnp.arange(extent, dtype=jnp.int32)
    inside = (places[:, None] >= starts[None, :]) & (places[:, None] < (starts + lengths)[None, :])
    validity = lax.optimization_barrier(jnp.sum(inside.astype(jnp.float32), axis=1))
    owners = lax.optimization_barrier(jnp.sum((places[:, None] >= endings[None, :]).astype(jnp.int32), axis=1))
    block_owner = owners[::SPAN]
    indices = jnp.arange(extent // SPAN, dtype=jnp.int32)
    earlier = (indices[None, :] < indices[:, None]) & (block_owner[None, :] == block_owner[:, None])
    return (validity, earlier.astype(jnp.float32))

def layer_norm(values):
    centered = values - lax.optimization_barrier(jnp.mean(values, axis=-1, keepdims=True))
    variance = lax.optimization_barrier(jnp.mean(centered * centered, axis=-1, keepdims=True))
    return centered * lax.rsqrt(variance + epsilon)

def feature_map(projected, weights, offsets):
    mapped = jnp.einsum('thd,hde->the', projected, weights, precision=precise) + offsets
    return jax.nn.softmax(jnp.concatenate([mapped, -mapped], axis=-1), axis=-1)

def attention(queries, key_feat, values, validity, earlier):
    blocks = queries.shape[0] // SPAN
    queries = queries.reshape(blocks, SPAN, queries.shape[1], -1)
    key_feat = key_feat.reshape(blocks, SPAN, key_feat.shape[1], -1)
    values = values.reshape(blocks, SPAN, values.shape[1], -1)
    lower_mask = jnp.tril(jnp.ones((SPAN, SPAN), jnp.float32))
    scores = low_back(jnp.einsum('cihf,cjhf->chij', queries, key_feat, precision=precise) * lower_mask)
    states = low_back(jnp.einsum('cjhf,cjhd->chfd', key_feat, values, precision=precise))
    key_sums = lax.optimization_barrier(jnp.sum(key_feat, axis=1))
    carried = jnp.einsum('ce,ehfd->chfd', earlier, states, precision=precise)
    carried_sums = jnp.einsum('ce,ehf->chf', earlier, key_sums, precision=precise)
    numerator = jnp.einsum('chij,cjhd->cihd', low(scores), values, precision=precise)
    numerator = numerator + jnp.einsum('cihf,chfd->cihd', queries, low(carried), precision=precise)
    numerator = low_back(numerator)
    row_mask = validity.reshape(blocks, SPAN, 1)
    denominator = jnp.transpose(lax.optimization_barrier(jnp.sum(scores, axis=-1)), (0, 2, 1))
    denominator = denominator + jnp.einsum('cihf,chf->cih', queries, carried_sums, precision=precise) + (1.0 - row_mask)
    output = row_mask[..., None] * numerator / denominator[..., None]
    return output.reshape(blocks * SPAN, -1)

def layer(residual, frozen, trained, validity, earlier):
    joined_matrix, out_matrix, upward, downward = frozen
    query_weights, query_offsets, key_weights, key_offsets = trained
    width = residual.shape[1]
    head_count = query_weights.shape[0]
    normed = low(layer_norm(residual))
    mixed = low_back(jnp.dot(normed, joined_matrix.reshape(width, -1), precision=precise))
    mixed = mixed.reshape(mixed.shape[0], 3, head_count, -1)
    queries = low(feature_map(mixed[:, 0], query_weights, query_offsets))
    key_feat = low(feature_map(mixed[:, 1], key_weights, key_offsets)) * validity[:, None, None]
    values = low(mixed[:, 2])
    attended = low(attention(queries, key_feat, values, validity, earlier))
    middle = residual + low_back(jnp.dot(attended, out_matrix, precision=precise))
    normed_two = low(layer_norm(middle))
    pre_act = low_back(jnp.dot(normed_two, upward, precision=precise))
    activated = low(jax.nn.gelu(pre_act, approximate=True))
    return middle + low_back(jnp.dot(activated, downward, precision=precise))

def group_pass(items, frozen, trained):
    rows_in, cot_rows, lengths = items
    validity, earlier = layout(lengths, rows_in.shape[0])

    def forward(residual, query_weights, query_offsets, key_weights, key_offsets):
        for layer_index in range(LAYERS):
            frozen_now = (frozen[0][layer_index], frozen[1][layer_index], frozen[2][layer_index], frozen[3][layer_index])
            trained_now = (query_weights[layer_index], query_offsets[layer_index], key_weights[layer_index], key_offsets[layer_index])
            residual = layer(residual, frozen_now, trained_now, validity, earlier)
        return residual
    result, pullback = jax.vjp(forward, rows_in.astype(jnp.float32), trained[0], trained[1], trained[2], trained[3])
    gradients = pullback(cot_rows.astype(jnp.float32))
    return (result.astype(jnp.bfloat16), gradients[0].astype(jnp.bfloat16), gradients[1], gradients[2], gradients[3], gradients[4])

def reference(tokens, cotangent, seq_lengths, joined_qkv, attn_proj, mlp_up, mlp_down, query_map, query_bias, key_map, key_bias):
    frozen = (joined_qkv.astype(jnp.float32), attn_proj.astype(jnp.float32), mlp_up.astype(jnp.float32), mlp_down.astype(jnp.float32))
    trained = (query_map.astype(jnp.float32), query_bias.astype(jnp.float32), key_map.astype(jnp.float32), key_bias.astype(jnp.float32))
    width = tokens.shape[1]
    grouped = tokens.reshape(N_BATCH, -1, width)
    cot_grouped = cotangent.reshape(N_BATCH, -1, width)

    def one_group(items):
        return group_pass(items, frozen, trained)
    results = lax.map(one_group, (grouped, cot_grouped, seq_lengths))
    return (results[0].reshape(-1, width), results[1].reshape(-1, width), lax.optimization_barrier(jnp.sum(results[2], axis=0)), lax.optimization_barrier(jnp.sum(results[3], axis=0)), lax.optimization_barrier(jnp.sum(results[4], axis=0)), lax.optimization_barrier(jnp.sum(results[5], axis=0)))
```

```python
import functools

import jax
import jax.numpy as jnp
from jax import lax
from jax.experimental import pallas as pl
from jax.experimental.pallas import tpu as pltpu
from jax.sharding import PartitionSpec as P

SPAN = 64
LAYERS = 2
EPS = 1e-05
F32, BF16 = jnp.float32, jnp.bfloat16
MESH = pl.DeviceIdType.MESH
ATTN, UP, DOWN = 0, 1, 2
CHUNKS = 3 * LAYERS
HD = 64
PAIR = 2 * HD
ROWS = 3 * HD + 16


def nn(a, b):
    return lax.dot_general(a, b, (((1,), (0,)), ((), ())), preferred_element_type=F32)


def nt(a, b):
    return lax.dot_general(a, b, (((1,), (1,)), ((), ())), preferred_element_type=F32)


def tn(a, b):
    return lax.dot_general(a, b, (((0,), (0,)), ((), ())), preferred_element_type=F32)


def moments(x):
    mean = jnp.mean(x, axis=-1, keepdims=True)
    centered = x - mean
    scale = lax.rsqrt(jnp.mean(centered * centered, axis=-1, keepdims=True) + EPS)
    return centered * scale, scale


def norm_back(x, g):
    y, scale = moments(x)
    mean_g = jnp.mean(g, axis=-1, keepdims=True)
    mean_gy = jnp.mean(g * y, axis=-1, keepdims=True)
    return scale * (g - mean_g - y * mean_gy)


GELU_C = 0.7978845608028654
GELU_A = 0.044715


def gelu(x):
    return 0.5 * x * (1.0 + jnp.tanh(GELU_C * (x + GELU_A * x * x * x)))


def gelu_slope(x):
    square = x * x
    t = jnp.tanh(GELU_C * x * (1.0 + GELU_A * square))
    inner = GELU_C * (1.0 + 3.0 * GELU_A * square)
    return 0.5 * (1.0 + t) + 0.5 * x * (1.0 - t * t) * inner


def split(x):
    high = x.astype(BF16)
    return high, (x - high.astype(F32)).astype(BF16)


def stack_rows(entries, rows):
    index = lax.broadcasted_iota(jnp.int32, (rows, entries[0].shape[1]), 0)
    out = jnp.zeros((rows, entries[0].shape[1]), F32)
    for i, entry in enumerate(entries):
        out = jnp.where(index == i, entry, out)
    return out


def body(n_batch, gathers, seq_ref, tok_ref, cot_ref, w_ref, mt_ref,
         out_ref, gin_ref, gq_ref, gqb_ref, gk_ref, gkb_ref,
         G, MT, BD, BIAS, R, MID, PRE, ACT, TQ, PF, ATT, RD, CAR, CS,
         N1, ACC, GRAD, GNH, GDEN, GPK, GV, TG, MASKS, SB, CH, OT,
         GRF, GRB, RB1, ACC2, RB2, DBL,
         own_sem, mt_sem, ex_send, ex_recv, rd_send, rd_recv,
         z_send, z_recv, cross_send, first_recv, last_recv, core_send, core_recv):
    width = tok_ref.shape[1]
    rows = tok_ref.shape[0]
    batch, mp = lax.axis_index("batch"), lax.axis_index("mp")
    yc, cc = mp // 2, mp % 2
    sister = (batch, yc * 2 + 1 - cc)
    across = (batch, (1 - yc) * 2 + cc)
    steps = n_batch.bit_length() - 1

    def partner(k):
        bit = (batch // (1 << k)) % 2
        return (batch + (1 - 2 * bit) * (1 << k), mp)

    def send(src, dst, send_sem, recv_sem, device):
        copy = pltpu.make_async_remote_copy(
            src_ref=src, dst_ref=dst, send_sem=send_sem, recv_sem=recv_sem,
            device_id=device, device_id_type=MESH)
        return copy

    if gathers:
        zc, xc = batch // 2, batch % 2
        x_side = (zc * 2 + 1 - xc, mp)
        z_up = (jnp.minimum(zc + 1, 3) * 2 + xc, mp)
        z_down = (jnp.maximum(zc - 1, 0) * 2 + xc, mp)
        for h in range(2):
            pltpu.make_async_copy(
                w_ref.at[:, h], G.at[:, yc, cc, zc, xc, h], own_sem.at[h]).start()
        greeted = [x_side] + [(((zc + k) % 4) * 2 + xc, mp) for k in (1, 2, 3)]
    else:
        for q in range(CHUNKS):
            pltpu.make_async_copy(w_ref.at[q], G.at[q], own_sem.at[q]).start()
        greeted = [partner(k) for k in range(steps)]
    own_maps = pltpu.make_async_copy(mt_ref, MT.at[yc, cc], mt_sem.at[0])
    own_maps.start()
    greeted += [sister, across]
    barrier = pltpu.get_barrier_semaphore()
    for device in greeted:
        pl.semaphore_signal(barrier, inc=1, device_id=device, device_id_type=MESH)

    row0 = mp * rows
    spans = []
    end = jnp.int32(0)
    for s in range(seq_ref.shape[1]):
        length = seq_ref[0, s]
        spans.append((end, end + length, end + ((length + SPAN - 1) // SPAN) * SPAN))
        end = spans[-1][2]

    def owner(place):
        return sum((place >= stop).astype(jnp.int32) for _, _, stop in spans)

    def owner_at(place):
        return sum(jnp.where(place >= stop, 1, 0) for _, _, stop in spans)

    def same(a, b):
        return jnp.where(owner_at(a) == owner_at(b), 1.0, 0.0).astype(F32)

    row = lax.broadcasted_iota(jnp.int32, (rows, rows), 0) + row0
    col = lax.broadcasted_iota(jnp.int32, (rows, rows), 1) + row0
    own_row, own_col = owner(row), owner(col)
    valid = sum(((row >= a) & (row < b)).astype(F32) for a, b, _ in spans)
    MASKS[0] = ((col <= row) & (own_row == own_col)).astype(F32)
    MASKS[1] = ((row <= col) & (own_row == own_col)).astype(F32)
    MASKS[2] = valid
    came_in = jnp.where(mp > 0, owner_at(row0 - 1), -1)
    MASKS[3] = (own_row == came_in).astype(F32)
    MASKS[4] = (own_row == owner_at(row0 + rows - 1)).astype(F32)
    LOWER, UPPER, VALID, CONT, LAST = range(5)

    def last_of(y, c):
        return (y * 2 + c) * rows + rows - 1

    in_chip = same(last_of(yc, 0), last_of(yc, 1))
    first, second = (cc == 0), (cc == 1)
    f_own = jnp.where(second, 1.0, in_chip)
    f_sis = jnp.where(second, in_chip, 1.0)
    f_a = jnp.where(second, 1.0, 0.0)
    f_b = jnp.where(yc == 1, jnp.where(second, same(last_of(0, 1), last_of(1, 0)), 1.0), 0.0)
    before = same(last_of(0, 1), last_of(1, 0))
    b_own = jnp.where(first, 1.0, before)
    b_sis = jnp.where(first, before, 1.0)
    b_a = jnp.where(first, 1.0, 0.0)
    b_b = jnp.where(yc == 0, jnp.where(first, same(last_of(0, 0), last_of(0, 1)), 1.0), 0.0)

    lane = lax.broadcasted_iota(jnp.int32, (rows, PAIR), 1)
    low = (lane < HD).astype(F32)
    high = 1.0 - low
    left = lane < HD

    x0 = tok_ref[...].astype(F32)
    R[0] = x0
    N1[...] = moments(x0)[0].astype(BF16)

    pl.semaphore_wait(barrier, len(greeted))

    def maps_start():
        own_maps.wait()
        send(MT.at[yc, cc], MT.at[yc, cc], mt_sem.at[1], mt_sem.at[2], across).start()
        send(MT.at[yc, cc], MT.at[yc, cc], mt_sem.at[3], mt_sem.at[4], sister).start()

    def maps_forward():
        send(MT.at[1 - yc, cc], MT.at[1 - yc, cc], mt_sem.at[1], mt_sem.at[2], across).wait()
        send(MT.at[1 - yc, cc], MT.at[1 - yc, cc], mt_sem.at[5], mt_sem.at[6], sister).start()

    def maps_build():
        send(MT.at[yc, cc], MT.at[yc, 1 - cc], mt_sem.at[3], mt_sem.at[4], sister).wait()
        send(MT.at[1 - yc, cc], MT.at[1 - yc, 1 - cc], mt_sem.at[5], mt_sem.at[6], sister).wait()
        half = lax.broadcasted_iota(jnp.int32, (HD, PAIR), 1) < HD
        none = jnp.zeros((HD, PAIR), F32)

        def one(i, carry):
            l, m = i // 4, i % 4
            block = MT[m // 2, m % 2, l].astype(F32)
            for t in range(3):
                pair = block[t * HD:(t + 1) * HD]
                turned = pltpu.roll(pair, HD, 1)
                a = jnp.where(half, pair, -turned)
                b = jnp.where(half, turned, -pair)
                wide = jnp.concatenate(
                    [jnp.concatenate([a, none], 1), jnp.concatenate([none, b], 1)], 0).astype(BF16)
                BD[l, m, t, 0:PAIR] = wide
                BD[l, m, t, PAIR:2 * PAIR] = wide
            BIAS[l, m] = block[3 * HD:3 * HD + 8]
            return carry

        lax.fori_loop(0, 2 * 4, one, 0)

    if gathers:
        def near(h):
            return (x_side, across)[h]

        def far(h):
            return (across, x_side)[h]

        def single(q, h, z):
            return G.at[q, yc, cc, z, xc, h]

        def neighbour(q, h, z):
            return (G.at[q, yc, cc, z, 1 - xc, h], G.at[q, 1 - yc, cc, z, xc, h])[h]

        def pair_of(q, h, z):
            return (G.at[q, yc, cc, z, :, h], G.at[q, :, cc, z, xc, h])[h]

        def other_pair(q, h, z):
            return (G.at[q, 1 - yc, cc, z, :, h], G.at[q, :, cc, z, 1 - xc, h])[h]

        def early(q):
            return q % 3 == 0

        def z_unit(q, h, z):
            return single(q, h, z) if early(q) else pair_of(q, h, z)

        def z_send_on(q, h, z, way, s):
            device = (z_up, z_down)[way]

            @pl.when((zc < 3) if way == 0 else (zc > 0))
            def _():
                send(z_unit(q, h, z), z_unit(q, h, z), z_send.at[q, way, s],
                     z_recv.at[q, h, way, s], device).start()

        def to_near(q, h, z, slot):
            send(single(q, h, z), single(q, h, z), cross_send.at[q, 0], first_recv.at[q, h, slot],
                 near(h)).start()

        def to_far(q, h, z):
            send(pair_of(q, h, z), pair_of(q, h, z), cross_send.at[q, 1], last_recv.at[q, h, z],
                 far(h)).start()

        def to_sister(q, h, ref):
            send(ref, ref, core_send.at[q], core_recv.at[q, h], sister).start()

        def wait_near(q, h, z, slot):
            ref = neighbour(q, h, z)
            send(ref, ref, cross_send.at[q, 0], first_recv.at[q, h, slot], near(h)).wait_recv()

        def wait_far(q, h, z):
            ref = other_pair(q, h, z)
            send(ref, ref, cross_send.at[q, 1], last_recv.at[q, h, z], far(h)).wait_recv()

        def have(q, h, z):
            if early(q):
                to_near(q, h, z, z)
            else:
                to_far(q, h, z)
                to_sister(q, h, pair_of(q, h, z))

        def each_place(s, do):
            pl.when(s == 0)(lambda: do(zc, None))
            pl.when((s > 0) & (zc - s >= 0))(lambda: do(zc - s, 0))
            pl.when((s > 0) & (zc + s <= 3))(lambda: do(zc + s, 1))

        def gather_start(q):
            for h in range(2):
                to_near(q, h, zc, 0)

        def along_z(q, s):
            def step(z, way):
                for h in range(2):
                    if way is None:
                        if not early(q):
                            wait_near(q, h, zc, 0)
                        for w in range(2):
                            z_send_on(q, h, z, w, 0)
                    else:
                        ref = z_unit(q, h, z)
                        send(ref, ref, z_send.at[q, way, s], z_recv.at[q, h, way, s - 1],
                             sister).wait_recv()
                        z_send_on(q, h, z, way, s)
                    have(q, h, z)

            each_place(s, step)

        def across_first(q, s):
            def step(z, way):
                for h in range(2):
                    wait_near(q, h, z, z)
                    to_far(q, h, z)
                    to_sister(q, h, pair_of(q, h, z))

            each_place(s, step)

        def across_last(q, s):
            def step(z, way):
                for h in range(2):
                    wait_far(q, h, z)
                    to_sister(q, h, other_pair(q, h, z))

            each_place(s, step)

        def comm(k, s):
            if k < CHUNKS:
                along_z(k, s)
                if early(k):
                    pl.when(s > 0)(lambda: across_first(k, s - 1))
                    pl.when(s == 3)(lambda: across_first(k, s))
            if k > 0:
                across_last(k - 1, s)

        def ready(q):
            for h in range(2):
                ref = G.at[q, :, 1 - cc, :, :, h]
                send(ref, ref, core_send.at[q], core_recv.at[q, h], sister).wait_recv()

        def drain():
            for q in range(CHUNKS):
                for way in range(2):
                    for s in range(3):
                        ref = G.at[q, 0, 0, 0, 0] if early(q) else G.at[q, 0, 0, 0]

                        @pl.when(((zc < 3) & (zc >= s)) if way == 0 else ((zc > 0) & (zc + s <= 3)))
                        def _():
                            send(ref, ref, z_send.at[q, way, s], z_recv.at[q, 0, way, s],
                                 sister).wait_send()
                ref = G.at[q, 0, 0] if early(q) else G.at[q, 0, 0, 0, 0]
                if early(q):
                    ref = G.at[q, 0, 0, :, 0]
                send(ref, ref, cross_send.at[q, 0], first_recv.at[q, 0, 0], sister).wait_send()
                ref = G.at[q, 0, 0]
                send(ref, ref, cross_send.at[q, 1], last_recv.at[q, 0, 0], sister).wait_send()
                ref = G.at[q, :, 0]
                send(ref, ref, core_send.at[q], core_recv.at[q, 0], sister).wait_send()
    else:
        def gather_start(q):
            pass

        def comm(k, s):
            pass

        def ready(q):
            pltpu.make_async_copy(w_ref.at[q], G.at[q], own_sem.at[q]).wait()

        def drain():
            pass

    def weight(q, m, lanes=None):
        if lanes is None:
            return G[q, m // 2, m % 2].reshape(width, width)
        return G[q, m // 2, m % 2, :, :, :, :, lanes].reshape(width, -1)

    def ex_start(e):
        send(SB.at[e, 0], SB.at[e, 1], ex_send.at[e, 0], ex_recv.at[e, 0], sister).start()

    def add_blocks(a, ca, b, cb):
        a, b = a.astype(F32), b.astype(F32)
        values = ca * a[:3 * HD] + cb * b[:3 * HD]
        sums = (ca * (a[3 * HD:3 * HD + 8] + a[3 * HD + 8:])
                + cb * (b[3 * HD:3 * HD + 8] + b[3 * HD + 8:]))
        return values, sums

    def ex_mid(e, own, sis):
        send(SB.at[e, 0], SB.at[e, 1], ex_send.at[e, 0], ex_recv.at[e, 0], sister).wait()

        def one(i, carry):
            m = 2 * cc + i
            values, sums = add_blocks(SB[e, 0, m], own, SB[e, 1, m], sis)
            CH[e, i, 0:3 * HD] = values.astype(BF16)
            CH[e, i, 3 * HD:] = jnp.concatenate(split(sums), 0)
            return carry

        lax.fori_loop(0, 2, one, 0)
        send(CH.at[e], OT.at[e, cc], ex_send.at[e, 1], ex_recv.at[e, 1], across).start()

    def ex_forward(e):
        send(CH.at[e], OT.at[e, cc], ex_send.at[e, 1], ex_recv.at[e, 1], across).wait()
        send(OT.at[e, cc], OT.at[e, cc], ex_send.at[e, 2], ex_recv.at[e, 2], sister).start()

    def ex_end(e):
        send(OT.at[e, cc], OT.at[e, 1 - cc], ex_send.at[e, 2], ex_recv.at[e, 2], sister).wait()

    def softmax(u):
        e = jnp.exp(u - jnp.max(u, axis=-1, keepdims=True))
        return e / jnp.sum(e, axis=-1, keepdims=True)

    def phi_q(l, m, h):
        return PF[l, m, h].astype(BF16)

    def phi_k(l, m, h):
        return (PF[l, m, 3 + h].astype(BF16).astype(F32) * MASKS[VALID]).astype(BF16)

    def lanes2(a, b):
        return jnp.concatenate([a, b], 1)

    def rows2(a, b):
        return jnp.concatenate([a, b], 0)

    def attend_features(l, m):
        mixed = nn(N1[...], weight(3 * l + ATTN, m, slice(0, 5 * PAIR)))
        hi, lo = split(mixed[:, :3 * PAIR])
        TQ[l, m, :, 0:3 * PAIR] = hi
        v01 = mixed[:, 3 * PAIR:4 * PAIR].astype(BF16)
        v2 = (mixed[:, 4 * PAIR:] * low).astype(BF16)
        TQ[l, m, :, 3 * PAIR:4 * PAIR] = v01
        TQ[l, m, :, 4 * PAIR:] = v2
        bias = BIAS[l, m]
        for t in range(3):
            tile = slice(t * PAIR, (t + 1) * PAIR)
            u = nn(lanes2(hi[:, tile], lo[:, tile]), BD[l, m, t])
            for e in range(2):
                h = 2 * t + e
                PF[l, m, h] = softmax(u[:, e * PAIR:(e + 1) * PAIR] + bias[h:h + 1])
        last = MASKS[LAST]
        keys = [phi_k(l, m, h).astype(F32) * last for h in range(3)]
        sums = stack_rows([jnp.sum(k, axis=0, keepdims=True) for k in keys], 8)
        keys = [k.astype(BF16) for k in keys]
        two = tn(v01, lanes2(keys[0], keys[1]))
        one = tn(v2, keys[2])
        SB[l, 0, m, 0:HD] = two[:HD, :PAIR].astype(BF16)
        SB[l, 0, m, HD:PAIR] = two[HD:, PAIR:].astype(BF16)
        SB[l, 0, m, PAIR:3 * HD] = one[:HD].astype(BF16)
        SB[l, 0, m, 3 * HD:] = rows2(*split(sums))

    none_b = jnp.zeros((HD, PAIR), BF16)

    def diagonal(block):
        return rows2(lanes2(block[:HD], none_b), lanes2(none_b, block[HD:PAIR]))

    def attend_out(l, m):
        values, sums = add_blocks(SB[l, 1, m], f_a, OT[l, m // 2, m % 2], f_b)
        carried = values.astype(BF16)
        CAR[l, m] = carried
        CS[l, m] = sums
        valid_now, cont = MASKS[VALID], MASKS[CONT]
        lower = MASKS[LOWER]
        scores, inverse = [], []
        queries = [phi_q(l, m, h) for h in range(3)]
        for h in range(3):
            s = nt(queries[h], phi_k(l, m, h)) * lower
            total = jnp.sum(s + queries[h].astype(F32) * (cont * sums[h:h + 1]), axis=-1, keepdims=True)
            inverse.append(1.0 / (total + (1.0 - valid_now)))
            scores.append(s.astype(BF16))
        v01 = TQ[l, m, :, 3 * PAIR:4 * PAIR].astype(F32)
        v2 = TQ[l, m, :, 4 * PAIR:]
        num = nn(lanes2(scores[0], scores[1]), rows2((v01 * low).astype(BF16), (v01 * high).astype(BF16)))
        num += cont * nt(lanes2(queries[0], queries[1]), diagonal(carried))
        num2 = nn(scores[2], v2) + cont * nt(queries[2], rows2(carried[PAIR:], none_b))
        rd = jnp.where(left, inverse[0], inverse[1])
        att, att2 = valid_now * num * rd, valid_now * num2 * inverse[2]
        RD[l, m, 0] = rd
        RD[l, m, 1] = inverse[2]
        ATT[l, m, 0] = att
        ATT[l, m, 1] = att2
        operand = lanes2(pltpu.roll(att2, HD, 1), att).astype(BF16)
        ACC[...] += nt(operand, weight(3 * l + ATTN, m, slice(4 * PAIR, 6 * PAIR)))

    def loop4(do):
        def one(m, carry):
            do(m)
            return carry

        lax.fori_loop(0, 4, one, 0)

    def attend_end(l):
        ACC[...] = jnp.zeros((rows, width), F32)
        loop4(functools.partial(attend_out, l))
        middle = R[l] + ACC[...]
        MID[l] = middle
        N1[...] = moments(middle)[0].astype(BF16)

    def up(l, m):
        pre = nn(N1[...], weight(3 * l + UP, m))
        PRE[l, m] = pre
        ACT[m] = gelu(pre).astype(BF16)

    def down(l, m):
        ACC[...] += nt(ACT[m], weight(3 * l + DOWN, m))

    def layer_end(l):
        after = MID[l] + ACC[...]
        if l + 1 < LAYERS:
            R[l + 1] = after
            N1[...] = moments(after)[0].astype(BF16)
        else:
            out_ref[...] = after.astype(BF16)

    def clear():
        ACC[...] = jnp.zeros((rows, width), F32)

    def stage(k, every=None, at=()):
        def one(s, carry):
            comm(k, s)
            if every is not None:
                every(s)
            for when, do in at:
                pl.when(s == when)(do)
            return carry

        lax.fori_loop(0, 4, one, 0)

    if gathers:
        for h in range(2):
            pltpu.make_async_copy(
                w_ref.at[:, h], G.at[:, yc, cc, zc, xc, h], own_sem.at[h]).wait()
        maps_start()
        for q in range(CHUNKS):
            if not early(q):
                gather_start(q)
    else:
        maps_start()
    stage(0, at=[(1, maps_forward), (3, maps_build)])
    stage(1)
    ready(0)
    stage(2, every=functools.partial(attend_features, 0))
    ex_start(0)
    ready(1)

    def middle_part(l):
        ex_end(l)
        attend_end(l)

    stage(3, at=[(0, lambda: ex_mid(0, f_own, f_sis)), (1, lambda: ex_forward(0)),
                 (2, lambda: middle_part(0)), (3, lambda: loop4(functools.partial(up, 0)))])
    ready(2)
    clear()
    stage(4, every=functools.partial(down, 0))
    layer_end(0)
    ready(3)
    stage(5, every=functools.partial(attend_features, 1))
    ex_start(1)
    ready(4)
    stage(6, at=[(0, lambda: ex_mid(1, f_own, f_sis)), (1, lambda: ex_forward(1)),
                 (2, lambda: middle_part(1)), (3, lambda: loop4(functools.partial(up, 1)))])
    ready(5)
    clear()
    loop4(functools.partial(down, 1))
    layer_end(1)

    def mlp_back(l, m):
        grad_act = nn(N1[...], weight(3 * l + DOWN, m))
        grad_pre = (gelu_slope(PRE[l, m]) * grad_act).astype(BF16)
        ACC[...] += nt(grad_pre, weight(3 * l + UP, m))

    def place(x, column, column_low, at_left):
        at = 0 if at_left else HD
        keep = high if at_left else low
        out = x * keep
        out = jnp.where(lane == at, column, out)
        return jnp.where(lane == at + 1, column_low, out)

    def heads_of(pair, single_tile, columns):
        return [place(pair, *columns[0], False), place(pair, *columns[1], True),
                place(single_tile, *columns[2], False)]

    ones = [(1.0, 1.0)] * 3

    def attend_back_start(l, m):
        e = 2 + l
        grads = nn(N1[...], weight(3 * l + ATTN, m, slice(4 * PAIR, 6 * PAIR)))
        g01, g2 = grads[:, PAIR:], pltpu.roll(grads[:, :PAIR], HD, 1) * low
        valid_now, cont = MASKS[VALID], MASKS[CONT]
        s01, s2 = g01 * RD[l, m, 0], g2 * RD[l, m, 1]
        p01, p2 = s01 * ATT[l, m, 0], s2 * ATT[l, m, 1]
        dens = [-jnp.sum(p01 * low, axis=-1, keepdims=True), -jnp.sum(p01 * high, axis=-1, keepdims=True),
                -jnp.sum(p2, axis=-1, keepdims=True)]
        num01 = (s01 * valid_now).astype(BF16).astype(F32)
        num2 = (s2 * valid_now).astype(BF16).astype(F32)
        columns = []
        for d in dens:
            top = d.astype(BF16).astype(F32)
            columns.append((top, d - top))
        tiles = heads_of(num01, num2, columns)
        sums = []
        for h in range(3):
            GNH[m, h] = tiles[h].astype(BF16)
            GDEN[m, h] = jnp.broadcast_to(dens[h], (rows, PAIR))
            state = tn((tiles[h] * cont).astype(BF16), phi_q(l, m, h))
            keep, extra = (state[HD:], state[:8]) if h == 1 else (state[:HD], state[HD:HD + 8])
            SB[e, 0, m, h * HD:(h + 1) * HD] = keep.astype(BF16)
            sums.append(extra[0:1] + extra[1:2])
        SB[e, 0, m, 3 * HD:] = rows2(*split(stack_rows(sums, 8)))

    def softmax_back(p, g):
        return p * (g - jnp.sum(p * g, axis=-1, keepdims=True))

    def attend_back_local(l, m):
        cont = MASKS[CONT]
        lower, upper = MASKS[LOWER], MASKS[UPPER]
        v01 = TQ[l, m, :, 3 * PAIR:4 * PAIR].astype(F32)
        v2 = TQ[l, m, :, 4 * PAIR:].astype(F32)
        vals = [v.astype(BF16) for v in heads_of(v01, v2, ones)]
        carried, sums = CAR[l, m], CS[l, m]
        nums = [GNH[m, h] for h in range(3)]
        num01 = (nums[0].astype(F32) * low + nums[1].astype(F32) * high).astype(BF16)
        num2 = (nums[2].astype(F32) * low).astype(BF16)
        from_two = nn(num01, diagonal(carried))
        from_one = nn(num2, rows2(carried[PAIR:], none_b))
        far_part = [from_two[:, :PAIR], from_two[:, PAIR:], from_one]
        back = []
        for h in range(3):
            q, k = phi_q(l, m, h), phi_k(l, m, h)
            ds = (nt(nums[h], vals[h]) * lower).astype(BF16)
            dst = (nt(vals[h], nums[h]) * upper).astype(BF16)
            back.append((nt(k, q) * upper).astype(BF16))
            g = nn(ds, k) + cont * (far_part[h] + GDEN[m, h] * sums[h:h + 1])
            TG[m, h] = softmax_back(PF[l, m, h], g)
            GPK[m, h] = nn(dst, q)
        GV[m, 0] = nn(lanes2(back[0], back[1]),
                      rows2((num01.astype(F32) * low).astype(BF16), (num01.astype(F32) * high).astype(BF16)))
        GV[m, 1] = nn(back[2], num2)

    def attend_back_end(l, m):
        e = 2 + l
        values, sums = add_blocks(SB[e, 1, m], b_a, OT[e, m // 2, m % 2], b_b)
        state = values.astype(BF16)
        valid_now, last = MASKS[VALID], MASKS[LAST]
        v01 = TQ[l, m, :, 3 * PAIR:4 * PAIR]
        v2 = TQ[l, m, :, 4 * PAIR:]
        wide, narrow = diagonal(state), rows2(state[PAIR:], none_b)
        from_two, from_one = nn(v01, wide), nn(v2, narrow)
        far_part = [from_two[:, :PAIR], from_two[:, PAIR:], from_one]
        turned = [TG[m, h] for h in range(3)]
        for h in range(3):
            g = valid_now * (GPK[m, h] + last * (far_part[h] + sums[h:h + 1]))
            turned.append(softmax_back(PF[l, m, 3 + h], g))
        grad_v = GV[m, 0] + last * nt(lanes2(phi_k(l, m, 0), phi_k(l, m, 1)), wide)
        grad_v2 = (GV[m, 1] + last * nt(phi_k(l, m, 2), narrow)) * low
        parts = []
        for t in range(3):
            two = lanes2(turned[2 * t], turned[2 * t + 1]).astype(BF16)
            parts.append(nt(two, BD[l, m, t, 0:PAIR]))
            maps = tn(TQ[l, m, :, t * PAIR:(t + 1) * PAIR], two)
            a, b = maps[:HD, :PAIR], maps[HD:, PAIR:]
            half = lax.broadcasted_iota(jnp.int32, (HD, PAIR), 1) < HD
            both = jnp.where(half, a - pltpu.roll(a, HD, 1), pltpu.roll(b, HD, 1) - b)
            GRF[l, m // 2, m % 2, t * HD:(t + 1) * HD] = both
            GRB[l, m // 2, m % 2, t * HD:(t + 1) * HD] = both.astype(BF16)
        offsets = stack_rows([jnp.sum(t, axis=0, keepdims=True) for t in turned], 16)
        GRF[l, m // 2, m % 2, 3 * HD:] = offsets
        GRB[l, m // 2, m % 2, 3 * HD:] = offsets.astype(BF16)
        mixed = jnp.concatenate(parts + [grad_v, grad_v2], 1).astype(BF16)
        ACC[...] += nt(mixed, weight(3 * l + ATTN, m, slice(0, 5 * PAIR)))

    def sum_start(l):
        send(GRB.at[l, :, 1 - cc], RB1.at[l], rd_send.at[l, 0], rd_recv.at[l, 0], sister).start()

    def sum_chip(l):
        send(GRB.at[l, :, cc], RB1.at[l], rd_send.at[l, 0], rd_recv.at[l, 0], sister).wait()
        RB2[l, 0] = (GRF[l, 1 - yc, cc] + RB1[l, 1 - yc].astype(F32)).astype(BF16)
        send(RB2.at[l, 0], RB2.at[l, 1], rd_send.at[l, 1], rd_recv.at[l, 1], across).start()
        ACC2[l] = GRF[l, yc, cc] + RB1[l, yc].astype(F32)

    def sum_batch(l, k):
        if k == 0:
            send(RB2.at[l, 0], RB2.at[l, 1], rd_send.at[l, 1], rd_recv.at[l, 1], across).wait()
            total = ACC2[l] + RB2[l, 1].astype(F32)
        else:
            send(DBL.at[l, k - 1, 0], DBL.at[l, k - 1, 1], rd_send.at[l, k + 1], rd_recv.at[l, k + 1],
                 partner(k - 1)).wait()
            total = DBL[l, k - 1, 0].astype(F32) + DBL[l, k - 1, 1].astype(F32)
        if k < steps:
            DBL[l, k, 0] = total.astype(BF16)
            send(DBL.at[l, k, 0], DBL.at[l, k, 1], rd_send.at[l, k + 2], rd_recv.at[l, k + 2],
                 partner(k)).start()
            return
        for ref, bias_ref, first_tile in ((gq_ref, gqb_ref, 0), (gk_ref, gkb_ref, 3)):
            for j in range(3):
                i = first_tile + j
                tile = total[(i // 2) * HD:(i // 2 + 1) * HD]
                if i % 2:
                    tile = pltpu.roll(tile, HD, 1)
                ref[l, j] = tile[:, :HD]
            offsets = total[3 * HD:3 * HD + 8]
            offsets = offsets - pltpu.roll(offsets, HD, 1)
            bias_ref[l] = offsets[first_tile:first_tile + 3, :HD]

    GRAD[...] = cot_ref[...].astype(F32)
    N1[...] = cot_ref[...]
    for l in reversed(range(LAYERS)):
        e = 2 + l
        clear()
        loop4(functools.partial(mlp_back, l))
        if l + 1 < LAYERS:
            sum_chip(l + 1)
        grad_mid = GRAD[...] + norm_back(MID[l], ACC[...])
        GRAD[...] = grad_mid
        N1[...] = grad_mid.astype(BF16)
        loop4(functools.partial(attend_back_start, l))
        ex_start(e)
        if l + 1 < LAYERS:
            sum_batch(l + 1, 0)

        def local(m, carry):
            attend_back_local(l, m)
            pl.when(m == 0)(lambda: ex_mid(e, b_own, b_sis))
            pl.when(m == 3)(lambda: ex_forward(e))
            return carry

        lax.fori_loop(0, 4, local, 0)
        if l + 1 < LAYERS:
            for k in range(1, steps):
                sum_batch(l + 1, k)
        ex_end(e)
        clear()
        loop4(functools.partial(attend_back_end, l))
        sum_start(l)
        if l + 1 < LAYERS:
            sum_batch(l + 1, steps)
        GRAD[...] = GRAD[...] + norm_back(R[l], ACC[...])
        N1[...] = GRAD[...].astype(BF16)
    gin_ref[...] = GRAD[...].astype(BF16)
    sum_chip(0)
    for k in range(steps + 1):
        sum_batch(0, k)
    drain()


def per_device(tokens, cotangent, seq_lengths, joined_qkv, attn_proj, mlp_up, mlp_down,
               query_map, query_bias, key_map, key_bias):
    n_batch, n_mp = lax.axis_size("batch"), lax.axis_size("mp")
    rows, width = tokens.shape
    slice_rows = joined_qkv.shape[1]
    heads = query_map.shape[1]
    assert n_mp == 4 and heads == 3 and rows == PAIR and query_map.shape[2] == HD
    assert n_batch & (n_batch - 1) == 0
    gathers = n_batch == 8 and slice_rows % 32 == 0
    turned = jnp.concatenate([attn_proj[:, PAIR:], attn_proj[:, :PAIR]], 1).transpose(0, 2, 1)
    attn = jnp.concatenate([joined_qkv.reshape(LAYERS, slice_rows, -1), turned], 2)
    blocks = jnp.stack([attn, mlp_up, mlp_down.transpose(0, 2, 1)], 1)
    blocks = blocks.reshape(CHUNKS, slice_rows, width)
    if gathers:
        weights = blocks.reshape(CHUNKS, 2, slice_rows // 2, width)
    else:
        weights = lax.all_gather(blocks, "batch", axis=1, tiled=True)
        weights = lax.all_gather(weights, "mp", axis=1, tiled=True)
        weights = weights.reshape(CHUNKS, 2, 2, 4, 2, 2, width // 16, width)
    maps = jnp.concatenate([query_map, key_map], 1).reshape(LAYERS, 3, 2, HD, HD)
    maps = maps.transpose(0, 1, 3, 2, 4).reshape(LAYERS, 3 * HD, PAIR)
    offsets = jnp.concatenate([query_bias, key_bias], 1)
    offsets = jnp.pad(jnp.concatenate([offsets, -offsets], 2), ((0, 0), (0, 10), (0, 0)))
    trained = jnp.concatenate([maps, offsets], 1)

    steps = n_batch.bit_length() - 1
    vmem, dma = pltpu.VMEM, pltpu.SemaphoreType.DMA
    scratch = [
        vmem((CHUNKS, 2, 2, 4, 2, 2, width // 16, width), BF16),
        vmem((2, 2, LAYERS, ROWS, PAIR), BF16),
        vmem((LAYERS, 4, 3, 2 * PAIR, 2 * PAIR), BF16),
        vmem((LAYERS, 4, 8, PAIR), F32),
        vmem((LAYERS, rows, width), F32),
        vmem((LAYERS, rows, width), F32),
        vmem((LAYERS, 4, rows, width), F32),
        vmem((4, rows, width), BF16),
        vmem((LAYERS, 4, rows, 5 * PAIR), BF16),
        vmem((LAYERS, 4, 6, rows, PAIR), F32),
        vmem((LAYERS, 4, 2, rows, PAIR), F32),
        vmem((LAYERS, 4, 2, rows, PAIR), F32),
        vmem((LAYERS, 4, 3 * HD, PAIR), BF16),
        vmem((LAYERS, 4, 8, PAIR), F32),
        vmem((rows, width), BF16),
        vmem((rows, width), F32),
        vmem((rows, width), F32),
        vmem((4, 3, rows, PAIR), BF16),
        vmem((4, 3, rows, PAIR), F32),
        vmem((4, 3, rows, PAIR), F32),
        vmem((4, 2, rows, PAIR), F32),
        vmem((4, 3, rows, PAIR), F32),
        vmem((5, rows, rows), F32),
        vmem((2 * LAYERS, 2, 4, ROWS, PAIR), BF16),
        vmem((2 * LAYERS, 2, ROWS, PAIR), BF16),
        vmem((2 * LAYERS, 2, 2, ROWS, PAIR), BF16),
        vmem((LAYERS, 2, 2, ROWS, PAIR), F32),
        vmem((LAYERS, 2, 2, ROWS, PAIR), BF16),
        vmem((LAYERS, 2, ROWS, PAIR), BF16),
        vmem((LAYERS, ROWS, PAIR), F32),
        vmem((LAYERS, 2, ROWS, PAIR), BF16),
        vmem((LAYERS, steps, 2, ROWS, PAIR), BF16),
        dma((CHUNKS,)),
        dma((7,)),
        dma((2 * LAYERS, 3)), dma((2 * LAYERS, 3)),
        dma((LAYERS, steps + 2)), dma((LAYERS, steps + 2)),
        dma((CHUNKS, 2, 4)), dma((CHUNKS, 2, 2, 4)),
        dma((CHUNKS, 2)), dma((CHUNKS, 2, 4)), dma((CHUNKS, 2, 4)),
        dma((CHUNKS,)), dma((CHUNKS, 2)),
    ]
    whole = pl.BlockSpec(memory_space=pltpu.VMEM)
    return pl.pallas_call(
        functools.partial(body, n_batch, gathers),
        out_shape=(
            jax.ShapeDtypeStruct(tokens.shape, BF16),
            jax.ShapeDtypeStruct(tokens.shape, BF16),
            jax.ShapeDtypeStruct(query_map.shape, F32),
            jax.ShapeDtypeStruct(query_bias.shape, F32),
            jax.ShapeDtypeStruct(key_map.shape, F32),
            jax.ShapeDtypeStruct(key_bias.shape, F32),
        ),
        in_specs=[pl.BlockSpec(memory_space=pltpu.SMEM), whole, whole,
                  pl.BlockSpec(memory_space=pl.ANY), pl.BlockSpec(memory_space=pl.ANY)],
        out_specs=(whole,) * 6,
        scratch_shapes=scratch,
        compiler_params=pltpu.CompilerParams(
            collective_id=0, has_side_effects=True, vmem_limit_bytes=62 * 2**20),
    )(seq_lengths, tokens, cotangent, weights, trained)


def solution(mesh):
    return jax.shard_map(
        per_device,
        mesh=mesh,
        in_specs=(
            P(("batch", "mp"), None),
            P(("batch", "mp"), None),
            P("batch", None),
            P(None, "batch", None, "mp"),
            P(None, "mp", "batch"),
            P(None, "batch", "mp"),
            P(None, "mp", "batch"),
            P(None, "mp", None, None),
            P(None, "mp", None),
            P(None, "mp", None, None),
            P(None, "mp", None),
        ),
        out_specs=(
            P(("batch", "mp"), None),
            P(("batch", "mp"), None),
            P(None, "mp", None, None),
            P(None, "mp", None),
            P(None, "mp", None, None),
            P(None, "mp", None),
        ),
        check_vma=False,
    )
```

```python
import functools

import jax
import jax.numpy as jnp
from jax import lax
from jax.experimental import pallas as pl
from jax.experimental.pallas import tpu as pltpu
from jax.sharding import PartitionSpec as P

SPAN = 64
LAYERS = 2
EPS = 1e-05
F32, BF16 = jnp.float32, jnp.bfloat16
MESH = pl.DeviceIdType.MESH
ATTN, UP, DOWN = 0, 1, 2
CHUNKS = 3 * LAYERS
HD = 64
PAIR = 2 * HD
ROWS = 3 * HD + 16


def nn(a, b):
    return lax.dot_general(a, b, (((1,), (0,)), ((), ())), preferred_element_type=F32)


def nt(a, b):
    return lax.dot_general(a, b, (((1,), (1,)), ((), ())), preferred_element_type=F32)


def tn(a, b):
    return lax.dot_general(a, b, (((0,), (0,)), ((), ())), preferred_element_type=F32)


def moments(x):
    mean = jnp.mean(x, axis=-1, keepdims=True)
    centered = x - mean
    scale = lax.rsqrt(jnp.mean(centered * centered, axis=-1, keepdims=True) + EPS)
    return centered * scale, scale


def norm_back(x, g):
    y, scale = moments(x)
    mean_g = jnp.mean(g, axis=-1, keepdims=True)
    mean_gy = jnp.mean(g * y, axis=-1, keepdims=True)
    return scale * (g - mean_g - y * mean_gy)


GELU_C = 0.7978845608028654
GELU_A = 0.044715


def gelu(x):
    return 0.5 * x * (1.0 + jnp.tanh(GELU_C * (x + GELU_A * x * x * x)))


def gelu_slope(x):
    square = x * x
    t = jnp.tanh(GELU_C * x * (1.0 + GELU_A * square))
    inner = GELU_C * (1.0 + 3.0 * GELU_A * square)
    return 0.5 * (1.0 + t) + 0.5 * x * (1.0 - t * t) * inner


def split(x):
    high = x.astype(BF16)
    return high, (x - high.astype(F32)).astype(BF16)


def stack_rows(entries, rows):
    index = lax.broadcasted_iota(jnp.int32, (rows, entries[0].shape[1]), 0)
    out = jnp.zeros((rows, entries[0].shape[1]), F32)
    for i, entry in enumerate(entries):
        out = jnp.where(index == i, entry, out)
    return out


def lanes2(a, b):
    return jnp.concatenate([a, b], 1)


def rows2(a, b):
    return jnp.concatenate([a, b], 0)


def body(n_batch, gathers, *refs):
    (seq_ref, tok_hbm, cot_hbm, qmap_ref, qbias_ref, kmap_ref, kbias_ref) = refs[:7]
    frozen, refs = (refs[7:11], refs[11:]) if gathers else (refs[7:8], refs[8:])
    (out_ref, gin_ref, gq_ref, gqb_ref, gk_ref, gkb_ref,
     G, TOK, COT, QKV, PROJ, MT, BD, BIAS, R, MID, PRE, ACT, TQ, PF, ATT, RD, CAR, CS,
     N1, ACC, GRAD, GNH, GDEN, GPK, GV, TG, MASKS, SB, CH, OT,
     GRF, GRB, RB1, ACC2, RB2, DBL,
     own_sem, in_sem, mt_sem, ex1_send, ex1_recv, ex2_send, ex2_recv, rd_send, rd_recv,
     z_send, z_recv, cross_send, first_recv, last_recv, core_send, core_recv) = refs
    rows, width = TOK.shape
    batch, mp = lax.axis_index("batch"), lax.axis_index("mp")
    yc, cc = mp // 2, mp % 2
    sister = (batch, yc * 2 + 1 - cc)
    across = (batch, (1 - yc) * 2 + cc)
    steps = n_batch.bit_length() - 1

    def partner(k):
        bit = (batch // (1 << k)) % 2
        return (batch + (1 - 2 * bit) * (1 << k), mp)

    def send(src, dst, send_sem, recv_sem, device):
        copy = pltpu.make_async_remote_copy(
            src_ref=src, dst_ref=dst, send_sem=send_sem, recv_sem=recv_sem,
            device_id=device, device_id_type=MESH)
        return copy

    tok_copy = pltpu.make_async_copy(tok_hbm, TOK, in_sem.at[0])
    cot_copy = pltpu.make_async_copy(cot_hbm, COT, in_sem.at[1])
    own_copies = []
    if gathers:
        zc, xc = batch // 2, batch % 2
        x_side = (zc * 2 + 1 - xc, mp)
        z_up = (jnp.minimum(zc + 1, 3) * 2 + xc, mp)
        z_down = (jnp.maximum(zc - 1, 0) * 2 + xc, mp)
        qkv_hbm, proj_hbm, up_hbm, down_hbm = frozen
        qkv_copy = pltpu.make_async_copy(qkv_hbm, QKV, in_sem.at[2])
        proj_copy = pltpu.make_async_copy(proj_hbm, PROJ, in_sem.at[3])
        qkv_copy.start()
        proj_copy.start()
        tok_copy.start()
        for l in range(LAYERS):
            for part, ref in ((UP, up_hbm), (DOWN, down_hbm)):
                own_copies.append(pltpu.make_async_copy(
                    ref.at[l], G.at[3 * l + part, yc, cc, zc, xc], own_sem.at[3 * l + part]))
        greeted = [x_side] + [(((zc + k) % 4) * 2 + xc, mp) for k in (1, 2, 3)]
    else:
        tok_copy.start()
        own_copies = [pltpu.make_async_copy(frozen[0].at[q], G.at[q], own_sem.at[q])
                      for q in range(CHUNKS)]
        greeted = [partner(k) for k in range(steps)]
    for copy in own_copies:
        copy.start()
    cot_copy.start()
    greeted += [sister, across]
    barrier = pltpu.get_barrier_semaphore()
    for device in greeted:
        pl.semaphore_signal(barrier, inc=1, device_id=device, device_id_type=MESH)

    for l in range(LAYERS):
        heads = [ref[l, h].astype(F32) for ref in (qmap_ref, kmap_ref) for h in range(3)]
        for t in range(3):
            MT[yc, cc, l, t * HD:(t + 1) * HD] = jnp.concatenate(
                [heads[2 * t], heads[2 * t + 1]], 1).astype(BF16)
        biases = [ref[h, l:l + 1].astype(F32) for ref in (qbias_ref, kbias_ref) for h in range(3)]
        MT[yc, cc, l, 3 * HD:] = stack_rows(
            [jnp.concatenate([b, -b], 1) for b in biases], 16).astype(BF16)

    if gathers:
        slice_rows = QKV.shape[2]
        eye = (lax.broadcasted_iota(jnp.int32, (slice_rows, slice_rows), 0)
               == lax.broadcasted_iota(jnp.int32, (slice_rows, slice_rows), 1)).astype(BF16)
        qkv_copy.wait()
        proj_copy.wait()
        for l in range(LAYERS):
            turned = nt(eye, PROJ[l])
            pieces = [QKV[l, i].astype(F32) for i in range(3)]
            block = jnp.concatenate(pieces + [turned[:, PAIR:], turned[:, :PAIR]], 1).astype(BF16)
            G[3 * l + ATTN, yc, cc, zc, xc] = block.reshape(G.shape[5:])

    row0 = mp * rows
    spans = []
    end = jnp.int32(0)
    for s in range(seq_ref.shape[1]):
        length = seq_ref[0, s]
        spans.append((end, end + length, end + ((length + SPAN - 1) // SPAN) * SPAN))
        end = spans[-1][2]

    def owner(place):
        return sum((place >= stop).astype(jnp.int32) for _, _, stop in spans)

    def owner_at(place):
        return sum(jnp.where(place >= stop, 1, 0) for _, _, stop in spans)

    def same(a, b):
        return jnp.where(owner_at(a) == owner_at(b), 1.0, 0.0).astype(F32)

    row = lax.broadcasted_iota(jnp.int32, (rows, rows), 0) + row0
    col = lax.broadcasted_iota(jnp.int32, (rows, rows), 1) + row0
    own_row, own_col = owner(row), owner(col)
    valid = sum(((row >= a) & (row < b)).astype(F32) for a, b, _ in spans)
    MASKS[0] = ((col <= row) & (own_row == own_col)).astype(F32)
    MASKS[1] = ((row <= col) & (own_row == own_col)).astype(F32)
    MASKS[2] = valid
    came_in = jnp.where(mp > 0, owner_at(row0 - 1), -1)
    MASKS[3] = (own_row == came_in).astype(F32)
    MASKS[4] = (own_row == owner_at(row0 + rows - 1)).astype(F32)
    LOWER, UPPER, VALID, CONT, LAST = range(5)

    def last_of(y, c):
        return (y * 2 + c) * rows + rows - 1

    in_chip = same(last_of(yc, 0), last_of(yc, 1))
    first, second = (cc == 0), (cc == 1)
    f_own = jnp.where(second, 1.0, in_chip)
    f_sis = jnp.where(second, in_chip, 1.0)
    f_a = jnp.where(second, 1.0, 0.0)
    f_b = jnp.where(yc == 1, jnp.where(second, same(last_of(0, 1), last_of(1, 0)), 1.0), 0.0)
    before = same(last_of(0, 1), last_of(1, 0))
    b_own = jnp.where(first, 1.0, before)
    b_sis = jnp.where(first, before, 1.0)
    b_a = jnp.where(first, 1.0, 0.0)
    b_b = jnp.where(yc == 0, jnp.where(first, same(last_of(0, 0), last_of(0, 1)), 1.0), 0.0)

    lane = lax.broadcasted_iota(jnp.int32, (rows, PAIR), 1)
    low = (lane < HD).astype(F32)
    high = 1.0 - low
    left = lane < HD

    pl.semaphore_wait(barrier, len(greeted))

    def maps_start():
        send(MT.at[yc, cc], MT.at[yc, cc], mt_sem.at[1], mt_sem.at[2], across).start()
        send(MT.at[yc, cc], MT.at[yc, cc], mt_sem.at[3], mt_sem.at[4], sister).start()

    def maps_forward():
        send(MT.at[1 - yc, cc], MT.at[1 - yc, cc], mt_sem.at[1], mt_sem.at[2], across).wait()
        send(MT.at[1 - yc, cc], MT.at[1 - yc, cc], mt_sem.at[5], mt_sem.at[6], sister).start()

    def maps_build():
        send(MT.at[yc, cc], MT.at[yc, 1 - cc], mt_sem.at[3], mt_sem.at[4], sister).wait()
        send(MT.at[1 - yc, cc], MT.at[1 - yc, 1 - cc], mt_sem.at[5], mt_sem.at[6], sister).wait()
        half = lax.broadcasted_iota(jnp.int32, (HD, PAIR), 1) < HD
        none = jnp.zeros((HD, PAIR), F32)

        def one(i, carry):
            l, m = i // 4, i % 4
            block = MT[m // 2, m % 2, l].astype(F32)
            for t in range(3):
                pair = block[t * HD:(t + 1) * HD]
                turned = pltpu.roll(pair, HD, 1)
                a = jnp.where(half, pair, -turned)
                b = jnp.where(half, turned, -pair)
                wide = jnp.concatenate(
                    [jnp.concatenate([a, none], 1), jnp.concatenate([none, b], 1)], 0).astype(BF16)
                BD[l, m, t, 0:PAIR] = wide
                BD[l, m, t, PAIR:2 * PAIR] = wide
            BIAS[l, m] = block[3 * HD:3 * HD + 8]
            return carry

        lax.fori_loop(0, 2 * 4, one, 0)

    if gathers:
        def turn(q, p):
            return (q % 2, 0, 1)[p]

        def near(q, p):
            return (x_side, across)[turn(q, p)]

        def far(q, p):
            return (across, x_side)[turn(q, p)]

        def single(q, p, z):
            return G.at[q, yc, cc, z, xc, p]

        def neighbour(q, p, z):
            return (G.at[q, yc, cc, z, 1 - xc, p], G.at[q, 1 - yc, cc, z, xc, p])[turn(q, p)]

        def pair_of(q, p, z):
            return (G.at[q, yc, cc, z, :, p], G.at[q, :, cc, z, xc, p])[turn(q, p)]

        def other_pair(q, p, z):
            return (G.at[q, 1 - yc, cc, z, :, p], G.at[q, :, cc, z, 1 - xc, p])[turn(q, p)]

        def z_unit(q, p, z):
            return single(q, p, z) if p == 0 else pair_of(q, p, z)

        def z_on(q, p, z, way, s):
            @pl.when((zc < 3) if way == 0 else (zc > 0))
            def _():
                send(z_unit(q, p, z), z_unit(q, p, z), z_send.at[q, way, s, min(p, 1)],
                     z_recv.at[q, p, way, s], (z_up, z_down)[way]).start()

        def to_near(q, p, z, slot):
            send(single(q, p, z), single(q, p, z), cross_send.at[q, min(p, 1)],
                 first_recv.at[q, p, slot], near(q, p)).start()

        def to_far(q, p, z):
            send(pair_of(q, p, z), pair_of(q, p, z), cross_send.at[q, 2], last_recv.at[q, p, z],
                 far(q, p)).start()

        def to_sister(q, p, ref):
            send(ref, ref, core_send.at[q], core_recv.at[q, p], sister).start()

        def wait_near(q, p, z, slot):
            ref = neighbour(q, p, z)
            send(ref, ref, cross_send.at[q, 0], first_recv.at[q, p, slot], near(q, p)).wait_recv()

        def wait_far(q, p, z):
            ref = other_pair(q, p, z)
            send(ref, ref, cross_send.at[q, 2], last_recv.at[q, p, z], far(q, p)).wait_recv()

        def have(q, p, z):
            if p == 0:
                to_near(q, p, z, z)
            else:
                to_far(q, p, z)
                to_sister(q, p, pair_of(q, p, z))

        def each_place(s, do):
            pl.when((s > 0) & (zc - s >= 0))(lambda: do(zc - s, 0))
            pl.when((s > 0) & (zc + s <= 3))(lambda: do(zc + s, 1))

        def gather_start(q):
            for p in (1, 2):
                to_near(q, p, zc, 0)

        def z_start(q):
            for p in range(3):
                if p > 0:
                    wait_near(q, p, zc, 0)
                for way in range(2):
                    z_on(q, p, zc, way, 0)
                have(q, p, zc)

        def along_z(q, s):
            def step(z, way):
                for p in range(3):
                    ref = z_unit(q, p, z)
                    send(ref, ref, z_send.at[q, way, s, 0], z_recv.at[q, p, way, s - 1],
                         sister).wait_recv()
                    z_on(q, p, z, way, s)
                    have(q, p, z)

            each_place(s, step)

        def across_first(q, s):
            def step(z, way):
                wait_near(q, 0, z, z)
                to_far(q, 0, z)
                to_sister(q, 0, pair_of(q, 0, z))

            pl.when(s == 0)(lambda: step(zc, None))
            each_place(s, step)

        def across_last(q, s):
            def step(z, way):
                for p in (1, 2, 0):
                    wait_far(q, p, z)
                    to_sister(q, p, other_pair(q, p, z))

            pl.when(s == 0)(lambda: step(zc, None))
            each_place(s, step)

        def comm(k, s):
            if k < CHUNKS:
                along_z(k, s)
            if k + 1 < CHUNKS:
                pl.when(s == 1)(lambda: z_start(k + 1))
            if k + 2 < CHUNKS:
                pl.when(s == 0)(lambda: gather_start(k + 2))
            if k < CHUNKS:
                pl.when(s > 0)(lambda: across_first(k, s - 1))
            if k > 0:
                pl.when(s == 0)(lambda: across_first(k - 1, 3))
                across_last(k - 1, s)

        def ready(q):
            for p in range(3):
                ref = G.at[q, :, 1 - cc, :, :, p]
                send(ref, ref, core_send.at[q], core_recv.at[q, p], sister).wait_recv()

        def drain():
            def sent(ref, sem):
                send(ref, ref, sem, core_recv.at[0, 0], sister).wait_send()

            def one(q, carry):
                for way in range(2):
                    for s in range(3):
                        @pl.when(((zc < 3) & (zc >= s)) if way == 0 else ((zc > 0) & (zc + s <= 3)))
                        def _():
                            sent(G.at[q, 0, 0, 0, 0, 0], z_send.at[q, way, s, 0])
                            sent(G.at[q, 0, 0, :, 0, 0], z_send.at[q, way, s, 1])
                sent(G.at[q, 0, 0, :, 0, 0], cross_send.at[q, 0])
                sent(G.at[q, 0, 0, 0, :, 0], cross_send.at[q, 1])
                sent(G.at[q, 0, 0], cross_send.at[q, 2])
                sent(G.at[q, :, 0], core_send.at[q])
                return carry

            lax.fori_loop(0, CHUNKS, one, 0)
    else:
        def gather_start(q):
            pass

        def z_start(q):
            pass

        def comm(k, s):
            pass

        def ready(q):
            own_copies[q].wait()

        def drain():
            pass

    def weight(q, m, lanes=None):
        if lanes is None:
            return G[q, m // 2, m % 2].reshape(width, width)
        return G[q, m // 2, m % 2, :, :, :, :, lanes].reshape(width, -1)

    def add_blocks(a, ca, b, cb):
        a, b = a.astype(F32), b.astype(F32)
        values = ca * a[:3 * HD] + cb * b[:3 * HD]
        sums = (ca * (a[3 * HD:3 * HD + 8] + a[3 * HD + 8:])
                + cb * (b[3 * HD:3 * HD + 8] + b[3 * HD + 8:]))
        return values, sums

    def block_at(i):
        return (2 * (1 - cc) + i) % 4

    def ex_sister(e, m):
        return send(SB.at[e, 0, m], SB.at[e, 1, m], ex1_send.at[e, m], ex1_recv.at[e, m], sister)

    def ex_across(e, j):
        return send(CH.at[e, j], OT.at[e, cc, j], ex2_send.at[e, 0, j], ex2_recv.at[e, 0, j], across)

    def ex_over(e, j):
        return send(OT.at[e, cc, j], OT.at[e, cc, j], ex2_send.at[e, 1, j], ex2_recv.at[e, 1, j], sister)

    def ex_step(e, i, own, sis):
        m = block_at(i)
        ex_sister(e, m).start()

        @pl.when(i >= 2)
        def _():
            ex_sister(e, m).wait_recv()
            values, sums = add_blocks(SB[e, 0, m], own, SB[e, 1, m], sis)
            CH[e, i - 2, 0:3 * HD] = values.astype(BF16)
            CH[e, i - 2, 3 * HD:] = rows2(*split(sums))
            ex_across(e, i - 2).start()

    def ex_forward(e, j):
        ex_across(e, j).wait_recv()
        ex_over(e, j).start()

    def ex_end(e):
        for j in range(2):
            m = block_at(j)
            ex_sister(e, m).wait_recv()
            ref = OT.at[e, 1 - cc, j]
            send(ref, ref, ex2_send.at[e, 1, j], ex2_recv.at[e, 1, j], sister).wait_recv()

    def ex_drain(e):
        for j in range(2):
            ex_across(e, j).wait_send()
            ex_over(e, j).wait_send()
        for m in range(4):
            ex_sister(e, m).wait_send()

    def softmax(u):
        e = jnp.exp(u - jnp.max(u, axis=-1, keepdims=True))
        return e / jnp.sum(e, axis=-1, keepdims=True)

    def phi_q(l, m, h):
        return PF[l, m, h].astype(BF16)

    def phi_k(l, m, h):
        return (PF[l, m, 3 + h].astype(BF16).astype(F32) * MASKS[VALID]).astype(BF16)

    def attend_features(l, m):
        mixed = nn(N1[...], weight(3 * l + ATTN, m, slice(0, 5 * PAIR)))
        hi, lo = split(mixed[:, :3 * PAIR])
        TQ[l, m, :, 0:3 * PAIR] = hi
        v01 = mixed[:, 3 * PAIR:4 * PAIR].astype(BF16)
        v2 = (mixed[:, 4 * PAIR:] * low).astype(BF16)
        TQ[l, m, :, 3 * PAIR:4 * PAIR] = v01
        TQ[l, m, :, 4 * PAIR:] = v2
        bias = BIAS[l, m]
        for t in range(3):
            tile = slice(t * PAIR, (t + 1) * PAIR)
            u = nn(lanes2(hi[:, tile], lo[:, tile]), BD[l, m, t])
            for e in range(2):
                h = 2 * t + e
                PF[l, m, h] = softmax(u[:, e * PAIR:(e + 1) * PAIR] + bias[h:h + 1])
        last = MASKS[LAST]
        keys = [phi_k(l, m, h).astype(F32) * last for h in range(3)]
        sums = stack_rows([jnp.sum(k, axis=0, keepdims=True) for k in keys], 8)
        keys = [k.astype(BF16) for k in keys]
        two = tn(v01, lanes2(keys[0], keys[1]))
        one = tn(v2, keys[2])
        SB[l, 0, m, 0:HD] = two[:HD, :PAIR].astype(BF16)
        SB[l, 0, m, HD:PAIR] = two[HD:, PAIR:].astype(BF16)
        SB[l, 0, m, PAIR:3 * HD] = one[:HD].astype(BF16)
        SB[l, 0, m, 3 * HD:] = rows2(*split(sums))

    def features_step(l, i):
        attend_features(l, block_at(i))
        ex_step(l, i, f_own, f_sis)

    none_b = jnp.zeros((HD, PAIR), BF16)

    def diagonal(block):
        return rows2(lanes2(block[:HD], none_b), lanes2(none_b, block[HD:PAIR]))

    def attend_out(l, m):
        values, sums = add_blocks(SB[l, 1, m], f_a, OT[l, m // 2, m % 2], f_b)
        carried = values.astype(BF16)
        CAR[l, m] = carried
        CS[l, m] = sums
        valid_now, cont = MASKS[VALID], MASKS[CONT]
        lower = MASKS[LOWER]
        scores, inverse = [], []
        queries = [phi_q(l, m, h) for h in range(3)]
        for h in range(3):
            s = nt(queries[h], phi_k(l, m, h)) * lower
            total = jnp.sum(s + queries[h].astype(F32) * (cont * sums[h:h + 1]), axis=-1, keepdims=True)
            inverse.append(1.0 / (total + (1.0 - valid_now)))
            scores.append(s.astype(BF16))
        v01 = TQ[l, m, :, 3 * PAIR:4 * PAIR].astype(F32)
        v2 = TQ[l, m, :, 4 * PAIR:]
        num = nn(lanes2(scores[0], scores[1]), rows2((v01 * low).astype(BF16), (v01 * high).astype(BF16)))
        num += cont * nt(lanes2(queries[0], queries[1]), diagonal(carried))
        num2 = nn(scores[2], v2) + cont * nt(queries[2], rows2(carried[PAIR:], none_b))
        rd = jnp.where(left, inverse[0], inverse[1])
        att, att2 = valid_now * num * rd, valid_now * num2 * inverse[2]
        RD[l, m, 0] = rd
        RD[l, m, 1] = inverse[2]
        ATT[l, m, 0] = att
        ATT[l, m, 1] = att2
        operand = lanes2(pltpu.roll(att2, HD, 1), att).astype(BF16)
        ACC[...] += nt(operand, weight(3 * l + ATTN, m, slice(4 * PAIR, 6 * PAIR)))

    def loop4(do):
        def one(m, carry):
            do(m)
            return carry

        lax.fori_loop(0, 4, one, 0)

    def attend_end(l):
        ACC[...] = jnp.zeros((rows, width), F32)
        loop4(functools.partial(attend_out, l))
        middle = R[l] + ACC[...]
        MID[l] = middle
        N1[...] = moments(middle)[0].astype(BF16)

    def up(l, m):
        pre = nn(N1[...], weight(3 * l + UP, m))
        PRE[l, m] = pre
        ACT[m] = gelu(pre).astype(BF16)

    def down(l, m):
        ACC[...] += nt(ACT[m], weight(3 * l + DOWN, m))

    def layer_end(l):
        after = MID[l] + ACC[...]
        if l + 1 < LAYERS:
            R[l + 1] = after
            N1[...] = moments(after)[0].astype(BF16)
        else:
            out_ref[...] = after.astype(BF16)

    def clear():
        ACC[...] = jnp.zeros((rows, width), F32)

    def stage(k, every=None, at=()):
        def one(s, carry):
            comm(k, s)
            if every is not None:
                every(s)
            for when, do in at:
                pl.when(s == when)(do)
            return carry

        lax.fori_loop(0, 4, one, 0)

    maps_start()
    gather_start(0)
    if gathers:
        for copy in own_copies:
            copy.wait()
    gather_start(1)
    z_start(0)
    tok_copy.wait()
    x0 = TOK[...].astype(F32)
    R[0] = x0
    N1[...] = moments(x0)[0].astype(BF16)
    stage(0, at=[(1, maps_forward), (3, maps_build)])
    stage(1)
    ready(0)
    stage(2, every=functools.partial(features_step, 0))
    ready(1)

    def middle_part(l):
        ex_end(l)
        attend_end(l)

    stage(3, at=[(0, lambda: ex_forward(0, 0)), (1, lambda: ex_forward(0, 1)),
                 (2, lambda: middle_part(0)), (3, lambda: loop4(functools.partial(up, 0)))])
    ready(2)
    clear()
    stage(4, every=functools.partial(down, 0))
    layer_end(0)
    ready(3)
    stage(5, every=functools.partial(features_step, 1))
    ready(4)
    stage(6, at=[(0, lambda: ex_forward(1, 0)), (1, lambda: ex_forward(1, 1)),
                 (2, lambda: middle_part(1)), (3, lambda: loop4(functools.partial(up, 1)))])
    ready(5)
    clear()
    loop4(functools.partial(down, 1))
    layer_end(1)

    def mlp_back(l, m):
        grad_act = nn(N1[...], weight(3 * l + DOWN, m))
        grad_pre = (gelu_slope(PRE[l, m]) * grad_act).astype(BF16)
        ACC[...] += nt(grad_pre, weight(3 * l + UP, m))

    def place(x, column, column_low, at_left):
        at = 0 if at_left else HD
        keep = high if at_left else low
        out = x * keep
        out = jnp.where(lane == at, column, out)
        return jnp.where(lane == at + 1, column_low, out)

    def heads_of(pair, single_tile, columns):
        return [place(pair, *columns[0], False), place(pair, *columns[1], True),
                place(single_tile, *columns[2], False)]

    ones = [(1.0, 1.0)] * 3

    def attend_back_start(l, m):
        e = 2 + l
        grads = nn(N1[...], weight(3 * l + ATTN, m, slice(4 * PAIR, 6 * PAIR)))
        g01, g2 = grads[:, PAIR:], pltpu.roll(grads[:, :PAIR], HD, 1) * low
        valid_now, cont = MASKS[VALID], MASKS[CONT]
        s01, s2 = g01 * RD[l, m, 0], g2 * RD[l, m, 1]
        p01, p2 = s01 * ATT[l, m, 0], s2 * ATT[l, m, 1]
        dens = [-jnp.sum(p01 * low, axis=-1, keepdims=True), -jnp.sum(p01 * high, axis=-1, keepdims=True),
                -jnp.sum(p2, axis=-1, keepdims=True)]
        num01 = (s01 * valid_now).astype(BF16).astype(F32)
        num2 = (s2 * valid_now).astype(BF16).astype(F32)
        columns = []
        for d in dens:
            top = d.astype(BF16).astype(F32)
            columns.append((top, d - top))
        tiles = heads_of(num01, num2, columns)
        sums = []
        for h in range(3):
            GNH[m, h] = tiles[h].astype(BF16)
            GDEN[m, h] = jnp.broadcast_to(dens[h], (rows, PAIR))
            state = tn((tiles[h] * cont).astype(BF16), phi_q(l, m, h))
            keep, extra = (state[HD:], state[:8]) if h == 1 else (state[:HD], state[HD:HD + 8])
            SB[e, 0, m, h * HD:(h + 1) * HD] = keep.astype(BF16)
            sums.append(extra[0:1] + extra[1:2])
        SB[e, 0, m, 3 * HD:] = rows2(*split(stack_rows(sums, 8)))

    def softmax_back(p, g):
        return p * (g - jnp.sum(p * g, axis=-1, keepdims=True))

    def attend_back_local(l, m):
        cont = MASKS[CONT]
        lower, upper = MASKS[LOWER], MASKS[UPPER]
        v01 = TQ[l, m, :, 3 * PAIR:4 * PAIR].astype(F32)
        v2 = TQ[l, m, :, 4 * PAIR:].astype(F32)
        vals = [v.astype(BF16) for v in heads_of(v01, v2, ones)]
        carried, sums = CAR[l, m], CS[l, m]
        nums = [GNH[m, h] for h in range(3)]
        num01 = (nums[0].astype(F32) * low + nums[1].astype(F32) * high).astype(BF16)
        num2 = (nums[2].astype(F32) * low).astype(BF16)
        from_two = nn(num01, diagonal(carried))
        from_one = nn(num2, rows2(carried[PAIR:], none_b))
        far_part = [from_two[:, :PAIR], from_two[:, PAIR:], from_one]
        back = []
        for h in range(3):
            q, k = phi_q(l, m, h), phi_k(l, m, h)
            ds = (nt(nums[h], vals[h]) * lower).astype(BF16)
            dst = (nt(vals[h], nums[h]) * upper).astype(BF16)
            back.append((nt(k, q) * upper).astype(BF16))
            g = nn(ds, k) + cont * (far_part[h] + GDEN[m, h] * sums[h:h + 1])
            TG[m, h] = softmax_back(PF[l, m, h], g)
            GPK[m, h] = nn(dst, q)
        GV[m, 0] = nn(lanes2(back[0], back[1]),
                      rows2((num01.astype(F32) * low).astype(BF16), (num01.astype(F32) * high).astype(BF16)))
        GV[m, 1] = nn(back[2], num2)

    def attend_back_end(l, m):
        e = 2 + l
        values, sums = add_blocks(SB[e, 1, m], b_a, OT[e, m // 2, m % 2], b_b)
        state = values.astype(BF16)
        valid_now, last = MASKS[VALID], MASKS[LAST]
        v01 = TQ[l, m, :, 3 * PAIR:4 * PAIR]
        v2 = TQ[l, m, :, 4 * PAIR:]
        wide, narrow = diagonal(state), rows2(state[PAIR:], none_b)
        from_two, from_one = nn(v01, wide), nn(v2, narrow)
        far_part = [from_two[:, :PAIR], from_two[:, PAIR:], from_one]
        turned = [TG[m, h] for h in range(3)]
        for h in range(3):
            g = valid_now * (GPK[m, h] + last * (far_part[h] + sums[h:h + 1]))
            turned.append(softmax_back(PF[l, m, 3 + h], g))
        grad_v = GV[m, 0] + last * nt(lanes2(phi_k(l, m, 0), phi_k(l, m, 1)), wide)
        grad_v2 = (GV[m, 1] + last * nt(phi_k(l, m, 2), narrow)) * low
        parts = []
        for t in range(3):
            two = lanes2(turned[2 * t], turned[2 * t + 1]).astype(BF16)
            parts.append(nt(two, BD[l, m, t, 0:PAIR]))
            maps = tn(TQ[l, m, :, t * PAIR:(t + 1) * PAIR], two)
            a, b = maps[:HD, :PAIR], maps[HD:, PAIR:]
            half = lax.broadcasted_iota(jnp.int32, (HD, PAIR), 1) < HD
            both = jnp.where(half, a - pltpu.roll(a, HD, 1), pltpu.roll(b, HD, 1) - b)
            GRF[l, m // 2, m % 2, t * HD:(t + 1) * HD] = both
            GRB[l, m // 2, m % 2, t * HD:(t + 1) * HD] = both.astype(BF16)
        offsets = stack_rows([jnp.sum(t, axis=0, keepdims=True) for t in turned], 16)
        GRF[l, m // 2, m % 2, 3 * HD:] = offsets
        GRB[l, m // 2, m % 2, 3 * HD:] = offsets.astype(BF16)
        mixed = jnp.concatenate(parts + [grad_v, grad_v2], 1).astype(BF16)
        ACC[...] += nt(mixed, weight(3 * l + ATTN, m, slice(0, 5 * PAIR)))

    def sum_start(l):
        send(GRB.at[l, :, 1 - cc], RB1.at[l], rd_send.at[l, 0], rd_recv.at[l, 0], sister).start()

    def sum_chip(l):
        send(GRB.at[l, :, cc], RB1.at[l], rd_send.at[l, 0], rd_recv.at[l, 0], sister).wait()
        RB2[l, 0] = (GRF[l, 1 - yc, cc] + RB1[l, 1 - yc].astype(F32)).astype(BF16)
        send(RB2.at[l, 0], RB2.at[l, 1], rd_send.at[l, 1], rd_recv.at[l, 1], across).start()
        ACC2[l] = GRF[l, yc, cc] + RB1[l, yc].astype(F32)

    def sum_batch(l, k):
        if k == 0:
            send(RB2.at[l, 0], RB2.at[l, 1], rd_send.at[l, 1], rd_recv.at[l, 1], across).wait()
            total = ACC2[l] + RB2[l, 1].astype(F32)
        else:
            send(DBL.at[l, k - 1, 0], DBL.at[l, k - 1, 1], rd_send.at[l, k + 1], rd_recv.at[l, k + 1],
                 partner(k - 1)).wait()
            total = DBL[l, k - 1, 0].astype(F32) + DBL[l, k - 1, 1].astype(F32)
        if k < steps:
            DBL[l, k, 0] = total.astype(BF16)
            send(DBL.at[l, k, 0], DBL.at[l, k, 1], rd_send.at[l, k + 2], rd_recv.at[l, k + 2],
                 partner(k)).start()
            return
        for ref, bias_ref, first_tile in ((gq_ref, gqb_ref, 0), (gk_ref, gkb_ref, 3)):
            for j in range(3):
                i = first_tile + j
                tile = total[(i // 2) * HD:(i // 2 + 1) * HD]
                if i % 2:
                    tile = pltpu.roll(tile, HD, 1)
                ref[l, j] = tile[:, :HD]
            offsets = total[3 * HD:3 * HD + 8]
            offsets = offsets - pltpu.roll(offsets, HD, 1)
            for j in range(3):
                bias_ref[j, l:l + 1] = offsets[first_tile + j:first_tile + j + 1, :HD]

    cot_copy.wait()
    GRAD[...] = COT[...].astype(F32)
    N1[...] = COT[...]
    for l in reversed(range(LAYERS)):
        e = 2 + l
        clear()
        loop4(functools.partial(mlp_back, l))
        if l + 1 < LAYERS:
            sum_chip(l + 1)
        grad_mid = GRAD[...] + norm_back(MID[l], ACC[...])
        GRAD[...] = grad_mid
        N1[...] = grad_mid.astype(BF16)

        def start(i):
            attend_back_start(l, block_at(i))
            ex_step(e, i, b_own, b_sis)

        loop4(start)
        if l + 1 < LAYERS:
            sum_batch(l + 1, 0)

        def local(m, carry):
            attend_back_local(l, m)
            pl.when(m == 1)(lambda: ex_forward(e, 0))
            pl.when(m == 2)(lambda: ex_forward(e, 1))
            return carry

        lax.fori_loop(0, 4, local, 0)
        if l + 1 < LAYERS:
            for k in range(1, steps):
                sum_batch(l + 1, k)
        ex_end(e)
        clear()
        loop4(functools.partial(attend_back_end, l))
        sum_start(l)
        if l + 1 < LAYERS:
            sum_batch(l + 1, steps)
        GRAD[...] = GRAD[...] + norm_back(R[l], ACC[...])
        N1[...] = GRAD[...].astype(BF16)
    gin_ref[...] = GRAD[...].astype(BF16)
    sum_chip(0)
    for k in range(steps + 1):
        sum_batch(0, k)
    for e in range(2 * LAYERS):
        ex_drain(e)
    drain()


def hand_out(*refs):
    count = len(refs) // 2
    for source, target in zip(refs[:count], refs[count:]):
        target[...] = source[...]


def per_device(tokens, cotangent, seq_lengths, joined_qkv, attn_proj, mlp_up, mlp_down,
               query_map, query_bias, key_map, key_bias):
    n_batch, n_mp = lax.axis_size("batch"), lax.axis_size("mp")
    rows, width = tokens.shape
    slice_rows = joined_qkv.shape[1]
    heads = query_map.shape[1]
    assert n_mp == 4 and heads == 3 and rows == PAIR and query_map.shape[2] == HD
    assert n_batch & (n_batch - 1) == 0
    parts = 3
    gathers = n_batch == 8 and slice_rows % (16 * parts) == 0
    part_rows = width // (8 * parts)
    qkv, down = joined_qkv.transpose(0, 2, 1, 3), mlp_down.transpose(0, 2, 1)
    if gathers:
        cut = (LAYERS, parts, part_rows, width)
        frozen = (qkv, attn_proj, mlp_up.reshape(cut), down.reshape(cut))
    else:
        turned = jnp.concatenate([attn_proj[:, PAIR:], attn_proj[:, :PAIR]], 1).transpose(0, 2, 1)
        attn = jnp.concatenate([joined_qkv.reshape(LAYERS, slice_rows, -1), turned], 2)
        blocks = jnp.stack([attn, mlp_up, down], 1).reshape(CHUNKS, slice_rows, width)
        weights = lax.all_gather(blocks, "batch", axis=1, tiled=True)
        weights = lax.all_gather(weights, "mp", axis=1, tiled=True)
        frozen = (weights.reshape(CHUNKS, 2, 2, 4, 2, parts, part_rows, width),)

    steps = n_batch.bit_length() - 1
    vmem, dma = pltpu.VMEM, pltpu.SemaphoreType.DMA
    scratch = [
        vmem((CHUNKS, 2, 2, 4, 2, parts, part_rows, width), BF16),
        vmem((rows, width), BF16),
        vmem((rows, width), BF16),
        vmem(qkv.shape, BF16),
        vmem(attn_proj.shape, BF16),
        vmem((2, 2, LAYERS, ROWS, PAIR), BF16),
        vmem((LAYERS, 4, 3, 2 * PAIR, 2 * PAIR), BF16),
        vmem((LAYERS, 4, 8, PAIR), F32),
        vmem((LAYERS, rows, width), F32),
        vmem((LAYERS, rows, width), F32),
        vmem((LAYERS, 4, rows, width), F32),
        vmem((4, rows, width), BF16),
        vmem((LAYERS, 4, rows, 5 * PAIR), BF16),
        vmem((LAYERS, 4, 6, rows, PAIR), F32),
        vmem((LAYERS, 4, 2, rows, PAIR), F32),
        vmem((LAYERS, 4, 2, rows, PAIR), F32),
        vmem((LAYERS, 4, 3 * HD, PAIR), BF16),
        vmem((LAYERS, 4, 8, PAIR), F32),
        vmem((rows, width), BF16),
        vmem((rows, width), F32),
        vmem((rows, width), F32),
        vmem((4, 3, rows, PAIR), BF16),
        vmem((4, 3, rows, PAIR), F32),
        vmem((4, 3, rows, PAIR), F32),
        vmem((4, 2, rows, PAIR), F32),
        vmem((4, 3, rows, PAIR), F32),
        vmem((5, rows, rows), F32),
        vmem((2 * LAYERS, 2, 4, ROWS, PAIR), BF16),
        vmem((2 * LAYERS, 2, ROWS, PAIR), BF16),
        vmem((2 * LAYERS, 2, 2, ROWS, PAIR), BF16),
        vmem((LAYERS, 2, 2, ROWS, PAIR), F32),
        vmem((LAYERS, 2, 2, ROWS, PAIR), BF16),
        vmem((LAYERS, 2, ROWS, PAIR), BF16),
        vmem((LAYERS, ROWS, PAIR), F32),
        vmem((LAYERS, 2, ROWS, PAIR), BF16),
        vmem((LAYERS, steps, 2, ROWS, PAIR), BF16),
        dma((CHUNKS,)), dma((4,)),
        dma((7,)),
        dma((2 * LAYERS, 4)), dma((2 * LAYERS, 4)),
        dma((2 * LAYERS, 2, 2)), dma((2 * LAYERS, 2, 2)),
        dma((LAYERS, steps + 2)), dma((LAYERS, steps + 2)),
        dma((CHUNKS, 2, 4, 2)), dma((CHUNKS, parts, 2, 4)),
        dma((CHUNKS, 3)), dma((CHUNKS, parts, 4)), dma((CHUNKS, parts, 4)),
        dma((CHUNKS,)), dma((CHUNKS, parts)),
    ]
    vmem_block, any_block = pl.BlockSpec(memory_space=pltpu.VMEM), pl.BlockSpec(memory_space=pl.ANY)
    shapes = [(tokens.shape, BF16), (tokens.shape, BF16), (query_map.shape, F32), ((heads, LAYERS, HD), F32),
              (key_map.shape, F32), ((heads, LAYERS, HD), F32)]
    shapes = [jax.ShapeDtypeStruct(*shape) for shape in shapes]
    results = pl.pallas_call(
        functools.partial(body, n_batch, gathers),
        out_shape=shapes,
        in_specs=[pl.BlockSpec(memory_space=pltpu.SMEM), any_block, any_block] + [vmem_block] * 4
        + [any_block] * len(frozen),
        out_specs=[vmem_block] * 6,
        scratch_shapes=scratch,
        compiler_params=pltpu.CompilerParams(
            collective_id=0, has_side_effects=True, vmem_limit_bytes=62 * 2**20),
    )(seq_lengths, tokens, cotangent, query_map, query_bias.transpose(1, 0, 2), key_map,
      key_bias.transpose(1, 0, 2), *frozen)
    results = pl.pallas_call(
        hand_out,
        out_shape=shapes,
        in_specs=[vmem_block] * 6,
        out_specs=[vmem_block] * 6,
    )(*results)
    out, grad_in, qmap, qbias, kmap, kbias = results
    return out, grad_in, qmap, qbias.transpose(1, 0, 2), kmap, kbias.transpose(1, 0, 2)


def solution(mesh):
    return jax.shard_map(
        per_device,
        mesh=mesh,
        in_specs=(
            P(("batch", "mp"), None),
            P(("batch", "mp"), None),
            P("batch", None),
            P(None, "batch", None, "mp"),
            P(None, "mp", "batch"),
            P(None, "batch", "mp"),
            P(None, "mp", "batch"),
            P(None, "mp", None, None),
            P(None, "mp", None),
            P(None, "mp", None, None),
            P(None, "mp", None),
        ),
        out_specs=(
            P(("batch", "mp"), None),
            P(("batch", "mp"), None),
            P(None, "mp", None, None),
            P(None, "mp", None),
            P(None, "mp", None, None),
            P(None, "mp", None),
        ),
        check_vma=False,
    )
```

```python
import functools

import jax
import jax.numpy as jnp
from jax import lax
from jax.experimental import pallas as pl
from jax.experimental.pallas import tpu as pltpu
from jax.sharding import PartitionSpec as P

SPAN = 64
LAYERS = 2
EPS = 1e-05
F32, BF16 = jnp.float32, jnp.bfloat16
MESH = pl.DeviceIdType.MESH
ATTN, UP, DOWN = 0, 1, 2
CHUNKS = 3 * LAYERS
HD = 64
PAIR = 2 * HD
ROWS = 3 * HD + 16


def nn(a, b):
    return lax.dot_general(a, b, (((1,), (0,)), ((), ())), preferred_element_type=F32)


def nt(a, b):
    return lax.dot_general(a, b, (((1,), (1,)), ((), ())), preferred_element_type=F32)


def tn(a, b):
    return lax.dot_general(a, b, (((0,), (0,)), ((), ())), preferred_element_type=F32)


def moments(x):
    mean = jnp.mean(x, axis=-1, keepdims=True)
    centered = x - mean
    scale = lax.rsqrt(jnp.mean(centered * centered, axis=-1, keepdims=True) + EPS)
    return centered * scale, scale


def norm_back(x, g):
    y, scale = moments(x)
    mean_g = jnp.mean(g, axis=-1, keepdims=True)
    mean_gy = jnp.mean(g * y, axis=-1, keepdims=True)
    return scale * (g - mean_g - y * mean_gy)


GELU_C = 0.7978845608028654
GELU_A = 0.044715


def gelu(x):
    return 0.5 * x * (1.0 + jnp.tanh(GELU_C * (x + GELU_A * x * x * x)))


def gelu_slope(x):
    square = x * x
    t = jnp.tanh(GELU_C * x * (1.0 + GELU_A * square))
    inner = GELU_C * (1.0 + 3.0 * GELU_A * square)
    return 0.5 * (1.0 + t) + 0.5 * x * (1.0 - t * t) * inner


def split(x):
    high = x.astype(BF16)
    return high, (x - high.astype(F32)).astype(BF16)


def stack_rows(entries, rows):
    index = lax.broadcasted_iota(jnp.int32, (rows, entries[0].shape[1]), 0)
    out = jnp.zeros((rows, entries[0].shape[1]), F32)
    for i, entry in enumerate(entries):
        out = jnp.where(index == i, entry, out)
    return out


def lanes2(a, b):
    return jnp.concatenate([a, b], 1)


def rows2(a, b):
    return jnp.concatenate([a, b], 0)


def body(n_batch, gathers, *refs):
    (seq_ref, tok_hbm, cot_hbm, qmap_ref, qbias_ref, kmap_ref, kbias_ref) = refs[:7]
    frozen, refs = (refs[7:11], refs[11:]) if gathers else (refs[7:8], refs[8:])
    (out_ref, gin_ref, gq_ref, gqb_ref, gk_ref, gkb_ref,
     G, TOK, COT, QKV, PROJ, MT, BD, BIAS, R, MID, PRE, ACT, TQ, PF, ATT, RD, CAR, CS,
     N1, ACC, GRAD, GNH, GDEN, GPK, GV, TG, MASKS, SB, CH, OT,
     MIX, OFF, GRF, GRB, RB1, PB, SQ, DBL,
     own_sem, in_sem, mt_sem, ex1_send, ex1_recv, ex2_send, ex2_recv, rd_send, rd_recv,
     z_send, z_recv, cross_send, first_recv, last_recv, core_send, core_recv) = refs
    rows, width = TOK.shape
    batch, mp = lax.axis_index("batch"), lax.axis_index("mp")
    yc, cc = mp // 2, mp % 2
    sister = (batch, yc * 2 + 1 - cc)
    across = (batch, (1 - yc) * 2 + cc)
    steps = n_batch.bit_length() - 1
    near_batch = batch + 1 - 2 * (batch % 2)
    opposite = (near_batch, (1 - yc) * 2 + cc)

    def partner(k):
        bit = (batch // (1 << k)) % 2
        return (batch + (1 - 2 * bit) * (1 << k), mp)

    def send(src, dst, send_sem, recv_sem, device):
        copy = pltpu.make_async_remote_copy(
            src_ref=src, dst_ref=dst, send_sem=send_sem, recv_sem=recv_sem,
            device_id=device, device_id_type=MESH)
        return copy

    tok_copy = pltpu.make_async_copy(tok_hbm, TOK, in_sem.at[0])
    cot_copy = pltpu.make_async_copy(cot_hbm, COT, in_sem.at[1])
    own_copies = []
    if gathers:
        zc, xc = batch // 2, batch % 2
        x_side = (zc * 2 + 1 - xc, mp)
        z_up = (jnp.minimum(zc + 1, 3) * 2 + xc, mp)
        z_down = (jnp.maximum(zc - 1, 0) * 2 + xc, mp)
        qkv_hbm, proj_hbm, up_hbm, down_hbm = frozen
        qkv_copy = pltpu.make_async_copy(qkv_hbm, QKV, in_sem.at[2])
        proj_copy = pltpu.make_async_copy(proj_hbm, PROJ, in_sem.at[3])
        qkv_copy.start()
        proj_copy.start()
        tok_copy.start()
        for l in range(LAYERS):
            for part, ref in ((UP, up_hbm), (DOWN, down_hbm)):
                own_copies.append(pltpu.make_async_copy(
                    ref.at[l], G.at[3 * l + part, yc, cc, zc, xc], own_sem.at[3 * l + part]))
        greeted = [(((zc + k) % 4) * 2 + xc, mp) for k in (1, 2, 3)]
    else:
        tok_copy.start()
        own_copies = [pltpu.make_async_copy(frozen[0].at[q], G.at[q], own_sem.at[q])
                      for q in range(CHUNKS)]
        greeted = [partner(k) for k in range(1, steps)]
    for copy in own_copies:
        copy.start()
    cot_copy.start()
    greeted += [partner(0), sister, across, opposite]
    barrier = pltpu.get_barrier_semaphore()
    for device in greeted:
        pl.semaphore_signal(barrier, inc=1, device_id=device, device_id_type=MESH)

    for l in range(LAYERS):
        heads = [ref[l, h].astype(F32) for ref in (qmap_ref, kmap_ref) for h in range(3)]
        for t in range(3):
            MT[yc, cc, l, t * HD:(t + 1) * HD] = jnp.concatenate(
                [heads[2 * t], heads[2 * t + 1]], 1).astype(BF16)
        biases = [ref[h, l:l + 1].astype(F32) for ref in (qbias_ref, kbias_ref) for h in range(3)]
        MT[yc, cc, l, 3 * HD:] = stack_rows(
            [jnp.concatenate([b, -b], 1) for b in biases], 16).astype(BF16)

    if gathers:
        slice_rows = QKV.shape[2]
        eye = (lax.broadcasted_iota(jnp.int32, (slice_rows, slice_rows), 0)
               == lax.broadcasted_iota(jnp.int32, (slice_rows, slice_rows), 1)).astype(BF16)
        qkv_copy.wait()
        proj_copy.wait()
        for l in range(LAYERS):
            turned = nt(eye, PROJ[l])
            pieces = [QKV[l, i].astype(F32) for i in range(3)]
            block = jnp.concatenate(pieces + [turned[:, PAIR:], turned[:, :PAIR]], 1).astype(BF16)
            G[3 * l + ATTN, yc, cc, zc, xc] = block.reshape(G.shape[5:])

    row0 = mp * rows
    spans = []
    end = jnp.int32(0)
    for s in range(seq_ref.shape[1]):
        length = seq_ref[0, s]
        spans.append((end, end + length, end + ((length + SPAN - 1) // SPAN) * SPAN))
        end = spans[-1][2]

    def owner(place):
        return sum((place >= stop).astype(jnp.int32) for _, _, stop in spans)

    def owner_at(place):
        return sum(jnp.where(place >= stop, 1, 0) for _, _, stop in spans)

    def same(a, b):
        return jnp.where(owner_at(a) == owner_at(b), 1.0, 0.0).astype(F32)

    row = lax.broadcasted_iota(jnp.int32, (rows, rows), 0) + row0
    col = lax.broadcasted_iota(jnp.int32, (rows, rows), 1) + row0
    own_row, own_col = owner(row), owner(col)
    valid = sum(((row >= a) & (row < b)).astype(F32) for a, b, _ in spans)
    MASKS[0] = ((col <= row) & (own_row == own_col)).astype(F32)
    MASKS[1] = ((row <= col) & (own_row == own_col)).astype(F32)
    MASKS[2] = valid
    came_in = jnp.where(mp > 0, owner_at(row0 - 1), -1)
    MASKS[3] = (own_row == came_in).astype(F32)
    MASKS[4] = (own_row == owner_at(row0 + rows - 1)).astype(F32)
    LOWER, UPPER, VALID, CONT, LAST = range(5)

    def last_of(y, c):
        return (y * 2 + c) * rows + rows - 1

    in_chip = same(last_of(yc, 0), last_of(yc, 1))
    first, second = (cc == 0), (cc == 1)
    f_own = jnp.where(second, 1.0, in_chip)
    f_sis = jnp.where(second, in_chip, 1.0)
    f_a = jnp.where(second, 1.0, 0.0)
    f_b = jnp.where(yc == 1, jnp.where(second, same(last_of(0, 1), last_of(1, 0)), 1.0), 0.0)
    before = same(last_of(0, 1), last_of(1, 0))
    b_own = jnp.where(first, 1.0, before)
    b_sis = jnp.where(first, before, 1.0)
    b_a = jnp.where(first, 1.0, 0.0)
    b_b = jnp.where(yc == 0, jnp.where(first, same(last_of(0, 0), last_of(0, 1)), 1.0), 0.0)

    lane = lax.broadcasted_iota(jnp.int32, (rows, PAIR), 1)
    low = (lane < HD).astype(F32)
    high = 1.0 - low
    left = lane < HD

    pl.semaphore_wait(barrier, len(greeted))

    def maps_start():
        send(MT.at[yc, cc], MT.at[yc, cc], mt_sem.at[1], mt_sem.at[2], across).start()
        send(MT.at[yc, cc], MT.at[yc, cc], mt_sem.at[3], mt_sem.at[4], sister).start()

    def maps_forward():
        send(MT.at[1 - yc, cc], MT.at[1 - yc, cc], mt_sem.at[1], mt_sem.at[2], across).wait()
        send(MT.at[1 - yc, cc], MT.at[1 - yc, cc], mt_sem.at[5], mt_sem.at[6], sister).start()

    def maps_build():
        send(MT.at[yc, cc], MT.at[yc, 1 - cc], mt_sem.at[3], mt_sem.at[4], sister).wait()
        send(MT.at[1 - yc, cc], MT.at[1 - yc, 1 - cc], mt_sem.at[5], mt_sem.at[6], sister).wait()
        half = lax.broadcasted_iota(jnp.int32, (HD, PAIR), 1) < HD
        none = jnp.zeros((HD, PAIR), F32)

        def one(i, carry):
            l, m = i // 4, i % 4
            block = MT[m // 2, m % 2, l].astype(F32)
            for t in range(3):
                pair = block[t * HD:(t + 1) * HD]
                turned = pltpu.roll(pair, HD, 1)
                a = jnp.where(half, pair, -turned)
                b = jnp.where(half, turned, -pair)
                wide = jnp.concatenate(
                    [jnp.concatenate([a, none], 1), jnp.concatenate([none, b], 1)], 0).astype(BF16)
                BD[l, m, t, 0:PAIR] = wide
                BD[l, m, t, PAIR:2 * PAIR] = wide
            BIAS[l, m] = block[3 * HD:3 * HD + 8]
            return carry

        lax.fori_loop(0, 2 * 4, one, 0)

    if gathers:
        def turn(q, p):
            return (q % 2, 0, 1)[p]

        def near(q, p):
            return (x_side, across)[turn(q, p)]

        def far(q, p):
            return (across, x_side)[turn(q, p)]

        def single(q, p, z):
            return G.at[q, yc, cc, z, xc, p]

        def neighbour(q, p, z):
            return (G.at[q, yc, cc, z, 1 - xc, p], G.at[q, 1 - yc, cc, z, xc, p])[turn(q, p)]

        def pair_of(q, p, z):
            return (G.at[q, yc, cc, z, :, p], G.at[q, :, cc, z, xc, p])[turn(q, p)]

        def other_pair(q, p, z):
            return (G.at[q, 1 - yc, cc, z, :, p], G.at[q, :, cc, z, 1 - xc, p])[turn(q, p)]

        def z_unit(q, p, z):
            return single(q, p, z) if p == 0 else pair_of(q, p, z)

        def z_on(q, p, z, way, s):
            @pl.when((zc < 3) if way == 0 else (zc > 0))
            def _():
                send(z_unit(q, p, z), z_unit(q, p, z), z_send.at[q, way, s, min(p, 1)],
                     z_recv.at[q, p, way, s], (z_up, z_down)[way]).start()

        def to_near(q, p, z, slot):
            send(single(q, p, z), single(q, p, z), cross_send.at[q, min(p, 1)],
                 first_recv.at[q, p, slot], near(q, p)).start()

        def to_far(q, p, z):
            send(pair_of(q, p, z), pair_of(q, p, z), cross_send.at[q, 2], last_recv.at[q, p, z],
                 far(q, p)).start()

        def to_sister(q, p, ref):
            send(ref, ref, core_send.at[q], core_recv.at[q, p], sister).start()

        def wait_near(q, p, z, slot):
            ref = neighbour(q, p, z)
            send(ref, ref, cross_send.at[q, 0], first_recv.at[q, p, slot], near(q, p)).wait_recv()

        def wait_far(q, p, z):
            ref = other_pair(q, p, z)
            send(ref, ref, cross_send.at[q, 2], last_recv.at[q, p, z], far(q, p)).wait_recv()

        def have(q, p, z):
            if p == 0:
                to_near(q, p, z, z)
            else:
                to_far(q, p, z)
                to_sister(q, p, pair_of(q, p, z))

        def each_place(s, do):
            pl.when((s > 0) & (zc - s >= 0))(lambda: do(zc - s, 0))
            pl.when((s > 0) & (zc + s <= 3))(lambda: do(zc + s, 1))

        def gather_start(q):
            for p in (1, 2):
                to_near(q, p, zc, 0)

        def z_start(q):
            for p in range(3):
                if p > 0:
                    wait_near(q, p, zc, 0)
                for way in range(2):
                    z_on(q, p, zc, way, 0)
                have(q, p, zc)

        def along_z(q, s):
            def step(z, way):
                for p in range(3):
                    ref = z_unit(q, p, z)
                    send(ref, ref, z_send.at[q, way, s, 0], z_recv.at[q, p, way, s - 1],
                         sister).wait_recv()
                    z_on(q, p, z, way, s)
                    have(q, p, z)

            each_place(s, step)

        def across_first(q, s):
            def step(z, way):
                wait_near(q, 0, z, z)
                to_far(q, 0, z)
                to_sister(q, 0, pair_of(q, 0, z))

            pl.when(s == 0)(lambda: step(zc, None))
            each_place(s, step)

        def across_last(q, s):
            def step(z, way):
                for p in (1, 2, 0):
                    wait_far(q, p, z)
                    to_sister(q, p, other_pair(q, p, z))

            pl.when(s == 0)(lambda: step(zc, None))
            each_place(s, step)

        def comm(k, s):
            if k + 1 < CHUNKS:
                pl.when(s == 0)(lambda: z_start(k + 1))
            if k < CHUNKS:
                along_z(k, s)
            if k + 2 < CHUNKS:
                pl.when(s == 0)(lambda: gather_start(k + 2))
            if k < CHUNKS:
                pl.when(s > 0)(lambda: across_first(k, s - 1))
            if k > 0:
                pl.when(s == 0)(lambda: across_first(k - 1, 3))
                across_last(k - 1, s)

        def ready(q):
            for p in range(3):
                ref = G.at[q, :, 1 - cc, :, :, p]
                send(ref, ref, core_send.at[q], core_recv.at[q, p], sister).wait_recv()

        def drain():
            def sent(ref, sem):
                send(ref, ref, sem, core_recv.at[0, 0], sister).wait_send()

            def one(q, carry):
                for way in range(2):
                    for s in range(3):
                        @pl.when(((zc < 3) & (zc >= s)) if way == 0 else ((zc > 0) & (zc + s <= 3)))
                        def _():
                            sent(G.at[q, 0, 0, 0, 0, 0], z_send.at[q, way, s, 0])
                            sent(G.at[q, 0, 0, :, 0, 0], z_send.at[q, way, s, 1])
                sent(G.at[q, 0, 0, :, 0, 0], cross_send.at[q, 0])
                sent(G.at[q, 0, 0, 0, :, 0], cross_send.at[q, 1])
                sent(G.at[q, 0, 0], cross_send.at[q, 2])
                sent(G.at[q, :, 0], core_send.at[q])
                return carry

            lax.fori_loop(0, CHUNKS, one, 0)
    else:
        def gather_start(q):
            pass

        def z_start(q):
            pass

        def comm(k, s):
            pass

        def ready(q):
            own_copies[q].wait()

        def drain():
            pass

    def weight(q, m, lanes=None):
        if lanes is None:
            return G[q, m // 2, m % 2].reshape(width, width)
        return G[q, m // 2, m % 2, :, :, :, :, lanes].reshape(width, -1)

    def add_blocks(a, ca, b, cb):
        a, b = a.astype(F32), b.astype(F32)
        values = ca * a[:3 * HD] + cb * b[:3 * HD]
        sums = (ca * (a[3 * HD:3 * HD + 8] + a[3 * HD + 8:])
                + cb * (b[3 * HD:3 * HD + 8] + b[3 * HD + 8:]))
        return values, sums

    def block_at(i):
        return (2 * (1 - cc) + i) % 4

    def ex_sister(e, m):
        return send(SB.at[e, 0, m], SB.at[e, 1, m], ex1_send.at[e, m], ex1_recv.at[e, m], sister)

    def ex_across(e, j):
        return send(CH.at[e, j], OT.at[e, cc, j], ex2_send.at[e, 0, j], ex2_recv.at[e, 0, j], across)

    def ex_over(e, j):
        return send(OT.at[e, cc, j], OT.at[e, cc, j], ex2_send.at[e, 1, j], ex2_recv.at[e, 1, j], sister)

    def ex_step(e, i, own, sis):
        m = block_at(i)
        ex_sister(e, m).start()

        @pl.when(i >= 2)
        def _():
            ex_sister(e, m).wait_recv()
            values, sums = add_blocks(SB[e, 0, m], own, SB[e, 1, m], sis)
            CH[e, i - 2, 0:3 * HD] = values.astype(BF16)
            CH[e, i - 2, 3 * HD:] = rows2(*split(sums))
            ex_across(e, i - 2).start()

    def ex_forward(e, j):
        ex_across(e, j).wait_recv()
        ex_over(e, j).start()

    def ex_end(e):
        for j in range(2):
            m = block_at(j)
            ex_sister(e, m).wait_recv()
            ref = OT.at[e, 1 - cc, j]
            send(ref, ref, ex2_send.at[e, 1, j], ex2_recv.at[e, 1, j], sister).wait_recv()

    def ex_drain(e):
        for j in range(2):
            ex_across(e, j).wait_send()
            ex_over(e, j).wait_send()
        for m in range(4):
            ex_sister(e, m).wait_send()

    def softmax(u):
        e = jnp.exp(u - jnp.max(u, axis=-1, keepdims=True))
        return e / jnp.sum(e, axis=-1, keepdims=True)

    def phi_q(l, m, h):
        return PF[l, m, h].astype(BF16)

    def phi_k(l, m, h):
        return (PF[l, m, 3 + h].astype(BF16).astype(F32) * MASKS[VALID]).astype(BF16)

    def attend_features(l, m):
        mixed = nn(N1[...], weight(3 * l + ATTN, m, slice(0, 5 * PAIR)))
        hi, lo = split(mixed[:, :3 * PAIR])
        TQ[l, m, :, 0:3 * PAIR] = hi
        v01 = mixed[:, 3 * PAIR:4 * PAIR].astype(BF16)
        v2 = (mixed[:, 4 * PAIR:] * low).astype(BF16)
        TQ[l, m, :, 3 * PAIR:4 * PAIR] = v01
        TQ[l, m, :, 4 * PAIR:] = v2
        bias = BIAS[l, m]
        for t in range(3):
            tile = slice(t * PAIR, (t + 1) * PAIR)
            u = nn(lanes2(hi[:, tile], lo[:, tile]), BD[l, m, t])
            for e in range(2):
                h = 2 * t + e
                PF[l, m, h] = softmax(u[:, e * PAIR:(e + 1) * PAIR] + bias[h:h + 1])
        last = MASKS[LAST]
        keys = [phi_k(l, m, h).astype(F32) * last for h in range(3)]
        sums = stack_rows([jnp.sum(k, axis=0, keepdims=True) for k in keys], 8)
        keys = [k.astype(BF16) for k in keys]
        two = tn(v01, lanes2(keys[0], keys[1]))
        one = tn(v2, keys[2])
        SB[l, 0, m, 0:HD] = two[:HD, :PAIR].astype(BF16)
        SB[l, 0, m, HD:PAIR] = two[HD:, PAIR:].astype(BF16)
        SB[l, 0, m, PAIR:3 * HD] = one[:HD].astype(BF16)
        SB[l, 0, m, 3 * HD:] = rows2(*split(sums))

    def features_step(l, i):
        attend_features(l, block_at(i))
        ex_step(l, i, f_own, f_sis)

    none_b = jnp.zeros((HD, PAIR), BF16)

    def diagonal(block):
        return rows2(lanes2(block[:HD], none_b), lanes2(none_b, block[HD:PAIR]))

    def attend_out(l, m):
        values, sums = add_blocks(SB[l, 1, m], f_a, OT[l, m // 2, m % 2], f_b)
        carried = values.astype(BF16)
        CAR[l, m] = carried
        CS[l, m] = sums
        valid_now, cont = MASKS[VALID], MASKS[CONT]
        lower = MASKS[LOWER]
        scores, inverse = [], []
        queries = [phi_q(l, m, h) for h in range(3)]
        for h in range(3):
            s = nt(queries[h], phi_k(l, m, h)) * lower
            total = jnp.sum(s + queries[h].astype(F32) * (cont * sums[h:h + 1]), axis=-1, keepdims=True)
            inverse.append(1.0 / (total + (1.0 - valid_now)))
            scores.append(s.astype(BF16))
        v01 = TQ[l, m, :, 3 * PAIR:4 * PAIR].astype(F32)
        v2 = TQ[l, m, :, 4 * PAIR:]
        num = nn(lanes2(scores[0], scores[1]), rows2((v01 * low).astype(BF16), (v01 * high).astype(BF16)))
        num += cont * nt(lanes2(queries[0], queries[1]), diagonal(carried))
        num2 = nn(scores[2], v2) + cont * nt(queries[2], rows2(carried[PAIR:], none_b))
        rd = jnp.where(left, inverse[0], inverse[1])
        att, att2 = valid_now * num * rd, valid_now * num2 * inverse[2]
        RD[l, m, 0] = rd
        RD[l, m, 1] = inverse[2]
        ATT[l, m, 0] = att
        ATT[l, m, 1] = att2
        operand = lanes2(pltpu.roll(att2, HD, 1), att).astype(BF16)
        ACC[...] += nt(operand, weight(3 * l + ATTN, m, slice(4 * PAIR, 6 * PAIR)))

    def loop4(do):
        def one(m, carry):
            do(m)
            return carry

        lax.fori_loop(0, 4, one, 0)

    def attend_end(l):
        ACC[...] = jnp.zeros((rows, width), F32)
        loop4(functools.partial(attend_out, l))
        middle = R[l] + ACC[...]
        MID[l] = middle
        N1[...] = moments(middle)[0].astype(BF16)

    def up(l, m):
        pre = nn(N1[...], weight(3 * l + UP, m))
        PRE[l, m] = pre
        ACT[m] = gelu(pre).astype(BF16)

    def down(l, m):
        ACC[...] += nt(ACT[m], weight(3 * l + DOWN, m))

    def layer_end(l):
        after = MID[l] + ACC[...]
        if l + 1 < LAYERS:
            R[l + 1] = after
            N1[...] = moments(after)[0].astype(BF16)
        else:
            out_ref[...] = after.astype(BF16)

    def clear():
        ACC[...] = jnp.zeros((rows, width), F32)

    def stage(k, every=None, at=()):
        def one(s, carry):
            comm(k, s)
            if every is not None:
                every(s)
            for when, do in at:
                pl.when(s == when)(do)
            return carry

        lax.fori_loop(0, 4, one, 0)

    maps_start()
    gather_start(0)
    if gathers:
        for copy in own_copies:
            copy.wait()
    gather_start(1)
    z_start(0)
    tok_copy.wait()
    x0 = TOK[...].astype(F32)
    R[0] = x0
    N1[...] = moments(x0)[0].astype(BF16)
    stage(0, at=[(1, maps_forward), (3, maps_build)])
    stage(1)
    ready(0)
    stage(2, every=functools.partial(features_step, 0))
    ready(1)

    def middle_part(l):
        ex_end(l)
        attend_end(l)

    stage(3, at=[(0, lambda: ex_forward(0, 0)), (1, lambda: ex_forward(0, 1)),
                 (2, lambda: middle_part(0)), (3, lambda: loop4(functools.partial(up, 0)))])
    ready(2)
    clear()
    stage(4, every=functools.partial(down, 0))
    layer_end(0)
    ready(3)
    stage(5, at=[(0, lambda: loop4(functools.partial(features_step, 1))), (1, lambda: ex_forward(1, 0)),
                 (2, lambda: ex_forward(1, 1)), (3, lambda: middle_part(1))])

    def up_last():
        ready(4)
        loop4(functools.partial(up, 1))
        clear()

    stage(6, at=[(0, up_last)])
    ready(5)
    loop4(functools.partial(down, 1))
    layer_end(1)

    def mlp_back(l, m):
        grad_act = nn(N1[...], weight(3 * l + DOWN, m))
        grad_pre = (gelu_slope(PRE[l, m]) * grad_act).astype(BF16)
        ACC[...] += nt(grad_pre, weight(3 * l + UP, m))

    def place(x, column, column_low, at_left):
        at = 0 if at_left else HD
        keep = high if at_left else low
        out = x * keep
        out = jnp.where(lane == at, column, out)
        return jnp.where(lane == at + 1, column_low, out)

    def heads_of(pair, single_tile, columns):
        return [place(pair, *columns[0], False), place(pair, *columns[1], True),
                place(single_tile, *columns[2], False)]

    ones = [(1.0, 1.0)] * 3

    def attend_back_start(l, m):
        e = 2 + l
        grads = nn(N1[...], weight(3 * l + ATTN, m, slice(4 * PAIR, 6 * PAIR)))
        g01, g2 = grads[:, PAIR:], pltpu.roll(grads[:, :PAIR], HD, 1) * low
        valid_now, cont = MASKS[VALID], MASKS[CONT]
        s01, s2 = g01 * RD[l, m, 0], g2 * RD[l, m, 1]
        p01, p2 = s01 * ATT[l, m, 0], s2 * ATT[l, m, 1]
        dens = [-jnp.sum(p01 * low, axis=-1, keepdims=True), -jnp.sum(p01 * high, axis=-1, keepdims=True),
                -jnp.sum(p2, axis=-1, keepdims=True)]
        num01 = (s01 * valid_now).astype(BF16).astype(F32)
        num2 = (s2 * valid_now).astype(BF16).astype(F32)
        columns = []
        for d in dens:
            top = d.astype(BF16).astype(F32)
            columns.append((top, d - top))
        tiles = heads_of(num01, num2, columns)
        sums = []
        for h in range(3):
            GNH[m, h] = tiles[h].astype(BF16)
            GDEN[m, h] = jnp.broadcast_to(dens[h], (rows, PAIR))
            state = tn((tiles[h] * cont).astype(BF16), phi_q(l, m, h))
            keep, extra = (state[HD:], state[:8]) if h == 1 else (state[:HD], state[HD:HD + 8])
            SB[e, 0, m, h * HD:(h + 1) * HD] = keep.astype(BF16)
            sums.append(extra[0:1] + extra[1:2])
        SB[e, 0, m, 3 * HD:] = rows2(*split(stack_rows(sums, 8)))

    def softmax_back(p, g):
        return p * (g - jnp.sum(p * g, axis=-1, keepdims=True))

    def map_back(l, m, t, a, b):
        two = lanes2(a, b).astype(BF16)
        MIX[m, :, t * PAIR:(t + 1) * PAIR] = nt(two, BD[l, m, t, 0:PAIR]).astype(BF16)
        maps = tn(TQ[l, m, :, t * PAIR:(t + 1) * PAIR], two)
        a, b = maps[:HD, :PAIR], maps[HD:, PAIR:]
        half = lax.broadcasted_iota(jnp.int32, (HD, PAIR), 1) < HD
        both = jnp.where(half, a - pltpu.roll(a, HD, 1), pltpu.roll(b, HD, 1) - b)
        GRF[l, m // 2, m % 2, t * HD:(t + 1) * HD] = both
        GRB[l, m // 2, m % 2, t * HD:(t + 1) * HD] = both.astype(BF16)

    def attend_back_local(l, m):
        cont = MASKS[CONT]
        lower, upper = MASKS[LOWER], MASKS[UPPER]
        v01 = TQ[l, m, :, 3 * PAIR:4 * PAIR].astype(F32)
        v2 = TQ[l, m, :, 4 * PAIR:].astype(F32)
        vals = [v.astype(BF16) for v in heads_of(v01, v2, ones)]
        carried, sums = CAR[l, m], CS[l, m]
        nums = [GNH[m, h] for h in range(3)]
        num01 = (nums[0].astype(F32) * low + nums[1].astype(F32) * high).astype(BF16)
        num2 = (nums[2].astype(F32) * low).astype(BF16)
        from_two = nn(num01, diagonal(carried))
        from_one = nn(num2, rows2(carried[PAIR:], none_b))
        far_part = [from_two[:, :PAIR], from_two[:, PAIR:], from_one]
        back, turned = [], []
        for h in range(3):
            q, k = phi_q(l, m, h), phi_k(l, m, h)
            ds = (nt(nums[h], vals[h]) * lower).astype(BF16)
            dst = (nt(vals[h], nums[h]) * upper).astype(BF16)
            back.append((nt(k, q) * upper).astype(BF16))
            g = nn(ds, k) + cont * (far_part[h] + GDEN[m, h] * sums[h:h + 1])
            turned.append(softmax_back(PF[l, m, h], g))
            GPK[m, h] = nn(dst, q)
        GV[m, 0] = nn(lanes2(back[0], back[1]),
                      rows2((num01.astype(F32) * low).astype(BF16), (num01.astype(F32) * high).astype(BF16)))
        GV[m, 1] = nn(back[2], num2)
        TG[m] = turned[2]
        OFF[m] = stack_rows([jnp.sum(t, axis=0, keepdims=True) for t in turned], 8)
        map_back(l, m, 0, turned[0], turned[1])

    def attend_back_end(l, m):
        e = 2 + l
        values, sums = add_blocks(SB[e, 1, m], b_a, OT[e, m // 2, m % 2], b_b)
        state = values.astype(BF16)
        valid_now, last = MASKS[VALID], MASKS[LAST]
        v01 = TQ[l, m, :, 3 * PAIR:4 * PAIR]
        v2 = TQ[l, m, :, 4 * PAIR:]
        wide, narrow = diagonal(state), rows2(state[PAIR:], none_b)
        from_two, from_one = nn(v01, wide), nn(v2, narrow)
        far_part = [from_two[:, :PAIR], from_two[:, PAIR:], from_one]
        turned = []
        for h in range(3):
            g = valid_now * (GPK[m, h] + last * (far_part[h] + sums[h:h + 1]))
            turned.append(softmax_back(PF[l, m, 3 + h], g))
        map_back(l, m, 1, TG[m], turned[0])
        map_back(l, m, 2, turned[1], turned[2])
        offsets = OFF[m] + stack_rows(
            [jnp.zeros((1, PAIR), F32)] * 3 + [jnp.sum(t, axis=0, keepdims=True) for t in turned], 8)
        offsets = rows2(offsets, jnp.zeros((8, PAIR), F32))
        GRF[l, m // 2, m % 2, 3 * HD:] = offsets
        GRB[l, m // 2, m % 2, 3 * HD:] = offsets.astype(BF16)
        grad_v = GV[m, 0] + last * nt(lanes2(phi_k(l, m, 0), phi_k(l, m, 1)), wide)
        grad_v2 = (GV[m, 1] + last * nt(phi_k(l, m, 2), narrow)) * low
        MIX[m, :, 3 * PAIR:] = lanes2(grad_v, grad_v2).astype(BF16)

    def qkv_back(l, m):
        ACC[...] += nt(MIX[m], weight(3 * l + ATTN, m, slice(0, 5 * PAIR)))

    def sum_at(i):
        return (yc + 1 + i) % 2 * 2 + (cc + 1 + i // 2) % 2

    def part_rows(part):
        return slice(0, HD) if part == 0 else slice(HD, ROWS)

    def sum_sister(l, part, y):
        at = part_rows(part)
        return send(GRB.at[l, y, 1 - cc, at], RB1.at[l, y, at], rd_send.at[l, part, y], rd_recv.at[l, part, y],
                    sister)

    def sum_square(l, part):
        at, bit = part_rows(part), batch % 2
        own, other = PB.at[l, yc, at], PB.at[l, 1 - yc, at]
        slot = SQ.at[l, bit, yc, at]
        return [send(other, slot, rd_send.at[l, part, 2], rd_recv.at[l, part, 2], across),
                send(own, slot, rd_send.at[l, part, 3], rd_recv.at[l, part, 3], partner(0)),
                send(other, slot, rd_send.at[l, part, 4], rd_recv.at[l, part, 4], opposite)]

    def sum_half(l, part, y):
        at = part_rows(part)
        sum_sister(l, part, y).wait_recv()
        PB[l, y, at] = (GRF[l, y, cc, at] + RB1[l, y, at].astype(F32)).astype(BF16)

    def sum_step(l, part, i):
        pl.when(i < 2)(lambda: sum_sister(l, part, sum_at(i) // 2).start())

        @pl.when(i == 2)
        def _():
            sum_half(l, part, 1 - yc)
            copies = sum_square(l, part)
            copies[0].start()
            copies[2].start()

    def sum_chip(l, part):
        at = part_rows(part)
        sum_half(l, part, yc)
        SQ[l, batch % 2, yc, at] = PB[l, yc, at]
        sum_square(l, part)[1].start()

    def sum_over(l, part, k, source, target, device):
        return send(source, target, rd_send.at[l, part, 4 + k], rd_recv.at[l, part, 4 + k], device)

    def sum_z(l, part, k):
        ref = DBL.at[l, zc, part_rows(part)]
        return sum_over(l, part, k, ref, ref, (((zc + k) % 4) * 2 + xc, mp))

    def sum_double(l, part, k):
        at = part_rows(part)
        return sum_over(l, part, k, DBL.at[l, 2 * k, at], DBL.at[l, 2 * k + 1, at], partner(k))

    def sum_batch(l, part):
        at = part_rows(part)
        for copy in sum_square(l, part):
            copy.wait()
        for y in range(2):
            sum_sister(l, part, y).wait_send()
        total = sum(SQ[l, i, j, at].astype(F32) for i in range(2) for j in range(2))
        if gathers:
            DBL[l, zc, at] = total.astype(BF16)
            for k in (1, 2, 3):
                sum_z(l, part, k).start()
        else:
            DBL[l, 2, at] = total.astype(BF16)
            sum_double(l, part, 1).start()

    def sum_end(l, part):
        at = part_rows(part)
        if gathers:
            for k in (1, 2, 3):
                sum_z(l, part, k).wait()
            total = sum(DBL[l, z, at].astype(F32) for z in range(4))
        else:
            for k in range(1, steps):
                sum_double(l, part, k).wait()
                total = DBL[l, 2 * k, at].astype(F32) + DBL[l, 2 * k + 1, at].astype(F32)
                if k + 1 < steps:
                    DBL[l, 2 * k + 2, at] = total.astype(BF16)
                    sum_double(l, part, k + 1).start()
        for i in ((0, 1) if part == 0 else (2, 3, 4, 5)):
            tile = total[(i // 2 - part) * HD:(i // 2 - part + 1) * HD]
            if i % 2:
                tile = pltpu.roll(tile, HD, 1)
            (gq_ref if i < 3 else gk_ref)[l, i % 3] = tile[:, :HD]
        if part == 1:
            offsets = total[2 * HD:2 * HD + 8]
            offsets = offsets - pltpu.roll(offsets, HD, 1)
            for i in range(6):
                (gqb_ref if i < 3 else gkb_ref)[i % 3, l:l + 1] = offsets[i:i + 1, :HD]

    cot_copy.wait()
    GRAD[...] = COT[...].astype(F32)
    N1[...] = COT[...]
    for l in reversed(range(LAYERS)):
        e = 2 + l
        above = l + 1 if l + 1 < LAYERS else None
        clear()
        loop4(functools.partial(mlp_back, l))
        if above is not None:
            sum_batch(above, 1)
        grad_mid = GRAD[...] + norm_back(MID[l], ACC[...])
        GRAD[...] = grad_mid
        N1[...] = grad_mid.astype(BF16)

        def start(i):
            attend_back_start(l, block_at(i))
            ex_step(e, i, b_own, b_sis)

        loop4(start)
        if above is not None:
            sum_end(above, 0)

        def local(i):
            attend_back_local(l, sum_at(i))
            pl.when(i == 1)(lambda: ex_forward(e, 0))
            pl.when(i == 2)(lambda: ex_forward(e, 1))
            sum_step(l, 0, i)

        loop4(local)
        if above is not None:
            sum_end(above, 1)
        ex_end(e)
        sum_chip(l, 0)

        def end(i):
            attend_back_end(l, sum_at(i))
            sum_step(l, 1, i)

        loop4(end)
        sum_chip(l, 1)
        sum_batch(l, 0)
        clear()
        loop4(functools.partial(qkv_back, l))
        if l == 0:
            sum_batch(0, 1)
        GRAD[...] = GRAD[...] + norm_back(R[l], ACC[...])
        N1[...] = GRAD[...].astype(BF16)
    gin_ref[...] = GRAD[...].astype(BF16)
    sum_end(0, 0)
    sum_end(0, 1)
    for e in range(2 * LAYERS):
        ex_drain(e)
    drain()


def hand_out(*refs):
    count = len(refs) // 2
    for source, target in zip(refs[:count], refs[count:]):
        target[...] = source[...]


def per_device(tokens, cotangent, seq_lengths, joined_qkv, attn_proj, mlp_up, mlp_down,
               query_map, query_bias, key_map, key_bias):
    n_batch, n_mp = lax.axis_size("batch"), lax.axis_size("mp")
    rows, width = tokens.shape
    slice_rows = joined_qkv.shape[1]
    heads = query_map.shape[1]
    assert n_mp == 4 and heads == 3 and rows == PAIR and query_map.shape[2] == HD
    assert n_batch & (n_batch - 1) == 0
    parts = 3
    gathers = n_batch == 8 and slice_rows % (16 * parts) == 0
    part_rows = width // (8 * parts)
    qkv, down = joined_qkv.transpose(0, 2, 1, 3), mlp_down.transpose(0, 2, 1)
    if gathers:
        cut = (LAYERS, parts, part_rows, width)
        frozen = (qkv, attn_proj, mlp_up.reshape(cut), down.reshape(cut))
    else:
        turned = jnp.concatenate([attn_proj[:, PAIR:], attn_proj[:, :PAIR]], 1).transpose(0, 2, 1)
        attn = jnp.concatenate([joined_qkv.reshape(LAYERS, slice_rows, -1), turned], 2)
        blocks = jnp.stack([attn, mlp_up, down], 1).reshape(CHUNKS, slice_rows, width)
        weights = lax.all_gather(blocks, "batch", axis=1, tiled=True)
        weights = lax.all_gather(weights, "mp", axis=1, tiled=True)
        frozen = (weights.reshape(CHUNKS, 2, 2, 4, 2, parts, part_rows, width),)

    steps = n_batch.bit_length() - 1
    vmem, dma = pltpu.VMEM, pltpu.SemaphoreType.DMA
    scratch = [
        vmem((CHUNKS, 2, 2, 4, 2, parts, part_rows, width), BF16),
        vmem((rows, width), BF16),
        vmem((rows, width), BF16),
        vmem(qkv.shape, BF16),
        vmem(attn_proj.shape, BF16),
        vmem((2, 2, LAYERS, ROWS, PAIR), BF16),
        vmem((LAYERS, 4, 3, 2 * PAIR, 2 * PAIR), BF16),
        vmem((LAYERS, 4, 8, PAIR), F32),
        vmem((LAYERS, rows, width), F32),
        vmem((LAYERS, rows, width), F32),
        vmem((LAYERS, 4, rows, width), F32),
        vmem((4, rows, width), BF16),
        vmem((LAYERS, 4, rows, 5 * PAIR), BF16),
        vmem((LAYERS, 4, 6, rows, PAIR), F32),
        vmem((LAYERS, 4, 2, rows, PAIR), F32),
        vmem((LAYERS, 4, 2, rows, PAIR), F32),
        vmem((LAYERS, 4, 3 * HD, PAIR), BF16),
        vmem((LAYERS, 4, 8, PAIR), F32),
        vmem((rows, width), BF16),
        vmem((rows, width), F32),
        vmem((rows, width), F32),
        vmem((4, 3, rows, PAIR), BF16),
        vmem((4, 3, rows, PAIR), F32),
        vmem((4, 3, rows, PAIR), F32),
        vmem((4, 2, rows, PAIR), F32),
        vmem((4, rows, PAIR), F32),
        vmem((5, rows, rows), F32),
        vmem((2 * LAYERS, 2, 4, ROWS, PAIR), BF16),
        vmem((2 * LAYERS, 2, ROWS, PAIR), BF16),
        vmem((2 * LAYERS, 2, 2, ROWS, PAIR), BF16),
        vmem((4, rows, 5 * PAIR), BF16),
        vmem((4, 8, PAIR), F32),
        vmem((LAYERS, 2, 2, ROWS, PAIR), F32),
        vmem((LAYERS, 2, 2, ROWS, PAIR), BF16),
        vmem((LAYERS, 2, ROWS, PAIR), BF16),
        vmem((LAYERS, 2, ROWS, PAIR), BF16),
        vmem((LAYERS, 2, 2, ROWS, PAIR), BF16),
        vmem((LAYERS, 4 if gathers else 2 * steps, ROWS, PAIR), BF16),
        dma((CHUNKS,)), dma((4,)),
        dma((7,)),
        dma((2 * LAYERS, 4)), dma((2 * LAYERS, 4)),
        dma((2 * LAYERS, 2, 2)), dma((2 * LAYERS, 2, 2)),
        dma((LAYERS, 2, steps + 5)), dma((LAYERS, 2, steps + 5)),
        dma((CHUNKS, 2, 4, 2)), dma((CHUNKS, parts, 2, 4)),
        dma((CHUNKS, 3)), dma((CHUNKS, parts, 4)), dma((CHUNKS, parts, 4)),
        dma((CHUNKS,)), dma((CHUNKS, parts)),
    ]
    vmem_block, any_block = pl.BlockSpec(memory_space=pltpu.VMEM), pl.BlockSpec(memory_space=pl.ANY)
    shapes = [(tokens.shape, BF16), (tokens.shape, BF16), (query_map.shape, F32), ((heads, LAYERS, HD), F32),
              (key_map.shape, F32), ((heads, LAYERS, HD), F32)]
    shapes = [jax.ShapeDtypeStruct(*shape) for shape in shapes]
    results = pl.pallas_call(
        functools.partial(body, n_batch, gathers),
        out_shape=shapes,
        in_specs=[pl.BlockSpec(memory_space=pltpu.SMEM), any_block, any_block] + [vmem_block] * 4
        + [any_block] * len(frozen),
        out_specs=[vmem_block] * 6,
        scratch_shapes=scratch,
        compiler_params=pltpu.CompilerParams(
            collective_id=0, has_side_effects=True, vmem_limit_bytes=62 * 2**20),
    )(seq_lengths, tokens, cotangent, query_map, query_bias.transpose(1, 0, 2), key_map,
      key_bias.transpose(1, 0, 2), *frozen)
    results = pl.pallas_call(
        hand_out,
        out_shape=shapes,
        in_specs=[vmem_block] * 6,
        out_specs=[vmem_block] * 6,
    )(*results)
    out, grad_in, qmap, qbias, kmap, kbias = results
    return out, grad_in, qmap, qbias.transpose(1, 0, 2), kmap, kbias.transpose(1, 0, 2)


def solution(mesh):
    return jax.shard_map(
        per_device,
        mesh=mesh,
        in_specs=(
            P(("batch", "mp"), None),
            P(("batch", "mp"), None),
            P("batch", None),
            P(None, "batch", None, "mp"),
            P(None, "mp", "batch"),
            P(None, "batch", "mp"),
            P(None, "mp", "batch"),
            P(None, "mp", None, None),
            P(None, "mp", None),
            P(None, "mp", None, None),
            P(None, "mp", None),
        ),
        out_specs=(
            P(("batch", "mp"), None),
            P(("batch", "mp"), None),
            P(None, "mp", None, None),
            P(None, "mp", None),
            P(None, "mp", None, None),
            P(None, "mp", None),
        ),
        check_vma=False,
    )
```

```python
import functools

import jax
import jax.numpy as jnp
from jax import lax
from jax.experimental import pallas as pl
from jax.experimental.pallas import tpu as pltpu
from jax.sharding import PartitionSpec as P

SPAN = 64
LAYERS = 2
EPS = 1e-05
F32, BF16 = jnp.float32, jnp.bfloat16
MESH = pl.DeviceIdType.MESH
ATTN, UP, DOWN = 0, 1, 2
CHUNKS = 3 * LAYERS
HD = 64
PAIR = 2 * HD
ROWS = 3 * HD + 16


def nn(a, b):
    return lax.dot_general(a, b, (((1,), (0,)), ((), ())), preferred_element_type=F32)


def nt(a, b):
    return lax.dot_general(a, b, (((1,), (1,)), ((), ())), preferred_element_type=F32)


def tn(a, b):
    return lax.dot_general(a, b, (((0,), (0,)), ((), ())), preferred_element_type=F32)


def moments(x):
    mean = jnp.mean(x, axis=-1, keepdims=True)
    centered = x - mean
    scale = lax.rsqrt(jnp.mean(centered * centered, axis=-1, keepdims=True) + EPS)
    return centered * scale, scale


def norm_back(y, scale, g):
    mean_g = jnp.mean(g, axis=-1, keepdims=True)
    mean_gy = jnp.mean(g * y, axis=-1, keepdims=True)
    return scale * (g - mean_g - y * mean_gy)


GELU_C = 0.7978845608028654
GELU_A = 0.044715


def gelu_and_slope(x):
    square = x * x
    t = jnp.tanh(GELU_C * x * (1.0 + GELU_A * square))
    inner = GELU_C * (1.0 + 3.0 * GELU_A * square)
    half = 0.5 * (1.0 + t)
    return x * half, half + 0.5 * x * (1.0 - t * t) * inner


def split(x):
    high = x.astype(BF16)
    return high, (x - high.astype(F32)).astype(BF16)


def stack_rows(entries, rows):
    index = lax.broadcasted_iota(jnp.int32, (rows, entries[0].shape[1]), 0)
    out = jnp.zeros((rows, entries[0].shape[1]), F32)
    for i, entry in enumerate(entries):
        out = jnp.where(index == i, entry, out)
    return out


def lanes2(a, b):
    return jnp.concatenate([a, b], 1)


def rows2(a, b):
    return jnp.concatenate([a, b], 0)


def body(n_batch, gathers, *refs):
    seq_ref, tok_hbm, cot_hbm, *map_hbm = refs[:7]
    frozen, refs = (refs[7:11], refs[11:]) if gathers else (refs[7:8], refs[8:])
    results, refs = refs[:6], refs[6:]
    (OUT, GIN, gq_ref, gqb_ref, gk_ref, gkb_ref, qmap_ref, qbias_ref, kmap_ref, kbias_ref,
     G, TOK, COT, QKV, PROJ, MT, BD, BIAS, RES, NORMED, SCALE, SLOPE, ACT, TQ, VH, PF, PHI, PT, ATT, RD, CAR, CS,
     N1, ACC, GRAD, GNH, GDEN, GPK, GV, TG, MASKS, SB, CH, OT,
     MIX, OFF, GRF, GRB, RB1, PB, SQ, DBL,
     own_sem, in_sem, out_sem, mt_sem, ex1_send, ex1_recv, ex2_send, ex2_recv, rd_send, rd_recv,
     z_send, z_recv, cross_send, far_send, first_recv, last_recv, core_send, core_recv) = refs
    rows, width = TOK.shape
    batch, mp = lax.axis_index("batch"), lax.axis_index("mp")
    yc, cc = mp // 2, mp % 2
    sister = (batch, yc * 2 + 1 - cc)
    across = (batch, (1 - yc) * 2 + cc)
    steps = n_batch.bit_length() - 1
    near_batch = batch + 1 - 2 * (batch % 2)
    opposite = (near_batch, (1 - yc) * 2 + cc)

    def partner(k):
        bit = (batch // (1 << k)) % 2
        return (batch + (1 - 2 * bit) * (1 << k), mp)

    def send(src, dst, send_sem, recv_sem, device):
        copy = pltpu.make_async_remote_copy(
            src_ref=src, dst_ref=dst, send_sem=send_sem, recv_sem=recv_sem,
            device_id=device, device_id_type=MESH)
        return copy

    if gathers:
        zc, xc = batch // 2, batch % 2
        greeted = [(((zc + k) % 4) * 2 + xc, mp) for k in (1, 2, 3)]
    else:
        greeted = [partner(k) for k in range(1, steps)]
    greeted += [partner(0), sister, across, opposite]
    barrier = pltpu.get_barrier_semaphore()
    for device in greeted:
        pl.semaphore_signal(barrier, inc=1, device_id=device, device_id_type=MESH)
    tok_copy = pltpu.make_async_copy(tok_hbm, TOK, in_sem.at[0])
    cot_copy = pltpu.make_async_copy(cot_hbm, COT, in_sem.at[1])
    map_copies = [pltpu.make_async_copy(source, target, in_sem.at[4 + i]) for i, (source, target) in enumerate(
        zip(map_hbm, (qmap_ref, qbias_ref, kmap_ref, kbias_ref)))]
    out_copies = [pltpu.make_async_copy(source, target, out_sem.at[i]) for i, (source, target) in enumerate(
        zip((OUT, GIN, gq_ref, gqb_ref, gk_ref, gkb_ref), results))]
    own_copies = []
    if gathers:
        x_side = (zc * 2 + 1 - xc, mp)
        z_up = (jnp.minimum(zc + 1, 3) * 2 + xc, mp)
        z_down = (jnp.maximum(zc - 1, 0) * 2 + xc, mp)
        qkv_hbm, proj_hbm, up_hbm, down_hbm = frozen
        qkv_copy = pltpu.make_async_copy(qkv_hbm, QKV, in_sem.at[2])
        proj_copy = pltpu.make_async_copy(proj_hbm, PROJ, in_sem.at[3])
        qkv_copy.start()
        proj_copy.start()
        tok_copy.start()
        for l in range(LAYERS):
            for part, ref in ((UP, up_hbm), (DOWN, down_hbm)):
                own_copies.append(pltpu.make_async_copy(
                    ref.at[l], G.at[3 * l + part, yc, cc, zc, xc], own_sem.at[3 * l + part]))
    else:
        tok_copy.start()
        own_copies = [pltpu.make_async_copy(frozen[0].at[q], G.at[q], own_sem.at[q])
                      for q in range(CHUNKS)]
    for copy in own_copies:
        copy.start()
    cot_copy.start()
    for copy in map_copies:
        copy.start()

    if gathers:
        slice_rows = QKV.shape[2]
        eye = (lax.broadcasted_iota(jnp.int32, (slice_rows, slice_rows), 0)
               == lax.broadcasted_iota(jnp.int32, (slice_rows, slice_rows), 1)).astype(BF16)
        qkv_copy.wait()
        proj_copy.wait()
        for l in range(LAYERS):
            turned = nt(eye, PROJ[l])
            pieces = [QKV[l, i].astype(F32) for i in range(3)]
            block = jnp.concatenate(pieces + [turned[:, PAIR:], turned[:, :PAIR]], 1).astype(BF16)
            G[3 * l + ATTN, yc, cc, zc, xc] = block.reshape(G.shape[5:])

    row0 = mp * rows
    spans = []
    end = jnp.int32(0)
    for s in range(seq_ref.shape[1]):
        length = seq_ref[0, s]
        spans.append((end, end + length, end + ((length + SPAN - 1) // SPAN) * SPAN))
        end = spans[-1][2]

    def owner(place):
        return sum((place >= stop).astype(jnp.int32) for _, _, stop in spans)

    def owner_at(place):
        return sum(jnp.where(place >= stop, 1, 0) for _, _, stop in spans)

    def same(a, b):
        return jnp.where(owner_at(a) == owner_at(b), 1.0, 0.0).astype(F32)

    row = lax.broadcasted_iota(jnp.int32, (rows, rows), 0) + row0
    col = lax.broadcasted_iota(jnp.int32, (rows, rows), 1) + row0
    own_row, own_col = owner(row), owner(col)
    valid = sum(((row >= a) & (row < b)).astype(F32) for a, b, _ in spans)
    MASKS[0] = ((col <= row) & (own_row == own_col)).astype(F32)
    MASKS[1] = ((row <= col) & (own_row == own_col)).astype(F32)
    MASKS[2] = valid
    came_in = jnp.where(mp > 0, owner_at(row0 - 1), -1)
    MASKS[3] = (own_row == came_in).astype(F32)
    MASKS[4] = (own_row == owner_at(row0 + rows - 1)).astype(F32)
    LOWER, UPPER, VALID, CONT, LAST = range(5)

    def last_of(y, c):
        return (y * 2 + c) * rows + rows - 1

    in_chip = same(last_of(yc, 0), last_of(yc, 1))
    first, second = (cc == 0), (cc == 1)
    f_own = jnp.where(second, 1.0, in_chip)
    f_sis = jnp.where(second, in_chip, 1.0)
    f_a = jnp.where(second, 1.0, 0.0)
    f_b = jnp.where(yc == 1, jnp.where(second, same(last_of(0, 1), last_of(1, 0)), 1.0), 0.0)
    before = same(last_of(0, 1), last_of(1, 0))
    b_own = jnp.where(first, 1.0, before)
    b_sis = jnp.where(first, before, 1.0)
    b_a = jnp.where(first, 1.0, 0.0)
    b_b = jnp.where(yc == 0, jnp.where(first, same(last_of(0, 0), last_of(0, 1)), 1.0), 0.0)

    lane = lax.broadcasted_iota(jnp.int32, (rows, PAIR), 1)
    low = (lane < HD).astype(F32)
    high = 1.0 - low
    left = lane < HD

    for copy in map_copies:
        copy.wait()
    for l in range(LAYERS):
        heads = [ref[l, h].astype(F32) for ref in (qmap_ref, kmap_ref) for h in range(3)]
        for t in range(3):
            MT[yc, cc, l, t * HD:(t + 1) * HD] = jnp.concatenate(
                [heads[2 * t], heads[2 * t + 1]], 1).astype(BF16)
        biases = [ref[h, l:l + 1].astype(F32) for ref in (qbias_ref, kbias_ref) for h in range(3)]
        MT[yc, cc, l, 3 * HD:] = stack_rows(
            [jnp.concatenate([b, -b], 1) for b in biases], 16).astype(BF16)

    pl.semaphore_wait(barrier, len(greeted))

    def maps_start():
        send(MT.at[yc, cc], MT.at[yc, cc], mt_sem.at[1], mt_sem.at[2], across).start()
        send(MT.at[yc, cc], MT.at[yc, cc], mt_sem.at[3], mt_sem.at[4], sister).start()

    def maps_forward():
        send(MT.at[1 - yc, cc], MT.at[1 - yc, cc], mt_sem.at[1], mt_sem.at[2], across).wait()
        send(MT.at[1 - yc, cc], MT.at[1 - yc, cc], mt_sem.at[5], mt_sem.at[6], sister).start()

    def maps_build():
        send(MT.at[yc, cc], MT.at[yc, 1 - cc], mt_sem.at[3], mt_sem.at[4], sister).wait()
        send(MT.at[1 - yc, cc], MT.at[1 - yc, 1 - cc], mt_sem.at[5], mt_sem.at[6], sister).wait()
        half = lax.broadcasted_iota(jnp.int32, (HD, PAIR), 1) < HD
        none = jnp.zeros((HD, PAIR), F32)

        def one(i, carry):
            l, m = i // 4, i % 4
            block = MT[m // 2, m % 2, l].astype(F32)
            for t in range(3):
                pair = block[t * HD:(t + 1) * HD]
                turned = pltpu.roll(pair, HD, 1)
                a = jnp.where(half, pair, -turned)
                b = jnp.where(half, turned, -pair)
                wide = jnp.concatenate(
                    [jnp.concatenate([a, none], 1), jnp.concatenate([none, b], 1)], 0).astype(BF16)
                BD[l, m, t, 0:PAIR] = wide
                BD[l, m, t, PAIR:2 * PAIR] = wide
            BIAS[l, m] = block[3 * HD:3 * HD + 8]
            return carry

        lax.fori_loop(0, 2 * 4, one, 0)

    if gathers:
        parts = (0, 1, 2)

        def turn(q, p):
            return (q % 2, 0, 1)[p]

        def near(q, p):
            return (x_side, across)[turn(q, p)]

        def far(q, p):
            return (across, x_side)[turn(q, p)]

        def single(q, p, z):
            return G.at[q, yc, cc, z, xc, p]

        def neighbour(q, p, z):
            return (G.at[q, yc, cc, z, 1 - xc, p], G.at[q, 1 - yc, cc, z, xc, p])[turn(q, p)]

        def pair_of(q, p, z):
            return (G.at[q, yc, cc, z, :, p], G.at[q, :, cc, z, xc, p])[turn(q, p)]

        def other_pair(q, p, z):
            return (G.at[q, 1 - yc, cc, z, :, p], G.at[q, :, cc, z, 1 - xc, p])[turn(q, p)]

        def early(q, p):
            return q == 0 or p == 0

        def z_unit(q, p, z):
            return single(q, p, z) if early(q, p) else pair_of(q, p, z)

        def arrived(ref, sem):
            send(ref, ref, core_send.at[0], sem, sister).wait_recv()

        def sent(ref, sem):
            send(ref, ref, sem, core_recv.at[0], sister).wait_send()

        def z_on(q, p, z, way, s):
            @pl.when((zc < 3) if way == 0 else (zc > 0))
            def _():
                send(z_unit(q, p, z), z_unit(q, p, z), z_send.at[way, s, 0 if early(q, p) else 1],
                     z_recv.at[q, p, way, s], (z_up, z_down)[way]).start()

        def near_sem(q, p, z):
            if p == 0:
                return first_recv.at[q, z]
            return first_recv.at[CHUNKS - 1 + p, z] if q == 0 else first_recv.at[q, 4]

        def to_near(q, p, z):
            send(single(q, p, z), single(q, p, z), cross_send.at[0 if early(q, p) else 1],
                 near_sem(q, p, z), near(q, p)).start()

        def to_far(q, p, z):
            send(pair_of(q, p, z), pair_of(q, p, z), far_send.at[q], last_recv.at[q, z, min(p, 1)],
                 far(q, p)).start()

        def to_sister(q, ref):
            send(ref, ref, core_send.at[q], core_recv.at[q], sister).start()

        def each_place(s, do):
            pl.when((s > 0) & (zc - s >= 0))(lambda: do(zc - s, 0))
            pl.when((s > 0) & (zc + s <= 3))(lambda: do(zc + s, 1))

        def have(q, p, z):
            if early(q, p):
                to_near(q, p, z)
            else:
                to_far(q, p, z)
                to_sister(q, pair_of(q, p, z))

        def gather_start(q):
            for p in (1, 2):
                if not early(q, p):
                    to_near(q, p, zc)

        def z_start(q):
            for p in parts:
                if p == 1 and not early(q, p):
                    arrived(G.at[q, 0, 0, 0, :, 0], first_recv.at[q, 4])
                for way in range(2):
                    z_on(q, p, zc, way, 0)
                have(q, p, zc)

        def along_z(q, s):
            def step(z, way):
                for p in parts:
                    arrived(z_unit(q, p, z), z_recv.at[q, p, way, s - 1])
                    z_on(q, p, z, way, s)
                    have(q, p, z)

            each_place(s, step)

        def across_first(q, s):
            def step(z, way):
                for p in parts if q == 0 else (0,):
                    arrived(neighbour(q, p, z), near_sem(q, p, z))
                    to_far(q, p, z)
                    to_sister(q, pair_of(q, p, z))

            pl.when(s == 0)(lambda: step(zc, None))
            each_place(s, step)

        def across_last(q, s):
            def step(z, way):
                arrived(G.at[q, 0, 0, 0, :, 0:2], last_recv.at[q, z, 1])
                for p in (1, 2):
                    to_sister(q, other_pair(q, p, z))
                arrived(other_pair(q, 0, z), last_recv.at[q, z, 0])
                to_sister(q, other_pair(q, 0, z))

            pl.when(s == 0)(lambda: step(zc, None))
            each_place(s, step)

        def comm(k, s):
            if 0 <= k - 2 < CHUNKS:
                pl.when(s < 2)(lambda: across_last(k - 2, s + 2))
            if 0 <= k - 1 < CHUNKS:
                pl.when(s > 1)(lambda: across_last(k - 1, s - 2))
            if k < CHUNKS:
                along_z(k, s)
            if k + 2 < CHUNKS:
                pl.when(s == 3)(lambda: z_start(k + 2))
            if 0 <= k - 1 < CHUNKS:
                pl.when(s == 0)(lambda: across_first(k - 1, 3))
            if k < CHUNKS:
                pl.when(s > 0)(lambda: across_first(k, s - 1))
            if k + 2 < CHUNKS:
                pl.when(s == 1)(lambda: gather_start(k + 2))

        def ready(q):
            arrived(G.at[q, :, 1 - cc], core_recv.at[q])

        def drain():
            for way in range(2):
                for s in range(3):
                    @pl.when(((zc < 3) & (zc >= s)) if way == 0 else ((zc > 0) & (zc + s <= 3)))
                    def _():
                        sent(G.at[0:4, 0, 0, 0, :, 0], z_send.at[way, s, 0])
                        sent(G.at[0:5, 0, 0, 0, :, 0:2], z_send.at[way, s, 1])
            sent(G.at[0:4, 0, 0, :, :, 0], cross_send.at[0])
            sent(G.at[0:5, 0, 0, 0, :, 0], cross_send.at[1])
            for q in range(CHUNKS):
                sent(G.at[q, 0, 0], far_send.at[q])
                sent(G.at[q, :, 0], core_send.at[q])
    else:
        def gather_start(q):
            pass

        def ready(q):
            own_copies[q].wait()

        def drain():
            pass

    def weight(q, m, lanes=None):
        if lanes is None:
            return G[q, m // 2, m % 2].reshape(width, width)
        return G[q, m // 2, m % 2, :, :, :, :, lanes].reshape(width, -1)

    def add_blocks(a, ca, b, cb):
        a, b = a.astype(F32), b.astype(F32)
        values = ca * a[:3 * HD] + cb * b[:3 * HD]
        sums = (ca * (a[3 * HD:3 * HD + 8] + a[3 * HD + 8:])
                + cb * (b[3 * HD:3 * HD + 8] + b[3 * HD + 8:]))
        return values, sums

    def block_at(i):
        return (2 * (1 - cc) + i) % 4

    def ex_sister(e, m):
        return send(SB.at[e, 0, m], SB.at[e, 1, m], ex1_send.at[e], ex1_recv.at[e, m], sister)

    def ex_across(e, j):
        return send(CH.at[e, j], OT.at[e, cc, j], ex2_send.at[e], ex2_recv.at[e, 0, j], across)

    def ex_over(e, j):
        return send(OT.at[e, cc, j], OT.at[e, cc, j], ex2_send.at[e], ex2_recv.at[e, 1, j], sister)

    def ex_step(e, i, own, sis):
        m = block_at(i)
        ex_sister(e, m).start()

        def combine():
            ex_sister(e, m).wait_recv()
            values, sums = add_blocks(SB[e, 0, m], own, SB[e, 1, m], sis)
            CH[e, i - 2, 0:3 * HD] = values.astype(BF16)
            CH[e, i - 2, 3 * HD:] = rows2(*split(sums))
            ex_across(e, i - 2).start()

        if isinstance(i, int):
            if i >= 2:
                combine()
        else:
            pl.when(i >= 2)(combine)

    def ex_forward(e, j):
        ex_across(e, j).wait_recv()
        ex_over(e, j).start()

    def ex_end(e):
        for j in range(2):
            m = block_at(j)
            ex_sister(e, m).wait_recv()
            ref = OT.at[e, 1 - cc, j]
            send(ref, ref, ex2_send.at[e], ex2_recv.at[e, 1, j], sister).wait_recv()

    def ex_drain(e):
        four = SB.at[e, 0]
        for sem in (ex1_send.at[e], ex2_send.at[e]):
            send(four, four, sem, ex1_recv.at[e, 0], sister).wait_send()

    def softmax(u):
        e = jnp.exp(u - jnp.max(u, axis=-1, keepdims=True))
        return e / jnp.sum(e, axis=-1, keepdims=True)

    def phi_q(l, m, h):
        return PHI[l, m, h]

    def phi_k(l, m, h):
        return PHI[l, m, 3 + h]

    def place(x, column, column_low, at_left):
        at = 0 if at_left else HD
        keep = high if at_left else low
        out = x * keep
        out = jnp.where(lane == at, column, out)
        return jnp.where(lane == at + 1, column_low, out)

    def heads_of(pair, single_tile, columns):
        return [place(pair, *columns[0], False), place(pair, *columns[1], True),
                place(single_tile, *columns[2], False)]

    ones = [(1.0, 1.0)] * 3

    def attend_features(l, m):
        mixed = nn(N1[...], weight(3 * l + ATTN, m, slice(0, 5 * PAIR)))
        hi, lo = split(mixed[:, :3 * PAIR])
        TQ[l, m, :, 0:3 * PAIR] = hi
        v01 = mixed[:, 3 * PAIR:4 * PAIR].astype(BF16)
        v2 = (mixed[:, 4 * PAIR:] * low).astype(BF16)
        TQ[l, m, :, 3 * PAIR:4 * PAIR] = v01
        TQ[l, m, :, 4 * PAIR:] = v2
        bias = BIAS[l, m]
        for t in range(3):
            tile = slice(t * PAIR, (t + 1) * PAIR)
            u = nn(lanes2(hi[:, tile], lo[:, tile]), BD[l, m, t])
            for e in range(2):
                h = 2 * t + e
                p = softmax(u[:, e * PAIR:(e + 1) * PAIR] + bias[h:h + 1])
                PF[l, m, h] = p
                p = p.astype(BF16)
                PHI[l, m, h] = p if h < 3 else (p.astype(F32) * MASKS[VALID]).astype(BF16)
        for h, v in enumerate(heads_of(v01.astype(F32), v2.astype(F32), ones)):
            VH[l, m, h] = v.astype(BF16)
        last = MASKS[LAST]
        keys = [phi_k(l, m, h).astype(F32) * last for h in range(3)]
        sums = stack_rows([jnp.sum(k, axis=0, keepdims=True) for k in keys], 8)
        keys = [k.astype(BF16) for k in keys]
        two = tn(v01, lanes2(keys[0], keys[1]))
        one = tn(v2, keys[2])
        SB[l, 0, m, 0:HD] = two[:HD, :PAIR].astype(BF16)
        SB[l, 0, m, HD:PAIR] = two[HD:, PAIR:].astype(BF16)
        SB[l, 0, m, PAIR:3 * HD] = one[:HD].astype(BF16)
        SB[l, 0, m, 3 * HD:] = rows2(*split(sums))

    def features_step(l, i):
        attend_features(l, block_at(i))
        ex_step(l, i, f_own, f_sis)

    none_b = jnp.zeros((HD, PAIR), BF16)

    def diagonal(block):
        return rows2(lanes2(block[:HD], none_b), lanes2(none_b, block[HD:PAIR]))

    def attend_out(l, m):
        values, sums = add_blocks(SB[l, 1, m], f_a, OT[l, m // 2, m % 2], f_b)
        carried = values.astype(BF16)
        CAR[l, m] = carried
        CS[l, m] = sums
        valid_now, cont = MASKS[VALID], MASKS[CONT]
        lower = MASKS[LOWER]
        scores, inverse = [], []
        queries = [phi_q(l, m, h) for h in range(3)]
        for h in range(3):
            keys = phi_k(l, m, h)
            s = nt(queries[h], keys) * lower
            PT[l, m, h] = (nt(keys, queries[h]) * MASKS[UPPER]).astype(BF16)
            total = jnp.sum(s + queries[h].astype(F32) * (cont * sums[h:h + 1]), axis=-1, keepdims=True)
            inverse.append(1.0 / (total + (1.0 - valid_now)))
            scores.append(s.astype(BF16))
        v01 = TQ[l, m, :, 3 * PAIR:4 * PAIR].astype(F32)
        v2 = TQ[l, m, :, 4 * PAIR:]
        num = nn(lanes2(scores[0], scores[1]), rows2((v01 * low).astype(BF16), (v01 * high).astype(BF16)))
        num += cont * nt(lanes2(queries[0], queries[1]), diagonal(carried))
        num2 = nn(scores[2], v2) + cont * nt(queries[2], rows2(carried[PAIR:], none_b))
        rd = jnp.where(left, inverse[0], inverse[1])
        att, att2 = valid_now * num * rd, valid_now * num2 * inverse[2]
        RD[l, m, 0] = rd
        RD[l, m, 1] = inverse[2]
        ATT[l, m, 0] = att
        ATT[l, m, 1] = att2
        operand = lanes2(pltpu.roll(att2, HD, 1), att).astype(BF16)
        ACC[...] += nt(operand, weight(3 * l + ATTN, m, slice(4 * PAIR, 6 * PAIR)))

    def loop4(do, unroll=False):
        def one(m, carry):
            do(m)
            return carry

        lax.fori_loop(0, 4, one, 0, unroll=unroll)

    def normalize(l, place, x):
        y, scale = moments(x)
        NORMED[l, place] = y
        SCALE[l, place] = jnp.broadcast_to(scale, (rows, PAIR))
        N1[...] = y.astype(BF16)

    def attend_end(l):
        ACC[...] = jnp.zeros((rows, width), F32)
        loop4(functools.partial(attend_out, l))
        middle = RES[...] + ACC[...]
        RES[...] = middle
        normalize(l, 1, middle)

    def up(l, m):
        pre = nn(N1[...], weight(3 * l + UP, m))
        act, SLOPE[l, m] = gelu_and_slope(pre)
        ACT[m] = act.astype(BF16)

    def down(l, m):
        ACC[...] += nt(ACT[m], weight(3 * l + DOWN, m))

    def layer_end(l):
        after = RES[...] + ACC[...]
        if l + 1 < LAYERS:
            RES[...] = after
            normalize(l + 1, 0, after)
        else:
            OUT[...] = after.astype(BF16)
            out_copies[0].start()

    def clear():
        ACC[...] = jnp.zeros((rows, width), F32)

    def stage(k, at=(), steps=4):
        def one(s, carry):
            comm(k, s)
            for when, do in at:
                pl.when(s == when)(do)
            return carry

        lax.fori_loop(0, steps, one, 0)

    if gathers:
        for copy in own_copies:
            copy.wait()
        for q in range(2):
            gather_start(q)
        z_start(0)
        z_start(1)
    maps_start()
    tok_copy.wait()
    x0 = TOK[...].astype(F32)
    RES[...] = x0
    normalize(0, 0, x0)

    def features(l):
        loop4(functools.partial(features_step, l))

    def forward_states(l):
        ex_forward(l, 0)
        ex_forward(l, 1)

    def middle_part(l):
        ex_end(l)
        attend_end(l)

    def up_all(l):
        loop4(functools.partial(up, l))

    def down_all(l):
        clear()
        loop4(functools.partial(down, l))
        layer_end(l)

    if gathers:
        def attend_first():
            ready(0)
            features(0)

        def feed_first():
            ready(1)
            up_all(0)
            ready(2)
            down_all(0)

        def attend_second():
            ready(3)
            features(1)

        def up_second():
            ready(4)
            up_all(1)

        stage(0)
        stage(1, at=[(1, maps_forward), (3, maps_build)])
        stage(2, at=[(1, attend_first)])
        stage(3, at=[(0, lambda: forward_states(0)), (1, lambda: middle_part(0))])
        stage(4, at=[(1, feed_first)])
        stage(5, at=[(1, attend_second), (3, lambda: forward_states(1))])
        stage(6, at=[(0, lambda: middle_part(1)), (3, up_second)])
        stage(7, steps=2)
        ready(5)
        down_all(1)
    else:
        maps_forward()
        maps_build()
        for l in range(LAYERS):
            ready(3 * l + ATTN)
            features(l)
            forward_states(l)
            middle_part(l)
            ready(3 * l + UP)
            up_all(l)
            ready(3 * l + DOWN)
            down_all(l)


    def mlp_back(l, m):
        grad_act = nn(N1[...], weight(3 * l + DOWN, m))
        grad_pre = (SLOPE[l, m] * grad_act).astype(BF16)
        ACC[...] += nt(grad_pre, weight(3 * l + UP, m))

    def attend_back_start(l, m):
        e = 2 + l
        grads = nn(N1[...], weight(3 * l + ATTN, m, slice(4 * PAIR, 6 * PAIR)))
        g01, g2 = grads[:, PAIR:], pltpu.roll(grads[:, :PAIR], HD, 1) * low
        valid_now, cont = MASKS[VALID], MASKS[CONT]
        s01, s2 = g01 * RD[l, m, 0], g2 * RD[l, m, 1]
        p01, p2 = s01 * ATT[l, m, 0], s2 * ATT[l, m, 1]
        dens = [-jnp.sum(p01 * low, axis=-1, keepdims=True), -jnp.sum(p01 * high, axis=-1, keepdims=True),
                -jnp.sum(p2, axis=-1, keepdims=True)]
        num01 = (s01 * valid_now).astype(BF16).astype(F32)
        num2 = (s2 * valid_now).astype(BF16).astype(F32)
        columns = []
        for d in dens:
            top = d.astype(BF16).astype(F32)
            columns.append((top, d - top))
        tiles = heads_of(num01, num2, columns)
        sums = []
        for h in range(3):
            GNH[m, h] = tiles[h].astype(BF16)
            GDEN[m, h] = jnp.broadcast_to(dens[h], (rows, PAIR))
            state = tn((tiles[h] * cont).astype(BF16), phi_q(l, m, h))
            keep, extra = (state[HD:], state[:8]) if h == 1 else (state[:HD], state[HD:HD + 8])
            SB[e, 0, m, h * HD:(h + 1) * HD] = keep.astype(BF16)
            sums.append(extra[0:1] + extra[1:2])
        SB[e, 0, m, 3 * HD:] = rows2(*split(stack_rows(sums, 8)))

    def softmax_back(p, g):
        return p * (g - jnp.sum(p * g, axis=-1, keepdims=True))

    def map_back(l, m, t, a, b):
        two = lanes2(a, b).astype(BF16)
        MIX[m, :, t * PAIR:(t + 1) * PAIR] = nt(two, BD[l, m, t, 0:PAIR]).astype(BF16)
        maps = tn(TQ[l, m, :, t * PAIR:(t + 1) * PAIR], two)
        a, b = maps[:HD, :PAIR], maps[HD:, PAIR:]
        half = lax.broadcasted_iota(jnp.int32, (HD, PAIR), 1) < HD
        both = jnp.where(half, a - pltpu.roll(a, HD, 1), pltpu.roll(b, HD, 1) - b)
        GRF[l, m // 2, m % 2, t * HD:(t + 1) * HD] = both
        GRB[l, m // 2, m % 2, t * HD:(t + 1) * HD] = both.astype(BF16)

    def attend_back_local(l, m):
        cont = MASKS[CONT]
        lower, upper = MASKS[LOWER], MASKS[UPPER]
        vals = [VH[l, m, h] for h in range(3)]
        carried, sums = CAR[l, m], CS[l, m]
        nums = [GNH[m, h] for h in range(3)]
        num01 = (nums[0].astype(F32) * low + nums[1].astype(F32) * high).astype(BF16)
        num2 = (nums[2].astype(F32) * low).astype(BF16)
        from_two = nn(num01, diagonal(carried))
        from_one = nn(num2, rows2(carried[PAIR:], none_b))
        far_part = [from_two[:, :PAIR], from_two[:, PAIR:], from_one]
        back, turned = [], []
        for h in range(3):
            q, k = phi_q(l, m, h), phi_k(l, m, h)
            ds = (nt(nums[h], vals[h]) * lower).astype(BF16)
            dst = (nt(vals[h], nums[h]) * upper).astype(BF16)
            back.append(PT[l, m, h])
            g = nn(ds, k) + cont * (far_part[h] + GDEN[m, h] * sums[h:h + 1])
            turned.append(softmax_back(PF[l, m, h], g))
            GPK[m, h] = nn(dst, q)
        GV[m, 0] = nn(lanes2(back[0], back[1]),
                      rows2((num01.astype(F32) * low).astype(BF16), (num01.astype(F32) * high).astype(BF16)))
        GV[m, 1] = nn(back[2], num2)
        TG[m] = turned[2]
        OFF[m] = stack_rows([jnp.sum(t, axis=0, keepdims=True) for t in turned], 8)
        map_back(l, m, 0, turned[0], turned[1])

    def attend_back_end(l, m):
        e = 2 + l
        values, sums = add_blocks(SB[e, 1, m], b_a, OT[e, m // 2, m % 2], b_b)
        state = values.astype(BF16)
        valid_now, last = MASKS[VALID], MASKS[LAST]
        v01 = TQ[l, m, :, 3 * PAIR:4 * PAIR]
        v2 = TQ[l, m, :, 4 * PAIR:]
        wide, narrow = diagonal(state), rows2(state[PAIR:], none_b)
        from_two, from_one = nn(v01, wide), nn(v2, narrow)
        far_part = [from_two[:, :PAIR], from_two[:, PAIR:], from_one]
        turned = []
        for h in range(3):
            g = valid_now * (GPK[m, h] + last * (far_part[h] + sums[h:h + 1]))
            turned.append(softmax_back(PF[l, m, 3 + h], g))
        map_back(l, m, 1, TG[m], turned[0])
        map_back(l, m, 2, turned[1], turned[2])
        offsets = OFF[m] + stack_rows(
            [jnp.zeros((1, PAIR), F32)] * 3 + [jnp.sum(t, axis=0, keepdims=True) for t in turned], 8)
        offsets = rows2(offsets, jnp.zeros((8, PAIR), F32))
        GRF[l, m // 2, m % 2, 3 * HD:] = offsets
        GRB[l, m // 2, m % 2, 3 * HD:] = offsets.astype(BF16)
        grad_v = GV[m, 0] + last * nt(lanes2(phi_k(l, m, 0), phi_k(l, m, 1)), wide)
        grad_v2 = (GV[m, 1] + last * nt(phi_k(l, m, 2), narrow)) * low
        MIX[m, :, 3 * PAIR:] = lanes2(grad_v, grad_v2).astype(BF16)

    def qkv_back(l, m):
        ACC[...] += nt(MIX[m], weight(3 * l + ATTN, m, slice(0, 5 * PAIR)))

    def sum_at(i):
        return (yc + 1 + i) % 2 * 2 + (cc + 1 + i // 2) % 2

    def part_rows(part):
        return slice(0, HD) if part == 0 else slice(HD, ROWS)

    def sum_sister(l, part, y):
        at = part_rows(part)
        return send(GRB.at[l, y, 1 - cc, at], RB1.at[l, y, at], rd_send.at[l, part, 0], rd_recv.at[l, part, y],
                    sister)

    def sum_square(l, part):
        at, bit = part_rows(part), batch % 2
        own, other = PB.at[l, yc, at], PB.at[l, 1 - yc, at]
        slot = SQ.at[l, bit, yc, at]
        sems = rd_send.at[l, part, 1], rd_recv.at[l, part, 2]
        return [send(other, slot, *sems, across), send(own, slot, *sems, partner(0)),
                send(other, slot, *sems, opposite)]

    def sum_wait(l, part, k, blocks, receives=True):
        ref = DBL.at[l, 0:blocks, part_rows(part)]
        copy = send(ref, ref, rd_send.at[l, part, k], rd_recv.at[l, part, k + 1], sister)
        copy.wait_send()
        if receives:
            copy.wait_recv()

    def sum_half(l, part, y):
        at = part_rows(part)
        sum_sister(l, part, y).wait_recv()
        PB[l, y, at] = (GRF[l, y, cc, at] + RB1[l, y, at].astype(F32)).astype(BF16)

    def sum_step(l, part, i):
        if i < 2:
            sum_sister(l, part, sum_at(i) // 2).start()
        if i == 2:
            sum_half(l, part, 1 - yc)
            copies = sum_square(l, part)
            copies[0].start()
            copies[2].start()

    def sum_chip(l, part):
        at = part_rows(part)
        sum_half(l, part, yc)
        SQ[l, batch % 2, yc, at] = PB[l, yc, at]
        sum_square(l, part)[1].start()

    def sum_z(l, part, k):
        ref = DBL.at[l, zc, part_rows(part)]
        return send(ref, ref, rd_send.at[l, part, 2], rd_recv.at[l, part, 3], (((zc + k) % 4) * 2 + xc, mp))

    def sum_double(l, part, k):
        at = part_rows(part)
        return send(DBL.at[l, 2 * k, at], DBL.at[l, 2 * k + 1, at], rd_send.at[l, part, 2],
                    rd_recv.at[l, part, 2 + k], partner(k))

    def sum_batch(l, part):
        at = part_rows(part)
        sum_wait(l, part, 1, 3)
        sum_wait(l, part, 0, 2, receives=False)
        total = sum(SQ[l, i, j, at].astype(F32) for i in range(2) for j in range(2))
        if gathers:
            DBL[l, zc, at] = total.astype(BF16)
            for k in (1, 2, 3):
                sum_z(l, part, k).start()
        else:
            DBL[l, 2, at] = total.astype(BF16)
            sum_double(l, part, 1).start()

    def sum_end(l, part):
        at = part_rows(part)
        if gathers:
            sum_wait(l, part, 2, 3)
            total = sum(DBL[l, z, at].astype(F32) for z in range(4))
        else:
            for k in range(1, steps):
                sum_double(l, part, k).wait()
                total = DBL[l, 2 * k, at].astype(F32) + DBL[l, 2 * k + 1, at].astype(F32)
                if k + 1 < steps:
                    DBL[l, 2 * k + 2, at] = total.astype(BF16)
                    sum_double(l, part, k + 1).start()
        for i in ((0, 1) if part == 0 else (2, 3, 4, 5)):
            tile = total[(i // 2 - part) * HD:(i // 2 - part + 1) * HD]
            if i % 2:
                tile = pltpu.roll(tile, HD, 1)
            (gq_ref if i < 3 else gk_ref)[l, i % 3] = tile[:, :HD]
        if part == 1:
            offsets = total[2 * HD:2 * HD + 8]
            offsets = offsets - pltpu.roll(offsets, HD, 1)
            for i in range(6):
                (gqb_ref if i < 3 else gkb_ref)[i % 3, l:l + 1] = offsets[i:i + 1, :HD]

    cot_copy.wait()
    GRAD[...] = COT[...].astype(F32)
    N1[...] = COT[...]
    for l in reversed(range(LAYERS)):
        e = 2 + l
        above = l + 1 if l + 1 < LAYERS else None
        clear()
        loop4(functools.partial(mlp_back, l), True)
        if above is not None:
            sum_batch(above, 0)
            sum_batch(above, 1)
        grad_mid = GRAD[...] + norm_back(NORMED[l, 1], SCALE[l, 1, :, :1], ACC[...])
        GRAD[...] = grad_mid
        N1[...] = grad_mid.astype(BF16)

        for j in range(2):
            for i in (2 * j, 2 * j + 1):
                attend_back_start(l, block_at(i))
            for i in (2 * j, 2 * j + 1):
                ex_step(e, i, b_own, b_sis)
        for j in range(2):
            for i in (2 * j, 2 * j + 1):
                attend_back_local(l, sum_at(i))
            ex_forward(e, j)
            for i in (2 * j, 2 * j + 1):
                sum_step(l, 0, i)
        ex_end(e)
        sum_chip(l, 0)
        for j in range(2):
            for i in (2 * j, 2 * j + 1):
                attend_back_end(l, sum_at(i))
            for i in (2 * j, 2 * j + 1):
                sum_step(l, 1, i)
        sum_chip(l, 1)
        clear()
        for m in range(4):
            qkv_back(l, m)
            if l == 0 and m == 1:
                sum_batch(0, 0)
        if l == 0:
            sum_batch(0, 1)
        GRAD[...] = GRAD[...] + norm_back(NORMED[l, 0], SCALE[l, 0, :, :1], ACC[...])
        N1[...] = GRAD[...].astype(BF16)
    GIN[...] = GRAD[...].astype(BF16)
    out_copies[1].start()
    for e in range(2 * LAYERS):
        ex_drain(e)
    drain()
    for part in range(2):
        sum_end(1, part)
    sum_end(0, 0)
    sum_end(0, 1)
    for copy in out_copies[2:]:
        copy.start()
    for copy in out_copies:
        copy.wait()


def hand_out(*refs):
    count = len(refs) // 2
    for source, target in zip(refs[:count], refs[count:]):
        target[...] = source[...]


def per_device(tokens, cotangent, seq_lengths, joined_qkv, attn_proj, mlp_up, mlp_down,
               query_map, query_bias, key_map, key_bias):
    n_batch, n_mp = lax.axis_size("batch"), lax.axis_size("mp")
    rows, width = tokens.shape
    slice_rows = joined_qkv.shape[1]
    heads = query_map.shape[1]
    assert n_mp == 4 and heads == 3 and rows == PAIR and query_map.shape[2] == HD
    assert n_batch & (n_batch - 1) == 0
    parts = 3
    gathers = n_batch == 8 and slice_rows % (16 * parts) == 0
    part_rows = width // (8 * parts)
    qkv, down = joined_qkv.transpose(0, 2, 1, 3), mlp_down.transpose(0, 2, 1)
    if gathers:
        cut = (LAYERS, parts, part_rows, width)
        frozen = (qkv, attn_proj, mlp_up.reshape(cut), down.reshape(cut))
    else:
        turned = jnp.concatenate([attn_proj[:, PAIR:], attn_proj[:, :PAIR]], 1).transpose(0, 2, 1)
        attn = jnp.concatenate([joined_qkv.reshape(LAYERS, slice_rows, -1), turned], 2)
        blocks = jnp.stack([attn, mlp_up, down], 1).reshape(CHUNKS, slice_rows, width)
        weights = lax.all_gather(blocks, "batch", axis=1, tiled=True)
        weights = lax.all_gather(weights, "mp", axis=1, tiled=True)
        frozen = (weights.reshape(CHUNKS, 2, 2, 4, 2, parts, part_rows, width),)

    steps = n_batch.bit_length() - 1
    vmem, dma = pltpu.VMEM, pltpu.SemaphoreType.DMA
    shapes = [(tokens.shape, BF16), (tokens.shape, BF16), (query_map.shape, F32), ((heads, LAYERS, HD), F32),
              (key_map.shape, F32), ((heads, LAYERS, HD), F32)]
    map_shapes = [query_map.shape, (heads, LAYERS, HD)] * 2
    scratch = [vmem(*shape) for shape in shapes] + [vmem(shape, BF16) for shape in map_shapes] + [
        vmem((CHUNKS, 2, 2, 4, 2, parts, part_rows, width), BF16),
        vmem((rows, width), BF16),
        vmem((rows, width), BF16),
        vmem(qkv.shape, BF16),
        vmem(attn_proj.shape, BF16),
        vmem((2, 2, LAYERS, ROWS, PAIR), BF16),
        vmem((LAYERS, 4, 3, 2 * PAIR, 2 * PAIR), BF16),
        vmem((LAYERS, 4, 8, PAIR), F32),
        vmem((rows, width), F32),
        vmem((LAYERS, 2, rows, width), F32),
        vmem((LAYERS, 2, rows, PAIR), F32),
        vmem((LAYERS, 4, rows, width), F32),
        vmem((4, rows, width), BF16),
        vmem((LAYERS, 4, rows, 5 * PAIR), BF16),
        vmem((LAYERS, 4, 3, rows, PAIR), BF16),
        vmem((LAYERS, 4, 6, rows, PAIR), F32),
        vmem((LAYERS, 4, 6, rows, PAIR), BF16),
        vmem((LAYERS, 4, 3, rows, PAIR), BF16),
        vmem((LAYERS, 4, 2, rows, PAIR), F32),
        vmem((LAYERS, 4, 2, rows, PAIR), F32),
        vmem((LAYERS, 4, 3 * HD, PAIR), BF16),
        vmem((LAYERS, 4, 8, PAIR), F32),
        vmem((rows, width), BF16),
        vmem((rows, width), F32),
        vmem((rows, width), F32),
        vmem((4, 3, rows, PAIR), BF16),
        vmem((4, 3, rows, PAIR), F32),
        vmem((4, 3, rows, PAIR), F32),
        vmem((4, 2, rows, PAIR), F32),
        vmem((4, rows, PAIR), F32),
        vmem((5, rows, rows), F32),
        vmem((2 * LAYERS, 2, 4, ROWS, PAIR), BF16),
        vmem((2 * LAYERS, 2, ROWS, PAIR), BF16),
        vmem((2 * LAYERS, 2, 2, ROWS, PAIR), BF16),
        vmem((4, rows, 5 * PAIR), BF16),
        vmem((4, 8, PAIR), F32),
        vmem((LAYERS, 2, 2, ROWS, PAIR), F32),
        vmem((LAYERS, 2, 2, ROWS, PAIR), BF16),
        vmem((LAYERS, 2, ROWS, PAIR), BF16),
        vmem((LAYERS, 2, ROWS, PAIR), BF16),
        vmem((LAYERS, 2, 2, ROWS, PAIR), BF16),
        vmem((LAYERS, 4 if gathers else 2 * steps, ROWS, PAIR), BF16),
        dma((CHUNKS,)), dma((8,)), dma((6,)),
        dma((7,)),
        dma((2 * LAYERS,)), dma((2 * LAYERS, 4)),
        dma((2 * LAYERS,)), dma((2 * LAYERS, 2, 2)),
        dma((LAYERS, 2, 3)), dma((LAYERS, 2, 4 if gathers else 3 + steps)),
        dma((2, 3, 2)), dma((CHUNKS, parts, 2, 3)),
        dma((2,)), dma((CHUNKS,)),
        dma((CHUNKS + 2, 5)), dma((CHUNKS, 4, 2)),
        dma((CHUNKS,)), dma((CHUNKS,)),
    ]
    vmem_block, any_block = pl.BlockSpec(memory_space=pltpu.VMEM), pl.BlockSpec(memory_space=pl.ANY)
    shapes = [jax.ShapeDtypeStruct(*shape) for shape in shapes]
    results = pl.pallas_call(
        functools.partial(body, n_batch, gathers),
        out_shape=shapes,
        in_specs=[pl.BlockSpec(memory_space=pltpu.SMEM)] + [any_block] * (6 + len(frozen)),
        out_specs=[any_block] * 6,
        scratch_shapes=scratch,
        compiler_params=pltpu.CompilerParams(
            collective_id=0, has_side_effects=True, vmem_limit_bytes=62 * 2**20),
    )(seq_lengths, tokens, cotangent, query_map, query_bias.transpose(1, 0, 2), key_map,
      key_bias.transpose(1, 0, 2), *frozen)
    results = pl.pallas_call(
        hand_out,
        out_shape=shapes,
        in_specs=[vmem_block] * 6,
        out_specs=[vmem_block] * 6,
    )(*results)
    out, grad_in, qmap, qbias, kmap, kbias = results
    return out, grad_in, qmap, qbias.transpose(1, 0, 2), kmap, kbias.transpose(1, 0, 2)


def solution(mesh):
    return jax.shard_map(
        per_device,
        mesh=mesh,
        in_specs=(
            P(("batch", "mp"), None),
            P(("batch", "mp"), None),
            P("batch", None),
            P(None, "batch", None, "mp"),
            P(None, "mp", "batch"),
            P(None, "batch", "mp"),
            P(None, "mp", "batch"),
            P(None, "mp", None, None),
            P(None, "mp", None),
            P(None, "mp", None, None),
            P(None, "mp", None),
        ),
        out_specs=(
            P(("batch", "mp"), None),
            P(("batch", "mp"), None),
            P(None, "mp", None, None),
            P(None, "mp", None),
            P(None, "mp", None, None),
            P(None, "mp", None),
        ),
        check_vma=False,
    )
```

```python
import functools

import jax
import jax.numpy as jnp
from jax import lax
from jax.experimental import pallas as pl
from jax.experimental.pallas import tpu as pltpu
from jax.sharding import PartitionSpec as P

SPAN = 64
LAYERS = 2
EPS = 1e-05
F32, BF16 = jnp.float32, jnp.bfloat16
MESH = pl.DeviceIdType.MESH
ATTN, UP, DOWN = 0, 1, 2
CHUNKS = 3 * LAYERS
FIRST_LAG, LAST_LAG, START_LEAD = 2, 6, 6
TURNS = (1, 1, 0, 1, 1, 0)
HD = 64
PAIR = 2 * HD
ROWS = 3 * HD + 16


def nn(a, b):
    return lax.dot_general(a, b, (((1,), (0,)), ((), ())), preferred_element_type=F32)


def nt(a, b):
    return lax.dot_general(a, b, (((1,), (1,)), ((), ())), preferred_element_type=F32)


def tn(a, b):
    return lax.dot_general(a, b, (((0,), (0,)), ((), ())), preferred_element_type=F32)


def moments(x):
    mean = jnp.mean(x, axis=-1, keepdims=True)
    centered = x - mean
    scale = lax.rsqrt(jnp.mean(centered * centered, axis=-1, keepdims=True) + EPS)
    return centered * scale, scale


def norm_back(y, scale, g):
    mean_g = jnp.mean(g, axis=-1, keepdims=True)
    mean_gy = jnp.mean(g * y, axis=-1, keepdims=True)
    return scale * (g - mean_g - y * mean_gy)


GELU_C = 0.7978845608028654
GELU_A = 0.044715


def gelu_and_slope(x):
    square = x * x
    t = jnp.tanh(GELU_C * x * (1.0 + GELU_A * square))
    inner = GELU_C * (1.0 + 3.0 * GELU_A * square)
    half = 0.5 * (1.0 + t)
    return x * half, half + 0.5 * x * (1.0 - t * t) * inner


def split(x):
    high = x.astype(BF16)
    return high, (x - high.astype(F32)).astype(BF16)


def stack_rows(entries, rows):
    index = lax.broadcasted_iota(jnp.int32, (rows, entries[0].shape[1]), 0)
    out = jnp.zeros((rows, entries[0].shape[1]), F32)
    for i, entry in enumerate(entries):
        out = jnp.where(index == i, entry, out)
    return out


def lanes2(a, b):
    return jnp.concatenate([a, b], 1)


def rows2(a, b):
    return jnp.concatenate([a, b], 0)


def body(n_batch, gathers, *refs):
    seq_ref, tok_hbm, cot_hbm, *map_hbm = refs[:7]
    frozen, refs = (refs[7:11], refs[11:]) if gathers else (refs[7:8], refs[8:])
    results, refs = refs[:6], refs[6:]
    (OUT, GIN, gq_ref, gqb_ref, gk_ref, gkb_ref, qmap_ref, qbias_ref, kmap_ref, kbias_ref,
     G, TOK, COT, QKV, PROJ, MT, BD, BIAS, RES, NORMED, SCALE, SLOPE, ACT, TQ, VH, VL, KL, PF, PHI, PT, ATT, RD, CX,
     N1, ACC, LASTACC, GRAD, GNH, GC, NM, DST, GV, TG, MASKS, SB, CH, OT,
     MIX, OFF, GRF, GRB, RB1, PB, SQ, DBL,
     own_sem, in_sem, out_sem, mt_sem, ex1_send, ex1_recv, ex2_send, ex2_recv, rd_send, rd_recv,
     z_send, z_recv, cross_send, far_send, first_recv, last_recv, core_send, core_recv) = refs
    rows, width = TOK.shape
    batch, mp = lax.axis_index("batch"), lax.axis_index("mp")
    yc, cc = mp // 2, mp % 2
    sister = (batch, yc * 2 + 1 - cc)
    across = (batch, (1 - yc) * 2 + cc)
    steps = n_batch.bit_length() - 1
    near_batch = batch + 1 - 2 * (batch % 2)
    opposite = (near_batch, (1 - yc) * 2 + cc)

    def partner(k):
        bit = (batch // (1 << k)) % 2
        return (batch + (1 - 2 * bit) * (1 << k), mp)

    def send(src, dst, send_sem, recv_sem, device):
        copy = pltpu.make_async_remote_copy(
            src_ref=src, dst_ref=dst, send_sem=send_sem, recv_sem=recv_sem,
            device_id=device, device_id_type=MESH)
        return copy

    if gathers:
        zc, xc = batch // 2, batch % 2
        greeted = [(((zc + k) % 4) * 2 + xc, mp) for k in (1, 2, 3)]
    else:
        greeted = [partner(k) for k in range(1, steps)]
    greeted += [partner(0), sister, across, opposite]
    barrier = pltpu.get_barrier_semaphore()
    for device in greeted:
        pl.semaphore_signal(barrier, inc=1, device_id=device, device_id_type=MESH)
    tok_copy = pltpu.make_async_copy(tok_hbm, TOK, in_sem.at[0])
    cot_copy = pltpu.make_async_copy(cot_hbm, COT, in_sem.at[1])
    map_copies = [pltpu.make_async_copy(source, target, in_sem.at[4 + i]) for i, (source, target) in enumerate(
        zip(map_hbm, (qmap_ref, qbias_ref, kmap_ref, kbias_ref)))]
    out_copies = [pltpu.make_async_copy(source, target, out_sem.at[i]) for i, (source, target) in enumerate(
        zip((OUT, GIN, gq_ref, gqb_ref, gk_ref, gkb_ref), results))]
    own_copies = []
    if gathers:
        x_side = (zc * 2 + 1 - xc, mp)
        z_up = (jnp.minimum(zc + 1, 3) * 2 + xc, mp)
        z_down = (jnp.maximum(zc - 1, 0) * 2 + xc, mp)
        qkv_hbm, proj_hbm, up_hbm, down_hbm = frozen
        qkv_copy = pltpu.make_async_copy(qkv_hbm, QKV, in_sem.at[2])
        proj_copy = pltpu.make_async_copy(proj_hbm, PROJ, in_sem.at[3])
        qkv_copy.start()
        proj_copy.start()
        tok_copy.start()
        for l in range(LAYERS):
            for part, ref in ((UP, up_hbm), (DOWN, down_hbm)):
                own_copies.append(pltpu.make_async_copy(
                    ref.at[l], G.at[3 * l + part, yc, cc, zc, xc], own_sem.at[3 * l + part]))
    else:
        tok_copy.start()
        own_copies = [pltpu.make_async_copy(frozen[0].at[q], G.at[q], own_sem.at[q])
                      for q in range(CHUNKS)]
    for copy in own_copies:
        copy.start()
    cot_copy.start()
    for copy in map_copies:
        copy.start()

    if gathers:
        slice_rows = QKV.shape[2]
        eye = (lax.broadcasted_iota(jnp.int32, (slice_rows, slice_rows), 0)
               == lax.broadcasted_iota(jnp.int32, (slice_rows, slice_rows), 1)).astype(BF16)
        qkv_copy.wait()
        proj_copy.wait()
        for l in range(LAYERS):
            turned = nt(eye, PROJ[l])
            pieces = [QKV[l, i].astype(F32) for i in range(3)]
            block = jnp.concatenate(pieces + [turned[:, PAIR:], turned[:, :PAIR]], 1).astype(BF16)
            G[3 * l + ATTN, yc, cc, zc, xc] = block.reshape(G.shape[5:])

    row0 = mp * rows
    spans = []
    end = jnp.int32(0)
    for s in range(seq_ref.shape[1]):
        length = seq_ref[0, s]
        spans.append((end, end + length, end + ((length + SPAN - 1) // SPAN) * SPAN))
        end = spans[-1][2]

    def owner(place):
        return sum((place >= stop).astype(jnp.int32) for _, _, stop in spans)

    def owner_at(place):
        return sum(jnp.where(place >= stop, 1, 0) for _, _, stop in spans)

    def same(a, b):
        return jnp.where(owner_at(a) == owner_at(b), 1.0, 0.0).astype(F32)

    row = lax.broadcasted_iota(jnp.int32, (rows, rows), 0) + row0
    col = lax.broadcasted_iota(jnp.int32, (rows, rows), 1) + row0
    own_row, own_col = owner(row), owner(col)
    valid = sum(((row >= a) & (row < b)).astype(F32) for a, b, _ in spans)
    MASKS[0] = ((col <= row) & (own_row == own_col)).astype(F32)
    MASKS[1] = ((row <= col) & (own_row == own_col)).astype(F32)
    MASKS[2] = valid
    came_in = jnp.where(mp > 0, owner_at(row0 - 1), -1)
    MASKS[3] = (own_row == came_in).astype(F32)
    MASKS[4] = (own_row == owner_at(row0 + rows - 1)).astype(F32)
    LOWER, UPPER, VALID, CONT, LAST = range(5)

    def last_of(y, c):
        return (y * 2 + c) * rows + rows - 1

    in_chip = same(last_of(yc, 0), last_of(yc, 1))
    first, second = (cc == 0), (cc == 1)
    f_own = jnp.where(second, 1.0, in_chip)
    f_sis = jnp.where(second, in_chip, 1.0)
    f_a = jnp.where(second, 1.0, 0.0)
    f_b = jnp.where(yc == 1, jnp.where(second, same(last_of(0, 1), last_of(1, 0)), 1.0), 0.0)
    before = same(last_of(0, 1), last_of(1, 0))
    b_own = jnp.where(first, 1.0, before)
    b_sis = jnp.where(first, before, 1.0)
    b_a = jnp.where(first, 1.0, 0.0)
    b_b = jnp.where(yc == 0, jnp.where(first, same(last_of(0, 0), last_of(0, 1)), 1.0), 0.0)

    lane = lax.broadcasted_iota(jnp.int32, (rows, PAIR), 1)
    low = (lane < HD).astype(F32)
    high = 1.0 - low
    left = lane < HD

    for copy in map_copies:
        copy.wait()
    for l in range(LAYERS):
        heads = [ref[l, h].astype(F32) for ref in (qmap_ref, kmap_ref) for h in range(3)]
        for t in range(3):
            MT[yc, cc, l, t * HD:(t + 1) * HD] = jnp.concatenate(
                [heads[2 * t], heads[2 * t + 1]], 1).astype(BF16)
        biases = [ref[h, l:l + 1].astype(F32) for ref in (qbias_ref, kbias_ref) for h in range(3)]
        MT[yc, cc, l, 3 * HD:] = stack_rows(
            [jnp.concatenate([b, -b], 1) for b in biases], 16).astype(BF16)

    pl.semaphore_wait(barrier, len(greeted))

    def maps_start():
        send(MT.at[yc, cc], MT.at[yc, cc], mt_sem.at[1], mt_sem.at[2], across).start()
        send(MT.at[yc, cc], MT.at[yc, cc], mt_sem.at[3], mt_sem.at[4], sister).start()

    def maps_forward():
        send(MT.at[1 - yc, cc], MT.at[1 - yc, cc], mt_sem.at[1], mt_sem.at[2], across).wait()
        send(MT.at[1 - yc, cc], MT.at[1 - yc, cc], mt_sem.at[5], mt_sem.at[6], sister).start()

    def maps_build():
        send(MT.at[yc, cc], MT.at[yc, 1 - cc], mt_sem.at[3], mt_sem.at[4], sister).wait()
        send(MT.at[1 - yc, cc], MT.at[1 - yc, 1 - cc], mt_sem.at[5], mt_sem.at[6], sister).wait()
        half = lax.broadcasted_iota(jnp.int32, (HD, PAIR), 1) < HD
        none = jnp.zeros((HD, PAIR), F32)

        def one(i, carry):
            l, m = i // 4, i % 4
            block = MT[m // 2, m % 2, l].astype(F32)
            for t in range(3):
                pair = block[t * HD:(t + 1) * HD]
                turned = pltpu.roll(pair, HD, 1)
                a = jnp.where(half, pair, -turned)
                b = jnp.where(half, turned, -pair)
                wide = jnp.concatenate(
                    [jnp.concatenate([a, none], 1), jnp.concatenate([none, b], 1)], 0).astype(BF16)
                BD[l, m, t, 0:PAIR] = wide
                BD[l, m, t, PAIR:2 * PAIR] = wide
            BIAS[l, m] = block[3 * HD:3 * HD + 8]
            return carry

        lax.fori_loop(0, 2 * 4, one, 0)

    if gathers:
        parts = (0, 1, 2)

        def turn(q, p):
            return (TURNS[q], 0, 1)[p]

        def near(q, p):
            return (x_side, across)[turn(q, p)]

        def far(q, p):
            return (across, x_side)[turn(q, p)]

        def single(q, p, z):
            return G.at[q, yc, cc, z, xc, p]

        def neighbour(q, p, z):
            return (G.at[q, yc, cc, z, 1 - xc, p], G.at[q, 1 - yc, cc, z, xc, p])[turn(q, p)]

        def pair_of(q, p, z):
            return (G.at[q, yc, cc, z, :, p], G.at[q, :, cc, z, xc, p])[turn(q, p)]

        def other_pair(q, p, z):
            return (G.at[q, 1 - yc, cc, z, :, p], G.at[q, :, cc, z, 1 - xc, p])[turn(q, p)]

        def early(q, p):
            return q == 0 or p == 0

        def z_unit(q, p, z):
            return single(q, p, z) if early(q, p) else pair_of(q, p, z)

        def arrived(ref, sem):
            send(ref, ref, core_send.at[0], sem, sister).wait_recv()

        def sent(ref, sem):
            send(ref, ref, sem, core_recv.at[0], sister).wait_send()

        def z_on(q, p, z, way, s):
            @pl.when((zc < 3) if way == 0 else (zc > 0))
            def _():
                send(z_unit(q, p, z), z_unit(q, p, z), z_send.at[way, s, 0 if early(q, p) else 1],
                     z_recv.at[q, p, way, s], (z_up, z_down)[way]).start()

        def near_sem(q, p, z):
            if p == 0:
                return first_recv.at[q, z]
            return first_recv.at[CHUNKS - 1 + p, z] if q == 0 else first_recv.at[q, 4]

        def to_near(q, p, z):
            send(single(q, p, z), single(q, p, z), cross_send.at[0 if early(q, p) else 1],
                 near_sem(q, p, z), near(q, p)).start()

        def to_far(q, p, z):
            send(pair_of(q, p, z), pair_of(q, p, z), far_send.at[q], last_recv.at[q, z, min(p, 1)],
                 far(q, p)).start()

        def to_sister(q, ref):
            send(ref, ref, core_send.at[q], core_recv.at[q], sister).start()

        def each_place(s, do):
            pl.when((s > 0) & (zc - s >= 0))(lambda: do(zc - s, 0))
            pl.when((s > 0) & (zc + s <= 3))(lambda: do(zc + s, 1))

        def have(q, p, z):
            if early(q, p):
                to_near(q, p, z)
            else:
                to_far(q, p, z)
                to_sister(q, pair_of(q, p, z))

        def gather_start(q):
            for p in (1, 2):
                if not early(q, p):
                    to_near(q, p, zc)

        def z_start(q):
            for p in parts:
                if p == 1 and not early(q, p):
                    arrived(G.at[q, 0, 0, 0, :, 0], first_recv.at[q, 4])
                for way in range(2):
                    z_on(q, p, zc, way, 0)
                have(q, p, zc)

        def along_z(q, s):
            def step(z, way):
                for p in parts:
                    arrived(z_unit(q, p, z), z_recv.at[q, p, way, s - 1])
                    z_on(q, p, z, way, s)
                    have(q, p, z)

            each_place(s, step)

        def across_first(q, s):
            def step(z, way):
                for p in parts if q == 0 else (0,):
                    arrived(neighbour(q, p, z), near_sem(q, p, z))
                    to_far(q, p, z)
                    to_sister(q, pair_of(q, p, z))

            pl.when(s == 0)(lambda: step(zc, None))
            each_place(s, step)

        def across_last(q, s):
            def step(z, way):
                arrived(G.at[q, 0, 0, 0, :, 0:2], last_recv.at[q, z, 1])
                for p in (1, 2):
                    to_sister(q, other_pair(q, p, z))
                arrived(other_pair(q, 0, z), last_recv.at[q, z, 0])
                to_sister(q, other_pair(q, 0, z))

            pl.when(s == 0)(lambda: step(zc, None))
            each_place(s, step)

        def later(k, s, lag, do):
            stages, steps = divmod(lag, 4)
            if 0 <= k - stages < CHUNKS:
                pl.when(s >= steps)(lambda: do(k - stages, s - steps))
            if steps and 0 <= k - stages - 1 < CHUNKS:
                pl.when(s < steps)(lambda: do(k - stages - 1, s + 4 - steps))

        start_step = -START_LEAD % 4
        ahead = (start_step + START_LEAD) // 4

        def comm(k, s):
            later(k, s, LAST_LAG, across_last)
            later(k, s, FIRST_LAG, across_first)
            if k < CHUNKS:
                along_z(k, s)
            if (k + ahead) < CHUNKS:
                pl.when(s == start_step)(lambda: z_start(k + ahead))

        def ready(q):
            arrived(G.at[q, :, 1 - cc], core_recv.at[q])

        def drain():
            for way in range(2):
                for s in range(3):
                    @pl.when(((zc < 3) & (zc >= s)) if way == 0 else ((zc > 0) & (zc + s <= 3)))
                    def _():
                        sent(G.at[0:4, 0, 0, 0, :, 0], z_send.at[way, s, 0])
                        sent(G.at[0:5, 0, 0, 0, :, 0:2], z_send.at[way, s, 1])
            sent(G.at[0:4, 0, 0, :, :, 0], cross_send.at[0])
            sent(G.at[0:5, 0, 0, 0, :, 0], cross_send.at[1])
            for q in range(CHUNKS):
                sent(G.at[q, 0, 0], far_send.at[q])
                sent(G.at[q, :, 0], core_send.at[q])
    else:
        def gather_start(q):
            pass

        def ready(q):
            own_copies[q].wait()

        def drain():
            pass

    def weight(q, m, lanes=None):
        if lanes is None:
            return G[q, m // 2, m % 2].reshape(width, width)
        return G[q, m // 2, m % 2, :, :, :, :, lanes].reshape(width, -1)

    def add_blocks(a, ca, b, cb):
        a, b = a.astype(F32), b.astype(F32)
        values = ca * a[:3 * HD] + cb * b[:3 * HD]
        sums = (ca * (a[3 * HD:3 * HD + 8] + a[3 * HD + 8:])
                + cb * (b[3 * HD:3 * HD + 8] + b[3 * HD + 8:]))
        return values, sums

    def block_at(i):
        return (2 * (1 - cc) + i) % 4

    def ex_sister(e, m):
        return send(SB.at[e, 0, m], SB.at[e, 1, m], ex1_send.at[e], ex1_recv.at[e, m], sister)

    def ex_across(e, j):
        return send(CH.at[e, j], OT.at[e, cc, j], ex2_send.at[e], ex2_recv.at[e, 0, j], across)

    def ex_over(e, j):
        return send(OT.at[e, cc, j], OT.at[e, cc, j], ex2_send.at[e], ex2_recv.at[e, 1, j], sister)

    def ex_step(e, i, own, sis):
        m = block_at(i)
        ex_sister(e, m).start()

        def combine():
            ex_sister(e, m).wait_recv()
            values, sums = add_blocks(SB[e, 0, m], own, SB[e, 1, m], sis)
            CH[e, i - 2, 0:3 * HD] = values.astype(BF16)
            CH[e, i - 2, 3 * HD:] = rows2(*split(sums))
            ex_across(e, i - 2).start()

        if isinstance(i, int):
            if i >= 2:
                combine()
        else:
            pl.when(i >= 2)(combine)

    def ex_forward(e, j):
        ex_across(e, j).wait_recv()
        ex_over(e, j).start()

    def ex_end(e):
        for j in range(2):
            m = block_at(j)
            ex_sister(e, m).wait_recv()
            ref = OT.at[e, 1 - cc, j]
            send(ref, ref, ex2_send.at[e], ex2_recv.at[e, 1, j], sister).wait_recv()

    def ex_drain(e):
        four = SB.at[e, 0]
        for sem in (ex1_send.at[e], ex2_send.at[e]):
            send(four, four, sem, ex1_recv.at[e, 0], sister).wait_send()

    def softmax(u):
        e = jnp.exp(u - jnp.max(u, axis=-1, keepdims=True))
        return e / jnp.sum(e, axis=-1, keepdims=True)

    def phi_q(l, m, h):
        return PHI[l, m, h]

    def phi_k(l, m, h):
        return PHI[l, m, 3 + h]

    def place(x, columns, at_left):
        at = 0 if at_left else HD
        out = x * (high if at_left else low)
        for i, column in enumerate(columns):
            out = jnp.where(lane == at + i, column, out)
        return out

    def heads_of(pair, single_tile, columns):
        return [place(pair, columns[0], False), place(pair, columns[1], True), place(single_tile, columns[2], False)]

    def attend_features(l, m):
        mixed = nn(N1[...], weight(3 * l + ATTN, m, slice(0, 5 * PAIR)))
        hi, lo = split(mixed[:, :3 * PAIR])
        TQ[l, m, :, 0:3 * PAIR] = hi
        v01 = mixed[:, 3 * PAIR:4 * PAIR].astype(BF16)
        v2 = (mixed[:, 4 * PAIR:] * low).astype(BF16)
        TQ[l, m, :, 3 * PAIR:4 * PAIR] = v01
        TQ[l, m, :, 4 * PAIR:] = v2
        bias = BIAS[l, m]
        for t in range(3):
            tile = slice(t * PAIR, (t + 1) * PAIR)
            u = nn(lanes2(hi[:, tile], lo[:, tile]), BD[l, m, t])
            for e in range(2):
                h = 2 * t + e
                p = softmax(u[:, e * PAIR:(e + 1) * PAIR] + bias[h:h + 1])
                PF[l, m, h] = p
                p = p.astype(BF16)
                PHI[l, m, h] = p if h < 3 else (p.astype(F32) * MASKS[VALID]).astype(BF16)
        last = MASKS[LAST]
        for h, v in enumerate(heads_of(v01.astype(F32), v2.astype(F32), [(1.0, 1.0)] * 3)):
            VH[l, m, h] = v.astype(BF16)
            VL[l, m, h] = (v * last).astype(BF16)
        keys = [phi_k(l, m, h).astype(F32) * last for h in range(3)]
        sums = stack_rows([jnp.sum(k, axis=0, keepdims=True) for k in keys], 8)
        keys = [k.astype(BF16) for k in keys]
        for h in range(3):
            KL[l, m, h] = keys[h]
        two = tn(v01, lanes2(keys[0], keys[1]))
        one = tn(v2, keys[2])
        SB[l, 0, m, 0:HD] = two[:HD, :PAIR].astype(BF16)
        SB[l, 0, m, HD:PAIR] = two[HD:, PAIR:].astype(BF16)
        SB[l, 0, m, PAIR:3 * HD] = one[:HD].astype(BF16)
        SB[l, 0, m, 3 * HD:] = rows2(*split(sums))

    def features_step(l, i):
        attend_features(l, block_at(i))
        ex_step(l, i, f_own, f_sis)

    none_b = jnp.zeros((HD, PAIR), BF16)

    def beside(block, h, entries):
        state = block[h * HD:(h + 1) * HD]
        extra = stack_rows([entry.astype(F32) for entry in entries], HD).astype(BF16)
        return rows2(extra, state) if h == 1 else rows2(state, extra)

    def diagonal(block):
        return rows2(lanes2(block[:HD], none_b), lanes2(none_b, block[HD:PAIR]))

    def attend_out(l, m):
        values, sums = add_blocks(SB[l, 1, m], f_a, OT[l, m // 2, m % 2], f_b)
        carried = values.astype(BF16)
        for h in range(3):
            top, rest = split(sums[h:h + 1])
            CX[l, m, h] = beside(carried, h, [top, top, rest])
        valid_now, cont = MASKS[VALID], MASKS[CONT]
        lower = MASKS[LOWER]
        scores, inverse = [], []
        queries = [phi_q(l, m, h) for h in range(3)]
        for h in range(3):
            keys = phi_k(l, m, h)
            s = nt(queries[h], keys) * lower
            PT[l, m, h] = (nt(keys, queries[h]) * MASKS[UPPER]).astype(BF16)
            total = jnp.sum(s + queries[h].astype(F32) * (cont * sums[h:h + 1]), axis=-1, keepdims=True)
            inverse.append(1.0 / (total + (1.0 - valid_now)))
            scores.append(s.astype(BF16))
        v01 = TQ[l, m, :, 3 * PAIR:4 * PAIR].astype(F32)
        v2 = TQ[l, m, :, 4 * PAIR:]
        num = nn(lanes2(scores[0], scores[1]), rows2((v01 * low).astype(BF16), (v01 * high).astype(BF16)))
        num += cont * nt(lanes2(queries[0], queries[1]), diagonal(carried))
        num2 = nn(scores[2], v2) + cont * nt(queries[2], rows2(carried[PAIR:], none_b))
        rd = jnp.where(left, inverse[0], inverse[1])
        att, att2 = valid_now * num * rd, valid_now * num2 * inverse[2]
        RD[l, m, 0] = rd
        RD[l, m, 1] = inverse[2]
        ATT[l, m, 0] = att
        ATT[l, m, 1] = att2
        operand = lanes2(pltpu.roll(att2, HD, 1), att).astype(BF16)
        ACC[...] += nt(operand, weight(3 * l + ATTN, m, slice(4 * PAIR, 6 * PAIR)))

    def loop4(do, unroll=False):
        def one(m, carry):
            do(m)
            return carry

        lax.fori_loop(0, 4, one, 0, unroll=unroll)

    def normalize(l, place, x):
        y, scale = moments(x)
        NORMED[l, place] = y
        SCALE[l, place] = jnp.broadcast_to(scale, (rows, PAIR))
        N1[...] = y.astype(BF16)

    def attend_end(l):
        ACC[...] = jnp.zeros((rows, width), F32)
        loop4(functools.partial(attend_out, l))
        middle = RES[...] + ACC[...]
        RES[...] = middle
        normalize(l, 1, middle)

    def up(l, m):
        pre = nn(N1[...], weight(3 * l + UP, m))
        act, SLOPE[l, m] = gelu_and_slope(pre)
        ACT[m] = act.astype(BF16)

    def down(l, m):
        ACC[...] += nt(ACT[m], weight(3 * l + DOWN, m))

    def layer_end(l):
        after = RES[...] + ACC[...]
        RES[...] = after
        normalize(l + 1, 0, after)

    def last_down(first, count):
        total = 0.0 if first == 0 else LASTACC[...]
        for m in range(first, first + count):
            total += nt(ACT[m], weight(3 * (LAYERS - 1) + DOWN, m))
        LASTACC[...] = total

    def last_end():
        OUT[...] = (RES[...] + LASTACC[...]).astype(BF16)
        out_copies[0].start()

    def clear():
        ACC[...] = jnp.zeros((rows, width), F32)

    def stage(k, at=(), steps=4):
        def one(s, carry):
            comm(k, s)
            for when, do in at:
                pl.when(s == when)(do)
            return carry

        lax.fori_loop(0, steps, one, 0)

    if gathers:
        for copy in own_copies:
            copy.wait()
        for q in range(CHUNKS):
            gather_start(q)
        for q in range(CHUNKS):
            if 4 * q < START_LEAD:
                z_start(q)
    maps_start()
    tok_copy.wait()
    x0 = TOK[...].astype(F32)
    RES[...] = x0
    normalize(0, 0, x0)

    def features(l):
        loop4(functools.partial(features_step, l))

    def forward_states(l):
        ex_forward(l, 0)
        ex_forward(l, 1)

    def middle_part(l):
        ex_end(l)
        attend_end(l)

    def up_all(l):
        loop4(functools.partial(up, l))

    def down_all(l):
        clear()
        loop4(functools.partial(down, l))
        layer_end(l)

    if gathers:
        def attend_first():
            ready(0)
            features(0)

        def up_first():
            ready(1)
            up_all(0)

        def down_first():
            ready(2)
            down_all(0)

        def attend_second():
            ready(3)
            features(1)

        def up_second():
            ready(4)
            up_all(1)

        stage(0, at=[(3, maps_forward)])
        stage(1, at=[(0, maps_build)])
        stage(2, at=[(1, attend_first)])
        stage(3, at=[(0, lambda: forward_states(0)), (1, lambda: middle_part(0)), (2, up_first)])
        stage(4, at=[(1, down_first)])
        stage(5, at=[(1, attend_second), (2, lambda: forward_states(1)), (3, lambda: middle_part(1))])
        stage(6, at=[(3, up_second)])
        stage(7, steps=2)
    else:
        maps_forward()
        maps_build()
        for l in range(LAYERS):
            ready(3 * l + ATTN)
            features(l)
            forward_states(l)
            middle_part(l)
            ready(3 * l + UP)
            up_all(l)
            if l + 1 < LAYERS:
                ready(3 * l + DOWN)
                down_all(l)


    def mlp_back(l, m):
        grad_act = nn(N1[...], weight(3 * l + DOWN, m))
        grad_pre = (SLOPE[l, m] * grad_act).astype(BF16)
        ACC[...] += nt(grad_pre, weight(3 * l + UP, m))

    row_half = lax.broadcasted_iota(jnp.int32, (2 * PAIR, PAIR), 0) % PAIR < HD
    lane_half = lax.broadcasted_iota(jnp.int32, (2 * PAIR, PAIR), 1) < HD
    across_halves = (row_half != lane_half).astype(BF16)

    def attend_back_start(l, m):
        e = 2 + l
        grads = nn(N1[...], weight(3 * l + ATTN, m, slice(4 * PAIR, 6 * PAIR)))
        g01, g2 = grads[:, PAIR:], pltpu.roll(grads[:, :PAIR], HD, 1) * low
        valid_now, cont = MASKS[VALID], MASKS[CONT]
        s01, s2 = g01 * RD[l, m, 0], g2 * RD[l, m, 1]
        p01, p2 = s01 * ATT[l, m, 0], s2 * ATT[l, m, 1]
        dens = [-nn(lanes2(*split(p)), across_halves) for p in (p01, p2)]
        num01 = (s01 * valid_now).astype(BF16)
        num2 = (s2 * valid_now).astype(BF16)
        NM[m, 0] = num01
        NM[m, 1] = num2
        columns = []
        for d in dens:
            top = d.astype(BF16).astype(F32)
            columns.append((top, d - top, top))
        tiles = heads_of(num01.astype(F32), num2.astype(F32), [columns[0], columns[0], columns[1]])
        sums = []
        for h in range(3):
            GNH[m, h] = tiles[h].astype(BF16)
            counted = (tiles[h] * cont).astype(BF16)
            GC[m, h] = counted
            state = tn(counted, phi_q(l, m, h))
            keep, extra = (state[HD:], state[:8]) if h == 1 else (state[:HD], state[HD:HD + 8])
            SB[e, 0, m, h * HD:(h + 1) * HD] = keep.astype(BF16)
            sums.append(extra[0:1] + extra[1:2])
        SB[e, 0, m, 3 * HD:] = rows2(*split(stack_rows(sums, 8)))

    def softmax_back(p, g):
        return p * (g - jnp.sum(p * g, axis=-1, keepdims=True))

    def map_back(l, m, t, a, b):
        two = lanes2(a, b).astype(BF16)
        MIX[m, :, t * PAIR:(t + 1) * PAIR] = nt(two, BD[l, m, t, 0:PAIR]).astype(BF16)
        maps = tn(TQ[l, m, :, t * PAIR:(t + 1) * PAIR], two)
        a, b = maps[:HD, :PAIR], maps[HD:, PAIR:]
        half = lax.broadcasted_iota(jnp.int32, (HD, PAIR), 1) < HD
        both = jnp.where(half, a - pltpu.roll(a, HD, 1), pltpu.roll(b, HD, 1) - b)
        GRF[l, m // 2, m % 2, t * HD:(t + 1) * HD] = both
        GRB[l, m // 2, m % 2, t * HD:(t + 1) * HD] = both.astype(BF16)

    def attend_back_local(l, m):
        lower, upper = MASKS[LOWER], MASKS[UPPER]
        turned = []
        for h in range(3):
            q, k = phi_q(l, m, h), phi_k(l, m, h)
            nums, vals = GNH[m, h], VH[l, m, h]
            ds = (nt(nums, vals) * lower).astype(BF16)
            DST[m, h] = (nt(vals, nums) * upper).astype(BF16)
            g = nn(lanes2(ds, GC[m, h]), rows2(k, CX[l, m, h]))
            turned.append(softmax_back(PF[l, m, h], g))
        num01 = NM[m, 0].astype(F32)
        GV[m, 0] = nn(lanes2(PT[l, m, 0], PT[l, m, 1]),
                      rows2((num01 * low).astype(BF16), (num01 * high).astype(BF16)))
        GV[m, 1] = nn(PT[l, m, 2], NM[m, 1])
        TG[m] = turned[2]
        OFF[m] = stack_rows([jnp.sum(t, axis=0, keepdims=True) for t in turned], 8)
        map_back(l, m, 0, turned[0], turned[1])

    def attend_back_end(l, m):
        e = 2 + l
        values, sums = add_blocks(SB[e, 1, m], b_a, OT[e, m // 2, m % 2], b_b)
        state = values.astype(BF16)
        valid_now = MASKS[VALID]
        turned = []
        for h in range(3):
            far = beside(state, h, split(sums[h:h + 1]))
            g = valid_now * nn(lanes2(DST[m, h], VL[l, m, h]), rows2(phi_q(l, m, h), far))
            turned.append(softmax_back(PF[l, m, 3 + h], g))
        map_back(l, m, 1, TG[m], turned[0])
        map_back(l, m, 2, turned[1], turned[2])
        offsets = OFF[m] + stack_rows(
            [jnp.zeros((1, PAIR), F32)] * 3 + [jnp.sum(t, axis=0, keepdims=True) for t in turned], 8)
        offsets = rows2(offsets, jnp.zeros((8, PAIR), F32))
        GRF[l, m // 2, m % 2, 3 * HD:] = offsets
        GRB[l, m // 2, m % 2, 3 * HD:] = offsets.astype(BF16)
        grad_v = GV[m, 0] + nt(lanes2(KL[l, m, 0], KL[l, m, 1]), diagonal(state))
        grad_v2 = (GV[m, 1] + nt(KL[l, m, 2], rows2(state[PAIR:], none_b))) * low
        MIX[m, :, 3 * PAIR:] = lanes2(grad_v, grad_v2).astype(BF16)

    def qkv_back(l, m):
        ACC[...] += nt(MIX[m], weight(3 * l + ATTN, m, slice(0, 5 * PAIR)))

    def sum_at(i):
        return (yc + 1 + i) % 2 * 2 + (cc + 1 + i // 2) % 2

    def part_rows(part):
        return slice(0, HD) if part == 0 else slice(HD, ROWS)

    def sum_sister(l, part, y):
        at = part_rows(part)
        return send(GRB.at[l, y, 1 - cc, at], RB1.at[l, y, at], rd_send.at[l, part, 0], rd_recv.at[l, part, y],
                    sister)

    def sum_square(l, part):
        at, bit = part_rows(part), batch % 2
        own, other = PB.at[l, yc, at], PB.at[l, 1 - yc, at]
        slot = SQ.at[l, bit, yc, at]
        sems = rd_send.at[l, part, 1], rd_recv.at[l, part, 2]
        return [send(other, slot, *sems, across), send(own, slot, *sems, partner(0)),
                send(other, slot, *sems, opposite)]

    def sum_wait(l, part, k, blocks, receives=True):
        ref = DBL.at[l, 0:blocks, part_rows(part)]
        copy = send(ref, ref, rd_send.at[l, part, k], rd_recv.at[l, part, k + 1], sister)
        copy.wait_send()
        if receives:
            copy.wait_recv()

    def sum_half(l, part, y):
        at = part_rows(part)
        sum_sister(l, part, y).wait_recv()
        PB[l, y, at] = (GRF[l, y, cc, at] + RB1[l, y, at].astype(F32)).astype(BF16)

    def sum_step(l, part, i):
        if i < 2:
            sum_sister(l, part, sum_at(i) // 2).start()
        if i == 2:
            sum_half(l, part, 1 - yc)
            copies = sum_square(l, part)
            copies[0].start()
            copies[2].start()

    def sum_chip(l, part):
        at = part_rows(part)
        sum_half(l, part, yc)
        SQ[l, batch % 2, yc, at] = PB[l, yc, at]
        sum_square(l, part)[1].start()

    def sum_z(l, part, k):
        ref = DBL.at[l, zc, part_rows(part)]
        return send(ref, ref, rd_send.at[l, part, 2], rd_recv.at[l, part, 3], (((zc + k) % 4) * 2 + xc, mp))

    def sum_double(l, part, k):
        at = part_rows(part)
        return send(DBL.at[l, 2 * k, at], DBL.at[l, 2 * k + 1, at], rd_send.at[l, part, 2],
                    rd_recv.at[l, part, 2 + k], partner(k))

    def sum_batch(l, part):
        at = part_rows(part)
        sum_wait(l, part, 1, 3)
        sum_wait(l, part, 0, 2, receives=False)
        total = sum(SQ[l, i, j, at].astype(F32) for i in range(2) for j in range(2))
        if gathers:
            DBL[l, zc, at] = total.astype(BF16)
            for k in (1, 2, 3):
                sum_z(l, part, k).start()
        else:
            DBL[l, 2, at] = total.astype(BF16)
            sum_double(l, part, 1).start()

    def sum_end(l, part):
        at = part_rows(part)
        if gathers:
            sum_wait(l, part, 2, 3)
            total = sum(DBL[l, z, at].astype(F32) for z in range(4))
        else:
            for k in range(1, steps):
                sum_double(l, part, k).wait()
                total = DBL[l, 2 * k, at].astype(F32) + DBL[l, 2 * k + 1, at].astype(F32)
                if k + 1 < steps:
                    DBL[l, 2 * k + 2, at] = total.astype(BF16)
                    sum_double(l, part, k + 1).start()
        for i in ((0, 1) if part == 0 else (2, 3, 4, 5)):
            tile = total[(i // 2 - part) * HD:(i // 2 - part + 1) * HD]
            if i % 2:
                tile = pltpu.roll(tile, HD, 1)
            (gq_ref if i < 3 else gk_ref)[l, i % 3] = tile[:, :HD]
        if part == 1:
            offsets = total[2 * HD:2 * HD + 8]
            offsets = offsets - pltpu.roll(offsets, HD, 1)
            for i in range(6):
                (gqb_ref if i < 3 else gkb_ref)[i % 3, l:l + 1] = offsets[i:i + 1, :HD]

    cot_copy.wait()
    GRAD[...] = COT[...].astype(F32)
    N1[...] = COT[...]
    for l in reversed(range(LAYERS)):
        e = 2 + l
        above = l + 1 if l + 1 < LAYERS else None
        clear()
        for i in range(4):
            if l + 1 == LAYERS and i == (2 if gathers else 0):
                ready(CHUNKS - 1)
            mlp_back(l, i % 2 * 2 + (cc if i < 2 else 1 - cc))
        grad_mid = GRAD[...] + norm_back(NORMED[l, 1], SCALE[l, 1, :, :1], ACC[...])
        GRAD[...] = grad_mid
        N1[...] = grad_mid.astype(BF16)

        for j in range(2):
            for i in (2 * j, 2 * j + 1):
                attend_back_start(l, block_at(i))
            if above is None and j == 1:
                last_down(0, 2)
            for i in (2 * j, 2 * j + 1):
                ex_step(e, i, b_own, b_sis)
        for i in range(4):
            attend_back_local(l, sum_at(i))
        if above is None:
            last_down(2, 2)
            last_end()
        for j in range(2):
            ex_forward(e, j)
        for i in range(4):
            sum_step(l, 0, i)
        ex_end(e)
        if above is not None:
            sum_batch(above, 0)
            sum_batch(above, 1)
        sum_chip(l, 0)
        for j in range(2):
            for i in (2 * j, 2 * j + 1):
                attend_back_end(l, sum_at(i))
            for i in (2 * j, 2 * j + 1):
                sum_step(l, 1, i)
        sum_chip(l, 1)
        clear()
        for m in range(4):
            qkv_back(l, m)
            if l == 0 and m == 1:
                sum_batch(0, 0)
        if l == 0:
            sum_batch(0, 1)
        GRAD[...] = GRAD[...] + norm_back(NORMED[l, 0], SCALE[l, 0, :, :1], ACC[...])
        N1[...] = GRAD[...].astype(BF16)
    GIN[...] = GRAD[...].astype(BF16)
    out_copies[1].start()
    for e in range(2 * LAYERS):
        ex_drain(e)
    drain()
    for part in range(2):
        sum_end(1, part)
    sum_end(0, 0)
    sum_end(0, 1)
    for copy in out_copies[2:]:
        copy.start()
    for copy in out_copies:
        copy.wait()


def hand_out(*refs):
    count = len(refs) // 2
    for source, target in zip(refs[:count], refs[count:]):
        target[...] = source[...]


def per_device(tokens, cotangent, seq_lengths, joined_qkv, attn_proj, mlp_up, mlp_down,
               query_map, query_bias, key_map, key_bias):
    n_batch, n_mp = lax.axis_size("batch"), lax.axis_size("mp")
    rows, width = tokens.shape
    slice_rows = joined_qkv.shape[1]
    heads = query_map.shape[1]
    assert n_mp == 4 and heads == 3 and rows == PAIR and query_map.shape[2] == HD
    assert n_batch & (n_batch - 1) == 0
    parts = 3
    gathers = n_batch == 8 and slice_rows % (16 * parts) == 0
    part_rows = width // (8 * parts)
    qkv, down = joined_qkv.transpose(0, 2, 1, 3), mlp_down.transpose(0, 2, 1)
    if gathers:
        cut = (LAYERS, parts, part_rows, width)
        frozen = (qkv, attn_proj, mlp_up.reshape(cut), down.reshape(cut))
    else:
        turned = jnp.concatenate([attn_proj[:, PAIR:], attn_proj[:, :PAIR]], 1).transpose(0, 2, 1)
        attn = jnp.concatenate([joined_qkv.reshape(LAYERS, slice_rows, -1), turned], 2)
        blocks = jnp.stack([attn, mlp_up, down], 1).reshape(CHUNKS, slice_rows, width)
        weights = lax.all_gather(blocks, "batch", axis=1, tiled=True)
        weights = lax.all_gather(weights, "mp", axis=1, tiled=True)
        frozen = (weights.reshape(CHUNKS, 2, 2, 4, 2, parts, part_rows, width),)

    steps = n_batch.bit_length() - 1
    vmem, dma = pltpu.VMEM, pltpu.SemaphoreType.DMA
    shapes = [(tokens.shape, BF16), (tokens.shape, BF16), (query_map.shape, F32), ((heads, LAYERS, HD), F32),
              (key_map.shape, F32), ((heads, LAYERS, HD), F32)]
    map_shapes = [query_map.shape, (heads, LAYERS, HD)] * 2
    scratch = [vmem(*shape) for shape in shapes] + [vmem(shape, BF16) for shape in map_shapes] + [
        vmem((CHUNKS, 2, 2, 4, 2, parts, part_rows, width), BF16),
        vmem((rows, width), BF16),
        vmem((rows, width), BF16),
        vmem(qkv.shape, BF16),
        vmem(attn_proj.shape, BF16),
        vmem((2, 2, LAYERS, ROWS, PAIR), BF16),
        vmem((LAYERS, 4, 3, 2 * PAIR, 2 * PAIR), BF16),
        vmem((LAYERS, 4, 8, PAIR), F32),
        vmem((rows, width), F32),
        vmem((LAYERS, 2, rows, width), F32),
        vmem((LAYERS, 2, rows, PAIR), F32),
        vmem((LAYERS, 4, rows, width), F32),
        vmem((4, rows, width), BF16),
        vmem((LAYERS, 4, rows, 5 * PAIR), BF16),
        vmem((LAYERS, 4, 3, rows, PAIR), BF16),
        vmem((LAYERS, 4, 3, rows, PAIR), BF16),
        vmem((LAYERS, 4, 3, rows, PAIR), BF16),
        vmem((LAYERS, 4, 6, rows, PAIR), F32),
        vmem((LAYERS, 4, 6, rows, PAIR), BF16),
        vmem((LAYERS, 4, 3, rows, PAIR), BF16),
        vmem((LAYERS, 4, 2, rows, PAIR), F32),
        vmem((LAYERS, 4, 2, rows, PAIR), F32),
        vmem((LAYERS, 4, 3, PAIR, PAIR), BF16),
        vmem((rows, width), BF16),
        vmem((rows, width), F32),
        vmem((rows, width), F32),
        vmem((rows, width), F32),
        vmem((4, 3, rows, PAIR), BF16),
        vmem((4, 3, rows, PAIR), BF16),
        vmem((4, 2, rows, PAIR), BF16),
        vmem((4, 3, rows, PAIR), BF16),
        vmem((4, 2, rows, PAIR), F32),
        vmem((4, rows, PAIR), F32),
        vmem((5, rows, rows), F32),
        vmem((2 * LAYERS, 2, 4, ROWS, PAIR), BF16),
        vmem((2 * LAYERS, 2, ROWS, PAIR), BF16),
        vmem((2 * LAYERS, 2, 2, ROWS, PAIR), BF16),
        vmem((4, rows, 5 * PAIR), BF16),
        vmem((4, 8, PAIR), F32),
        vmem((LAYERS, 2, 2, ROWS, PAIR), F32),
        vmem((LAYERS, 2, 2, ROWS, PAIR), BF16),
        vmem((LAYERS, 2, ROWS, PAIR), BF16),
        vmem((LAYERS, 2, ROWS, PAIR), BF16),
        vmem((LAYERS, 2, 2, ROWS, PAIR), BF16),
        vmem((LAYERS, 4 if gathers else 2 * steps, ROWS, PAIR), BF16),
        dma((CHUNKS,)), dma((8,)), dma((6,)),
        dma((7,)),
        dma((2 * LAYERS,)), dma((2 * LAYERS, 4)),
        dma((2 * LAYERS,)), dma((2 * LAYERS, 2, 2)),
        dma((LAYERS, 2, 3)), dma((LAYERS, 2, 4 if gathers else 3 + steps)),
        dma((2, 3, 2)), dma((CHUNKS, parts, 2, 3)),
        dma((2,)), dma((CHUNKS,)),
        dma((CHUNKS + 2, 5)), dma((CHUNKS, 4, 2)),
        dma((CHUNKS,)), dma((CHUNKS,)),
    ]
    vmem_block, any_block = pl.BlockSpec(memory_space=pltpu.VMEM), pl.BlockSpec(memory_space=pl.ANY)
    shapes = [jax.ShapeDtypeStruct(*shape) for shape in shapes]
    results = pl.pallas_call(
        functools.partial(body, n_batch, gathers),
        out_shape=shapes,
        in_specs=[pl.BlockSpec(memory_space=pltpu.SMEM)] + [any_block] * (6 + len(frozen)),
        out_specs=[any_block] * 6,
        scratch_shapes=scratch,
        compiler_params=pltpu.CompilerParams(
            collective_id=0, has_side_effects=True, vmem_limit_bytes=62 * 2**20),
    )(seq_lengths, tokens, cotangent, query_map, query_bias.transpose(1, 0, 2), key_map,
      key_bias.transpose(1, 0, 2), *frozen)
    results = pl.pallas_call(
        hand_out,
        out_shape=shapes,
        in_specs=[vmem_block] * 6,
        out_specs=[vmem_block] * 6,
    )(*results)
    out, grad_in, qmap, qbias, kmap, kbias = results
    return out, grad_in, qmap, qbias.transpose(1, 0, 2), kmap, kbias.transpose(1, 0, 2)


def solution(mesh):
    return jax.shard_map(
        per_device,
        mesh=mesh,
        in_specs=(
            P(("batch", "mp"), None),
            P(("batch", "mp"), None),
            P("batch", None),
            P(None, "batch", None, "mp"),
            P(None, "mp", "batch"),
            P(None, "batch", "mp"),
            P(None, "mp", "batch"),
            P(None, "mp", None, None),
            P(None, "mp", None),
            P(None, "mp", None, None),
            P(None, "mp", None),
        ),
        out_specs=(
            P(("batch", "mp"), None),
            P(("batch", "mp"), None),
            P(None, "mp", None, None),
            P(None, "mp", None),
            P(None, "mp", None, None),
            P(None, "mp", None),
        ),
        check_vma=False,
    )
```

```python
import functools

import jax
import jax.numpy as jnp
from jax import lax
from jax.experimental import pallas as pl
from jax.experimental.pallas import tpu as pltpu
from jax.sharding import PartitionSpec as P

SPAN = 64
LAYERS = 2
EPS = 1e-05
F32, BF16 = jnp.float32, jnp.bfloat16
MESH = pl.DeviceIdType.MESH
ATTN, UP, DOWN = 0, 1, 2
CHUNKS = 3 * LAYERS
FIRST_LAG, LAST_LAG, START_LEAD = 2, 6, 6
TURNS = (1, 1, 0, 1, 1, 0)
HD = 64
PAIR = 2 * HD
EARLY = HD + HD // 2
ROWS = 3 * HD + 16


def nn(a, b):
    return lax.dot_general(a, b, (((1,), (0,)), ((), ())), preferred_element_type=F32)


def nt(a, b):
    return lax.dot_general(a, b, (((1,), (1,)), ((), ())), preferred_element_type=F32)


def tn(a, b):
    return lax.dot_general(a, b, (((0,), (0,)), ((), ())), preferred_element_type=F32)


def moments(x):
    mean = jnp.mean(x, axis=-1, keepdims=True)
    centered = x - mean
    scale = lax.rsqrt(jnp.mean(centered * centered, axis=-1, keepdims=True) + EPS)
    return centered * scale, scale


def norm_back(y, scale, g):
    mean_g = jnp.mean(g, axis=-1, keepdims=True)
    mean_gy = jnp.mean(g * y, axis=-1, keepdims=True)
    return scale * (g - mean_g - y * mean_gy)


GELU_C = 0.7978845608028654
GELU_A = 0.044715


def gelu_and_slope(x):
    square = x * x
    t = jnp.tanh(GELU_C * x * (1.0 + GELU_A * square))
    inner = GELU_C * (1.0 + 3.0 * GELU_A * square)
    half = 0.5 * (1.0 + t)
    return x * half, half + 0.5 * x * (1.0 - t * t) * inner


def split(x):
    high = x.astype(BF16)
    return high, (x - high.astype(F32)).astype(BF16)


def stack_rows(entries, rows):
    index = lax.broadcasted_iota(jnp.int32, (rows, entries[0].shape[1]), 0)
    out = jnp.zeros((rows, entries[0].shape[1]), F32)
    for i, entry in enumerate(entries):
        out = jnp.where(index == i, entry, out)
    return out


def lanes2(a, b):
    return jnp.concatenate([a, b], 1)


def rows2(a, b):
    return jnp.concatenate([a, b], 0)


def body(n_batch, gathers, *refs):
    seq_hbm, tok_hbm, cot_hbm, *map_hbm = refs[:7]
    frozen, refs = (refs[7:11], refs[11:]) if gathers else (refs[7:8], refs[8:])
    (OUT, GIN, gq_ref, gqb_ref, gk_ref, gkb_ref, qmap_ref, qbias_ref, kmap_ref, kbias_ref,
     seq_ref, G, TOK, COT, QKV, PROJ, MT, BD, BIAS, RES, NORMED, SCALE, SLOPE, ACT, TQ, VH, VL, KL, PF, PHI, PT, ATT, RD, CX,
     N1, ACC, LASTACC, GRAD, GNH, GC, NM, DST, GV, TG, MASKS, SB, CH, OT,
     MIX, OFF, GRF, GRB, RB1, PB, SQ, DBL,
     own_sem, in_sem, mt_sem, ex1_send, ex1_recv, ex2_send, ex2_recv, rd_send, rd_recv,
     z_send, z_recv, cross_send, far_send, first_recv, last_recv, core_send, core_recv) = refs
    rows, width = TOK.shape
    batch, mp = lax.axis_index("batch"), lax.axis_index("mp")
    yc, cc = mp // 2, mp % 2
    sister = (batch, yc * 2 + 1 - cc)
    across = (batch, (1 - yc) * 2 + cc)
    steps = n_batch.bit_length() - 1
    near_batch = batch + 1 - 2 * (batch % 2)
    opposite = (near_batch, (1 - yc) * 2 + cc)

    def partner(k):
        bit = (batch // (1 << k)) % 2
        return (batch + (1 - 2 * bit) * (1 << k), mp)

    def send(src, dst, send_sem, recv_sem, device):
        copy = pltpu.make_async_remote_copy(
            src_ref=src, dst_ref=dst, send_sem=send_sem, recv_sem=recv_sem,
            device_id=device, device_id_type=MESH)
        return copy

    if gathers:
        zc, xc = batch // 2, batch % 2
        greeted = [(((zc + k) % 4) * 2 + xc, mp) for k in (1, 2, 3)]
    else:
        greeted = [partner(k) for k in range(1, steps)]
    greeted += [partner(0), sister, across, opposite]
    barrier = pltpu.get_barrier_semaphore()
    for device in greeted:
        pl.semaphore_signal(barrier, inc=1, device_id=device, device_id_type=MESH)
    tok_copy = pltpu.make_async_copy(tok_hbm, TOK, in_sem.at[0])
    cot_copy = pltpu.make_async_copy(cot_hbm, COT, in_sem.at[1])
    seq_copy = pltpu.make_async_copy(seq_hbm, seq_ref, in_sem.at[8])
    map_copies = [pltpu.make_async_copy(source, target, in_sem.at[4 + i]) for i, (source, target) in enumerate(
        zip(map_hbm, (qmap_ref, qbias_ref, kmap_ref, kbias_ref)))]
    own_copies = []
    if gathers:
        x_side = (zc * 2 + 1 - xc, mp)
        z_up = (jnp.minimum(zc + 1, 3) * 2 + xc, mp)
        z_down = (jnp.maximum(zc - 1, 0) * 2 + xc, mp)
        qkv_hbm, proj_hbm, up_hbm, down_hbm = frozen
        qkv_copy = pltpu.make_async_copy(qkv_hbm, QKV, in_sem.at[2])
        proj_copy = pltpu.make_async_copy(proj_hbm, PROJ, in_sem.at[3])
        qkv_copy.start()
        proj_copy.start()
        tok_copy.start()
        for l in range(LAYERS):
            for part, ref in ((UP, up_hbm), (DOWN, down_hbm)):
                own_copies.append(pltpu.make_async_copy(
                    ref.at[l], G.at[3 * l + part, yc, cc, zc, xc], own_sem.at[0]))
    else:
        tok_copy.start()
        own_copies = [pltpu.make_async_copy(frozen[0].at[q], G.at[q], own_sem.at[q])
                      for q in range(CHUNKS)]
    for copy in own_copies:
        copy.start()
    cot_copy.start()
    for copy in [seq_copy] + map_copies:
        copy.start()

    if gathers:
        slice_rows = QKV.shape[2]
        eye = (lax.broadcasted_iota(jnp.int32, (slice_rows, slice_rows), 0)
               == lax.broadcasted_iota(jnp.int32, (slice_rows, slice_rows), 1)).astype(BF16)
        qkv_copy.wait()
        proj_copy.wait()
        for l in range(LAYERS):
            turned = nt(eye, PROJ[l])
            pieces = [QKV[l, i].astype(F32) for i in range(3)]
            block = jnp.concatenate(pieces + [turned[:, PAIR:], turned[:, :PAIR]], 1).astype(BF16)
            G[3 * l + ATTN, yc, cc, zc, xc] = block.reshape(G.shape[5:])

    seq_copy.wait()
    row0 = mp * rows
    spans = []
    end = jnp.int32(0)
    for s in range(seq_ref.shape[1]):
        length = seq_ref[0, s]
        spans.append((end, end + length, end + ((length + SPAN - 1) // SPAN) * SPAN))
        end = spans[-1][2]

    def owner(place):
        return sum((place >= stop).astype(jnp.int32) for _, _, stop in spans)

    def owner_at(place):
        return sum(jnp.where(place >= stop, 1, 0) for _, _, stop in spans)

    def same(a, b):
        return jnp.where(owner_at(a) == owner_at(b), 1.0, 0.0).astype(F32)

    row = lax.broadcasted_iota(jnp.int32, (rows, rows), 0) + row0
    col = lax.broadcasted_iota(jnp.int32, (rows, rows), 1) + row0
    own_row, own_col = owner(row), owner(col)
    valid = sum(((row >= a) & (row < b)).astype(F32) for a, b, _ in spans)
    MASKS[0] = ((col <= row) & (own_row == own_col)).astype(F32)
    MASKS[1] = ((row <= col) & (own_row == own_col)).astype(F32)
    MASKS[2] = valid
    came_in = jnp.where(mp > 0, owner_at(row0 - 1), -1)
    MASKS[3] = (own_row == came_in).astype(F32)
    MASKS[4] = (own_row == owner_at(row0 + rows - 1)).astype(F32)
    LOWER, UPPER, VALID, CONT, LAST = range(5)

    def last_of(y, c):
        return (y * 2 + c) * rows + rows - 1

    in_chip = same(last_of(yc, 0), last_of(yc, 1))
    first, second = (cc == 0), (cc == 1)
    f_own = jnp.where(second, 1.0, in_chip)
    f_sis = jnp.where(second, in_chip, 1.0)
    f_a = jnp.where(second, 1.0, 0.0)
    f_b = jnp.where(yc == 1, jnp.where(second, same(last_of(0, 1), last_of(1, 0)), 1.0), 0.0)
    before = same(last_of(0, 1), last_of(1, 0))
    b_own = jnp.where(first, 1.0, before)
    b_sis = jnp.where(first, before, 1.0)
    b_a = jnp.where(first, 1.0, 0.0)
    b_b = jnp.where(yc == 0, jnp.where(first, same(last_of(0, 0), last_of(0, 1)), 1.0), 0.0)

    lane = lax.broadcasted_iota(jnp.int32, (rows, PAIR), 1)
    low = (lane < HD).astype(F32)
    high = 1.0 - low
    left = lane < HD

    for copy in map_copies:
        copy.wait()
    for l in range(LAYERS):
        heads = [ref[l, h].astype(F32) for ref in (qmap_ref, kmap_ref) for h in range(3)]
        for t in range(3):
            MT[yc, cc, l, t * HD:(t + 1) * HD] = jnp.concatenate(
                [heads[2 * t], heads[2 * t + 1]], 1).astype(BF16)
        biases = [ref[h, l:l + 1].astype(F32) for ref in (qbias_ref, kbias_ref) for h in range(3)]
        MT[yc, cc, l, 3 * HD:] = stack_rows(
            [jnp.concatenate([b, -b], 1) for b in biases], 16).astype(BF16)

    pl.semaphore_wait(barrier, len(greeted))

    def maps_start():
        send(MT.at[yc, cc], MT.at[yc, cc], mt_sem.at[1], mt_sem.at[2], across).start()
        send(MT.at[yc, cc], MT.at[yc, cc], mt_sem.at[3], mt_sem.at[4], sister).start()

    def maps_forward():
        send(MT.at[1 - yc, cc], MT.at[1 - yc, cc], mt_sem.at[1], mt_sem.at[2], across).wait()
        send(MT.at[1 - yc, cc], MT.at[1 - yc, cc], mt_sem.at[5], mt_sem.at[6], sister).start()

    def maps_build():
        send(MT.at[yc, cc], MT.at[yc, 1 - cc], mt_sem.at[3], mt_sem.at[4], sister).wait()
        send(MT.at[1 - yc, cc], MT.at[1 - yc, 1 - cc], mt_sem.at[5], mt_sem.at[6], sister).wait()
        half = lax.broadcasted_iota(jnp.int32, (HD, PAIR), 1) < HD
        none = jnp.zeros((HD, PAIR), F32)

        def one(i, carry):
            l, m = i // 4, i % 4
            block = MT[m // 2, m % 2, l].astype(F32)
            for t in range(3):
                pair = block[t * HD:(t + 1) * HD]
                turned = pltpu.roll(pair, HD, 1)
                a = jnp.where(half, pair, -turned)
                b = jnp.where(half, turned, -pair)
                wide = jnp.concatenate(
                    [jnp.concatenate([a, none], 1), jnp.concatenate([none, b], 1)], 0).astype(BF16)
                BD[l, m, t, 0:PAIR] = wide
                BD[l, m, t, PAIR:2 * PAIR] = wide
            BIAS[l, m] = block[3 * HD:3 * HD + 8]
            return carry

        lax.fori_loop(0, 2 * 4, one, 0)

    if gathers:
        parts = (0, 1, 2)

        def turn(q, p):
            return (TURNS[q], 0, 1)[p]

        def near(q, p):
            return (x_side, across)[turn(q, p)]

        def far(q, p):
            return (across, x_side)[turn(q, p)]

        def single(q, p, z):
            return G.at[q, yc, cc, z, xc, p]

        def neighbour(q, p, z):
            return (G.at[q, yc, cc, z, 1 - xc, p], G.at[q, 1 - yc, cc, z, xc, p])[turn(q, p)]

        def pair_of(q, p, z):
            return (G.at[q, yc, cc, z, :, p], G.at[q, :, cc, z, xc, p])[turn(q, p)]

        def other_pair(q, p, z):
            return (G.at[q, 1 - yc, cc, z, :, p], G.at[q, :, cc, z, 1 - xc, p])[turn(q, p)]

        def early(q, p):
            return q == 0 or p == 0

        def z_unit(q, p, z):
            return single(q, p, z) if early(q, p) else pair_of(q, p, z)

        def arrived(ref, sem):
            send(ref, ref, core_send.at[0], sem, sister).wait_recv()

        def sent(ref, sem):
            send(ref, ref, sem, core_recv.at[0], sister).wait_send()

        def z_on(q, p, z, way, s):
            @pl.when((zc < 3) if way == 0 else (zc > 0))
            def _():
                send(z_unit(q, p, z), z_unit(q, p, z), z_send.at[way, s, 0 if early(q, p) else 1],
                     z_recv.at[q, p, (z - zc + (7, 5)[way]) % 4 - 1], (z_up, z_down)[way]).start()

        def near_sem(q, p, z):
            if p == 0:
                return first_recv.at[q, z]
            return first_recv.at[CHUNKS - 1 + p, z] if q == 0 else first_recv.at[q, 4]

        def to_near(q, p, z):
            send(single(q, p, z), single(q, p, z), cross_send.at[0 if early(q, p) else 1],
                 near_sem(q, p, z), near(q, p)).start()

        def to_far(q, p, z):
            send(pair_of(q, p, z), pair_of(q, p, z), far_send.at[q], last_recv.at[q, z, min(p, 1)],
                 far(q, p)).start()

        def to_sister(q, ref):
            send(ref, ref, core_send.at[q], core_recv.at[q], sister).start()

        def each_place(s, do):
            pl.when((s > 0) & (zc - s >= 0))(lambda: do(zc - s, 0))
            pl.when((s > 0) & (zc + s <= 3))(lambda: do(zc + s, 1))

        def have(q, p, z):
            if early(q, p):
                to_near(q, p, z)
            else:
                to_far(q, p, z)
                to_sister(q, pair_of(q, p, z))

        def gather_start(q):
            for p in (1, 2):
                if not early(q, p):
                    to_near(q, p, zc)

        def z_start(q):
            for p in parts:
                if p == 1 and not early(q, p):
                    arrived(G.at[q, 0, 0, 0, :, 0], first_recv.at[q, 4])
                for way in range(2):
                    z_on(q, p, zc, way, 0)
                have(q, p, zc)

        def along_z(q, s):
            def step(z, way):
                for p in parts:
                    arrived(z_unit(q, p, z), z_recv.at[q, p, (z - zc + 4) % 4 - 1])
                    z_on(q, p, z, way, s)
                    have(q, p, z)

            each_place(s, step)

        def across_first(q, s):
            def step(z, way):
                for p in parts if q == 0 else (0,):
                    arrived(neighbour(q, p, z), near_sem(q, p, z))
                    to_far(q, p, z)
                    to_sister(q, pair_of(q, p, z))

            pl.when(s == 0)(lambda: step(zc, None))
            each_place(s, step)

        def across_last(q, s):
            def step(z, way):
                arrived(G.at[q, 0, 0, 0, :, 0:2], last_recv.at[q, z, 1])
                for p in (1, 2):
                    to_sister(q, other_pair(q, p, z))
                arrived(other_pair(q, 0, z), last_recv.at[q, z, 0])
                to_sister(q, other_pair(q, 0, z))

            pl.when(s == 0)(lambda: step(zc, None))
            each_place(s, step)

        def later(k, s, lag, do):
            stages, steps = divmod(lag, 4)
            if 0 <= k - stages < CHUNKS:
                pl.when(s >= steps)(lambda: do(k - stages, s - steps))
            if steps and 0 <= k - stages - 1 < CHUNKS:
                pl.when(s < steps)(lambda: do(k - stages - 1, s + 4 - steps))

        start_step = -START_LEAD % 4
        ahead = (start_step + START_LEAD) // 4

        def comm(k, s):
            later(k, s, LAST_LAG, across_last)
            later(k, s, FIRST_LAG, across_first)
            if k < CHUNKS:
                along_z(k, s)
            if (k + ahead) < CHUNKS:
                pl.when(s == start_step)(lambda: z_start(k + ahead))

        def ready(q):
            arrived(G.at[q, :, 1 - cc], core_recv.at[q])

        def drain():
            for way in range(2):
                for s in range(3):
                    @pl.when(((zc < 3) & (zc >= s)) if way == 0 else ((zc > 0) & (zc + s <= 3)))
                    def _():
                        sent(G.at[0:4, 0, 0, 0, :, 0], z_send.at[way, s, 0])
                        sent(G.at[0:5, 0, 0, 0, :, 0:2], z_send.at[way, s, 1])
            sent(G.at[0:4, 0, 0, :, :, 0], cross_send.at[0])
            sent(G.at[0:5, 0, 0, 0, :, 0], cross_send.at[1])
            for q in range(CHUNKS):
                sent(G.at[q, 0, 0], far_send.at[q])
                sent(G.at[q, :, 0], core_send.at[q])
    else:
        def gather_start(q):
            pass

        def ready(q):
            own_copies[q].wait()

        def drain():
            pass

    def weight(q, m, lanes=None):
        if lanes is None:
            return G[q, m // 2, m % 2].reshape(width, width)
        return G[q, m // 2, m % 2, :, :, :, :, lanes].reshape(width, -1)

    def add_blocks(a, ca, b, cb):
        a, b = a.astype(F32), b.astype(F32)
        values = ca * a[:3 * HD] + cb * b[:3 * HD]
        sums = (ca * (a[3 * HD:3 * HD + 8] + a[3 * HD + 8:])
                + cb * (b[3 * HD:3 * HD + 8] + b[3 * HD + 8:]))
        return values, sums

    def block_at(i):
        return (2 * (1 - cc) + i) % 4

    def ex_sister(e, m):
        return send(SB.at[e, 0, m], SB.at[e, 1, m], ex1_send.at[e], ex1_recv.at[e, m], sister)

    def ex_across(e, j):
        return send(CH.at[e, j], OT.at[e, cc, j], ex2_send.at[e], ex2_recv.at[e, 0, j], across)

    def ex_over(e, j):
        return send(OT.at[e, cc, j], OT.at[e, cc, j], ex2_send.at[e], ex2_recv.at[e, 1, j], sister)

    def ex_step(e, i, own, sis):
        m = block_at(i)
        ex_sister(e, m).start()

        def combine():
            ex_sister(e, m).wait_recv()
            values, sums = add_blocks(SB[e, 0, m], own, SB[e, 1, m], sis)
            CH[e, i - 2, 0:3 * HD] = values.astype(BF16)
            CH[e, i - 2, 3 * HD:] = rows2(*split(sums))
            ex_across(e, i - 2).start()

        if isinstance(i, int):
            if i >= 2:
                combine()
        else:
            pl.when(i >= 2)(combine)

    def ex_forward(e, j):
        ex_across(e, j).wait_recv()
        ex_over(e, j).start()

    def ex_end(e):
        for j in range(2):
            m = block_at(j)
            ex_sister(e, m).wait_recv()
            ref = OT.at[e, 1 - cc, j]
            send(ref, ref, ex2_send.at[e], ex2_recv.at[e, 1, j], sister).wait_recv()

    def ex_drain(e):
        four = SB.at[e, 0]
        for sem in (ex1_send.at[e], ex2_send.at[e]):
            send(four, four, sem, ex1_recv.at[e, 0], sister).wait_send()

    def softmax(u):
        e = jnp.exp(u - jnp.max(u, axis=-1, keepdims=True))
        return e / jnp.sum(e, axis=-1, keepdims=True)

    def phi_q(l, m, h):
        return PHI[l, m, h]

    def phi_k(l, m, h):
        return PHI[l, m, 3 + h]

    def place(x, columns, at_left):
        at = 0 if at_left else HD
        out = x * (high if at_left else low)
        for i, column in enumerate(columns):
            out = jnp.where(lane == at + i, column, out)
        return out

    def heads_of(pair, single_tile, columns):
        return [place(pair, columns[0], False), place(pair, columns[1], True), place(single_tile, columns[2], False)]

    def attend_features(l, m):
        mixed = nn(N1[...], weight(3 * l + ATTN, m, slice(0, 5 * PAIR)))
        hi, lo = split(mixed[:, :3 * PAIR])
        TQ[l, m, :, 0:3 * PAIR] = hi
        v01 = mixed[:, 3 * PAIR:4 * PAIR].astype(BF16)
        v2 = (mixed[:, 4 * PAIR:] * low).astype(BF16)
        TQ[l, m, :, 3 * PAIR:4 * PAIR] = v01
        TQ[l, m, :, 4 * PAIR:] = v2
        bias = BIAS[l, m]
        for t in range(3):
            tile = slice(t * PAIR, (t + 1) * PAIR)
            u = nn(lanes2(hi[:, tile], lo[:, tile]), BD[l, m, t])
            for e in range(2):
                h = 2 * t + e
                p = softmax(u[:, e * PAIR:(e + 1) * PAIR] + bias[h:h + 1])
                PF[l, m, h] = p
                p = p.astype(BF16)
                PHI[l, m, h] = p if h < 3 else (p.astype(F32) * MASKS[VALID]).astype(BF16)
        last = MASKS[LAST]
        for h, v in enumerate(heads_of(v01.astype(F32), v2.astype(F32), [(1.0, 1.0)] * 3)):
            VH[l, m, h] = v.astype(BF16)
            VL[l, m, h] = (v * last).astype(BF16)
        keys = [phi_k(l, m, h).astype(F32) * last for h in range(3)]
        sums = stack_rows([jnp.sum(k, axis=0, keepdims=True) for k in keys], 8)
        keys = [k.astype(BF16) for k in keys]
        for h in range(3):
            KL[l, m, h] = keys[h]
        two = tn(v01, lanes2(keys[0], keys[1]))
        one = tn(v2, keys[2])
        SB[l, 0, m, 0:HD] = two[:HD, :PAIR].astype(BF16)
        SB[l, 0, m, HD:PAIR] = two[HD:, PAIR:].astype(BF16)
        SB[l, 0, m, PAIR:3 * HD] = one[:HD].astype(BF16)
        SB[l, 0, m, 3 * HD:] = rows2(*split(sums))

    def features_step(l, i):
        attend_features(l, block_at(i))
        ex_step(l, i, f_own, f_sis)

    none_b = jnp.zeros((HD, PAIR), BF16)

    def beside(block, h, entries):
        state = block[h * HD:(h + 1) * HD]
        extra = stack_rows([entry.astype(F32) for entry in entries], HD).astype(BF16)
        return rows2(extra, state) if h == 1 else rows2(state, extra)

    def diagonal(block):
        return rows2(lanes2(block[:HD], none_b), lanes2(none_b, block[HD:PAIR]))

    def attend_out(l, m):
        values, sums = add_blocks(SB[l, 1, m], f_a, OT[l, m // 2, m % 2], f_b)
        carried = values.astype(BF16)
        for h in range(3):
            top, rest = split(sums[h:h + 1])
            CX[l, m, h] = beside(carried, h, [top, top, rest])
        valid_now, cont = MASKS[VALID], MASKS[CONT]
        lower = MASKS[LOWER]
        scores, inverse = [], []
        queries = [phi_q(l, m, h) for h in range(3)]
        for h in range(3):
            keys = phi_k(l, m, h)
            s = nt(queries[h], keys) * lower
            PT[l, m, h] = (nt(keys, queries[h]) * MASKS[UPPER]).astype(BF16)
            total = jnp.sum(s + queries[h].astype(F32) * (cont * sums[h:h + 1]), axis=-1, keepdims=True)
            inverse.append(1.0 / (total + (1.0 - valid_now)))
            scores.append(s.astype(BF16))
        v01 = TQ[l, m, :, 3 * PAIR:4 * PAIR].astype(F32)
        v2 = TQ[l, m, :, 4 * PAIR:]
        num = nn(lanes2(scores[0], scores[1]), rows2((v01 * low).astype(BF16), (v01 * high).astype(BF16)))
        num += cont * nt(lanes2(queries[0], queries[1]), diagonal(carried))
        num2 = nn(scores[2], v2) + cont * nt(queries[2], rows2(carried[PAIR:], none_b))
        rd = jnp.where(left, inverse[0], inverse[1])
        att, att2 = valid_now * num * rd, valid_now * num2 * inverse[2]
        RD[l, m, 0] = rd
        RD[l, m, 1] = inverse[2]
        ATT[l, m, 0] = att
        ATT[l, m, 1] = att2
        operand = lanes2(pltpu.roll(att2, HD, 1), att).astype(BF16)
        ACC[...] += nt(operand, weight(3 * l + ATTN, m, slice(4 * PAIR, 6 * PAIR)))

    def loop4(do, unroll=False):
        def one(m, carry):
            do(m)
            return carry

        lax.fori_loop(0, 4, one, 0, unroll=unroll)

    def normalize(l, place, x):
        y, scale = moments(x)
        NORMED[l, place] = y
        SCALE[l, place] = jnp.broadcast_to(scale, (rows, PAIR))
        N1[...] = y.astype(BF16)

    def attend_end(l):
        ACC[...] = jnp.zeros((rows, width), F32)
        loop4(functools.partial(attend_out, l))
        middle = RES[...] + ACC[...]
        RES[...] = middle
        normalize(l, 1, middle)

    def up(l, m):
        pre = nn(N1[...], weight(3 * l + UP, m))
        act, SLOPE[l, m] = gelu_and_slope(pre)
        ACT[m] = act.astype(BF16)

    def down(l, m):
        ACC[...] += nt(ACT[m], weight(3 * l + DOWN, m))

    def layer_end(l):
        after = RES[...] + ACC[...]
        RES[...] = after
        normalize(l + 1, 0, after)

    def last_down(first, count):
        total = 0.0 if first == 0 else LASTACC[...]
        for m in range(first, first + count):
            total += nt(ACT[m], weight(3 * (LAYERS - 1) + DOWN, m))
        LASTACC[...] = total

    def last_end():
        OUT[...] = (RES[...] + LASTACC[...]).astype(BF16)

    def clear():
        ACC[...] = jnp.zeros((rows, width), F32)

    def stage(k, at=(), steps=4):
        def one(s, carry):
            comm(k, s)
            for when, do in at:
                pl.when(s == when)(do)
            return carry

        lax.fori_loop(0, steps, one, 0)

    if gathers:
        blocks = G.at[0, 0, 0, :, 0]
        pltpu.make_async_copy(blocks, blocks, own_sem.at[0]).wait()
        for q in range(CHUNKS):
            gather_start(q)
        for q in range(CHUNKS):
            if 4 * q < START_LEAD:
                z_start(q)
    maps_start()
    tok_copy.wait()
    x0 = TOK[...].astype(F32)
    RES[...] = x0
    normalize(0, 0, x0)

    def features(l):
        loop4(functools.partial(features_step, l))

    def forward_states(l):
        ex_forward(l, 0)
        ex_forward(l, 1)

    def middle_part(l):
        ex_end(l)
        attend_end(l)

    def up_all(l):
        loop4(functools.partial(up, l))

    def down_all(l):
        clear()
        loop4(functools.partial(down, l))
        layer_end(l)

    if gathers:
        def attend_first():
            ready(0)
            features(0)

        def up_first():
            ready(1)
            up_all(0)

        def down_first():
            ready(2)
            down_all(0)

        def attend_second():
            ready(3)
            features(1)

        def up_second():
            ready(4)
            up_all(1)

        stage(0, at=[(3, maps_forward)])
        stage(1, at=[(0, maps_build)])
        stage(2, at=[(1, attend_first)])
        stage(3, at=[(0, lambda: forward_states(0)), (1, lambda: middle_part(0)), (2, up_first)])
        stage(4, at=[(1, down_first)])
        stage(5, at=[(1, attend_second), (2, lambda: forward_states(1)), (3, lambda: middle_part(1))])
        stage(6, at=[(3, up_second)])
        stage(7, steps=2)
    else:
        maps_forward()
        maps_build()
        for l in range(LAYERS):
            ready(3 * l + ATTN)
            features(l)
            forward_states(l)
            middle_part(l)
            ready(3 * l + UP)
            up_all(l)
            if l + 1 < LAYERS:
                ready(3 * l + DOWN)
                down_all(l)


    def mlp_back(l, m):
        grad_act = nn(N1[...], weight(3 * l + DOWN, m))
        grad_pre = (SLOPE[l, m] * grad_act).astype(BF16)
        ACC[...] += nt(grad_pre, weight(3 * l + UP, m))

    row_half = lax.broadcasted_iota(jnp.int32, (2 * PAIR, PAIR), 0) % PAIR < HD
    lane_half = lax.broadcasted_iota(jnp.int32, (2 * PAIR, PAIR), 1) < HD
    across_halves = (row_half != lane_half).astype(BF16)

    def attend_back_start(l, m):
        e = 2 + l
        grads = nn(N1[...], weight(3 * l + ATTN, m, slice(4 * PAIR, 6 * PAIR)))
        g01, g2 = grads[:, PAIR:], pltpu.roll(grads[:, :PAIR], HD, 1) * low
        valid_now, cont = MASKS[VALID], MASKS[CONT]
        s01, s2 = g01 * RD[l, m, 0], g2 * RD[l, m, 1]
        p01, p2 = s01 * ATT[l, m, 0], s2 * ATT[l, m, 1]
        dens = [-nn(lanes2(*split(p)), across_halves) for p in (p01, p2)]
        num01 = (s01 * valid_now).astype(BF16)
        num2 = (s2 * valid_now).astype(BF16)
        NM[m, 0] = num01
        NM[m, 1] = num2
        columns = []
        for d in dens:
            top = d.astype(BF16).astype(F32)
            columns.append((top, d - top, top))
        tiles = heads_of(num01.astype(F32), num2.astype(F32), [columns[0], columns[0], columns[1]])
        sums = []
        for h in range(3):
            GNH[m, h] = tiles[h].astype(BF16)
            counted = (tiles[h] * cont).astype(BF16)
            GC[m, h] = counted
            state = tn(counted, phi_q(l, m, h))
            keep, extra = (state[HD:], state[:8]) if h == 1 else (state[:HD], state[HD:HD + 8])
            SB[e, 0, m, h * HD:(h + 1) * HD] = keep.astype(BF16)
            sums.append(extra[0:1] + extra[1:2])
        SB[e, 0, m, 3 * HD:] = rows2(*split(stack_rows(sums, 8)))

    def softmax_back(p, g):
        return p * (g - jnp.sum(p * g, axis=-1, keepdims=True))

    def keep_maps(l, m, first, x):
        GRF[l, m // 2, m % 2, first:first + x.shape[0]] = x
        GRB[l, m // 2, m % 2, first:first + x.shape[0]] = x.astype(BF16)

    def keep_two(l, m, t, first, two):
        maps = tn(TQ[l, m, :, t * PAIR:(t + 1) * PAIR], two)
        a, b = maps[:HD, :PAIR], maps[HD:, PAIR:]
        keep_maps(l, m, first, jnp.where(left[:HD], a - pltpu.roll(a, HD, 1), pltpu.roll(b, HD, 1) - b))

    def keep_one(l, m, second, first, one):
        maps = tn(TQ[l, m, :, PAIR:2 * PAIR], one.astype(BF16))
        a = maps[HD:] if second else maps[:HD]
        a = a - pltpu.roll(a, HD, 1)
        keep_maps(l, m, first, jnp.where(left[:HD // 2], a[:HD // 2], -a[HD // 2:]))

    def map_back(l, m, t, a, b):
        two = lanes2(a, b).astype(BF16)
        MIX[m, :, t * PAIR:(t + 1) * PAIR] = nt(two, BD[l, m, t, 0:PAIR]).astype(BF16)
        return two

    def attend_back_local(l, m):
        lower, upper = MASKS[LOWER], MASKS[UPPER]
        turned = []
        for h in range(3):
            q, k = phi_q(l, m, h), phi_k(l, m, h)
            nums, vals = GNH[m, h], VH[l, m, h]
            ds = (nt(nums, vals) * lower).astype(BF16)
            DST[m, h] = (nt(vals, nums) * upper).astype(BF16)
            g = nn(lanes2(ds, GC[m, h]), rows2(k, CX[l, m, h]))
            turned.append(softmax_back(PF[l, m, h], g))
        num01 = NM[m, 0].astype(F32)
        GV[m, 0] = nn(lanes2(PT[l, m, 0], PT[l, m, 1]),
                      rows2((num01 * low).astype(BF16), (num01 * high).astype(BF16)))
        GV[m, 1] = nn(PT[l, m, 2], NM[m, 1])
        TG[m] = turned[2]
        OFF[m] = stack_rows([jnp.sum(t, axis=0, keepdims=True) for t in turned], 8)
        keep_two(l, m, 0, 0, map_back(l, m, 0, turned[0], turned[1]))
        keep_one(l, m, False, HD, turned[2])

    def attend_back_end(l, m):
        e = 2 + l
        values, sums = add_blocks(SB[e, 1, m], b_a, OT[e, m // 2, m % 2], b_b)
        state = values.astype(BF16)
        valid_now = MASKS[VALID]
        turned = []
        for h in range(3):
            far = beside(state, h, split(sums[h:h + 1]))
            g = valid_now * nn(lanes2(DST[m, h], VL[l, m, h]), rows2(phi_q(l, m, h), far))
            turned.append(softmax_back(PF[l, m, 3 + h], g))
        keep_one(l, m, True, EARLY + HD, turned[0])
        keep_two(l, m, 2, EARLY, map_back(l, m, 2, turned[1], turned[2]))
        map_back(l, m, 1, TG[m], turned[0])
        offsets = OFF[m] + stack_rows(
            [jnp.zeros((1, PAIR), F32)] * 3 + [jnp.sum(t, axis=0, keepdims=True) for t in turned], 8)
        offsets = rows2(offsets, jnp.zeros((8, PAIR), F32))
        GRF[l, m // 2, m % 2, 3 * HD:] = offsets
        GRB[l, m // 2, m % 2, 3 * HD:] = offsets.astype(BF16)
        grad_v = GV[m, 0] + nt(lanes2(KL[l, m, 0], KL[l, m, 1]), diagonal(state))
        grad_v2 = (GV[m, 1] + nt(KL[l, m, 2], rows2(state[PAIR:], none_b))) * low
        MIX[m, :, 3 * PAIR:] = lanes2(grad_v, grad_v2).astype(BF16)

    def qkv_back(l, m):
        ACC[...] += nt(MIX[m], weight(3 * l + ATTN, m, slice(0, 5 * PAIR)))

    def sum_at(i):
        return (yc + 1 + i) % 2 * 2 + (cc + 1 + i // 2) % 2

    def part_rows(part):
        return slice(0, EARLY) if part == 0 else slice(EARLY, ROWS)

    def sum_sister(l, part, y):
        at = part_rows(part)
        return send(GRB.at[l, y, 1 - cc, at], RB1.at[l, y, at], rd_send.at[l, part, 0], rd_recv.at[l, part, y],
                    sister)

    def sum_square(l, part):
        at, bit = part_rows(part), batch % 2
        own, other = PB.at[l, yc, at], PB.at[l, 1 - yc, at]
        slot = SQ.at[l, bit, yc, at]
        sems = rd_send.at[l, part, 1], rd_recv.at[l, part, 2]
        return [send(other, slot, *sems, across), send(own, slot, *sems, partner(0)),
                send(other, slot, *sems, opposite)]

    def sum_wait(l, part, k, blocks, receives=True):
        ref = DBL.at[l, 0:blocks, part_rows(part)]
        copy = send(ref, ref, rd_send.at[l, part, k], rd_recv.at[l, part, k + 1], sister)
        copy.wait_send()
        if receives:
            copy.wait_recv()

    def sum_half(l, part, y):
        at = part_rows(part)
        sum_sister(l, part, y).wait_recv()
        PB[l, y, at] = (GRF[l, y, cc, at] + RB1[l, y, at].astype(F32)).astype(BF16)

    def sum_step(l, part, i):
        if i < 2:
            sum_sister(l, part, sum_at(i) // 2).start()
        if i == 2:
            sum_half(l, part, 1 - yc)
            copies = sum_square(l, part)
            copies[0].start()
            copies[2].start()

    def sum_chip(l, part):
        at = part_rows(part)
        sum_half(l, part, yc)
        SQ[l, batch % 2, yc, at] = PB[l, yc, at]
        sum_square(l, part)[1].start()

    def sum_z(l, part, k):
        ref = DBL.at[l, zc, part_rows(part)]
        return send(ref, ref, rd_send.at[l, part, 2], rd_recv.at[l, part, 3], (((zc + k) % 4) * 2 + xc, mp))

    def sum_double(l, part, k):
        at = part_rows(part)
        return send(DBL.at[l, 2 * k, at], DBL.at[l, 2 * k + 1, at], rd_send.at[l, part, 2],
                    rd_recv.at[l, part, 2 + k], partner(k))

    def sum_batch(l, part):
        at = part_rows(part)
        sum_wait(l, part, 1, 3)
        sum_wait(l, part, 0, 2, receives=False)
        total = sum(SQ[l, i, j, at].astype(F32) for i in range(2) for j in range(2))
        if gathers:
            DBL[l, zc, at] = total.astype(BF16)
            for k in (1, 2, 3):
                sum_z(l, part, k).start()
        else:
            DBL[l, 2, at] = total.astype(BF16)
            sum_double(l, part, 1).start()

    def sum_end(l, part):
        at = part_rows(part)
        if gathers:
            sum_wait(l, part, 2, 3)
            total = sum(DBL[l, z, at].astype(F32) for z in range(4))
        else:
            for k in range(1, steps):
                sum_double(l, part, k).wait()
                total = DBL[l, 2 * k, at].astype(F32) + DBL[l, 2 * k + 1, at].astype(F32)
                if k + 1 < steps:
                    DBL[l, 2 * k + 2, at] = total.astype(BF16)
                    sum_double(l, part, k + 1).start()
        ref, alone, beside_it = (gq_ref, 2, (0, 1)) if part == 0 else (gk_ref, 0, (1, 2))
        two, folded = total[:HD], total[HD:HD + HD // 2]
        ref[l, beside_it[0]] = two[:, :HD]
        ref[l, beside_it[1]] = pltpu.roll(two, HD, 1)[:, :HD]
        ref[l, alone, :HD // 2] = folded[:, :HD]
        ref[l, alone, HD // 2:] = pltpu.roll(folded, HD, 1)[:, :HD]
        if part == 1:
            offsets = total[EARLY:EARLY + 8]
            offsets = offsets - pltpu.roll(offsets, HD, 1)
            for i in range(6):
                (gqb_ref if i < 3 else gkb_ref)[i % 3, l:l + 1] = offsets[i:i + 1, :HD]

    cot_copy.wait()
    GRAD[...] = COT[...].astype(F32)
    N1[...] = COT[...]
    for l in reversed(range(LAYERS)):
        e = 2 + l
        above = l + 1 if l + 1 < LAYERS else None
        clear()
        for i in range(4):
            if l + 1 == LAYERS and i == (2 if gathers else 0):
                ready(CHUNKS - 1)
            mlp_back(l, i % 2 * 2 + (cc if i < 2 else 1 - cc))
        grad_mid = GRAD[...] + norm_back(NORMED[l, 1], SCALE[l, 1, :, :1], ACC[...])
        GRAD[...] = grad_mid
        N1[...] = grad_mid.astype(BF16)

        for j in range(2):
            for i in (2 * j, 2 * j + 1):
                attend_back_start(l, block_at(i))
            if above is None and j == 1:
                last_down(0, 2)
            for i in (2 * j, 2 * j + 1):
                ex_step(e, i, b_own, b_sis)
        for i in range(4):
            attend_back_local(l, sum_at(i))
        if above is None:
            last_down(2, 2)
            last_end()
        for j in range(2):
            ex_forward(e, j)
        for i in range(2):
            sum_step(l, 0, i)
        ex_end(e)
        if above is not None:
            sum_batch(above, 0)
            sum_batch(above, 1)
        for j in range(2):
            for i in (2 * j, 2 * j + 1):
                attend_back_end(l, sum_at(i))
            if above and j == 0:
                sum_step(l, 0, 2)
                sum_chip(l, 0)
            for i in (2 * j, 2 * j + 1):
                if above or i < 2:
                    sum_step(l, 1, i)
        if above:
            sum_chip(l, 1)
        clear()
        for m in range(4):
            qkv_back(l, m)
            if l == 0 and m == 1:
                sum_batch(0, 0)
        if l == 0:
            sum_batch(0, 1)
        if not above:
            for part in range(2):
                sum_step(l, part, 2)
                sum_chip(l, part)
        GRAD[...] = GRAD[...] + norm_back(NORMED[l, 0], SCALE[l, 0, :, :1], ACC[...])
        N1[...] = GRAD[...].astype(BF16)
    GIN[...] = GRAD[...].astype(BF16)
    for e in range(2 * LAYERS):
        ex_drain(e)
    drain()
    for part in range(2):
        sum_end(1, part)
    sum_end(0, 0)
    sum_end(0, 1)


def hand_out(*refs):
    count = len(refs) // 2
    for source, target in zip(refs[:count], refs[count:]):
        target[...] = source[...]


def per_device(tokens, cotangent, seq_lengths, joined_qkv, attn_proj, mlp_up, mlp_down,
               query_map, query_bias, key_map, key_bias):
    n_batch, n_mp = lax.axis_size("batch"), lax.axis_size("mp")
    rows, width = tokens.shape
    slice_rows = joined_qkv.shape[1]
    heads = query_map.shape[1]
    assert n_mp == 4 and heads == 3 and rows == PAIR and query_map.shape[2] == HD
    assert n_batch & (n_batch - 1) == 0
    parts = 3
    gathers = n_batch == 8 and slice_rows % (16 * parts) == 0
    part_rows = width // (8 * parts)
    qkv, down = joined_qkv.transpose(0, 2, 1, 3), mlp_down.transpose(0, 2, 1)
    if gathers:
        cut = (LAYERS, parts, part_rows, width)
        frozen = (qkv, attn_proj, mlp_up.reshape(cut), down.reshape(cut))
    else:
        turned = jnp.concatenate([attn_proj[:, PAIR:], attn_proj[:, :PAIR]], 1).transpose(0, 2, 1)
        attn = jnp.concatenate([joined_qkv.reshape(LAYERS, slice_rows, -1), turned], 2)
        blocks = jnp.stack([attn, mlp_up, down], 1).reshape(CHUNKS, slice_rows, width)
        weights = lax.all_gather(blocks, "batch", axis=1, tiled=True)
        weights = lax.all_gather(weights, "mp", axis=1, tiled=True)
        frozen = (weights.reshape(CHUNKS, 2, 2, 4, 2, parts, part_rows, width),)

    steps = n_batch.bit_length() - 1
    vmem, dma = pltpu.VMEM, pltpu.SemaphoreType.DMA
    shapes = [(tokens.shape, BF16), (tokens.shape, BF16), (query_map.shape, F32), ((heads, LAYERS, HD), F32),
              (key_map.shape, F32), ((heads, LAYERS, HD), F32)]
    map_shapes = [query_map.shape, (heads, LAYERS, HD)] * 2
    scratch = [vmem(shape, BF16) for shape in map_shapes] + [pltpu.SMEM(seq_lengths.shape, jnp.int32)] + [
        vmem((CHUNKS, 2, 2, 4, 2, parts, part_rows, width), BF16),
        vmem((rows, width), BF16),
        vmem((rows, width), BF16),
        vmem(qkv.shape, BF16),
        vmem(attn_proj.shape, BF16),
        vmem((2, 2, LAYERS, ROWS, PAIR), BF16),
        vmem((LAYERS, 4, 3, 2 * PAIR, 2 * PAIR), BF16),
        vmem((LAYERS, 4, 8, PAIR), F32),
        vmem((rows, width), F32),
        vmem((LAYERS, 2, rows, width), F32),
        vmem((LAYERS, 2, rows, PAIR), F32),
        vmem((LAYERS, 4, rows, width), F32),
        vmem((4, rows, width), BF16),
        vmem((LAYERS, 4, rows, 5 * PAIR), BF16),
        vmem((LAYERS, 4, 3, rows, PAIR), BF16),
        vmem((LAYERS, 4, 3, rows, PAIR), BF16),
        vmem((LAYERS, 4, 3, rows, PAIR), BF16),
        vmem((LAYERS, 4, 6, rows, PAIR), F32),
        vmem((LAYERS, 4, 6, rows, PAIR), BF16),
        vmem((LAYERS, 4, 3, rows, PAIR), BF16),
        vmem((LAYERS, 4, 2, rows, PAIR), F32),
        vmem((LAYERS, 4, 2, rows, PAIR), F32),
        vmem((LAYERS, 4, 3, PAIR, PAIR), BF16),
        vmem((rows, width), BF16),
        vmem((rows, width), F32),
        vmem((rows, width), F32),
        vmem((rows, width), F32),
        vmem((4, 3, rows, PAIR), BF16),
        vmem((4, 3, rows, PAIR), BF16),
        vmem((4, 2, rows, PAIR), BF16),
        vmem((4, 3, rows, PAIR), BF16),
        vmem((4, 2, rows, PAIR), F32),
        vmem((4, rows, PAIR), F32),
        vmem((5, rows, rows), F32),
        vmem((2 * LAYERS, 2, 4, ROWS, PAIR), BF16),
        vmem((2 * LAYERS, 2, ROWS, PAIR), BF16),
        vmem((2 * LAYERS, 2, 2, ROWS, PAIR), BF16),
        vmem((4, rows, 5 * PAIR), BF16),
        vmem((4, 8, PAIR), F32),
        vmem((LAYERS, 2, 2, ROWS, PAIR), F32),
        vmem((LAYERS, 2, 2, ROWS, PAIR), BF16),
        vmem((LAYERS, 2, ROWS, PAIR), BF16),
        vmem((LAYERS, 2, ROWS, PAIR), BF16),
        vmem((LAYERS, 2, 2, ROWS, PAIR), BF16),
        vmem((LAYERS, 4 if gathers else 2 * steps, ROWS, PAIR), BF16),
        dma((1 if gathers else CHUNKS,)), dma((9,)),
        dma((7,)),
        dma((2 * LAYERS,)), dma((2 * LAYERS, 4)),
        dma((2 * LAYERS,)), dma((2 * LAYERS, 2, 2)),
        dma((LAYERS, 2, 3)), dma((LAYERS, 2, 4 if gathers else 3 + steps)),
        dma((2, 3, 2)), dma((CHUNKS, parts, 3)),
        dma((2,)), dma((CHUNKS,)),
        dma((CHUNKS + 2, 5)), dma((CHUNKS, 4, 2)),
        dma((CHUNKS,)), dma((CHUNKS,)),
    ]
    vmem_block, any_block = pl.BlockSpec(memory_space=pltpu.VMEM), pl.BlockSpec(memory_space=pl.ANY)
    shapes = [jax.ShapeDtypeStruct(*shape) for shape in shapes]
    results = pl.pallas_call(
        functools.partial(body, n_batch, gathers),
        out_shape=[pltpu.VMEM(shape.shape, shape.dtype) for shape in shapes],
        in_specs=[any_block] * (7 + len(frozen)),
        out_specs=[vmem_block] * 6,
        scratch_shapes=scratch,
        compiler_params=pltpu.CompilerParams(
            collective_id=0, has_side_effects=True, vmem_limit_bytes=62 * 2**20),
    )(seq_lengths, tokens, cotangent, query_map, query_bias.transpose(1, 0, 2), key_map,
      key_bias.transpose(1, 0, 2), *frozen)
    results = pl.pallas_call(
        hand_out,
        out_shape=shapes,
        in_specs=[vmem_block] * 6,
        out_specs=[vmem_block] * 6,
    )(*[pltpu.with_memory_space_constraint(result, pltpu.VMEM) for result in results])
    out, grad_in, qmap, qbias, kmap, kbias = results
    return out, grad_in, qmap, qbias.transpose(1, 0, 2), kmap, kbias.transpose(1, 0, 2)


def solution(mesh):
    return jax.shard_map(
        per_device,
        mesh=mesh,
        in_specs=(
            P(("batch", "mp"), None),
            P(("batch", "mp"), None),
            P("batch", None),
            P(None, "batch", None, "mp"),
            P(None, "mp", "batch"),
            P(None, "batch", "mp"),
            P(None, "mp", "batch"),
            P(None, "mp", None, None),
            P(None, "mp", None),
            P(None, "mp", None, None),
            P(None, "mp", None),
        ),
        out_specs=(
            P(("batch", "mp"), None),
            P(("batch", "mp"), None),
            P(None, "mp", None, None),
            P(None, "mp", None),
            P(None, "mp", None, None),
            P(None, "mp", None),
        ),
        check_vma=False,
    )
```

```python
import functools

import jax
import jax.numpy as jnp
from jax import lax
from jax.experimental import pallas as pl
from jax.experimental.pallas import tpu as pltpu
from jax.sharding import PartitionSpec as P

SPAN = 64
LAYERS = 2
EPS = 1e-05
F32, BF16 = jnp.float32, jnp.bfloat16
MESH = pl.DeviceIdType.MESH
ATTN, UP, DOWN = 0, 1, 2
CHUNKS = 3 * LAYERS
FIRST_LAG, LAST_LAG, START_LEAD = 2, 6, 6
TURNS = (1, 1, 0, 1, 1, 0)
HD = 64
PAIR = 2 * HD
EARLY = HD + HD // 2
ROWS = 3 * HD + 16


def nn(a, b):
    return lax.dot_general(a, b, (((1,), (0,)), ((), ())), preferred_element_type=F32)


def nt(a, b):
    return lax.dot_general(a, b, (((1,), (1,)), ((), ())), preferred_element_type=F32)


def tn(a, b):
    return lax.dot_general(a, b, (((0,), (0,)), ((), ())), preferred_element_type=F32)


def moments(x):
    mean = jnp.mean(x, axis=-1, keepdims=True)
    centered = x - mean
    scale = lax.rsqrt(jnp.mean(centered * centered, axis=-1, keepdims=True) + EPS)
    return centered * scale, scale


def norm_back(y, scale, g):
    mean_g = jnp.mean(g, axis=-1, keepdims=True)
    mean_gy = jnp.mean(g * y, axis=-1, keepdims=True)
    return scale * (g - mean_g - y * mean_gy)


GELU_C = 0.7978845608028654
GELU_A = 0.044715


def gelu_and_slope(x):
    square = x * x
    t = jnp.tanh(GELU_C * x * (1.0 + GELU_A * square))
    inner = GELU_C * (1.0 + 3.0 * GELU_A * square)
    half = 0.5 * (1.0 + t)
    return x * half, half + 0.5 * x * (1.0 - t * t) * inner


def split(x):
    high = x.astype(BF16)
    return high, (x - high.astype(F32)).astype(BF16)


def stack_rows(entries, rows):
    index = lax.broadcasted_iota(jnp.int32, (rows, entries[0].shape[1]), 0)
    out = jnp.zeros((rows, entries[0].shape[1]), F32)
    for i, entry in enumerate(entries):
        out = jnp.where(index == i, entry, out)
    return out


def lanes2(a, b):
    return jnp.concatenate([a, b], 1)


def rows2(a, b):
    return jnp.concatenate([a, b], 0)


def body(n_batch, gathers, *refs):
    seq_hbm, tok_hbm, cot_hbm, *map_hbm = refs[:7]
    frozen, refs = (refs[7:11], refs[11:]) if gathers else (refs[7:8], refs[8:])
    (OUT, GIN, gq_ref, gqb_ref, gk_ref, gkb_ref, qmap_ref, qbias_ref, kmap_ref, kbias_ref,
     seq_ref, G, TOK, COT, QKV, PROJ, MT, BD, BIAS, RES, NORMED, SCALE, SLOPE, ACT, TQ, VH, VL, KL, PF, PHI, PT, ATT, RD, CX,
     N1, ACC, LASTACC, GRAD, GNH, GC, NM, DST, GV, TG, MASKS, SB, CH, OT,
     MIX, OFF, GRF, GRB, RB1, PB, SQ, DBL,
     own_sem, in_sem, mt_sem, ex1_send, ex1_recv, ex2_send, ex2_recv, rd_send, rd_recv,
     z_send, z_recv, cross_send, far_send, first_recv, last_recv, core_send, core_recv) = refs
    rows, width = TOK.shape
    batch, mp = lax.axis_index("batch"), lax.axis_index("mp")
    yc, cc = mp // 2, mp % 2
    sister = (batch, yc * 2 + 1 - cc)
    across = (batch, (1 - yc) * 2 + cc)
    steps = n_batch.bit_length() - 1
    near_batch = batch + 1 - 2 * (batch % 2)
    opposite = (near_batch, (1 - yc) * 2 + cc)

    def partner(k):
        bit = (batch // (1 << k)) % 2
        return (batch + (1 - 2 * bit) * (1 << k), mp)

    def send(src, dst, send_sem, recv_sem, device):
        copy = pltpu.make_async_remote_copy(
            src_ref=src, dst_ref=dst, send_sem=send_sem, recv_sem=recv_sem,
            device_id=device, device_id_type=MESH)
        return copy

    if gathers:
        zc, xc = batch // 2, batch % 2
        greeted = [(((zc + k) % 4) * 2 + xc, mp) for k in (1, 2, 3)]
    else:
        greeted = [partner(k) for k in range(1, steps)]
    greeted += [partner(0), sister, across, opposite]
    barrier = pltpu.get_barrier_semaphore()
    for device in greeted:
        pl.semaphore_signal(barrier, inc=1, device_id=device, device_id_type=MESH)
    tok_copy = pltpu.make_async_copy(tok_hbm, TOK, in_sem.at[0])
    cot_copy = pltpu.make_async_copy(cot_hbm, COT, in_sem.at[1])
    seq_copy = pltpu.make_async_copy(seq_hbm, seq_ref, in_sem.at[8])
    map_copies = [pltpu.make_async_copy(source, target, in_sem.at[4 + i]) for i, (source, target) in enumerate(
        zip(map_hbm, (qmap_ref, qbias_ref, kmap_ref, kbias_ref)))]
    own_copies = []
    if gathers:
        x_side = (zc * 2 + 1 - xc, mp)
        z_up = (jnp.minimum(zc + 1, 3) * 2 + xc, mp)
        z_down = (jnp.maximum(zc - 1, 0) * 2 + xc, mp)
        qkv_hbm, proj_hbm, up_hbm, down_hbm = frozen
        qkv_copy = pltpu.make_async_copy(qkv_hbm, QKV, in_sem.at[2])
        proj_copy = pltpu.make_async_copy(proj_hbm, PROJ, in_sem.at[3])
        qkv_copy.start()
        proj_copy.start()
        tok_copy.start()
        for l in range(LAYERS):
            for part, ref in ((UP, up_hbm), (DOWN, down_hbm)):
                own_copies.append(pltpu.make_async_copy(
                    ref.at[l], G.at[3 * l + part, yc, cc, zc, xc], own_sem.at[0]))
    else:
        tok_copy.start()
        own_copies = [pltpu.make_async_copy(frozen[0].at[q], G.at[q], own_sem.at[q])
                      for q in range(CHUNKS)]
    for copy in own_copies:
        copy.start()
    cot_copy.start()
    for copy in [seq_copy] + map_copies:
        copy.start()

    if gathers:
        slice_rows = QKV.shape[2]
        eye = (lax.broadcasted_iota(jnp.int32, (slice_rows, slice_rows), 0)
               == lax.broadcasted_iota(jnp.int32, (slice_rows, slice_rows), 1)).astype(BF16)
        qkv_copy.wait()
        proj_copy.wait()
        for l in range(LAYERS):
            turned = nt(eye, PROJ[l])
            pieces = [QKV[l, i].astype(F32) for i in range(3)]
            block = jnp.concatenate(pieces + [turned[:, PAIR:], turned[:, :PAIR]], 1).astype(BF16)
            G[3 * l + ATTN, yc, cc, zc, xc] = block.reshape(G.shape[5:])

    seq_copy.wait()
    row0 = mp * rows
    spans = []
    end = jnp.int32(0)
    for s in range(seq_ref.shape[1]):
        length = seq_ref[0, s]
        spans.append((end, end + length, end + ((length + SPAN - 1) // SPAN) * SPAN))
        end = spans[-1][2]

    def owner(place):
        return sum((place >= stop).astype(jnp.int32) for _, _, stop in spans)

    def owner_at(place):
        return sum(jnp.where(place >= stop, 1, 0) for _, _, stop in spans)

    def same(a, b):
        return jnp.where(owner_at(a) == owner_at(b), 1.0, 0.0).astype(F32)

    row = lax.broadcasted_iota(jnp.int32, (rows, rows), 0) + row0
    col = lax.broadcasted_iota(jnp.int32, (rows, rows), 1) + row0
    own_row, own_col = owner(row), owner(col)
    valid = sum(((row >= a) & (row < b)).astype(F32) for a, b, _ in spans)
    MASKS[0] = ((col <= row) & (own_row == own_col)).astype(F32)
    MASKS[1] = ((row <= col) & (own_row == own_col)).astype(F32)
    MASKS[2] = valid
    came_in = jnp.where(mp > 0, owner_at(row0 - 1), -1)
    MASKS[3] = (own_row == came_in).astype(F32)
    MASKS[4] = (own_row == owner_at(row0 + rows - 1)).astype(F32)
    LOWER, UPPER, VALID, CONT, LAST = range(5)

    def last_of(y, c):
        return (y * 2 + c) * rows + rows - 1

    in_chip = same(last_of(yc, 0), last_of(yc, 1))
    first, second = (cc == 0), (cc == 1)
    f_own = jnp.where(second, 1.0, in_chip)
    f_sis = jnp.where(second, in_chip, 1.0)
    f_a = jnp.where(second, 1.0, 0.0)
    f_b = jnp.where(yc == 1, jnp.where(second, same(last_of(0, 1), last_of(1, 0)), 1.0), 0.0)
    before = same(last_of(0, 1), last_of(1, 0))
    b_own = jnp.where(first, 1.0, before)
    b_sis = jnp.where(first, before, 1.0)
    b_a = jnp.where(first, 1.0, 0.0)
    b_b = jnp.where(yc == 0, jnp.where(first, same(last_of(0, 0), last_of(0, 1)), 1.0), 0.0)

    lane = lax.broadcasted_iota(jnp.int32, (rows, PAIR), 1)
    low = (lane < HD).astype(F32)
    high = 1.0 - low
    left = lane < HD

    for copy in map_copies:
        copy.wait()
    for l in range(LAYERS):
        heads = [ref[l, h].astype(F32) for ref in (qmap_ref, kmap_ref) for h in range(3)]
        for t in range(3):
            MT[yc, cc, l, t * HD:(t + 1) * HD] = jnp.concatenate(
                [heads[2 * t], heads[2 * t + 1]], 1).astype(BF16)
        biases = [ref[h, l:l + 1].astype(F32) for ref in (qbias_ref, kbias_ref) for h in range(3)]
        MT[yc, cc, l, 3 * HD:] = stack_rows(
            [jnp.concatenate([b, -b], 1) for b in biases], 16).astype(BF16)

    pl.semaphore_wait(barrier, len(greeted))

    def maps_start():
        send(MT.at[yc, cc], MT.at[yc, cc], mt_sem.at[1], mt_sem.at[2], across).start()
        send(MT.at[yc, cc], MT.at[yc, cc], mt_sem.at[3], mt_sem.at[4], sister).start()

    def maps_forward():
        send(MT.at[1 - yc, cc], MT.at[1 - yc, cc], mt_sem.at[1], mt_sem.at[2], across).wait()
        send(MT.at[1 - yc, cc], MT.at[1 - yc, cc], mt_sem.at[5], mt_sem.at[6], sister).start()

    def maps_build():
        send(MT.at[yc, cc], MT.at[yc, 1 - cc], mt_sem.at[3], mt_sem.at[4], sister).wait()
        send(MT.at[1 - yc, cc], MT.at[1 - yc, 1 - cc], mt_sem.at[5], mt_sem.at[6], sister).wait()
        half = lax.broadcasted_iota(jnp.int32, (HD, PAIR), 1) < HD
        none = jnp.zeros((HD, PAIR), F32)

        def one(i, carry):
            l, m = i // 4, i % 4
            block = MT[m // 2, m % 2, l].astype(F32)
            for t in range(3):
                pair = block[t * HD:(t + 1) * HD]
                turned = pltpu.roll(pair, HD, 1)
                a = jnp.where(half, pair, -turned)
                b = jnp.where(half, turned, -pair)
                wide = jnp.concatenate(
                    [jnp.concatenate([a, none], 1), jnp.concatenate([none, b], 1)], 0).astype(BF16)
                BD[l, m, t, 0:PAIR] = wide
                BD[l, m, t, PAIR:2 * PAIR] = wide
            BIAS[l, m] = block[3 * HD:3 * HD + 8]
            return carry

        lax.fori_loop(0, 2 * 4, one, 0)

    if gathers:
        parts = (0, 1, 2)

        def turn(q, p):
            return (TURNS[q], 0, 1)[p]

        def near(q, p):
            return (x_side, across)[turn(q, p)]

        def far(q, p):
            return (across, x_side)[turn(q, p)]

        def single(q, p, z):
            return G.at[q, yc, cc, z, xc, p]

        def neighbour(q, p, z):
            return (G.at[q, yc, cc, z, 1 - xc, p], G.at[q, 1 - yc, cc, z, xc, p])[turn(q, p)]

        def pair_of(q, p, z):
            return (G.at[q, yc, cc, z, :, p], G.at[q, :, cc, z, xc, p])[turn(q, p)]

        def other_pair(q, p, z):
            return (G.at[q, 1 - yc, cc, z, :, p], G.at[q, :, cc, z, 1 - xc, p])[turn(q, p)]

        def early(q, p):
            return q == 0 or p == 0

        def z_unit(q, p, z):
            return single(q, p, z) if early(q, p) else pair_of(q, p, z)

        def arrived(ref, sem):
            send(ref, ref, core_send.at[0], sem, sister).wait_recv()

        def sent(ref, sem):
            send(ref, ref, sem, core_recv.at[0], sister).wait_send()

        def z_on(q, p, z, way, s):
            @pl.when((zc < 3) if way == 0 else (zc > 0))
            def _():
                send(z_unit(q, p, z), z_unit(q, p, z), z_send.at[way, s, 0 if early(q, p) else 1],
                     z_recv.at[q, p, (z - zc + (7, 5)[way]) % 4 - 1], (z_up, z_down)[way]).start()

        def near_sem(q, p, z):
            if p == 0:
                return first_recv.at[q, z]
            return first_recv.at[CHUNKS - 1 + p, z] if q == 0 else first_recv.at[q, 4]

        def to_near(q, p, z):
            send(single(q, p, z), single(q, p, z), cross_send.at[0 if early(q, p) else 1],
                 near_sem(q, p, z), near(q, p)).start()

        def to_far(q, p, z):
            send(pair_of(q, p, z), pair_of(q, p, z), far_send.at[q], last_recv.at[q, z, min(p, 1)],
                 far(q, p)).start()

        def to_sister(q, ref):
            send(ref, ref, core_send.at[q], core_recv.at[q], sister).start()

        def each_place(s, do):
            pl.when((s > 0) & (zc - s >= 0))(lambda: do(zc - s, 0))
            pl.when((s > 0) & (zc + s <= 3))(lambda: do(zc + s, 1))

        def have(q, p, z):
            if early(q, p):
                to_near(q, p, z)
            else:
                to_far(q, p, z)
                to_sister(q, pair_of(q, p, z))

        def gather_start(q):
            for p in (1, 2):
                if not early(q, p):
                    to_near(q, p, zc)

        def z_start(q):
            for p in parts:
                if p == 1 and not early(q, p):
                    arrived(G.at[q, 0, 0, 0, :, 0], first_recv.at[q, 4])
                for way in range(2):
                    z_on(q, p, zc, way, 0)
                have(q, p, zc)

        def along_z(q, s):
            def step(z, way):
                for p in parts:
                    arrived(z_unit(q, p, z), z_recv.at[q, p, (z - zc + 4) % 4 - 1])
                    z_on(q, p, z, way, s)
                    have(q, p, z)

            each_place(s, step)

        def across_first(q, s):
            def step(z, way):
                for p in parts if q == 0 else (0,):
                    arrived(neighbour(q, p, z), near_sem(q, p, z))
                    to_far(q, p, z)
                    to_sister(q, pair_of(q, p, z))

            pl.when(s == 0)(lambda: step(zc, None))
            each_place(s, step)

        def across_last(q, s):
            def step(z, way):
                arrived(G.at[q, 0, 0, 0, :, 0:2], last_recv.at[q, z, 1])
                for p in (1, 2):
                    to_sister(q, other_pair(q, p, z))
                arrived(other_pair(q, 0, z), last_recv.at[q, z, 0])
                to_sister(q, other_pair(q, 0, z))

            pl.when(s == 0)(lambda: step(zc, None))
            each_place(s, step)

        def later(k, s, lag, do):
            stages, steps = divmod(lag, 4)
            if 0 <= k - stages < CHUNKS:
                pl.when(s >= steps)(lambda: do(k - stages, s - steps))
            if steps and 0 <= k - stages - 1 < CHUNKS:
                pl.when(s < steps)(lambda: do(k - stages - 1, s + 4 - steps))

        start_step = -START_LEAD % 4
        ahead = (start_step + START_LEAD) // 4

        def comm(k, s):
            later(k, s, LAST_LAG, across_last)
            later(k, s, FIRST_LAG, across_first)
            if k < CHUNKS:
                along_z(k, s)
            if (k + ahead) < CHUNKS:
                pl.when(s == start_step)(lambda: z_start(k + ahead))

        def ready(q):
            arrived(G.at[q, :, 1 - cc], core_recv.at[q])

        def drain():
            for way in range(2):
                for s in range(3):
                    @pl.when(((zc < 3) & (zc >= s)) if way == 0 else ((zc > 0) & (zc + s <= 3)))
                    def _():
                        sent(G.at[0:4, 0, 0, 0, :, 0], z_send.at[way, s, 0])
                        sent(G.at[0:5, 0, 0, 0, :, 0:2], z_send.at[way, s, 1])
            sent(G.at[0:4, 0, 0, :, :, 0], cross_send.at[0])
            sent(G.at[0:5, 0, 0, 0, :, 0], cross_send.at[1])
            for q in range(CHUNKS):
                sent(G.at[q, 0, 0], far_send.at[q])
                sent(G.at[q, :, 0], core_send.at[q])
    else:
        def gather_start(q):
            pass

        def ready(q):
            own_copies[q].wait()

        def drain():
            pass

    def weight(q, m, lanes=None):
        if lanes is None:
            return G[q, m // 2, m % 2].reshape(width, width)
        return G[q, m // 2, m % 2, :, :, :, :, lanes].reshape(width, -1)

    def add_blocks(a, ca, b, cb):
        a, b = a.astype(F32), b.astype(F32)
        values = ca * a[:3 * HD] + cb * b[:3 * HD]
        sums = (ca * (a[3 * HD:3 * HD + 8] + a[3 * HD + 8:])
                + cb * (b[3 * HD:3 * HD + 8] + b[3 * HD + 8:]))
        return values, sums

    def block_at(i):
        return (2 * (1 - cc) + i) % 4

    def ex_sister(e, m):
        return send(SB.at[e, 0, m], SB.at[e, 1, m], ex1_send.at[e], ex1_recv.at[e, m], sister)

    def ex_across(e, j):
        return send(CH.at[e, j], OT.at[e, cc, j], ex2_send.at[e], ex2_recv.at[e, 0, j], across)

    def ex_over(e, j):
        return send(OT.at[e, cc, j], OT.at[e, cc, j], ex2_send.at[e], ex2_recv.at[e, 1, j], sister)

    def ex_step(e, i, own, sis):
        m = block_at(i)
        ex_sister(e, m).start()

        def combine():
            ex_sister(e, m).wait_recv()
            values, sums = add_blocks(SB[e, 0, m], own, SB[e, 1, m], sis)
            CH[e, i - 2, 0:3 * HD] = values.astype(BF16)
            CH[e, i - 2, 3 * HD:] = rows2(*split(sums))
            ex_across(e, i - 2).start()

        if isinstance(i, int):
            if i >= 2:
                combine()
        else:
            pl.when(i >= 2)(combine)

    def ex_forward(e, j):
        ex_across(e, j).wait_recv()
        ex_over(e, j).start()

    def ex_end(e):
        for j in range(2):
            m = block_at(j)
            ex_sister(e, m).wait_recv()
            ref = OT.at[e, 1 - cc, j]
            send(ref, ref, ex2_send.at[e], ex2_recv.at[e, 1, j], sister).wait_recv()

    def ex_drain(e):
        four = SB.at[e, 0]
        for sem in (ex1_send.at[e], ex2_send.at[e]):
            send(four, four, sem, ex1_recv.at[e, 0], sister).wait_send()

    def softmax(u):
        e = jnp.exp(u - jnp.max(u, axis=-1, keepdims=True))
        return e / jnp.sum(e, axis=-1, keepdims=True)

    def phi_q(l, m, h):
        return PHI[l, m, h]

    def phi_k(l, m, h):
        return PHI[l, m, 3 + h]

    def place(x, columns, at_left):
        at = 0 if at_left else HD
        out = x * (high if at_left else low)
        for i, column in enumerate(columns):
            out = jnp.where(lane == at + i, column, out)
        return out

    def heads_of(pair, single_tile, columns):
        return [place(pair, columns[0], False), place(pair, columns[1], True), place(single_tile, columns[2], False)]

    def attend_features(l, m):
        mixed = nn(N1[...], weight(3 * l + ATTN, m, slice(0, 5 * PAIR)))
        hi, lo = split(mixed[:, :3 * PAIR])
        TQ[l, m, :, 0:3 * PAIR] = hi
        v01 = mixed[:, 3 * PAIR:4 * PAIR].astype(BF16)
        v2 = (mixed[:, 4 * PAIR:] * low).astype(BF16)
        TQ[l, m, :, 3 * PAIR:4 * PAIR] = v01
        TQ[l, m, :, 4 * PAIR:] = v2
        bias = BIAS[l, m]
        for t in range(3):
            tile = slice(t * PAIR, (t + 1) * PAIR)
            u = nn(lanes2(hi[:, tile], lo[:, tile]), BD[l, m, t])
            for e in range(2):
                h = 2 * t + e
                p = softmax(u[:, e * PAIR:(e + 1) * PAIR] + bias[h:h + 1])
                PF[l, m, h] = p
                p = p.astype(BF16)
                PHI[l, m, h] = p if h < 3 else (p.astype(F32) * MASKS[VALID]).astype(BF16)
        last = MASKS[LAST]
        for h, v in enumerate(heads_of(v01.astype(F32), v2.astype(F32), [(1.0, 1.0)] * 3)):
            VH[l, m, h] = v.astype(BF16)
            VL[l, m, h] = (v * last).astype(BF16)
        keys = [phi_k(l, m, h).astype(F32) * last for h in range(3)]
        sums = stack_rows([jnp.sum(k, axis=0, keepdims=True) for k in keys], 8)
        keys = [k.astype(BF16) for k in keys]
        for h in range(3):
            KL[l, m, h] = keys[h]
        two = tn(v01, lanes2(keys[0], keys[1]))
        one = tn(v2, keys[2])
        SB[l, 0, m, 0:HD] = two[:HD, :PAIR].astype(BF16)
        SB[l, 0, m, HD:PAIR] = two[HD:, PAIR:].astype(BF16)
        SB[l, 0, m, PAIR:3 * HD] = one[:HD].astype(BF16)
        SB[l, 0, m, 3 * HD:] = rows2(*split(sums))

    def features_step(l, i):
        attend_features(l, block_at(i))
        ex_step(l, i, f_own, f_sis)

    none_b = jnp.zeros((HD, PAIR), BF16)

    def beside(block, h, entries):
        state = block[h * HD:(h + 1) * HD]
        extra = stack_rows([entry.astype(F32) for entry in entries], HD).astype(BF16)
        return rows2(extra, state) if h == 1 else rows2(state, extra)

    def diagonal(block):
        return rows2(lanes2(block[:HD], none_b), lanes2(none_b, block[HD:PAIR]))

    def attend_out(l, m):
        values, sums = add_blocks(SB[l, 1, m], f_a, OT[l, m // 2, m % 2], f_b)
        carried = values.astype(BF16)
        for h in range(3):
            top, rest = split(sums[h:h + 1])
            CX[l, m, h] = beside(carried, h, [top, top, rest])
        valid_now, cont = MASKS[VALID], MASKS[CONT]
        lower = MASKS[LOWER]
        scores, inverse = [], []
        queries = [phi_q(l, m, h) for h in range(3)]
        for h in range(3):
            keys = phi_k(l, m, h)
            s = nt(queries[h], keys) * lower
            PT[l, m, h] = (nt(keys, queries[h]) * MASKS[UPPER]).astype(BF16)
            total = jnp.sum(s + queries[h].astype(F32) * (cont * sums[h:h + 1]), axis=-1, keepdims=True)
            inverse.append(1.0 / (total + (1.0 - valid_now)))
            scores.append(s.astype(BF16))
        v01 = TQ[l, m, :, 3 * PAIR:4 * PAIR].astype(F32)
        v2 = TQ[l, m, :, 4 * PAIR:]
        num = nn(lanes2(scores[0], scores[1]), rows2((v01 * low).astype(BF16), (v01 * high).astype(BF16)))
        num += cont * nt(lanes2(queries[0], queries[1]), diagonal(carried))
        num2 = nn(scores[2], v2) + cont * nt(queries[2], rows2(carried[PAIR:], none_b))
        rd = jnp.where(left, inverse[0], inverse[1])
        att, att2 = valid_now * num * rd, valid_now * num2 * inverse[2]
        RD[l, m, 0] = rd
        RD[l, m, 1] = inverse[2]
        ATT[l, m, 0] = att
        ATT[l, m, 1] = att2
        operand = lanes2(pltpu.roll(att2, HD, 1), att).astype(BF16)
        ACC[...] += nt(operand, weight(3 * l + ATTN, m, slice(4 * PAIR, 6 * PAIR)))

    def loop4(do, unroll=False):
        def one(m, carry):
            do(m)
            return carry

        lax.fori_loop(0, 4, one, 0, unroll=unroll)

    def normalize(l, place, x):
        y, scale = moments(x)
        NORMED[l, place] = y
        SCALE[l, place] = jnp.broadcast_to(scale, (rows, PAIR))
        N1[...] = y.astype(BF16)

    def attend_end(l):
        ACC[...] = jnp.zeros((rows, width), F32)
        loop4(functools.partial(attend_out, l))
        middle = RES[...] + ACC[...]
        RES[...] = middle
        normalize(l, 1, middle)

    def up(l, m):
        pre = nn(N1[...], weight(3 * l + UP, m))
        act, SLOPE[l, m] = gelu_and_slope(pre)
        ACT[m] = act.astype(BF16)

    def down(l, m):
        ACC[...] += nt(ACT[m], weight(3 * l + DOWN, m))

    def layer_end(l):
        after = RES[...] + ACC[...]
        RES[...] = after
        normalize(l + 1, 0, after)

    def last_down(first, count):
        total = 0.0 if first == 0 else LASTACC[...]
        for m in range(first, first + count):
            total += nt(ACT[m], weight(3 * (LAYERS - 1) + DOWN, m))
        LASTACC[...] = total

    def last_end():
        OUT[...] = (RES[...] + LASTACC[...]).astype(BF16)

    def clear():
        ACC[...] = jnp.zeros((rows, width), F32)

    def stage(k, at=(), steps=4):
        def one(s, carry):
            comm(k, s)
            for when, do in at:
                pl.when(s == when)(do)
            return carry

        lax.fori_loop(0, steps, one, 0)

    if gathers:
        blocks = G.at[0, 0, 0, :, 0]
        pltpu.make_async_copy(blocks, blocks, own_sem.at[0]).wait()
        for q in range(CHUNKS):
            gather_start(q)
        for q in range(CHUNKS):
            if 4 * q < START_LEAD:
                z_start(q)
    maps_start()
    tok_copy.wait()
    x0 = TOK[...].astype(F32)
    RES[...] = x0
    normalize(0, 0, x0)

    def features(l):
        loop4(functools.partial(features_step, l))

    def forward_states(l):
        ex_forward(l, 0)
        ex_forward(l, 1)

    def middle_part(l):
        ex_end(l)
        attend_end(l)

    def up_all(l):
        loop4(functools.partial(up, l))

    def down_all(l):
        clear()
        loop4(functools.partial(down, l))
        layer_end(l)

    if gathers:
        def attend_first():
            ready(0)
            features(0)

        def up_first():
            ready(1)
            up_all(0)

        def down_first():
            ready(2)
            down_all(0)

        def attend_second():
            ready(3)
            features(1)

        def up_second():
            ready(4)
            up_all(1)

        stage(0, at=[(3, maps_forward)])
        stage(1, at=[(0, maps_build)])
        stage(2, at=[(1, attend_first)])
        stage(3, at=[(0, lambda: forward_states(0)), (1, lambda: middle_part(0)), (2, up_first)])
        stage(4, at=[(1, down_first)])
        stage(5, at=[(1, attend_second), (2, lambda: forward_states(1)), (3, lambda: middle_part(1))])
        stage(6, at=[(3, up_second)])
        stage(7, steps=2)
    else:
        maps_forward()
        maps_build()
        for l in range(LAYERS):
            ready(3 * l + ATTN)
            features(l)
            forward_states(l)
            middle_part(l)
            ready(3 * l + UP)
            up_all(l)
            if l + 1 < LAYERS:
                ready(3 * l + DOWN)
                down_all(l)


    def mlp_back(l, m):
        grad_act = nn(N1[...], weight(3 * l + DOWN, m))
        grad_pre = (SLOPE[l, m] * grad_act).astype(BF16)
        ACC[...] += nt(grad_pre, weight(3 * l + UP, m))

    row_half = lax.broadcasted_iota(jnp.int32, (2 * PAIR, PAIR), 0) % PAIR < HD
    lane_half = lax.broadcasted_iota(jnp.int32, (2 * PAIR, PAIR), 1) < HD
    across_halves = (row_half != lane_half).astype(BF16)

    def attend_back_start(l, m):
        e = 2 + l
        grads = nn(N1[...], weight(3 * l + ATTN, m, slice(4 * PAIR, 6 * PAIR)))
        g01, g2 = grads[:, PAIR:], pltpu.roll(grads[:, :PAIR], HD, 1) * low
        valid_now, cont = MASKS[VALID], MASKS[CONT]
        s01, s2 = g01 * RD[l, m, 0], g2 * RD[l, m, 1]
        p01, p2 = s01 * ATT[l, m, 0], s2 * ATT[l, m, 1]
        dens = [-nn(lanes2(*split(p)), across_halves) for p in (p01, p2)]
        num01 = (s01 * valid_now).astype(BF16)
        num2 = (s2 * valid_now).astype(BF16)
        NM[m, 0] = num01
        NM[m, 1] = num2
        columns = []
        for d in dens:
            top = d.astype(BF16).astype(F32)
            columns.append((top, d - top, top))
        tiles = heads_of(num01.astype(F32), num2.astype(F32), [columns[0], columns[0], columns[1]])
        sums = []
        for h in range(3):
            GNH[m, h] = tiles[h].astype(BF16)
            counted = (tiles[h] * cont).astype(BF16)
            GC[m, h] = counted
            state = tn(counted, phi_q(l, m, h))
            keep, extra = (state[HD:], state[:8]) if h == 1 else (state[:HD], state[HD:HD + 8])
            SB[e, 0, m, h * HD:(h + 1) * HD] = keep.astype(BF16)
            sums.append(extra[0:1] + extra[1:2])
        SB[e, 0, m, 3 * HD:] = rows2(*split(stack_rows(sums, 8)))

    def softmax_back(p, g):
        return p * (g - jnp.sum(p * g, axis=-1, keepdims=True))

    def keep_maps(l, m, first, x):
        GRF[l, m // 2, m % 2, first:first + x.shape[0]] = x
        GRB[l, m // 2, m % 2, first:first + x.shape[0]] = x.astype(BF16)

    def keep_two(l, m, t, first, two):
        maps = tn(TQ[l, m, :, t * PAIR:(t + 1) * PAIR], two)
        a, b = maps[:HD, :PAIR], maps[HD:, PAIR:]
        keep_maps(l, m, first, jnp.where(left[:HD], a - pltpu.roll(a, HD, 1), pltpu.roll(b, HD, 1) - b))

    def keep_one(l, m, second, first, one):
        maps = tn(TQ[l, m, :, PAIR:2 * PAIR], one.astype(BF16))
        a = maps[HD:] if second else maps[:HD]
        a = a - pltpu.roll(a, HD, 1)
        keep_maps(l, m, first, jnp.where(left[:HD // 2], a[:HD // 2], -a[HD // 2:]))

    def map_back(l, m, t, a, b):
        two = lanes2(a, b).astype(BF16)
        MIX[m, :, t * PAIR:(t + 1) * PAIR] = nt(two, BD[l, m, t, 0:PAIR]).astype(BF16)
        return two

    def attend_back_local(l, m):
        lower, upper = MASKS[LOWER], MASKS[UPPER]
        turned = []
        for h in range(3):
            q, k = phi_q(l, m, h), phi_k(l, m, h)
            nums, vals = GNH[m, h], VH[l, m, h]
            ds = (nt(nums, vals) * lower).astype(BF16)
            DST[m, h] = (nt(vals, nums) * upper).astype(BF16)
            g = nn(lanes2(ds, GC[m, h]), rows2(k, CX[l, m, h]))
            turned.append(softmax_back(PF[l, m, h], g))
        num01 = NM[m, 0].astype(F32)
        GV[m, 0] = nn(lanes2(PT[l, m, 0], PT[l, m, 1]),
                      rows2((num01 * low).astype(BF16), (num01 * high).astype(BF16)))
        GV[m, 1] = nn(PT[l, m, 2], NM[m, 1])
        TG[m] = turned[2]
        OFF[m] = stack_rows([jnp.sum(t, axis=0, keepdims=True) for t in turned], 8)
        keep_two(l, m, 0, 0, map_back(l, m, 0, turned[0], turned[1]))
        keep_one(l, m, False, HD, turned[2])

    def attend_back_end(l, m):
        e = 2 + l
        values, sums = add_blocks(SB[e, 1, m], b_a, OT[e, m // 2, m % 2], b_b)
        state = values.astype(BF16)
        valid_now = MASKS[VALID]
        turned = []
        for h in range(3):
            far = beside(state, h, split(sums[h:h + 1]))
            g = valid_now * nn(lanes2(DST[m, h], VL[l, m, h]), rows2(phi_q(l, m, h), far))
            turned.append(softmax_back(PF[l, m, 3 + h], g))
        keep_one(l, m, True, EARLY + HD, turned[0])
        keep_two(l, m, 2, EARLY, map_back(l, m, 2, turned[1], turned[2]))
        map_back(l, m, 1, TG[m], turned[0])
        offsets = OFF[m] + stack_rows(
            [jnp.zeros((1, PAIR), F32)] * 3 + [jnp.sum(t, axis=0, keepdims=True) for t in turned], 8)
        offsets = rows2(offsets, jnp.zeros((8, PAIR), F32))
        GRF[l, m // 2, m % 2, 3 * HD:] = offsets
        GRB[l, m // 2, m % 2, 3 * HD:] = offsets.astype(BF16)
        grad_v = GV[m, 0] + nt(lanes2(KL[l, m, 0], KL[l, m, 1]), diagonal(state))
        grad_v2 = (GV[m, 1] + nt(KL[l, m, 2], rows2(state[PAIR:], none_b))) * low
        MIX[m, :, 3 * PAIR:] = lanes2(grad_v, grad_v2).astype(BF16)

    def qkv_back(l, m):
        ACC[...] += nt(MIX[m], weight(3 * l + ATTN, m, slice(0, 5 * PAIR)))

    def sum_at(i):
        return (yc + 1 + i) % 2 * 2 + (cc + 1 + i // 2) % 2

    def part_rows(part):
        return slice(0, EARLY) if part == 0 else slice(EARLY, ROWS)

    def sum_sister(l, part, y):
        at = part_rows(part)
        return send(GRB.at[l, y, 1 - cc, at], RB1.at[l, y, at], rd_send.at[l, part, 0], rd_recv.at[l, part, y],
                    sister)

    def sum_square(l, part):
        at, bit = part_rows(part), batch % 2
        own, other = PB.at[l, yc, at], PB.at[l, 1 - yc, at]
        slot = SQ.at[l, bit, yc, at]
        sems = rd_send.at[l, part, 1], rd_recv.at[l, part, 2]
        return [send(other, slot, *sems, across), send(own, slot, *sems, partner(0)),
                send(other, slot, *sems, opposite)]

    def sum_wait(l, part, k, blocks, receives=True):
        ref = DBL.at[l, 0:blocks, part_rows(part)]
        copy = send(ref, ref, rd_send.at[l, part, k], rd_recv.at[l, part, k + 1], sister)
        copy.wait_send()
        if receives:
            copy.wait_recv()

    def sum_half(l, part, y):
        at = part_rows(part)
        sum_sister(l, part, y).wait_recv()
        PB[l, y, at] = (GRF[l, y, cc, at] + RB1[l, y, at].astype(F32)).astype(BF16)

    def sum_step(l, part, i):
        if i < 2:
            sum_sister(l, part, sum_at(i) // 2).start()
        if i == 2:
            sum_half(l, part, 1 - yc)
            copies = sum_square(l, part)
            copies[0].start()
            copies[2].start()

    def sum_chip(l, part):
        at = part_rows(part)
        sum_half(l, part, yc)
        SQ[l, batch % 2, yc, at] = PB[l, yc, at]
        sum_square(l, part)[1].start()

    def sum_z(l, part, k):
        ref = DBL.at[l, zc, part_rows(part)]
        return send(ref, ref, rd_send.at[l, part, 2], rd_recv.at[l, part, 3], (((zc + k) % 4) * 2 + xc, mp))

    def sum_double(l, part, k):
        at = part_rows(part)
        return send(DBL.at[l, 2 * k, at], DBL.at[l, 2 * k + 1, at], rd_send.at[l, part, 2],
                    rd_recv.at[l, part, 2 + k], partner(k))

    def sum_batch(l, part):
        at = part_rows(part)
        sum_wait(l, part, 1, 3)
        sum_wait(l, part, 0, 2, receives=False)
        total = sum(SQ[l, i, j, at].astype(F32) for i in range(2) for j in range(2))
        if gathers:
            DBL[l, zc, at] = total.astype(BF16)
            for k in (1, 2, 3):
                sum_z(l, part, k).start()
        else:
            DBL[l, 2, at] = total.astype(BF16)
            sum_double(l, part, 1).start()

    def sum_end(l, part):
        at = part_rows(part)
        if gathers:
            sum_wait(l, part, 2, 3)
            total = sum(DBL[l, z, at].astype(F32) for z in range(4))
        else:
            for k in range(1, steps):
                sum_double(l, part, k).wait()
                total = DBL[l, 2 * k, at].astype(F32) + DBL[l, 2 * k + 1, at].astype(F32)
                if k + 1 < steps:
                    DBL[l, 2 * k + 2, at] = total.astype(BF16)
                    sum_double(l, part, k + 1).start()
        ref, alone, beside_it = (gq_ref, 2, (0, 1)) if part == 0 else (gk_ref, 0, (1, 2))
        two, folded = total[:HD], total[HD:HD + HD // 2]
        ref[l, beside_it[0]] = two[:, :HD]
        ref[l, beside_it[1]] = pltpu.roll(two, HD, 1)[:, :HD]
        ref[l, alone, :HD // 2] = folded[:, :HD]
        ref[l, alone, HD // 2:] = pltpu.roll(folded, HD, 1)[:, :HD]
        if part == 1:
            offsets = total[EARLY:EARLY + 8]
            offsets = offsets - pltpu.roll(offsets, HD, 1)
            for i in range(6):
                (gqb_ref if i < 3 else gkb_ref)[i % 3, l:l + 1] = offsets[i:i + 1, :HD]

    cot_copy.wait()
    GRAD[...] = COT[...].astype(F32)
    N1[...] = COT[...]
    for l in reversed(range(LAYERS)):
        e = 2 + l
        above = l + 1 if l + 1 < LAYERS else None
        clear()
        for i in range(4):
            if l + 1 == LAYERS and i == (2 if gathers else 0):
                ready(CHUNKS - 1)
            mlp_back(l, i % 2 * 2 + (cc if i < 2 else 1 - cc))
        grad_mid = GRAD[...] + norm_back(NORMED[l, 1], SCALE[l, 1, :, :1], ACC[...])
        GRAD[...] = grad_mid
        N1[...] = grad_mid.astype(BF16)

        for j in range(2):
            for i in (2 * j, 2 * j + 1):
                attend_back_start(l, block_at(i))
            if above is None and j == 1:
                last_down(0, 2)
            for i in (2 * j, 2 * j + 1):
                ex_step(e, i, b_own, b_sis)
        if above is not None:
            sum_batch(above, 0)
            sum_batch(above, 1)
        for i in range(4):
            attend_back_local(l, sum_at(i))
        for i in range(2):
            sum_step(l, 0, i)
        if above is None:
            last_down(2, 2)
            last_end()
        for j in range(2):
            ex_forward(e, j)
        if above:
            sum_step(l, 0, 2)
            sum_chip(l, 0)
        ex_end(e)
        for j in range(2):
            for i in (2 * j, 2 * j + 1):
                attend_back_end(l, sum_at(i))
            for i in (2 * j, 2 * j + 1):
                if above or i < 2:
                    sum_step(l, 1, i)
        if above:
            sum_chip(l, 1)
        else:
            sum_step(l, 0, 2)
            sum_chip(l, 0)
        clear()
        for m in range(4):
            qkv_back(l, m)
            if l == 0 and m == 0:
                sum_batch(0, 0)
        if l == 0:
            sum_batch(0, 1)
        if not above:
            sum_step(l, 1, 2)
            sum_chip(l, 1)
        GRAD[...] = GRAD[...] + norm_back(NORMED[l, 0], SCALE[l, 0, :, :1], ACC[...])
        N1[...] = GRAD[...].astype(BF16)
    GIN[...] = GRAD[...].astype(BF16)
    for e in range(2 * LAYERS):
        ex_drain(e)
    drain()
    for part in range(2):
        sum_end(1, part)
    sum_end(0, 0)
    sum_end(0, 1)


def hand_out(*refs):
    count = len(refs) // 2
    for source, target in zip(refs[:count], refs[count:]):
        target[...] = source[...]


def per_device(tokens, cotangent, seq_lengths, joined_qkv, attn_proj, mlp_up, mlp_down,
               query_map, query_bias, key_map, key_bias):
    n_batch, n_mp = lax.axis_size("batch"), lax.axis_size("mp")
    rows, width = tokens.shape
    slice_rows = joined_qkv.shape[1]
    heads = query_map.shape[1]
    assert n_mp == 4 and heads == 3 and rows == PAIR and query_map.shape[2] == HD
    assert n_batch & (n_batch - 1) == 0
    parts = 3
    gathers = n_batch == 8 and slice_rows % (16 * parts) == 0
    part_rows = width // (8 * parts)
    qkv, down = joined_qkv.transpose(0, 2, 1, 3), mlp_down.transpose(0, 2, 1)
    if gathers:
        cut = (LAYERS, parts, part_rows, width)
        frozen = (qkv, attn_proj, mlp_up.reshape(cut), down.reshape(cut))
    else:
        turned = jnp.concatenate([attn_proj[:, PAIR:], attn_proj[:, :PAIR]], 1).transpose(0, 2, 1)
        attn = jnp.concatenate([joined_qkv.reshape(LAYERS, slice_rows, -1), turned], 2)
        blocks = jnp.stack([attn, mlp_up, down], 1).reshape(CHUNKS, slice_rows, width)
        weights = lax.all_gather(blocks, "batch", axis=1, tiled=True)
        weights = lax.all_gather(weights, "mp", axis=1, tiled=True)
        frozen = (weights.reshape(CHUNKS, 2, 2, 4, 2, parts, part_rows, width),)

    steps = n_batch.bit_length() - 1
    vmem, dma = pltpu.VMEM, pltpu.SemaphoreType.DMA
    shapes = [(tokens.shape, BF16), (tokens.shape, BF16), (query_map.shape, F32), ((heads, LAYERS, HD), F32),
              (key_map.shape, F32), ((heads, LAYERS, HD), F32)]
    map_shapes = [query_map.shape, (heads, LAYERS, HD)] * 2
    scratch = [vmem(shape, BF16) for shape in map_shapes] + [pltpu.SMEM(seq_lengths.shape, jnp.int32)] + [
        vmem((CHUNKS, 2, 2, 4, 2, parts, part_rows, width), BF16),
        vmem((rows, width), BF16),
        vmem((rows, width), BF16),
        vmem(qkv.shape, BF16),
        vmem(attn_proj.shape, BF16),
        vmem((2, 2, LAYERS, ROWS, PAIR), BF16),
        vmem((LAYERS, 4, 3, 2 * PAIR, 2 * PAIR), BF16),
        vmem((LAYERS, 4, 8, PAIR), F32),
        vmem((rows, width), F32),
        vmem((LAYERS, 2, rows, width), F32),
        vmem((LAYERS, 2, rows, PAIR), F32),
        vmem((LAYERS, 4, rows, width), F32),
        vmem((4, rows, width), BF16),
        vmem((LAYERS, 4, rows, 5 * PAIR), BF16),
        vmem((LAYERS, 4, 3, rows, PAIR), BF16),
        vmem((LAYERS, 4, 3, rows, PAIR), BF16),
        vmem((LAYERS, 4, 3, rows, PAIR), BF16),
        vmem((LAYERS, 4, 6, rows, PAIR), F32),
        vmem((LAYERS, 4, 6, rows, PAIR), BF16),
        vmem((LAYERS, 4, 3, rows, PAIR), BF16),
        vmem((LAYERS, 4, 2, rows, PAIR), F32),
        vmem((LAYERS, 4, 2, rows, PAIR), F32),
        vmem((LAYERS, 4, 3, PAIR, PAIR), BF16),
        vmem((rows, width), BF16),
        vmem((rows, width), F32),
        vmem((rows, width), F32),
        vmem((rows, width), F32),
        vmem((4, 3, rows, PAIR), BF16),
        vmem((4, 3, rows, PAIR), BF16),
        vmem((4, 2, rows, PAIR), BF16),
        vmem((4, 3, rows, PAIR), BF16),
        vmem((4, 2, rows, PAIR), F32),
        vmem((4, rows, PAIR), F32),
        vmem((5, rows, rows), F32),
        vmem((2 * LAYERS, 2, 4, ROWS, PAIR), BF16),
        vmem((2 * LAYERS, 2, ROWS, PAIR), BF16),
        vmem((2 * LAYERS, 2, 2, ROWS, PAIR), BF16),
        vmem((4, rows, 5 * PAIR), BF16),
        vmem((4, 8, PAIR), F32),
        vmem((LAYERS, 2, 2, ROWS, PAIR), F32),
        vmem((LAYERS, 2, 2, ROWS, PAIR), BF16),
        vmem((LAYERS, 2, ROWS, PAIR), BF16),
        vmem((LAYERS, 2, ROWS, PAIR), BF16),
        vmem((LAYERS, 2, 2, ROWS, PAIR), BF16),
        vmem((LAYERS, 4 if gathers else 2 * steps, ROWS, PAIR), BF16),
        dma((1 if gathers else CHUNKS,)), dma((9,)),
        dma((7,)),
        dma((2 * LAYERS,)), dma((2 * LAYERS, 4)),
        dma((2 * LAYERS,)), dma((2 * LAYERS, 2, 2)),
        dma((LAYERS, 2, 3)), dma((LAYERS, 2, 4 if gathers else 3 + steps)),
        dma((2, 3, 2)), dma((CHUNKS, parts, 3)),
        dma((2,)), dma((CHUNKS,)),
        dma((CHUNKS + 2, 5)), dma((CHUNKS, 4, 2)),
        dma((CHUNKS,)), dma((CHUNKS,)),
    ]
    vmem_block, any_block = pl.BlockSpec(memory_space=pltpu.VMEM), pl.BlockSpec(memory_space=pl.ANY)
    shapes = [jax.ShapeDtypeStruct(*shape) for shape in shapes]
    results = pl.pallas_call(
        functools.partial(body, n_batch, gathers),
        out_shape=[pltpu.VMEM(shape.shape, shape.dtype) for shape in shapes],
        in_specs=[any_block] * (7 + len(frozen)),
        out_specs=[vmem_block] * 6,
        scratch_shapes=scratch,
        compiler_params=pltpu.CompilerParams(
            collective_id=0, has_side_effects=True, vmem_limit_bytes=62 * 2**20),
    )(seq_lengths, tokens, cotangent, query_map, query_bias.transpose(1, 0, 2), key_map,
      key_bias.transpose(1, 0, 2), *frozen)
    results = pl.pallas_call(
        hand_out,
        out_shape=shapes,
        in_specs=[vmem_block] * 6,
        out_specs=[vmem_block] * 6,
    )(*[pltpu.with_memory_space_constraint(result, pltpu.VMEM) for result in results])
    out, grad_in, qmap, qbias, kmap, kbias = results
    return out, grad_in, qmap, qbias.transpose(1, 0, 2), kmap, kbias.transpose(1, 0, 2)


def solution(mesh):
    return jax.shard_map(
        per_device,
        mesh=mesh,
        in_specs=(
            P(("batch", "mp"), None),
            P(("batch", "mp"), None),
            P("batch", None),
            P(None, "batch", None, "mp"),
            P(None, "mp", "batch"),
            P(None, "batch", "mp"),
            P(None, "mp", "batch"),
            P(None, "mp", None, None),
            P(None, "mp", None),
            P(None, "mp", None, None),
            P(None, "mp", None),
        ),
        out_specs=(
            P(("batch", "mp"), None),
            P(("batch", "mp"), None),
            P(None, "mp", None, None),
            P(None, "mp", None),
            P(None, "mp", None, None),
            P(None, "mp", None),
        ),
        check_vma=False,
    )
```

```python
import functools

import jax
import jax.numpy as jnp
from jax import lax
from jax.experimental import pallas as pl
from jax.experimental.pallas import tpu as pltpu
from jax.sharding import PartitionSpec as P

SPAN = 64
LAYERS = 2
EPS = 1e-05
F32, BF16 = jnp.float32, jnp.bfloat16
MESH = pl.DeviceIdType.MESH
ATTN, UP, DOWN = 0, 1, 2
CHUNKS = 3 * LAYERS
FIRST_LAG, LAST_LAG, START_LEAD = 2, 6, 6
TURNS = (1, 1, 0, 1, 1, 0)
HD = 64
PAIR = 2 * HD
EARLY = HD + HD // 2
ROWS = 3 * HD + 16


def nn(a, b):
    return lax.dot_general(a, b, (((1,), (0,)), ((), ())), preferred_element_type=F32)


def nt(a, b):
    return lax.dot_general(a, b, (((1,), (1,)), ((), ())), preferred_element_type=F32)


def tn(a, b):
    return lax.dot_general(a, b, (((0,), (0,)), ((), ())), preferred_element_type=F32)


def moments(x):
    mean = jnp.mean(x, axis=-1, keepdims=True)
    centered = x - mean
    scale = lax.rsqrt(jnp.mean(centered * centered, axis=-1, keepdims=True) + EPS)
    return centered * scale, scale


def norm_back(y, scale, g):
    mean_g = jnp.mean(g, axis=-1, keepdims=True)
    mean_gy = jnp.mean(g * y, axis=-1, keepdims=True)
    return scale * (g - mean_g - y * mean_gy)


GELU_C = 0.7978845608028654
GELU_A = 0.044715


def gelu_and_slope(x):
    square = x * x
    t = jnp.tanh(GELU_C * x * (1.0 + GELU_A * square))
    inner = GELU_C * (1.0 + 3.0 * GELU_A * square)
    half = 0.5 * (1.0 + t)
    return x * half, half + 0.5 * x * (1.0 - t * t) * inner


def split(x):
    high = x.astype(BF16)
    return high, (x - high.astype(F32)).astype(BF16)


def stack_rows(entries, rows):
    index = lax.broadcasted_iota(jnp.int32, (rows, entries[0].shape[1]), 0)
    out = jnp.zeros((rows, entries[0].shape[1]), F32)
    for i, entry in enumerate(entries):
        out = jnp.where(index == i, entry, out)
    return out


def lanes2(a, b):
    return jnp.concatenate([a, b], 1)


def rows2(a, b):
    return jnp.concatenate([a, b], 0)


def body(n_batch, gathers, *refs):
    seq_hbm, tok_hbm, cot_hbm, *map_hbm = refs[:7]
    frozen, refs = (refs[7:11], refs[11:]) if gathers else (refs[7:8], refs[8:])
    (OUT, GIN, gq_ref, gqb_ref, gk_ref, gkb_ref, qmap_ref, qbias_ref, kmap_ref, kbias_ref,
     seq_ref, G, TOK, COT, QKV, PROJ, MT, BD, BIAS, RES, NORMED, SCALE, SLOPE, ACT, TQ, VH, VL, KL, PF, PHI, PT, ATT, RD, CX,
     N1, ACC, LASTACC, GRAD, GNH, GC, NM, DST, GV, TG, MASKS, SB, CH, OT,
     MIX, OFF, GRF, GRB, RB1, PB, SQ, DBL,
     own_sem, in_sem, mt_sem, ex1_send, ex1_recv, ex2_send, ex2_recv, rd_send, rd_recv,
     z_send, z_recv, cross_send, far_send, first_recv, last_recv, core_send, core_recv) = refs
    rows, width = TOK.shape
    batch, mp = lax.axis_index("batch"), lax.axis_index("mp")
    yc, cc = mp // 2, mp % 2
    sister = (batch, yc * 2 + 1 - cc)
    across = (batch, (1 - yc) * 2 + cc)
    steps = n_batch.bit_length() - 1
    near_batch = batch + 1 - 2 * (batch % 2)
    opposite = (near_batch, (1 - yc) * 2 + cc)

    def partner(k):
        bit = (batch // (1 << k)) % 2
        return (batch + (1 - 2 * bit) * (1 << k), mp)

    def send(src, dst, send_sem, recv_sem, device):
        copy = pltpu.make_async_remote_copy(
            src_ref=src, dst_ref=dst, send_sem=send_sem, recv_sem=recv_sem,
            device_id=device, device_id_type=MESH)
        return copy

    if gathers:
        zc, xc = batch // 2, batch % 2
        greeted = [(((zc + k) % 4) * 2 + xc, mp) for k in (1, 2, 3)]
    else:
        greeted = [partner(k) for k in range(1, steps)]
    greeted += [partner(0), sister, across, opposite]
    barrier = pltpu.get_barrier_semaphore()
    for device in greeted:
        pl.semaphore_signal(barrier, inc=1, device_id=device, device_id_type=MESH)
    tok_copy = pltpu.make_async_copy(tok_hbm, TOK, in_sem.at[0])
    cot_copy = pltpu.make_async_copy(cot_hbm, COT, in_sem.at[1])
    seq_copy = pltpu.make_async_copy(seq_hbm, seq_ref, in_sem.at[8])
    map_copies = [pltpu.make_async_copy(source, target, in_sem.at[4 + i]) for i, (source, target) in enumerate(
        zip(map_hbm, (qmap_ref, qbias_ref, kmap_ref, kbias_ref)))]
    own_copies = []
    if gathers:
        x_side = (zc * 2 + 1 - xc, mp)
        z_up = (jnp.minimum(zc + 1, 3) * 2 + xc, mp)
        z_down = (jnp.maximum(zc - 1, 0) * 2 + xc, mp)
        qkv_hbm, proj_hbm, up_hbm, down_hbm = frozen
        qkv_copy = pltpu.make_async_copy(qkv_hbm, QKV, in_sem.at[2])
        proj_copy = pltpu.make_async_copy(proj_hbm, PROJ, in_sem.at[3])
        qkv_copy.start()
        proj_copy.start()
        tok_copy.start()
        for l in range(LAYERS):
            for part, ref in ((UP, up_hbm), (DOWN, down_hbm)):
                own_copies.append(pltpu.make_async_copy(
                    ref.at[l], G.at[3 * l + part, yc, cc, zc, xc], own_sem.at[0]))
    else:
        tok_copy.start()
        own_copies = [pltpu.make_async_copy(frozen[0].at[q], G.at[q], own_sem.at[q])
                      for q in range(CHUNKS)]
    for copy in own_copies:
        copy.start()
    cot_copy.start()
    for copy in [seq_copy] + map_copies:
        copy.start()

    if gathers:
        slice_rows = QKV.shape[2]
        eye = (lax.broadcasted_iota(jnp.int32, (slice_rows, slice_rows), 0)
               == lax.broadcasted_iota(jnp.int32, (slice_rows, slice_rows), 1)).astype(BF16)
        qkv_copy.wait()
        proj_copy.wait()
        for l in range(LAYERS):
            turned = nt(eye, PROJ[l])
            pieces = [QKV[l, i].astype(F32) for i in range(3)]
            block = jnp.concatenate(pieces + [turned[:, PAIR:], turned[:, :PAIR]], 1).astype(BF16)
            G[3 * l + ATTN, yc, cc, zc, xc] = block.reshape(G.shape[5:])

    seq_copy.wait()
    row0 = mp * rows
    spans = []
    end = jnp.int32(0)
    for s in range(seq_ref.shape[1]):
        length = seq_ref[0, s]
        spans.append((end, end + length, end + ((length + SPAN - 1) // SPAN) * SPAN))
        end = spans[-1][2]

    def owner(place):
        return sum((place >= stop).astype(jnp.int32) for _, _, stop in spans)

    def owner_at(place):
        return sum(jnp.where(place >= stop, 1, 0) for _, _, stop in spans)

    def same(a, b):
        return jnp.where(owner_at(a) == owner_at(b), 1.0, 0.0).astype(F32)

    row = lax.broadcasted_iota(jnp.int32, (rows, rows), 0) + row0
    col = lax.broadcasted_iota(jnp.int32, (rows, rows), 1) + row0
    own_row, own_col = owner(row), owner(col)
    valid = sum(((row >= a) & (row < b)).astype(F32) for a, b, _ in spans)
    MASKS[0] = ((col <= row) & (own_row == own_col)).astype(F32)
    MASKS[1] = ((row <= col) & (own_row == own_col)).astype(F32)
    MASKS[2] = valid
    came_in = jnp.where(mp > 0, owner_at(row0 - 1), -1)
    MASKS[3] = (own_row == came_in).astype(F32)
    MASKS[4] = (own_row == owner_at(row0 + rows - 1)).astype(F32)
    LOWER, UPPER, VALID, CONT, LAST = range(5)

    def last_of(y, c):
        return (y * 2 + c) * rows + rows - 1

    in_chip = same(last_of(yc, 0), last_of(yc, 1))
    first, second = (cc == 0), (cc == 1)
    f_own = jnp.where(second, 1.0, in_chip)
    f_sis = jnp.where(second, in_chip, 1.0)
    f_a = jnp.where(second, 1.0, 0.0)
    f_b = jnp.where(yc == 1, jnp.where(second, same(last_of(0, 1), last_of(1, 0)), 1.0), 0.0)
    before = same(last_of(0, 1), last_of(1, 0))
    b_own = jnp.where(first, 1.0, before)
    b_sis = jnp.where(first, before, 1.0)
    b_a = jnp.where(first, 1.0, 0.0)
    b_b = jnp.where(yc == 0, jnp.where(first, same(last_of(0, 0), last_of(0, 1)), 1.0), 0.0)

    lane = lax.broadcasted_iota(jnp.int32, (rows, PAIR), 1)
    low = (lane < HD).astype(F32)
    high = 1.0 - low
    left = lane < HD

    for copy in map_copies:
        copy.wait()
    for l in range(LAYERS):
        heads = [ref[l, h].astype(F32) for ref in (qmap_ref, kmap_ref) for h in range(3)]
        for t in range(3):
            MT[yc, cc, l, t * HD:(t + 1) * HD] = jnp.concatenate(
                [heads[2 * t], heads[2 * t + 1]], 1).astype(BF16)
        biases = [ref[h, l:l + 1].astype(F32) for ref in (qbias_ref, kbias_ref) for h in range(3)]
        MT[yc, cc, l, 3 * HD:] = stack_rows(
            [jnp.concatenate([b, -b], 1) for b in biases], 16).astype(BF16)

    pl.semaphore_wait(barrier, len(greeted))

    def maps_start():
        send(MT.at[yc, cc], MT.at[yc, cc], mt_sem.at[1], mt_sem.at[2], across).start()
        send(MT.at[yc, cc], MT.at[yc, cc], mt_sem.at[3], mt_sem.at[4], sister).start()

    def maps_forward():
        send(MT.at[1 - yc, cc], MT.at[1 - yc, cc], mt_sem.at[1], mt_sem.at[2], across).wait()
        send(MT.at[1 - yc, cc], MT.at[1 - yc, cc], mt_sem.at[5], mt_sem.at[6], sister).start()

    def maps_build():
        send(MT.at[yc, cc], MT.at[yc, 1 - cc], mt_sem.at[3], mt_sem.at[4], sister).wait()
        send(MT.at[1 - yc, cc], MT.at[1 - yc, 1 - cc], mt_sem.at[5], mt_sem.at[6], sister).wait()
        half = lax.broadcasted_iota(jnp.int32, (HD, PAIR), 1) < HD
        none = jnp.zeros((HD, PAIR), F32)

        def one(i, carry):
            l, m = i // 4, i % 4
            block = MT[m // 2, m % 2, l].astype(F32)
            for t in range(3):
                pair = block[t * HD:(t + 1) * HD]
                turned = pltpu.roll(pair, HD, 1)
                a = jnp.where(half, pair, -turned)
                b = jnp.where(half, turned, -pair)
                wide = jnp.concatenate(
                    [jnp.concatenate([a, none], 1), jnp.concatenate([none, b], 1)], 0).astype(BF16)
                BD[l, m, t, 0:PAIR] = wide
                BD[l, m, t, PAIR:2 * PAIR] = wide
            BIAS[l, m] = block[3 * HD:3 * HD + 8]
            return carry

        lax.fori_loop(0, 2 * 4, one, 0)

    if gathers:
        parts = (0, 1, 2)

        def turn(q, p):
            return (TURNS[q], 0, 1)[p]

        def near(q, p):
            return (x_side, across)[turn(q, p)]

        def far(q, p):
            return (across, x_side)[turn(q, p)]

        def single(q, p, z):
            return G.at[q, yc, cc, z, xc, p]

        def neighbour(q, p, z):
            return (G.at[q, yc, cc, z, 1 - xc, p], G.at[q, 1 - yc, cc, z, xc, p])[turn(q, p)]

        def pair_of(q, p, z):
            return (G.at[q, yc, cc, z, :, p], G.at[q, :, cc, z, xc, p])[turn(q, p)]

        def other_pair(q, p, z):
            return (G.at[q, 1 - yc, cc, z, :, p], G.at[q, :, cc, z, 1 - xc, p])[turn(q, p)]

        def early(q, p):
            return q == 0 or p == 0

        def z_unit(q, p, z):
            return single(q, p, z) if early(q, p) else pair_of(q, p, z)

        def arrived(ref, sem):
            send(ref, ref, core_send.at[0], sem, sister).wait_recv()

        def sent(ref, sem):
            send(ref, ref, sem, core_recv.at[0], sister).wait_send()

        def z_on(q, p, z, way, s):
            @pl.when((zc < 3) if way == 0 else (zc > 0))
            def _():
                send(z_unit(q, p, z), z_unit(q, p, z), z_send.at[way, s, 0 if early(q, p) else 1],
                     z_recv.at[q, p, (z - zc + (7, 5)[way]) % 4 - 1], (z_up, z_down)[way]).start()

        def near_sem(q, p, z):
            if p == 0:
                return first_recv.at[q, z]
            return first_recv.at[CHUNKS - 1 + p, z] if q == 0 else first_recv.at[q, 4]

        def to_near(q, p, z):
            send(single(q, p, z), single(q, p, z), cross_send.at[0 if early(q, p) else 1],
                 near_sem(q, p, z), near(q, p)).start()

        def to_far(q, p, z):
            send(pair_of(q, p, z), pair_of(q, p, z), far_send.at[q], last_recv.at[q, z, min(p, 1)],
                 far(q, p)).start()

        def to_sister(q, ref):
            send(ref, ref, core_send.at[q], core_recv.at[q], sister).start()

        def each_place(s, do):
            pl.when((s > 0) & (zc - s >= 0))(lambda: do(zc - s, 0))
            pl.when((s > 0) & (zc + s <= 3))(lambda: do(zc + s, 1))

        def have(q, p, z):
            if early(q, p):
                to_near(q, p, z)
            else:
                to_far(q, p, z)
                to_sister(q, pair_of(q, p, z))

        def gather_start(q):
            for p in (1, 2):
                if not early(q, p):
                    to_near(q, p, zc)

        def z_start(q):
            for p in parts:
                if p == 1 and not early(q, p):
                    arrived(G.at[q, 0, 0, 0, :, 0], first_recv.at[q, 4])
                for way in range(2):
                    z_on(q, p, zc, way, 0)
                have(q, p, zc)

        def along_z(q, s):
            def step(z, way):
                for p in parts:
                    arrived(z_unit(q, p, z), z_recv.at[q, p, (z - zc + 4) % 4 - 1])
                    z_on(q, p, z, way, s)
                    have(q, p, z)

            each_place(s, step)

        def across_first(q, s):
            def step(z, way):
                for p in parts if q == 0 else (0,):
                    arrived(neighbour(q, p, z), near_sem(q, p, z))
                    to_far(q, p, z)
                    to_sister(q, pair_of(q, p, z))

            pl.when(s == 0)(lambda: step(zc, None))
            each_place(s, step)

        def across_last(q, s):
            def step(z, way):
                arrived(G.at[q, 0, 0, 0, :, 0:2], last_recv.at[q, z, 1])
                for p in (1, 2):
                    to_sister(q, other_pair(q, p, z))
                arrived(other_pair(q, 0, z), last_recv.at[q, z, 0])
                to_sister(q, other_pair(q, 0, z))

            pl.when(s == 0)(lambda: step(zc, None))
            each_place(s, step)

        def later(k, s, lag, do):
            stages, steps = divmod(lag, 4)
            if 0 <= k - stages < CHUNKS:
                pl.when(s >= steps)(lambda: do(k - stages, s - steps))
            if steps and 0 <= k - stages - 1 < CHUNKS:
                pl.when(s < steps)(lambda: do(k - stages - 1, s + 4 - steps))

        start_step = -START_LEAD % 4
        ahead = (start_step + START_LEAD) // 4

        def comm(k, s):
            later(k, s, LAST_LAG, across_last)
            later(k, s, FIRST_LAG, across_first)
            if k < CHUNKS:
                along_z(k, s)
            if (k + ahead) < CHUNKS:
                pl.when(s == start_step)(lambda: z_start(k + ahead))

        def ready(q):
            arrived(G.at[q, :, 1 - cc], core_recv.at[q])

        def drain():
            for way in range(2):
                for s in range(3):
                    @pl.when(((zc < 3) & (zc >= s)) if way == 0 else ((zc > 0) & (zc + s <= 3)))
                    def _():
                        sent(G.at[0:4, 0, 0, 0, :, 0], z_send.at[way, s, 0])
                        sent(G.at[0:5, 0, 0, 0, :, 0:2], z_send.at[way, s, 1])
            sent(G.at[0:4, 0, 0, :, :, 0], cross_send.at[0])
            sent(G.at[0:5, 0, 0, 0, :, 0], cross_send.at[1])
            for q in range(CHUNKS):
                sent(G.at[q, 0, 0], far_send.at[q])
                sent(G.at[q, :, 0], core_send.at[q])
    else:
        def gather_start(q):
            pass

        def ready(q):
            own_copies[q].wait()

        def drain():
            pass

    def weight(q, m, lanes=None):
        if lanes is None:
            return G[q, m // 2, m % 2].reshape(width, width)
        return G[q, m // 2, m % 2, :, :, :, :, lanes].reshape(width, -1)

    def add_blocks(a, ca, b, cb):
        a, b = a.astype(F32), b.astype(F32)
        values = ca * a[:3 * HD] + cb * b[:3 * HD]
        sums = (ca * (a[3 * HD:3 * HD + 8] + a[3 * HD + 8:])
                + cb * (b[3 * HD:3 * HD + 8] + b[3 * HD + 8:]))
        return values, sums

    def block_at(i):
        return (2 * (1 - cc) + i) % 4

    def ex_sister(e, m):
        return send(SB.at[e, 0, m], SB.at[e, 1, m], ex1_send.at[e], ex1_recv.at[e, m], sister)

    def ex_across(e, j):
        return send(CH.at[e, j], OT.at[e, cc, j], ex2_send.at[e], ex2_recv.at[e, 0, j], across)

    def ex_over(e, j):
        return send(OT.at[e, cc, j], OT.at[e, cc, j], ex2_send.at[e], ex2_recv.at[e, 1, j], sister)

    def ex_step(e, i, own, sis):
        m = block_at(i)
        ex_sister(e, m).start()

        def combine():
            ex_sister(e, m).wait_recv()
            values, sums = add_blocks(SB[e, 0, m], own, SB[e, 1, m], sis)
            CH[e, i - 2, 0:3 * HD] = values.astype(BF16)
            CH[e, i - 2, 3 * HD:] = rows2(*split(sums))
            ex_across(e, i - 2).start()

        if isinstance(i, int):
            if i >= 2:
                combine()
        else:
            pl.when(i >= 2)(combine)

    def ex_forward(e, j):
        ex_across(e, j).wait_recv()
        ex_over(e, j).start()

    def ex_end(e):
        for j in range(2):
            m = block_at(j)
            ex_sister(e, m).wait_recv()
            ref = OT.at[e, 1 - cc, j]
            send(ref, ref, ex2_send.at[e], ex2_recv.at[e, 1, j], sister).wait_recv()

    def ex_drain(e):
        four = SB.at[e, 0]
        for sem in (ex1_send.at[e], ex2_send.at[e]):
            send(four, four, sem, ex1_recv.at[e, 0], sister).wait_send()

    def softmax(u):
        e = jnp.exp(u - jnp.max(u, axis=-1, keepdims=True))
        return e / jnp.sum(e, axis=-1, keepdims=True)

    def phi_q(l, m, h):
        return PHI[l, m, h]

    def phi_k(l, m, h):
        return PHI[l, m, 3 + h]

    def place(x, columns, at_left):
        at = 0 if at_left else HD
        out = x * (high if at_left else low)
        for i, column in enumerate(columns):
            out = jnp.where(lane == at + i, column, out)
        return out

    def heads_of(pair, single_tile, columns):
        return [place(pair, columns[0], False), place(pair, columns[1], True), place(single_tile, columns[2], False)]

    def attend_features(l, m):
        mixed = nn(N1[...], weight(3 * l + ATTN, m, slice(0, 5 * PAIR)))
        hi, lo = split(mixed[:, :3 * PAIR])
        TQ[l, m, :, 0:3 * PAIR] = hi
        v01 = mixed[:, 3 * PAIR:4 * PAIR].astype(BF16)
        v2 = (mixed[:, 4 * PAIR:] * low).astype(BF16)
        TQ[l, m, :, 3 * PAIR:4 * PAIR] = v01
        TQ[l, m, :, 4 * PAIR:] = v2
        bias = BIAS[l, m]
        for t in range(3):
            tile = slice(t * PAIR, (t + 1) * PAIR)
            u = nn(lanes2(hi[:, tile], lo[:, tile]), BD[l, m, t])
            for e in range(2):
                h = 2 * t + e
                p = softmax(u[:, e * PAIR:(e + 1) * PAIR] + bias[h:h + 1])
                PF[l, m, h] = p
                p = p.astype(BF16)
                PHI[l, m, h] = p if h < 3 else (p.astype(F32) * MASKS[VALID]).astype(BF16)
        last = MASKS[LAST]
        for h, v in enumerate(heads_of(v01.astype(F32), v2.astype(F32), [(1.0, 1.0)] * 3)):
            VH[l, m, h] = v.astype(BF16)
            VL[l, m, h] = (v * last).astype(BF16)
        keys = [phi_k(l, m, h).astype(F32) * last for h in range(3)]
        sums = stack_rows([jnp.sum(k, axis=0, keepdims=True) for k in keys], 8)
        keys = [k.astype(BF16) for k in keys]
        for h in range(3):
            KL[l, m, h] = keys[h]
        two = tn(v01, lanes2(keys[0], keys[1]))
        one = tn(v2, keys[2])
        SB[l, 0, m, 0:HD] = two[:HD, :PAIR].astype(BF16)
        SB[l, 0, m, HD:PAIR] = two[HD:, PAIR:].astype(BF16)
        SB[l, 0, m, PAIR:3 * HD] = one[:HD].astype(BF16)
        SB[l, 0, m, 3 * HD:] = rows2(*split(sums))

    def features_step(l, i):
        attend_features(l, block_at(i))
        ex_step(l, i, f_own, f_sis)

    none_b = jnp.zeros((HD, PAIR), BF16)

    def beside(block, h, entries):
        state = block[h * HD:(h + 1) * HD]
        extra = stack_rows([entry.astype(F32) for entry in entries], HD).astype(BF16)
        return rows2(extra, state) if h == 1 else rows2(state, extra)

    def diagonal(block):
        return rows2(lanes2(block[:HD], none_b), lanes2(none_b, block[HD:PAIR]))

    def attend_out(l, m):
        values, sums = add_blocks(SB[l, 1, m], f_a, OT[l, m // 2, m % 2], f_b)
        carried = values.astype(BF16)
        for h in range(3):
            top, rest = split(sums[h:h + 1])
            CX[l, m, h] = beside(carried, h, [top, top, rest])
        valid_now, cont = MASKS[VALID], MASKS[CONT]
        lower = MASKS[LOWER]
        scores, inverse = [], []
        queries = [phi_q(l, m, h) for h in range(3)]
        for h in range(3):
            keys = phi_k(l, m, h)
            s = nt(queries[h], keys) * lower
            PT[l, m, h] = (nt(keys, queries[h]) * MASKS[UPPER]).astype(BF16)
            total = jnp.sum(s + queries[h].astype(F32) * (cont * sums[h:h + 1]), axis=-1, keepdims=True)
            inverse.append(1.0 / (total + (1.0 - valid_now)))
            scores.append(s.astype(BF16))
        v01 = TQ[l, m, :, 3 * PAIR:4 * PAIR].astype(F32)
        v2 = TQ[l, m, :, 4 * PAIR:]
        num = nn(lanes2(scores[0], scores[1]), rows2((v01 * low).astype(BF16), (v01 * high).astype(BF16)))
        num += cont * nt(lanes2(queries[0], queries[1]), diagonal(carried))
        num2 = nn(scores[2], v2) + cont * nt(queries[2], rows2(carried[PAIR:], none_b))
        rd = jnp.where(left, inverse[0], inverse[1])
        att, att2 = valid_now * num * rd, valid_now * num2 * inverse[2]
        RD[l, m, 0] = rd
        RD[l, m, 1] = inverse[2]
        ATT[l, m, 0] = att
        ATT[l, m, 1] = att2
        operand = lanes2(pltpu.roll(att2, HD, 1), att).astype(BF16)
        ACC[...] += nt(operand, weight(3 * l + ATTN, m, slice(4 * PAIR, 6 * PAIR)))

    def loop4(do, unroll=False):
        def one(m, carry):
            do(m)
            return carry

        lax.fori_loop(0, 4, one, 0, unroll=unroll)

    def normalize(l, place, x):
        y, scale = moments(x)
        NORMED[l, place] = y
        SCALE[l, place] = jnp.broadcast_to(scale, (rows, PAIR))
        N1[...] = y.astype(BF16)

    def attend_end(l):
        ACC[...] = jnp.zeros((rows, width), F32)
        loop4(functools.partial(attend_out, l))
        middle = RES[...] + ACC[...]
        RES[...] = middle
        normalize(l, 1, middle)

    def up(l, m):
        pre = nn(N1[...], weight(3 * l + UP, m))
        act, SLOPE[l, m] = gelu_and_slope(pre)
        ACT[m] = act.astype(BF16)

    def down(l, m):
        ACC[...] += nt(ACT[m], weight(3 * l + DOWN, m))

    def layer_end(l):
        after = RES[...] + ACC[...]
        RES[...] = after
        normalize(l + 1, 0, after)

    def last_down(first, count):
        total = 0.0 if first == 0 else LASTACC[...]
        for m in range(first, first + count):
            total += nt(ACT[m], weight(3 * (LAYERS - 1) + DOWN, m))
        LASTACC[...] = total

    def last_end():
        OUT[...] = (RES[...] + LASTACC[...]).astype(BF16)

    def clear():
        ACC[...] = jnp.zeros((rows, width), F32)

    def stage(k, at=(), steps=4):
        def one(s, carry):
            comm(k, s)
            for when, do in at:
                pl.when(s == when)(do)
            return carry

        lax.fori_loop(0, steps, one, 0)

    if gathers:
        blocks = G.at[0, 0, 0, :, 0]
        pltpu.make_async_copy(blocks, blocks, own_sem.at[0]).wait()
        for q in range(CHUNKS):
            gather_start(q)
        for q in range(CHUNKS):
            if 4 * q < START_LEAD:
                z_start(q)
    maps_start()
    tok_copy.wait()
    x0 = TOK[...].astype(F32)
    RES[...] = x0
    normalize(0, 0, x0)

    def features(l):
        loop4(functools.partial(features_step, l))

    def forward_states(l):
        ex_forward(l, 0)
        ex_forward(l, 1)

    def middle_part(l):
        ex_end(l)
        attend_end(l)

    def up_all(l):
        loop4(functools.partial(up, l))

    def down_all(l):
        clear()
        loop4(functools.partial(down, l))
        layer_end(l)

    if gathers:
        def attend_first():
            ready(0)
            features(0)

        def up_first():
            ready(1)
            up_all(0)

        def down_first():
            ready(2)
            down_all(0)

        def attend_second():
            ready(3)
            features(1)

        def up_second():
            ready(4)
            up_all(1)

        stage(0, at=[(3, maps_forward)])
        stage(1, at=[(0, maps_build)])
        stage(2, at=[(1, attend_first)])
        stage(3, at=[(0, lambda: forward_states(0)), (1, lambda: middle_part(0)), (2, up_first)])
        stage(4, at=[(1, down_first)])
        stage(5, at=[(1, attend_second), (2, lambda: forward_states(1)), (3, lambda: middle_part(1))])
        stage(6, at=[(3, up_second)])
        stage(7, steps=2)
    else:
        maps_forward()
        maps_build()
        for l in range(LAYERS):
            ready(3 * l + ATTN)
            features(l)
            forward_states(l)
            middle_part(l)
            ready(3 * l + UP)
            up_all(l)
            if l + 1 < LAYERS:
                ready(3 * l + DOWN)
                down_all(l)


    def mlp_back(l, m):
        grad_act = nn(N1[...], weight(3 * l + DOWN, m))
        grad_pre = (SLOPE[l, m] * grad_act).astype(BF16)
        ACC[...] += nt(grad_pre, weight(3 * l + UP, m))

    row_half = lax.broadcasted_iota(jnp.int32, (2 * PAIR, PAIR), 0) % PAIR < HD
    lane_half = lax.broadcasted_iota(jnp.int32, (2 * PAIR, PAIR), 1) < HD
    across_halves = (row_half != lane_half).astype(BF16)

    def attend_back_start(l, m):
        e = 2 + l
        grads = nn(N1[...], weight(3 * l + ATTN, m, slice(4 * PAIR, 6 * PAIR)))
        g01, g2 = grads[:, PAIR:], pltpu.roll(grads[:, :PAIR], HD, 1) * low
        valid_now, cont = MASKS[VALID], MASKS[CONT]
        s01, s2 = g01 * RD[l, m, 0], g2 * RD[l, m, 1]
        p01, p2 = s01 * ATT[l, m, 0], s2 * ATT[l, m, 1]
        dens = [-nn(lanes2(*split(p)), across_halves) for p in (p01, p2)]
        num01 = (s01 * valid_now).astype(BF16)
        num2 = (s2 * valid_now).astype(BF16)
        NM[m, 0] = num01
        NM[m, 1] = num2
        columns = []
        for d in dens:
            top = d.astype(BF16).astype(F32)
            columns.append((top, d - top, top))
        tiles = heads_of(num01.astype(F32), num2.astype(F32), [columns[0], columns[0], columns[1]])
        sums = []
        for h in range(3):
            GNH[m, h] = tiles[h].astype(BF16)
            counted = (tiles[h] * cont).astype(BF16)
            GC[m, h] = counted
            state = tn(counted, phi_q(l, m, h))
            keep, extra = (state[HD:], state[:8]) if h == 1 else (state[:HD], state[HD:HD + 8])
            SB[e, 0, m, h * HD:(h + 1) * HD] = keep.astype(BF16)
            sums.append(extra[0:1] + extra[1:2])
        SB[e, 0, m, 3 * HD:] = rows2(*split(stack_rows(sums, 8)))

    def softmax_back(p, g):
        return p * (g - jnp.sum(p * g, axis=-1, keepdims=True))

    def keep_maps(l, m, first, x):
        GRF[l, m // 2, m % 2, first:first + x.shape[0]] = x
        GRB[l, m // 2, m % 2, first:first + x.shape[0]] = x.astype(BF16)

    def keep_two(l, m, t, first, two):
        maps = tn(TQ[l, m, :, t * PAIR:(t + 1) * PAIR], two)
        a, b = maps[:HD, :PAIR], maps[HD:, PAIR:]
        keep_maps(l, m, first, jnp.where(left[:HD], a - pltpu.roll(a, HD, 1), pltpu.roll(b, HD, 1) - b))

    def keep_one(l, m, second, first, one):
        maps = tn(TQ[l, m, :, PAIR:2 * PAIR], one.astype(BF16))
        a = maps[HD:] if second else maps[:HD]
        a = a - pltpu.roll(a, HD, 1)
        keep_maps(l, m, first, jnp.where(left[:HD // 2], a[:HD // 2], -a[HD // 2:]))

    def map_back(l, m, t, a, b):
        two = lanes2(a, b).astype(BF16)
        MIX[m, :, t * PAIR:(t + 1) * PAIR] = nt(two, BD[l, m, t, 0:PAIR]).astype(BF16)
        return two

    def attend_back_local(l, m):
        lower, upper = MASKS[LOWER], MASKS[UPPER]
        turned = []
        for h in range(3):
            q, k = phi_q(l, m, h), phi_k(l, m, h)
            nums, vals = GNH[m, h], VH[l, m, h]
            ds = (nt(nums, vals) * lower).astype(BF16)
            DST[m, h] = (nt(vals, nums) * upper).astype(BF16)
            g = nn(lanes2(ds, GC[m, h]), rows2(k, CX[l, m, h]))
            turned.append(softmax_back(PF[l, m, h], g))
        num01 = NM[m, 0].astype(F32)
        GV[m, 0] = nn(lanes2(PT[l, m, 0], PT[l, m, 1]),
                      rows2((num01 * low).astype(BF16), (num01 * high).astype(BF16)))
        GV[m, 1] = nn(PT[l, m, 2], NM[m, 1])
        TG[m] = turned[2]
        OFF[m] = stack_rows([jnp.sum(t, axis=0, keepdims=True) for t in turned], 8)
        keep_two(l, m, 0, 0, map_back(l, m, 0, turned[0], turned[1]))
        keep_one(l, m, False, HD, turned[2])

    def attend_back_end(l, m):
        e = 2 + l
        values, sums = add_blocks(SB[e, 1, m], b_a, OT[e, m // 2, m % 2], b_b)
        state = values.astype(BF16)
        valid_now = MASKS[VALID]
        turned = []
        for h in range(3):
            far = beside(state, h, split(sums[h:h + 1]))
            g = valid_now * nn(lanes2(DST[m, h], VL[l, m, h]), rows2(phi_q(l, m, h), far))
            turned.append(softmax_back(PF[l, m, 3 + h], g))
        keep_one(l, m, True, EARLY + HD, turned[0])
        keep_two(l, m, 2, EARLY, map_back(l, m, 2, turned[1], turned[2]))
        map_back(l, m, 1, TG[m], turned[0])
        offsets = OFF[m] + stack_rows(
            [jnp.zeros((1, PAIR), F32)] * 3 + [jnp.sum(t, axis=0, keepdims=True) for t in turned], 8)
        offsets = rows2(offsets, jnp.zeros((8, PAIR), F32))
        GRF[l, m // 2, m % 2, 3 * HD:] = offsets
        GRB[l, m // 2, m % 2, 3 * HD:] = offsets.astype(BF16)
        grad_v = GV[m, 0] + nt(lanes2(KL[l, m, 0], KL[l, m, 1]), diagonal(state))
        grad_v2 = (GV[m, 1] + nt(KL[l, m, 2], rows2(state[PAIR:], none_b))) * low
        MIX[m, :, 3 * PAIR:] = lanes2(grad_v, grad_v2).astype(BF16)

    def qkv_back(l, m):
        ACC[...] += nt(MIX[m], weight(3 * l + ATTN, m, slice(0, 5 * PAIR)))

    def sum_at(i):
        return (yc + 1 + i) % 2 * 2 + (cc + 1 + i // 2) % 2

    def part_rows(part):
        return slice(0, EARLY) if part == 0 else slice(EARLY, ROWS)

    def sum_sister(l, part, y):
        at = part_rows(part)
        return send(GRB.at[l, y, 1 - cc, at], RB1.at[l, y, at], rd_send.at[l, part, 0], rd_recv.at[l, part, y],
                    sister)

    def sum_square(l, part):
        at, bit = part_rows(part), batch % 2
        own, other = PB.at[l, yc, at], PB.at[l, 1 - yc, at]
        slot = SQ.at[l, bit, yc, at]
        sems = rd_send.at[l, part, 1], rd_recv.at[l, part, 2]
        return [send(other, slot, *sems, across), send(own, slot, *sems, partner(0)),
                send(other, slot, *sems, opposite)]

    def sum_wait(l, part, k, blocks, receives=True):
        ref = DBL.at[l, 0:blocks, part_rows(part)]
        copy = send(ref, ref, rd_send.at[l, part, k], rd_recv.at[l, part, k + 1], sister)
        copy.wait_send()
        if receives:
            copy.wait_recv()

    def sum_half(l, part, y):
        at = part_rows(part)
        sum_sister(l, part, y).wait_recv()
        PB[l, y, at] = (GRF[l, y, cc, at] + RB1[l, y, at].astype(F32)).astype(BF16)

    def sum_step(l, part, i):
        if i < 2:
            sum_sister(l, part, sum_at(i) // 2).start()
        if i == 2:
            sum_half(l, part, 1 - yc)
            copies = sum_square(l, part)
            copies[0].start()
            copies[2].start()

    def sum_chip(l, part):
        at = part_rows(part)
        sum_half(l, part, yc)
        SQ[l, batch % 2, yc, at] = PB[l, yc, at]
        sum_square(l, part)[1].start()

    def sum_z(l, part, k):
        ref = DBL.at[l, zc, part_rows(part)]
        return send(ref, ref, rd_send.at[l, part, 2], rd_recv.at[l, part, 3], (((zc + k) % 4) * 2 + xc, mp))

    def sum_double(l, part, k):
        at = part_rows(part)
        return send(DBL.at[l, 2 * k, at], DBL.at[l, 2 * k + 1, at], rd_send.at[l, part, 2],
                    rd_recv.at[l, part, 2 + k], partner(k))

    def sum_batch(l, part):
        at = part_rows(part)
        sum_wait(l, part, 1, 3)
        sum_wait(l, part, 0, 2, receives=False)
        total = sum(SQ[l, i, j, at].astype(F32) for i in range(2) for j in range(2))
        if gathers:
            DBL[l, zc, at] = total.astype(BF16)
            for k in (1, 2, 3):
                sum_z(l, part, k).start()
        else:
            DBL[l, 2, at] = total.astype(BF16)
            sum_double(l, part, 1).start()

    def sum_end(l, part):
        at = part_rows(part)
        if gathers:
            sum_wait(l, part, 2, 3)
            total = sum(DBL[l, z, at].astype(F32) for z in range(4))
        else:
            for k in range(1, steps):
                sum_double(l, part, k).wait()
                total = DBL[l, 2 * k, at].astype(F32) + DBL[l, 2 * k + 1, at].astype(F32)
                if k + 1 < steps:
                    DBL[l, 2 * k + 2, at] = total.astype(BF16)
                    sum_double(l, part, k + 1).start()
        ref, alone, beside_it = (gq_ref, 2, (0, 1)) if part == 0 else (gk_ref, 0, (1, 2))
        two, folded = total[:HD], total[HD:HD + HD // 2]
        ref[l, beside_it[0]] = two[:, :HD]
        ref[l, beside_it[1]] = pltpu.roll(two, HD, 1)[:, :HD]
        ref[l, alone, :HD // 2] = folded[:, :HD]
        ref[l, alone, HD // 2:] = pltpu.roll(folded, HD, 1)[:, :HD]
        if part == 1:
            offsets = total[EARLY:EARLY + 8]
            offsets = offsets - pltpu.roll(offsets, HD, 1)
            for i in range(6):
                (gqb_ref if i < 3 else gkb_ref)[i % 3, l:l + 1] = offsets[i:i + 1, :HD]

    cot_copy.wait()
    GRAD[...] = COT[...].astype(F32)
    N1[...] = COT[...]
    for l in reversed(range(LAYERS)):
        e = 2 + l
        above = l + 1 if l + 1 < LAYERS else None
        clear()
        for i in range(4):
            if l + 1 == LAYERS and i == (2 if gathers else 0):
                ready(CHUNKS - 1)
            mlp_back(l, i % 2 * 2 + (cc if i < 2 else 1 - cc))
        grad_mid = GRAD[...] + norm_back(NORMED[l, 1], SCALE[l, 1, :, :1], ACC[...])
        GRAD[...] = grad_mid
        N1[...] = grad_mid.astype(BF16)

        for j in range(2):
            for i in (2 * j, 2 * j + 1):
                attend_back_start(l, block_at(i))
            if above is None and j == 1:
                last_down(0, 2)
            for i in (2 * j, 2 * j + 1):
                ex_step(e, i, b_own, b_sis)
        if above is not None:
            sum_batch(above, 0)
            sum_batch(above, 1)
        for i in range(4):
            attend_back_local(l, sum_at(i))
        for i in range(2):
            sum_step(l, 0, i)
        if above is None:
            last_down(2, 2)
            last_end()
        for j in range(2):
            ex_forward(e, j)
        if above:
            sum_step(l, 0, 2)
            sum_chip(l, 0)
        ex_end(e)
        for group in ((0, 1), (2, 3)) if above else ((0, 1, 2, 3),):
            for i in group:
                attend_back_end(l, sum_at(i))
            for i in group:
                if above or i < 2:
                    sum_step(l, 1, i)
        if above:
            sum_chip(l, 1)
        else:
            sum_step(l, 0, 2)
            sum_chip(l, 0)
        clear()
        if l == 0:
            sum_batch(0, 0)
        for m in range(4):
            qkv_back(l, m)
        if l == 0:
            sum_batch(0, 1)
        if not above:
            sum_step(l, 1, 2)
            sum_chip(l, 1)
        GRAD[...] = GRAD[...] + norm_back(NORMED[l, 0], SCALE[l, 0, :, :1], ACC[...])
        N1[...] = GRAD[...].astype(BF16)
    GIN[...] = GRAD[...].astype(BF16)
    for e in range(2 * LAYERS):
        ex_drain(e)
    drain()
    for part in range(2):
        sum_end(1, part)
    sum_end(0, 0)
    sum_end(0, 1)


def hand_out(*refs):
    count = len(refs) // 2
    for source, target in zip(refs[:count], refs[count:]):
        target[...] = source[...]


def per_device(tokens, cotangent, seq_lengths, joined_qkv, attn_proj, mlp_up, mlp_down,
               query_map, query_bias, key_map, key_bias):
    n_batch, n_mp = lax.axis_size("batch"), lax.axis_size("mp")
    rows, width = tokens.shape
    slice_rows = joined_qkv.shape[1]
    heads = query_map.shape[1]
    assert n_mp == 4 and heads == 3 and rows == PAIR and query_map.shape[2] == HD
    assert n_batch & (n_batch - 1) == 0
    parts = 3
    gathers = n_batch == 8 and slice_rows % (16 * parts) == 0
    part_rows = width // (8 * parts)
    qkv, down = joined_qkv.transpose(0, 2, 1, 3), mlp_down.transpose(0, 2, 1)
    if gathers:
        cut = (LAYERS, parts, part_rows, width)
        frozen = (qkv, attn_proj, mlp_up.reshape(cut), down.reshape(cut))
    else:
        turned = jnp.concatenate([attn_proj[:, PAIR:], attn_proj[:, :PAIR]], 1).transpose(0, 2, 1)
        attn = jnp.concatenate([joined_qkv.reshape(LAYERS, slice_rows, -1), turned], 2)
        blocks = jnp.stack([attn, mlp_up, down], 1).reshape(CHUNKS, slice_rows, width)
        weights = lax.all_gather(blocks, "batch", axis=1, tiled=True)
        weights = lax.all_gather(weights, "mp", axis=1, tiled=True)
        frozen = (weights.reshape(CHUNKS, 2, 2, 4, 2, parts, part_rows, width),)

    steps = n_batch.bit_length() - 1
    vmem, dma = pltpu.VMEM, pltpu.SemaphoreType.DMA
    shapes = [(tokens.shape, BF16), (tokens.shape, BF16), (query_map.shape, F32), ((heads, LAYERS, HD), F32),
              (key_map.shape, F32), ((heads, LAYERS, HD), F32)]
    map_shapes = [query_map.shape, (heads, LAYERS, HD)] * 2
    scratch = [vmem(shape, BF16) for shape in map_shapes] + [pltpu.SMEM(seq_lengths.shape, jnp.int32)] + [
        vmem((CHUNKS, 2, 2, 4, 2, parts, part_rows, width), BF16),
        vmem((rows, width), BF16),
        vmem((rows, width), BF16),
        vmem(qkv.shape, BF16),
        vmem(attn_proj.shape, BF16),
        vmem((2, 2, LAYERS, ROWS, PAIR), BF16),
        vmem((LAYERS, 4, 3, 2 * PAIR, 2 * PAIR), BF16),
        vmem((LAYERS, 4, 8, PAIR), F32),
        vmem((rows, width), F32),
        vmem((LAYERS, 2, rows, width), F32),
        vmem((LAYERS, 2, rows, PAIR), F32),
        vmem((LAYERS, 4, rows, width), F32),
        vmem((4, rows, width), BF16),
        vmem((LAYERS, 4, rows, 5 * PAIR), BF16),
        vmem((LAYERS, 4, 3, rows, PAIR), BF16),
        vmem((LAYERS, 4, 3, rows, PAIR), BF16),
        vmem((LAYERS, 4, 3, rows, PAIR), BF16),
        vmem((LAYERS, 4, 6, rows, PAIR), F32),
        vmem((LAYERS, 4, 6, rows, PAIR), BF16),
        vmem((LAYERS, 4, 3, rows, PAIR), BF16),
        vmem((LAYERS, 4, 2, rows, PAIR), F32),
        vmem((LAYERS, 4, 2, rows, PAIR), F32),
        vmem((LAYERS, 4, 3, PAIR, PAIR), BF16),
        vmem((rows, width), BF16),
        vmem((rows, width), F32),
        vmem((rows, width), F32),
        vmem((rows, width), F32),
        vmem((4, 3, rows, PAIR), BF16),
        vmem((4, 3, rows, PAIR), BF16),
        vmem((4, 2, rows, PAIR), BF16),
        vmem((4, 3, rows, PAIR), BF16),
        vmem((4, 2, rows, PAIR), F32),
        vmem((4, rows, PAIR), F32),
        vmem((5, rows, rows), F32),
        vmem((2 * LAYERS, 2, 4, ROWS, PAIR), BF16),
        vmem((2 * LAYERS, 2, ROWS, PAIR), BF16),
        vmem((2 * LAYERS, 2, 2, ROWS, PAIR), BF16),
        vmem((4, rows, 5 * PAIR), BF16),
        vmem((4, 8, PAIR), F32),
        vmem((LAYERS, 2, 2, ROWS, PAIR), F32),
        vmem((LAYERS, 2, 2, ROWS, PAIR), BF16),
        vmem((LAYERS, 2, ROWS, PAIR), BF16),
        vmem((LAYERS, 2, ROWS, PAIR), BF16),
        vmem((LAYERS, 2, 2, ROWS, PAIR), BF16),
        vmem((LAYERS, 4 if gathers else 2 * steps, ROWS, PAIR), BF16),
        dma((1 if gathers else CHUNKS,)), dma((9,)),
        dma((7,)),
        dma((2 * LAYERS,)), dma((2 * LAYERS, 4)),
        dma((2 * LAYERS,)), dma((2 * LAYERS, 2, 2)),
        dma((LAYERS, 2, 3)), dma((LAYERS, 2, 4 if gathers else 3 + steps)),
        dma((2, 3, 2)), dma((CHUNKS, parts, 3)),
        dma((2,)), dma((CHUNKS,)),
        dma((CHUNKS + 2, 5)), dma((CHUNKS, 4, 2)),
        dma((CHUNKS,)), dma((CHUNKS,)),
    ]
    vmem_block, any_block = pl.BlockSpec(memory_space=pltpu.VMEM), pl.BlockSpec(memory_space=pl.ANY)
    shapes = [jax.ShapeDtypeStruct(*shape) for shape in shapes]
    results = pl.pallas_call(
        functools.partial(body, n_batch, gathers),
        out_shape=[pltpu.VMEM(shape.shape, shape.dtype) for shape in shapes],
        in_specs=[any_block] * (7 + len(frozen)),
        out_specs=[vmem_block] * 6,
        scratch_shapes=scratch,
        compiler_params=pltpu.CompilerParams(
            collective_id=0, has_side_effects=True, vmem_limit_bytes=62 * 2**20),
    )(seq_lengths, tokens, cotangent, query_map, query_bias.transpose(1, 0, 2), key_map,
      key_bias.transpose(1, 0, 2), *frozen)
    results = pl.pallas_call(
        hand_out,
        out_shape=shapes,
        in_specs=[vmem_block] * 6,
        out_specs=[vmem_block] * 6,
    )(*[pltpu.with_memory_space_constraint(result, pltpu.VMEM) for result in results])
    out, grad_in, qmap, qbias, kmap, kbias = results
    return out, grad_in, qmap, qbias.transpose(1, 0, 2), kmap, kbias.transpose(1, 0, 2)


def solution(mesh):
    return jax.shard_map(
        per_device,
        mesh=mesh,
        in_specs=(
            P(("batch", "mp"), None),
            P(("batch", "mp"), None),
            P("batch", None),
            P(None, "batch", None, "mp"),
            P(None, "mp", "batch"),
            P(None, "batch", "mp"),
            P(None, "mp", "batch"),
            P(None, "mp", None, None),
            P(None, "mp", None),
            P(None, "mp", None, None),
            P(None, "mp", None),
        ),
        out_specs=(
            P(("batch", "mp"), None),
            P(("batch", "mp"), None),
            P(None, "mp", None, None),
            P(None, "mp", None),
            P(None, "mp", None, None),
            P(None, "mp", None),
        ),
        check_vma=False,
    )
```

```python
import functools

import jax
import jax.numpy as jnp
from jax import lax
from jax.experimental import pallas as pl
from jax.experimental.pallas import tpu as pltpu
from jax.sharding import PartitionSpec as P

SPAN = 64
LAYERS = 2
EPS = 1e-05
F32, BF16 = jnp.float32, jnp.bfloat16
MESH = pl.DeviceIdType.MESH
ATTN, UP, DOWN = 0, 1, 2
CHUNKS = 3 * LAYERS
FIRST_LAG, LAST_LAG, START_LEAD = 2, 6, 6
TURNS = (1, 1, 0, 1, 1, 0)
HD = 64
PAIR = 2 * HD
EARLY = HD + HD // 2
ROWS = 3 * HD + 16


def nn(a, b):
    return lax.dot_general(a, b, (((1,), (0,)), ((), ())), preferred_element_type=F32)


def nt(a, b):
    return lax.dot_general(a, b, (((1,), (1,)), ((), ())), preferred_element_type=F32)


def tn(a, b):
    return lax.dot_general(a, b, (((0,), (0,)), ((), ())), preferred_element_type=F32)


def moments(x):
    mean = jnp.mean(x, axis=-1, keepdims=True)
    centered = x - mean
    scale = lax.rsqrt(jnp.mean(centered * centered, axis=-1, keepdims=True) + EPS)
    return centered * scale, scale


def norm_back(y, scale, g):
    mean_g = jnp.mean(g, axis=-1, keepdims=True)
    mean_gy = jnp.mean(g * y, axis=-1, keepdims=True)
    return scale * (g - mean_g - y * mean_gy)


GELU_C = 0.7978845608028654
GELU_A = 0.044715


def gelu_and_slope(x):
    square = x * x
    t = jnp.tanh(GELU_C * x * (1.0 + GELU_A * square))
    inner = GELU_C * (1.0 + 3.0 * GELU_A * square)
    half = 0.5 * (1.0 + t)
    return x * half, half + 0.5 * x * (1.0 - t * t) * inner


def split(x):
    high = x.astype(BF16)
    return high, (x - high.astype(F32)).astype(BF16)


def stack_rows(entries, rows):
    index = lax.broadcasted_iota(jnp.int32, (rows, entries[0].shape[1]), 0)
    out = jnp.zeros((rows, entries[0].shape[1]), F32)
    for i, entry in enumerate(entries):
        out = jnp.where(index == i, entry, out)
    return out


def lanes2(a, b):
    return jnp.concatenate([a, b], 1)


def rows2(a, b):
    return jnp.concatenate([a, b], 0)


def body(n_batch, gathers, *refs):
    seq_hbm, tok_hbm, cot_hbm, *map_hbm = refs[:7]
    frozen, refs = (refs[7:11], refs[11:]) if gathers else (refs[7:8], refs[8:])
    (OUT, GIN, gq_ref, gqb_ref, gk_ref, gkb_ref, qmap_ref, qbias_ref, kmap_ref, kbias_ref,
     seq_ref, G, TOK, COT, QKV, PROJ, MT, BD, BIAS, RES, NORMED, SCALE, SLOPE, ACT, TQ, VH, VL, KL, PF, PHI, PT, ATT, RD, CX,
     N1, ACC, LASTACC, GRAD, GNH, GC, NM, DST, GV, TG, MASKS, SB, CH, OT,
     MIX, OFF, GRF, GRB, RB1, PB, SQ, DBL,
     own_sem, in_sem, mt_sem, ex1_send, ex1_recv, ex2_send, ex2_recv, rd_send, rd_recv,
     z_send, z_recv, cross_send, far_send, first_recv, last_recv, core_send, core_recv) = refs
    rows, width = TOK.shape
    batch, mp = lax.axis_index("batch"), lax.axis_index("mp")
    yc, cc = mp // 2, mp % 2
    sister = (batch, yc * 2 + 1 - cc)
    across = (batch, (1 - yc) * 2 + cc)
    steps = n_batch.bit_length() - 1
    near_batch = batch + 1 - 2 * (batch % 2)
    opposite = (near_batch, (1 - yc) * 2 + cc)

    def partner(k):
        bit = (batch // (1 << k)) % 2
        return (batch + (1 - 2 * bit) * (1 << k), mp)

    def send(src, dst, send_sem, recv_sem, device):
        copy = pltpu.make_async_remote_copy(
            src_ref=src, dst_ref=dst, send_sem=send_sem, recv_sem=recv_sem,
            device_id=device, device_id_type=MESH)
        return copy

    if gathers:
        zc, xc = batch // 2, batch % 2
        greeted = [(((zc + k) % 4) * 2 + xc, mp) for k in (1, 2, 3)]
    else:
        greeted = [partner(k) for k in range(1, steps)]
    greeted += [partner(0), sister, across, opposite]
    barrier = pltpu.get_barrier_semaphore()
    for device in greeted:
        pl.semaphore_signal(barrier, inc=1, device_id=device, device_id_type=MESH)
    tok_copy = pltpu.make_async_copy(tok_hbm, TOK, in_sem.at[0])
    cot_copy = pltpu.make_async_copy(cot_hbm, COT, in_sem.at[1])
    seq_copy = pltpu.make_async_copy(seq_hbm, seq_ref, in_sem.at[8])
    map_copies = [pltpu.make_async_copy(source, target, in_sem.at[4 + i]) for i, (source, target) in enumerate(
        zip(map_hbm, (qmap_ref, qbias_ref, kmap_ref, kbias_ref)))]
    own_copies = []
    if gathers:
        x_side = (zc * 2 + 1 - xc, mp)
        z_up = (jnp.minimum(zc + 1, 3) * 2 + xc, mp)
        z_down = (jnp.maximum(zc - 1, 0) * 2 + xc, mp)
        qkv_hbm, proj_hbm, up_hbm, down_hbm = frozen
        qkv_copy = pltpu.make_async_copy(qkv_hbm, QKV, in_sem.at[2])
        proj_copy = pltpu.make_async_copy(proj_hbm, PROJ, in_sem.at[3])
        qkv_copy.start()
        proj_copy.start()
        tok_copy.start()
        for l in range(LAYERS):
            for part, ref in ((UP, up_hbm), (DOWN, down_hbm)):
                own_copies.append(pltpu.make_async_copy(
                    ref.at[l], G.at[3 * l + part, yc, cc, zc, xc], own_sem.at[0]))
    else:
        tok_copy.start()
        own_copies = [pltpu.make_async_copy(frozen[0].at[q], G.at[q], own_sem.at[q])
                      for q in range(CHUNKS)]
    for copy in own_copies:
        copy.start()
    cot_copy.start()
    for copy in [seq_copy] + map_copies:
        copy.start()

    if gathers:
        slice_rows = QKV.shape[2]
        eye = (lax.broadcasted_iota(jnp.int32, (slice_rows, slice_rows), 0)
               == lax.broadcasted_iota(jnp.int32, (slice_rows, slice_rows), 1)).astype(BF16)
        qkv_copy.wait()
        proj_copy.wait()
        for l in range(LAYERS):
            turned = nt(eye, PROJ[l])
            pieces = [QKV[l, i].astype(F32) for i in range(3)]
            block = jnp.concatenate(pieces + [turned[:, PAIR:], turned[:, :PAIR]], 1).astype(BF16)
            G[3 * l + ATTN, yc, cc, zc, xc] = block.reshape(G.shape[5:])

    seq_copy.wait()
    row0 = mp * rows
    spans = []
    end = jnp.int32(0)
    for s in range(seq_ref.shape[1]):
        length = seq_ref[0, s]
        spans.append((end, end + length, end + ((length + SPAN - 1) // SPAN) * SPAN))
        end = spans[-1][2]

    def owner(place):
        return sum((place >= stop).astype(jnp.int32) for _, _, stop in spans)

    def owner_at(place):
        return sum(jnp.where(place >= stop, 1, 0) for _, _, stop in spans)

    def same(a, b):
        return jnp.where(owner_at(a) == owner_at(b), 1.0, 0.0).astype(F32)

    row = lax.broadcasted_iota(jnp.int32, (rows, rows), 0) + row0
    col = lax.broadcasted_iota(jnp.int32, (rows, rows), 1) + row0
    own_row, own_col = owner(row), owner(col)
    valid = sum(((row >= a) & (row < b)).astype(F32) for a, b, _ in spans)
    MASKS[0] = ((col <= row) & (own_row == own_col)).astype(F32)
    MASKS[1] = ((row <= col) & (own_row == own_col)).astype(F32)
    MASKS[2] = valid
    came_in = jnp.where(mp > 0, owner_at(row0 - 1), -1)
    MASKS[3] = (own_row == came_in).astype(F32)
    MASKS[4] = (own_row == owner_at(row0 + rows - 1)).astype(F32)
    LOWER, UPPER, VALID, CONT, LAST = range(5)

    def last_of(y, c):
        return (y * 2 + c) * rows + rows - 1

    in_chip = same(last_of(yc, 0), last_of(yc, 1))
    first, second = (cc == 0), (cc == 1)
    f_own = jnp.where(second, 1.0, in_chip)
    f_sis = jnp.where(second, in_chip, 1.0)
    f_a = jnp.where(second, 1.0, 0.0)
    f_b = jnp.where(yc == 1, jnp.where(second, same(last_of(0, 1), last_of(1, 0)), 1.0), 0.0)
    before = same(last_of(0, 1), last_of(1, 0))
    b_own = jnp.where(first, 1.0, before)
    b_sis = jnp.where(first, before, 1.0)
    b_a = jnp.where(first, 1.0, 0.0)
    b_b = jnp.where(yc == 0, jnp.where(first, same(last_of(0, 0), last_of(0, 1)), 1.0), 0.0)

    lane = lax.broadcasted_iota(jnp.int32, (rows, PAIR), 1)
    low = (lane < HD).astype(F32)
    high = 1.0 - low
    left = lane < HD

    for copy in map_copies:
        copy.wait()
    for l in range(LAYERS):
        heads = [ref[l, h].astype(F32) for ref in (qmap_ref, kmap_ref) for h in range(3)]
        for t in range(3):
            MT[yc, cc, l, t * HD:(t + 1) * HD] = jnp.concatenate(
                [heads[2 * t], heads[2 * t + 1]], 1).astype(BF16)
        biases = [ref[h, l:l + 1].astype(F32) for ref in (qbias_ref, kbias_ref) for h in range(3)]
        MT[yc, cc, l, 3 * HD:] = stack_rows(
            [jnp.concatenate([b, -b], 1) for b in biases], 16).astype(BF16)

    pl.semaphore_wait(barrier, len(greeted))

    def maps_start():
        send(MT.at[yc, cc], MT.at[yc, cc], mt_sem.at[1], mt_sem.at[2], across).start()
        send(MT.at[yc, cc], MT.at[yc, cc], mt_sem.at[3], mt_sem.at[4], sister).start()

    def maps_forward():
        send(MT.at[1 - yc, cc], MT.at[1 - yc, cc], mt_sem.at[1], mt_sem.at[2], across).wait()
        send(MT.at[1 - yc, cc], MT.at[1 - yc, cc], mt_sem.at[5], mt_sem.at[6], sister).start()

    def maps_build():
        send(MT.at[yc, cc], MT.at[yc, 1 - cc], mt_sem.at[3], mt_sem.at[4], sister).wait()
        send(MT.at[1 - yc, cc], MT.at[1 - yc, 1 - cc], mt_sem.at[5], mt_sem.at[6], sister).wait()
        half = lax.broadcasted_iota(jnp.int32, (HD, PAIR), 1) < HD
        none = jnp.zeros((HD, PAIR), F32)

        def one(i, carry):
            l, m = i // 4, i % 4
            block = MT[m // 2, m % 2, l].astype(F32)
            for t in range(3):
                pair = block[t * HD:(t + 1) * HD]
                turned = pltpu.roll(pair, HD, 1)
                a = jnp.where(half, pair, -turned)
                b = jnp.where(half, turned, -pair)
                wide = jnp.concatenate(
                    [jnp.concatenate([a, none], 1), jnp.concatenate([none, b], 1)], 0).astype(BF16)
                BD[l, m, t, 0:PAIR] = wide
                BD[l, m, t, PAIR:2 * PAIR] = wide
            BIAS[l, m] = block[3 * HD:3 * HD + 8]
            return carry

        lax.fori_loop(0, 2 * 4, one, 0)

    if gathers:
        parts = (0, 1, 2)

        def turn(q, p):
            return (TURNS[q], 0, 1)[p]

        def near(q, p):
            return (x_side, across)[turn(q, p)]

        def far(q, p):
            return (across, x_side)[turn(q, p)]

        def single(q, p, z):
            return G.at[q, yc, cc, z, xc, p]

        def neighbour(q, p, z):
            return (G.at[q, yc, cc, z, 1 - xc, p], G.at[q, 1 - yc, cc, z, xc, p])[turn(q, p)]

        def pair_of(q, p, z):
            return (G.at[q, yc, cc, z, :, p], G.at[q, :, cc, z, xc, p])[turn(q, p)]

        def other_pair(q, p, z):
            return (G.at[q, 1 - yc, cc, z, :, p], G.at[q, :, cc, z, 1 - xc, p])[turn(q, p)]

        def early(q, p):
            return q == 0 or p == 0

        def z_unit(q, p, z):
            return single(q, p, z) if early(q, p) else pair_of(q, p, z)

        def arrived(ref, sem):
            send(ref, ref, core_send.at[0], sem, sister).wait_recv()

        def sent(ref, sem):
            send(ref, ref, sem, core_recv.at[0], sister).wait_send()

        def z_on(q, p, z, way, s):
            @pl.when((zc < 3) if way == 0 else (zc > 0))
            def _():
                send(z_unit(q, p, z), z_unit(q, p, z), z_send.at[way, s, 0 if early(q, p) else 1],
                     z_recv.at[q, p, (z - zc + (7, 5)[way]) % 4 - 1], (z_up, z_down)[way]).start()

        def near_sem(q, p, z):
            if p == 0:
                return first_recv.at[q, z]
            return first_recv.at[CHUNKS - 1 + p, z] if q == 0 else first_recv.at[q, 4]

        def to_near(q, p, z):
            send(single(q, p, z), single(q, p, z), cross_send.at[0 if early(q, p) else 1],
                 near_sem(q, p, z), near(q, p)).start()

        def to_far(q, p, z):
            send(pair_of(q, p, z), pair_of(q, p, z), far_send.at[q], last_recv.at[q, z],
                 far(q, p)).start()

        def to_sister(q, ref):
            send(ref, ref, core_send.at[q], core_recv.at[q], sister).start()

        def each_place(s, do):
            pl.when((s > 0) & (zc - s >= 0))(lambda: do(zc - s, 0))
            pl.when((s > 0) & (zc + s <= 3))(lambda: do(zc + s, 1))

        def have(q, p, z):
            if early(q, p):
                to_near(q, p, z)
            else:
                to_far(q, p, z)
                to_sister(q, pair_of(q, p, z))

        def gather_start(q):
            for p in (1, 2):
                if not early(q, p):
                    to_near(q, p, zc)

        def z_start(q):
            for p in parts:
                if p == 1 and not early(q, p):
                    arrived(G.at[q, 0, 0, 0, :, 0], first_recv.at[q, 4])
                for way in range(2):
                    z_on(q, p, zc, way, 0)
                have(q, p, zc)

        def along_z(q, s):
            def step(z, way):
                for p in parts:
                    arrived(z_unit(q, p, z), z_recv.at[q, p, (z - zc + 4) % 4 - 1])
                    z_on(q, p, z, way, s)
                    have(q, p, z)

            each_place(s, step)

        def across_first(q, s):
            def step(z, way):
                for p in parts if q == 0 else (0,):
                    arrived(neighbour(q, p, z), near_sem(q, p, z))
                    to_far(q, p, z)
                    to_sister(q, pair_of(q, p, z))

            pl.when(s == 0)(lambda: step(zc, None))
            each_place(s, step)

        def across_last(q, s):
            def step(z, way):
                arrived(G.at[q, 0, 0, 0], last_recv.at[q, z])
                for p in parts:
                    to_sister(q, other_pair(q, p, z))

            pl.when(s == 0)(lambda: step(zc, None))
            each_place(s, step)

        def later(k, s, lag, do):
            stages, steps = divmod(lag, 4)
            if 0 <= k - stages < CHUNKS:
                pl.when(s >= steps)(lambda: do(k - stages, s - steps))
            if steps and 0 <= k - stages - 1 < CHUNKS:
                pl.when(s < steps)(lambda: do(k - stages - 1, s + 4 - steps))

        start_step = -START_LEAD % 4
        ahead = (start_step + START_LEAD) // 4

        def comm(k, s):
            later(k, s, LAST_LAG, across_last)
            later(k, s, FIRST_LAG, across_first)
            if k < CHUNKS:
                along_z(k, s)
            if k == 0:
                pl.when(s == 1)(lambda: z_start(1))
            if (k + ahead) < CHUNKS:
                pl.when(s == start_step)(lambda: z_start(k + ahead))

        def ready(q):
            arrived(G.at[q, :, 1 - cc], core_recv.at[q])

        def drain():
            for way in range(2):
                for s in range(3):
                    @pl.when(((zc < 3) & (zc >= s)) if way == 0 else ((zc > 0) & (zc + s <= 3)))
                    def _():
                        sent(G.at[0:4, 0, 0, 0, :, 0], z_send.at[way, s, 0])
                        sent(G.at[0:5, 0, 0, 0, :, 0:2], z_send.at[way, s, 1])
            sent(G.at[0:4, 0, 0, :, :, 0], cross_send.at[0])
            sent(G.at[0:5, 0, 0, 0, :, 0], cross_send.at[1])
            for q in range(CHUNKS):
                sent(G.at[q, 0, 0], far_send.at[q])
                sent(G.at[q, :, 0], core_send.at[q])
    else:
        def gather_start(q):
            pass

        def ready(q):
            own_copies[q].wait()

        def drain():
            pass

    def weight(q, m, lanes=None):
        if lanes is None:
            return G[q, m // 2, m % 2].reshape(width, width)
        return G[q, m // 2, m % 2, :, :, :, :, lanes].reshape(width, -1)

    def add_blocks(a, ca, b, cb):
        a, b = a.astype(F32), b.astype(F32)
        values = ca * a[:3 * HD] + cb * b[:3 * HD]
        sums = (ca * (a[3 * HD:3 * HD + 8] + a[3 * HD + 8:])
                + cb * (b[3 * HD:3 * HD + 8] + b[3 * HD + 8:]))
        return values, sums

    def block_at(i):
        return (2 * (1 - cc) + i) % 4

    def ex_sister(e, m):
        return send(SB.at[e, 0, m], SB.at[e, 1, m], ex1_send.at[e], ex1_recv.at[e, m], sister)

    def ex_across(e, j):
        return send(CH.at[e, j], OT.at[e, cc, j], ex2_send.at[e], ex2_recv.at[e, 0, j], across)

    def ex_over(e, j):
        return send(OT.at[e, cc, j], OT.at[e, cc, j], ex2_send.at[e], ex2_recv.at[e, 1, j], sister)

    def ex_step(e, i, own, sis):
        m = block_at(i)
        ex_sister(e, m).start()

        def combine():
            ex_sister(e, m).wait_recv()
            values, sums = add_blocks(SB[e, 0, m], own, SB[e, 1, m], sis)
            CH[e, i - 2, 0:3 * HD] = values.astype(BF16)
            CH[e, i - 2, 3 * HD:] = rows2(*split(sums))
            ex_across(e, i - 2).start()

        if isinstance(i, int):
            if i >= 2:
                combine()
        else:
            pl.when(i >= 2)(combine)

    def ex_forward(e, j):
        ex_across(e, j).wait_recv()
        ex_over(e, j).start()

    def ex_end(e):
        for j in range(2):
            m = block_at(j)
            ex_sister(e, m).wait_recv()
            ref = OT.at[e, 1 - cc, j]
            send(ref, ref, ex2_send.at[e], ex2_recv.at[e, 1, j], sister).wait_recv()

    def ex_drain(e):
        four = SB.at[e, 0]
        for sem in (ex1_send.at[e], ex2_send.at[e]):
            send(four, four, sem, ex1_recv.at[e, 0], sister).wait_send()

    def softmax(u):
        e = jnp.exp(u - jnp.max(u, axis=-1, keepdims=True))
        return e / jnp.sum(e, axis=-1, keepdims=True)

    def phi_q(l, m, h):
        return PHI[l, m, h]

    def phi_k(l, m, h):
        return PHI[l, m, 3 + h]

    def place(x, columns, at_left):
        at = 0 if at_left else HD
        out = x * (high if at_left else low)
        for i, column in enumerate(columns):
            out = jnp.where(lane == at + i, column, out)
        return out

    def heads_of(pair, single_tile, columns):
        return [place(pair, columns[0], False), place(pair, columns[1], True), place(single_tile, columns[2], False)]

    def attend_features(l, m):
        mixed = nn(N1[...], weight(3 * l + ATTN, m, slice(0, 5 * PAIR)))
        hi, lo = split(mixed[:, :3 * PAIR])
        TQ[l, m, :, 0:3 * PAIR] = hi
        v01 = mixed[:, 3 * PAIR:4 * PAIR].astype(BF16)
        v2 = (mixed[:, 4 * PAIR:] * low).astype(BF16)
        TQ[l, m, :, 3 * PAIR:4 * PAIR] = v01
        TQ[l, m, :, 4 * PAIR:] = v2
        bias = BIAS[l, m]
        for t in range(3):
            tile = slice(t * PAIR, (t + 1) * PAIR)
            u = nn(lanes2(hi[:, tile], lo[:, tile]), BD[l, m, t])
            for e in range(2):
                h = 2 * t + e
                p = softmax(u[:, e * PAIR:(e + 1) * PAIR] + bias[h:h + 1])
                PF[l, m, h] = p
                p = p.astype(BF16)
                PHI[l, m, h] = p if h < 3 else (p.astype(F32) * MASKS[VALID]).astype(BF16)
        last = MASKS[LAST]
        for h, v in enumerate(heads_of(v01.astype(F32), v2.astype(F32), [(1.0, 1.0)] * 3)):
            VH[l, m, h] = v.astype(BF16)
            VL[l, m, h] = (v * last).astype(BF16)
        keys = [phi_k(l, m, h).astype(F32) * last for h in range(3)]
        sums = stack_rows([jnp.sum(k, axis=0, keepdims=True) for k in keys], 8)
        keys = [k.astype(BF16) for k in keys]
        for h in range(3):
            KL[l, m, h] = keys[h]
        two = tn(v01, lanes2(keys[0], keys[1]))
        one = tn(v2, keys[2])
        SB[l, 0, m, 0:HD] = two[:HD, :PAIR].astype(BF16)
        SB[l, 0, m, HD:PAIR] = two[HD:, PAIR:].astype(BF16)
        SB[l, 0, m, PAIR:3 * HD] = one[:HD].astype(BF16)
        SB[l, 0, m, 3 * HD:] = rows2(*split(sums))

    def features_step(l, i):
        attend_features(l, block_at(i))
        ex_step(l, i, f_own, f_sis)

    none_b = jnp.zeros((HD, PAIR), BF16)

    def beside(block, h, entries):
        state = block[h * HD:(h + 1) * HD]
        extra = stack_rows([entry.astype(F32) for entry in entries], HD).astype(BF16)
        return rows2(extra, state) if h == 1 else rows2(state, extra)

    def diagonal(block):
        return rows2(lanes2(block[:HD], none_b), lanes2(none_b, block[HD:PAIR]))

    def attend_out(l, m):
        values, sums = add_blocks(SB[l, 1, m], f_a, OT[l, m // 2, m % 2], f_b)
        carried = values.astype(BF16)
        for h in range(3):
            top, rest = split(sums[h:h + 1])
            CX[l, m, h] = beside(carried, h, [top, top, rest])
        valid_now, cont = MASKS[VALID], MASKS[CONT]
        lower = MASKS[LOWER]
        scores, inverse = [], []
        queries = [phi_q(l, m, h) for h in range(3)]
        for h in range(3):
            keys = phi_k(l, m, h)
            s = nt(queries[h], keys) * lower
            PT[l, m, h] = (nt(keys, queries[h]) * MASKS[UPPER]).astype(BF16)
            total = jnp.sum(s + queries[h].astype(F32) * (cont * sums[h:h + 1]), axis=-1, keepdims=True)
            inverse.append(1.0 / (total + (1.0 - valid_now)))
            scores.append(s.astype(BF16))
        v01 = TQ[l, m, :, 3 * PAIR:4 * PAIR].astype(F32)
        v2 = TQ[l, m, :, 4 * PAIR:]
        num = nn(lanes2(scores[0], scores[1]), rows2((v01 * low).astype(BF16), (v01 * high).astype(BF16)))
        num += cont * nt(lanes2(queries[0], queries[1]), diagonal(carried))
        num2 = nn(scores[2], v2) + cont * nt(queries[2], rows2(carried[PAIR:], none_b))
        rd = jnp.where(left, inverse[0], inverse[1])
        att, att2 = valid_now * num * rd, valid_now * num2 * inverse[2]
        RD[l, m, 0] = rd
        RD[l, m, 1] = inverse[2]
        ATT[l, m, 0] = att
        ATT[l, m, 1] = att2
        operand = lanes2(pltpu.roll(att2, HD, 1), att).astype(BF16)
        ACC[...] += nt(operand, weight(3 * l + ATTN, m, slice(4 * PAIR, 6 * PAIR)))

    def loop4(do, unroll=False):
        def one(m, carry):
            do(m)
            return carry

        lax.fori_loop(0, 4, one, 0, unroll=unroll)

    def normalize(l, place, x):
        y, scale = moments(x)
        NORMED[l, place] = y
        SCALE[l, place] = jnp.broadcast_to(scale, (rows, PAIR))
        N1[...] = y.astype(BF16)

    def attend_end(l):
        ACC[...] = jnp.zeros((rows, width), F32)
        loop4(functools.partial(attend_out, l))
        middle = RES[...] + ACC[...]
        RES[...] = middle
        normalize(l, 1, middle)

    def up(l, m):
        pre = nn(N1[...], weight(3 * l + UP, m))
        act, SLOPE[l, m] = gelu_and_slope(pre)
        ACT[m] = act.astype(BF16)

    def down(l, m):
        ACC[...] += nt(ACT[m], weight(3 * l + DOWN, m))

    def layer_end(l):
        after = RES[...] + ACC[...]
        RES[...] = after
        normalize(l + 1, 0, after)

    def last_down(first, count):
        total = 0.0 if first == 0 else LASTACC[...]
        for m in range(first, first + count):
            total += nt(ACT[m], weight(3 * (LAYERS - 1) + DOWN, m))
        LASTACC[...] = total

    def last_end():
        OUT[...] = (RES[...] + LASTACC[...]).astype(BF16)

    def clear():
        ACC[...] = jnp.zeros((rows, width), F32)

    def stage(k, at=(), steps=4):
        def one(s, carry):
            comm(k, s)
            for when, do in at:
                pl.when(s == when)(do)
            return carry

        lax.fori_loop(0, steps, one, 0)

    if gathers:
        blocks = G.at[0, 0, 0, :, 0]
        pltpu.make_async_copy(blocks, blocks, own_sem.at[0]).wait()
        for q in range(CHUNKS):
            gather_start(q)
        z_start(0)
    maps_start()
    tok_copy.wait()
    x0 = TOK[...].astype(F32)
    RES[...] = x0
    normalize(0, 0, x0)

    def features(l):
        loop4(functools.partial(features_step, l))

    def forward_states(l):
        ex_forward(l, 0)
        ex_forward(l, 1)

    def middle_part(l):
        ex_end(l)
        attend_end(l)

    def up_all(l):
        loop4(functools.partial(up, l))

    def down_all(l):
        clear()
        loop4(functools.partial(down, l))
        layer_end(l)

    if gathers:
        def attend_first():
            ready(0)
            features(0)

        def up_first():
            ready(1)
            up_all(0)

        def down_first():
            ready(2)
            down_all(0)

        def attend_second():
            ready(3)
            features(1)

        def up_second():
            ready(4)
            up_all(1)

        stage(0, at=[(3, maps_forward)])
        stage(1, at=[(0, maps_build)])
        stage(2, at=[(1, attend_first)])
        stage(3, at=[(0, lambda: forward_states(0)), (1, lambda: middle_part(0)), (2, up_first)])
        stage(4, at=[(1, down_first)])
        stage(5, at=[(1, attend_second), (2, lambda: forward_states(1)), (3, lambda: middle_part(1))])
        stage(6, at=[(3, up_second)])
        stage(7, steps=2)
    else:
        maps_forward()
        maps_build()
        for l in range(LAYERS):
            ready(3 * l + ATTN)
            features(l)
            forward_states(l)
            middle_part(l)
            ready(3 * l + UP)
            up_all(l)
            if l + 1 < LAYERS:
                ready(3 * l + DOWN)
                down_all(l)


    def mlp_back(l, m):
        grad_act = nn(N1[...], weight(3 * l + DOWN, m))
        grad_pre = (SLOPE[l, m] * grad_act).astype(BF16)
        ACC[...] += nt(grad_pre, weight(3 * l + UP, m))

    row_half = lax.broadcasted_iota(jnp.int32, (2 * PAIR, PAIR), 0) % PAIR < HD
    lane_half = lax.broadcasted_iota(jnp.int32, (2 * PAIR, PAIR), 1) < HD
    across_halves = (row_half != lane_half).astype(BF16)

    def attend_back_start(l, m):
        e = 2 + l
        grads = nn(N1[...], weight(3 * l + ATTN, m, slice(4 * PAIR, 6 * PAIR)))
        g01, g2 = grads[:, PAIR:], pltpu.roll(grads[:, :PAIR], HD, 1) * low
        valid_now, cont = MASKS[VALID], MASKS[CONT]
        s01, s2 = g01 * RD[l, m, 0], g2 * RD[l, m, 1]
        p01, p2 = s01 * ATT[l, m, 0], s2 * ATT[l, m, 1]
        dens = [-nn(lanes2(*split(p)), across_halves) for p in (p01, p2)]
        num01 = (s01 * valid_now).astype(BF16)
        num2 = (s2 * valid_now).astype(BF16)
        NM[m, 0] = num01
        NM[m, 1] = num2
        columns = []
        for d in dens:
            top = d.astype(BF16).astype(F32)
            columns.append((top, d - top, top))
        tiles = heads_of(num01.astype(F32), num2.astype(F32), [columns[0], columns[0], columns[1]])
        sums = []
        for h in range(3):
            GNH[m, h] = tiles[h].astype(BF16)
            counted = (tiles[h] * cont).astype(BF16)
            GC[m, h] = counted
            state = tn(counted, phi_q(l, m, h))
            keep, extra = (state[HD:], state[:8]) if h == 1 else (state[:HD], state[HD:HD + 8])
            SB[e, 0, m, h * HD:(h + 1) * HD] = keep.astype(BF16)
            sums.append(extra[0:1] + extra[1:2])
        SB[e, 0, m, 3 * HD:] = rows2(*split(stack_rows(sums, 8)))

    def softmax_back(p, g):
        return p * (g - jnp.sum(p * g, axis=-1, keepdims=True))

    def keep_maps(l, m, first, x):
        GRF[l, m // 2, m % 2, first:first + x.shape[0]] = x
        GRB[l, m // 2, m % 2, first:first + x.shape[0]] = x.astype(BF16)

    def keep_two(l, m, t, first, two):
        maps = tn(TQ[l, m, :, t * PAIR:(t + 1) * PAIR], two)
        a, b = maps[:HD, :PAIR], maps[HD:, PAIR:]
        keep_maps(l, m, first, jnp.where(left[:HD], a - pltpu.roll(a, HD, 1), pltpu.roll(b, HD, 1) - b))

    def keep_one(l, m, second, first, one):
        maps = tn(TQ[l, m, :, PAIR:2 * PAIR], one.astype(BF16))
        a = maps[HD:] if second else maps[:HD]
        a = a - pltpu.roll(a, HD, 1)
        keep_maps(l, m, first, jnp.where(left[:HD // 2], a[:HD // 2], -a[HD // 2:]))

    def map_back(l, m, t, a, b):
        two = lanes2(a, b).astype(BF16)
        MIX[m, :, t * PAIR:(t + 1) * PAIR] = nt(two, BD[l, m, t, 0:PAIR]).astype(BF16)
        return two

    def attend_back_local(l, m):
        lower, upper = MASKS[LOWER], MASKS[UPPER]
        turned = []
        for h in range(3):
            q, k = phi_q(l, m, h), phi_k(l, m, h)
            nums, vals = GNH[m, h], VH[l, m, h]
            ds = (nt(nums, vals) * lower).astype(BF16)
            DST[m, h] = (nt(vals, nums) * upper).astype(BF16)
            g = nn(lanes2(ds, GC[m, h]), rows2(k, CX[l, m, h]))
            turned.append(softmax_back(PF[l, m, h], g))
        num01 = NM[m, 0].astype(F32)
        GV[m, 0] = nn(lanes2(PT[l, m, 0], PT[l, m, 1]),
                      rows2((num01 * low).astype(BF16), (num01 * high).astype(BF16)))
        GV[m, 1] = nn(PT[l, m, 2], NM[m, 1])
        TG[m] = turned[2]
        OFF[m] = stack_rows([jnp.sum(t, axis=0, keepdims=True) for t in turned], 8)
        keep_two(l, m, 0, 0, map_back(l, m, 0, turned[0], turned[1]))
        keep_one(l, m, False, HD, turned[2])

    def attend_back_end(l, m):
        e = 2 + l
        values, sums = add_blocks(SB[e, 1, m], b_a, OT[e, m // 2, m % 2], b_b)
        state = values.astype(BF16)
        valid_now = MASKS[VALID]
        turned = []
        for h in range(3):
            far = beside(state, h, split(sums[h:h + 1]))
            g = valid_now * nn(lanes2(DST[m, h], VL[l, m, h]), rows2(phi_q(l, m, h), far))
            turned.append(softmax_back(PF[l, m, 3 + h], g))
        keep_one(l, m, True, EARLY + HD, turned[0])
        keep_two(l, m, 2, EARLY, map_back(l, m, 2, turned[1], turned[2]))
        map_back(l, m, 1, TG[m], turned[0])
        offsets = OFF[m] + stack_rows(
            [jnp.zeros((1, PAIR), F32)] * 3 + [jnp.sum(t, axis=0, keepdims=True) for t in turned], 8)
        offsets = rows2(offsets, jnp.zeros((8, PAIR), F32))
        GRF[l, m // 2, m % 2, 3 * HD:] = offsets
        GRB[l, m // 2, m % 2, 3 * HD:] = offsets.astype(BF16)
        grad_v = GV[m, 0] + nt(lanes2(KL[l, m, 0], KL[l, m, 1]), diagonal(state))
        grad_v2 = (GV[m, 1] + nt(KL[l, m, 2], rows2(state[PAIR:], none_b))) * low
        MIX[m, :, 3 * PAIR:] = lanes2(grad_v, grad_v2).astype(BF16)

    def qkv_back(l, m):
        ACC[...] += nt(MIX[m], weight(3 * l + ATTN, m, slice(0, 5 * PAIR)))

    def sum_at(i):
        return (yc + 1 + i) % 2 * 2 + (cc + 1 + i // 2) % 2

    def part_rows(part):
        return slice(0, EARLY) if part == 0 else slice(EARLY, ROWS)

    def sum_sister(l, part, y):
        at = part_rows(part)
        return send(GRB.at[l, y, 1 - cc, at], RB1.at[l, y, at], rd_send.at[l, part, 0], rd_recv.at[l, part, y],
                    sister)

    def sum_square(l, part):
        at, bit = part_rows(part), batch % 2
        own, other = PB.at[l, yc, at], PB.at[l, 1 - yc, at]
        slot = SQ.at[l, bit, yc, at]
        sems = rd_send.at[l, part, 1], rd_recv.at[l, part, 2]
        return [send(other, slot, *sems, across), send(own, slot, *sems, partner(0)),
                send(other, slot, *sems, opposite)]

    def sum_wait(l, part, k, blocks, receives=True):
        ref = DBL.at[l, 0:blocks, part_rows(part)]
        copy = send(ref, ref, rd_send.at[l, part, k], rd_recv.at[l, part, k + 1], sister)
        copy.wait_send()
        if receives:
            copy.wait_recv()

    def sum_half(l, part, y):
        at = part_rows(part)
        sum_sister(l, part, y).wait_recv()
        PB[l, y, at] = (GRF[l, y, cc, at] + RB1[l, y, at].astype(F32)).astype(BF16)

    def sum_step(l, part, i):
        if i < 2:
            sum_sister(l, part, sum_at(i) // 2).start()
        if i == 2:
            sum_half(l, part, 1 - yc)
            copies = sum_square(l, part)
            copies[0].start()
            copies[2].start()

    def sum_chip(l, part):
        at = part_rows(part)
        sum_half(l, part, yc)
        SQ[l, batch % 2, yc, at] = PB[l, yc, at]
        sum_square(l, part)[1].start()

    def sum_z(l, part, k):
        ref = DBL.at[l, zc, part_rows(part)]
        return send(ref, ref, rd_send.at[l, part, 2], rd_recv.at[l, part, 3], (((zc + k) % 4) * 2 + xc, mp))

    def sum_double(l, part, k):
        at = part_rows(part)
        return send(DBL.at[l, 2 * k, at], DBL.at[l, 2 * k + 1, at], rd_send.at[l, part, 2],
                    rd_recv.at[l, part, 2 + k], partner(k))

    def sum_batch(l, part):
        at = part_rows(part)
        sum_wait(l, part, 1, 3)
        sum_wait(l, part, 0, 2, receives=False)
        total = sum(SQ[l, i, j, at].astype(F32) for i in range(2) for j in range(2))
        if gathers:
            DBL[l, zc, at] = total.astype(BF16)
            for k in (1, 2, 3):
                sum_z(l, part, k).start()
        else:
            DBL[l, 2, at] = total.astype(BF16)
            sum_double(l, part, 1).start()

    def sum_end(l, part):
        at = part_rows(part)
        if gathers:
            sum_wait(l, part, 2, 3)
            total = sum(DBL[l, z, at].astype(F32) for z in range(4))
        else:
            for k in range(1, steps):
                sum_double(l, part, k).wait()
                total = DBL[l, 2 * k, at].astype(F32) + DBL[l, 2 * k + 1, at].astype(F32)
                if k + 1 < steps:
                    DBL[l, 2 * k + 2, at] = total.astype(BF16)
                    sum_double(l, part, k + 1).start()
        ref, alone, beside_it = (gq_ref, 2, (0, 1)) if part == 0 else (gk_ref, 0, (1, 2))
        two, folded = total[:HD], total[HD:HD + HD // 2]
        ref[l, beside_it[0]] = two[:, :HD]
        ref[l, beside_it[1]] = pltpu.roll(two, HD, 1)[:, :HD]
        ref[l, alone, :HD // 2] = folded[:, :HD]
        ref[l, alone, HD // 2:] = pltpu.roll(folded, HD, 1)[:, :HD]
        if part == 1:
            offsets = total[EARLY:EARLY + 8]
            offsets = offsets - pltpu.roll(offsets, HD, 1)
            for i in range(6):
                (gqb_ref if i < 3 else gkb_ref)[i % 3, l:l + 1] = offsets[i:i + 1, :HD]

    cot_copy.wait()
    GRAD[...] = COT[...].astype(F32)
    N1[...] = COT[...]
    for l in reversed(range(LAYERS)):
        e = 2 + l
        above = l + 1 if l + 1 < LAYERS else None
        clear()
        for i in range(4):
            if l + 1 == LAYERS and i == (2 if gathers else 0):
                ready(CHUNKS - 1)
            mlp_back(l, i % 2 * 2 + (cc if i < 2 else 1 - cc))
        grad_mid = GRAD[...] + norm_back(NORMED[l, 1], SCALE[l, 1, :, :1], ACC[...])
        GRAD[...] = grad_mid
        N1[...] = grad_mid.astype(BF16)

        for j in range(2):
            for i in (2 * j, 2 * j + 1):
                attend_back_start(l, block_at(i))
            if above is None and j == 1:
                last_down(0, 2)
            for i in (2 * j, 2 * j + 1):
                ex_step(e, i, b_own, b_sis)
        if above is not None:
            sum_batch(above, 0)
            sum_batch(above, 1)
        for i in range(4):
            attend_back_local(l, sum_at(i))
        for i in range(2):
            sum_step(l, 0, i)
        if above is None:
            last_down(2, 2)
            last_end()
        for j in range(2):
            ex_forward(e, j)
        if above:
            sum_step(l, 0, 2)
            sum_chip(l, 0)
        ex_end(e)
        for j in range(2):
            for i in (2 * j, 2 * j + 1):
                attend_back_end(l, sum_at(i))
            for i in (2 * j, 2 * j + 1):
                if above or i < 2:
                    sum_step(l, 1, i)
        if above:
            sum_chip(l, 1)
        else:
            sum_step(l, 0, 2)
            sum_chip(l, 0)
        clear()
        for m in range(4):
            qkv_back(l, m)
            if l == 0 and m == 0:
                sum_batch(0, 0)
        if l == 0:
            sum_batch(0, 1)
        if not above:
            sum_step(l, 1, 2)
            sum_chip(l, 1)
        GRAD[...] = GRAD[...] + norm_back(NORMED[l, 0], SCALE[l, 0, :, :1], ACC[...])
        N1[...] = GRAD[...].astype(BF16)
    GIN[...] = GRAD[...].astype(BF16)
    for e in range(2 * LAYERS):
        ex_drain(e)
    drain()
    for part in range(2):
        sum_end(1, part)
    sum_end(0, 0)
    sum_end(0, 1)


def hand_out(*refs):
    count = len(refs) // 2
    for source, target in zip(refs[:count], refs[count:]):
        target[...] = source[...]


def per_device(tokens, cotangent, seq_lengths, joined_qkv, attn_proj, mlp_up, mlp_down,
               query_map, query_bias, key_map, key_bias):
    n_batch, n_mp = lax.axis_size("batch"), lax.axis_size("mp")
    rows, width = tokens.shape
    slice_rows = joined_qkv.shape[1]
    heads = query_map.shape[1]
    assert n_mp == 4 and heads == 3 and rows == PAIR and query_map.shape[2] == HD
    assert n_batch & (n_batch - 1) == 0
    parts = 3
    gathers = n_batch == 8 and slice_rows % (16 * parts) == 0
    part_rows = width // (8 * parts)
    qkv, down = joined_qkv.transpose(0, 2, 1, 3), mlp_down.transpose(0, 2, 1)
    if gathers:
        cut = (LAYERS, parts, part_rows, width)
        frozen = (qkv, attn_proj, mlp_up.reshape(cut), down.reshape(cut))
    else:
        turned = jnp.concatenate([attn_proj[:, PAIR:], attn_proj[:, :PAIR]], 1).transpose(0, 2, 1)
        attn = jnp.concatenate([joined_qkv.reshape(LAYERS, slice_rows, -1), turned], 2)
        blocks = jnp.stack([attn, mlp_up, down], 1).reshape(CHUNKS, slice_rows, width)
        weights = lax.all_gather(blocks, "batch", axis=1, tiled=True)
        weights = lax.all_gather(weights, "mp", axis=1, tiled=True)
        frozen = (weights.reshape(CHUNKS, 2, 2, 4, 2, parts, part_rows, width),)

    steps = n_batch.bit_length() - 1
    vmem, dma = pltpu.VMEM, pltpu.SemaphoreType.DMA
    shapes = [(tokens.shape, BF16), (tokens.shape, BF16), (query_map.shape, F32), ((heads, LAYERS, HD), F32),
              (key_map.shape, F32), ((heads, LAYERS, HD), F32)]
    map_shapes = [query_map.shape, (heads, LAYERS, HD)] * 2
    scratch = [vmem(shape, BF16) for shape in map_shapes] + [pltpu.SMEM(seq_lengths.shape, jnp.int32)] + [
        vmem((CHUNKS, 2, 2, 4, 2, parts, part_rows, width), BF16),
        vmem((rows, width), BF16),
        vmem((rows, width), BF16),
        vmem(qkv.shape, BF16),
        vmem(attn_proj.shape, BF16),
        vmem((2, 2, LAYERS, ROWS, PAIR), BF16),
        vmem((LAYERS, 4, 3, 2 * PAIR, 2 * PAIR), BF16),
        vmem((LAYERS, 4, 8, PAIR), F32),
        vmem((rows, width), F32),
        vmem((LAYERS, 2, rows, width), F32),
        vmem((LAYERS, 2, rows, PAIR), F32),
        vmem((LAYERS, 4, rows, width), F32),
        vmem((4, rows, width), BF16),
        vmem((LAYERS, 4, rows, 5 * PAIR), BF16),
        vmem((LAYERS, 4, 3, rows, PAIR), BF16),
        vmem((LAYERS, 4, 3, rows, PAIR), BF16),
        vmem((LAYERS, 4, 3, rows, PAIR), BF16),
        vmem((LAYERS, 4, 6, rows, PAIR), F32),
        vmem((LAYERS, 4, 6, rows, PAIR), BF16),
        vmem((LAYERS, 4, 3, rows, PAIR), BF16),
        vmem((LAYERS, 4, 2, rows, PAIR), F32),
        vmem((LAYERS, 4, 2, rows, PAIR), F32),
        vmem((LAYERS, 4, 3, PAIR, PAIR), BF16),
        vmem((rows, width), BF16),
        vmem((rows, width), F32),
        vmem((rows, width), F32),
        vmem((rows, width), F32),
        vmem((4, 3, rows, PAIR), BF16),
        vmem((4, 3, rows, PAIR), BF16),
        vmem((4, 2, rows, PAIR), BF16),
        vmem((4, 3, rows, PAIR), BF16),
        vmem((4, 2, rows, PAIR), F32),
        vmem((4, rows, PAIR), F32),
        vmem((5, rows, rows), F32),
        vmem((2 * LAYERS, 2, 4, ROWS, PAIR), BF16),
        vmem((2 * LAYERS, 2, ROWS, PAIR), BF16),
        vmem((2 * LAYERS, 2, 2, ROWS, PAIR), BF16),
        vmem((4, rows, 5 * PAIR), BF16),
        vmem((4, 8, PAIR), F32),
        vmem((LAYERS, 2, 2, ROWS, PAIR), F32),
        vmem((LAYERS, 2, 2, ROWS, PAIR), BF16),
        vmem((LAYERS, 2, ROWS, PAIR), BF16),
        vmem((LAYERS, 2, ROWS, PAIR), BF16),
        vmem((LAYERS, 2, 2, ROWS, PAIR), BF16),
        vmem((LAYERS, 4 if gathers else 2 * steps, ROWS, PAIR), BF16),
        dma((1 if gathers else CHUNKS,)), dma((9,)),
        dma((7,)),
        dma((2 * LAYERS,)), dma((2 * LAYERS, 4)),
        dma((2 * LAYERS,)), dma((2 * LAYERS, 2, 2)),
        dma((LAYERS, 2, 3)), dma((LAYERS, 2, 4 if gathers else 3 + steps)),
        dma((2, 3, 2)), dma((CHUNKS, parts, 3)),
        dma((2,)), dma((CHUNKS,)),
        dma((CHUNKS + 2, 5)), dma((CHUNKS, 4)),
        dma((CHUNKS,)), dma((CHUNKS,)),
    ]
    vmem_block, any_block = pl.BlockSpec(memory_space=pltpu.VMEM), pl.BlockSpec(memory_space=pl.ANY)
    shapes = [jax.ShapeDtypeStruct(*shape) for shape in shapes]
    results = pl.pallas_call(
        functools.partial(body, n_batch, gathers),
        out_shape=[pltpu.VMEM(shape.shape, shape.dtype) for shape in shapes],
        in_specs=[any_block] * (7 + len(frozen)),
        out_specs=[vmem_block] * 6,
        scratch_shapes=scratch,
        compiler_params=pltpu.CompilerParams(
            collective_id=0, has_side_effects=True, vmem_limit_bytes=62 * 2**20),
    )(seq_lengths, tokens, cotangent, query_map, query_bias.transpose(1, 0, 2), key_map,
      key_bias.transpose(1, 0, 2), *frozen)
    results = pl.pallas_call(
        hand_out,
        out_shape=shapes,
        in_specs=[vmem_block] * 6,
        out_specs=[vmem_block] * 6,
    )(*[pltpu.with_memory_space_constraint(result, pltpu.VMEM) for result in results])
    out, grad_in, qmap, qbias, kmap, kbias = results
    return out, grad_in, qmap, qbias.transpose(1, 0, 2), kmap, kbias.transpose(1, 0, 2)


def solution(mesh):
    return jax.shard_map(
        per_device,
        mesh=mesh,
        in_specs=(
            P(("batch", "mp"), None),
            P(("batch", "mp"), None),
            P("batch", None),
            P(None, "batch", None, "mp"),
            P(None, "mp", "batch"),
            P(None, "batch", "mp"),
            P(None, "mp", "batch"),
            P(None, "mp", None, None),
            P(None, "mp", None),
            P(None, "mp", None, None),
            P(None, "mp", None),
        ),
        out_specs=(
            P(("batch", "mp"), None),
            P(("batch", "mp"), None),
            P(None, "mp", None, None),
            P(None, "mp", None),
            P(None, "mp", None, None),
            P(None, "mp", None),
        ),
        check_vma=False,
    )
```
